32 devices in a mesh: groups: 2 (over y), expert: 8 (over z, x), section: 2 (over core).
Axes of the slice: x: 2, y: 2, z: 4, core: 2. Of those that a mesh axis runs over, the one named last changes fastest.
Arguments:
- decoder_states: bfloat16 [32, 128, 1024], P(('groups', 'expert', 'section')), parts along dimension 0, may hold values from -8 to 8
- memory_keys: bfloat16 [32, 80, 1024], P(('groups', 'expert'), None, 'section'), parts along dimension 0, may hold values from -48 to 48
- memory_values: bfloat16 [32, 80, 1024], P(('groups', 'expert'), None, 'section'), parts along dimension 0, may hold values from -6 to 6
- source_lengths: int32 [32], P(('groups', 'expert', 'section')), parts along dimension 0, may hold values from 2 to 80
- target_lengths: int32 [32], P(('groups', 'expert')), parts along dimension 0, may hold values from 64 to 128
- routes: int32 [32, 128, 2], P(('groups', 'expert')), parts along dimension 0, may hold values from 0 to 3, all different within a row; in each aligned block of 256 rows (0 to 255, 256 to 511, ..., all dimensions but the last counted through in order) at most 192 rows name the same one
- attn_gain: float32 [1024], replicated, may hold values from 0.25 to 1.75
- ffn_gain: float32 [1024], replicated, may hold values from 0.25 to 1.75
- router: bfloat16 [1024, 4], replicated, may hold values from -0.1875 to 0.1875
- fc_in: bfloat16 [1024, 16384], P(None, ('expert', 'section')), may hold values from -0.1875 to 0.1875
- fc_out: bfloat16 [16384, 1024], P(('expert', 'section')), may hold values from -0.09375 to 0.09375
Outputs:
- mixed: bfloat16 [32, 128, 1024], P(('groups', 'expert', 'section')), parts along dimension 0
The draws below stay inside these ranges and needn't reach their ends.
There are 2 independent parts, one for each index of `groups`. The reference program is written for one: setup_inputs(seed, part) draws one part's arguments, and reference() takes and returns one part's arrays. A program takes and returns all parts, laid end to end along the dimension named above; an argument that names none is the same for every part. Nothing has to cross between parts.
Inputs may be any that keep to these rules, and one draw needn't show every extreme that they name: `routes`: in each block of 256 rows (the tokens of one index of expert) no expert is named by more than 192 pairs.
All inputs are finite; a program needn't handle non-finite values.
Results may differ from the reference program's by a relative error of at most 0.006.
Values may be sent and summed in bfloat16 or wider, within the bound.
No kernel may reach another device: no remote copies, remote signals or barrier semaphores. Data moves between devices by JAX's collectives and lax.ppermute only.
A program may use at most 64 MiB of HBM per device.

```python
import math
import jax
import jax.numpy as jnp
import numpy as np
from jax import lax

HEAD_DIM = 128
D = 1024
FF = 4096
EXPERTS = 4
SENT_DEV = 2
TLEN = 128
SLEN = 80
SENTS = 16
CAP = 192


def draw_memory_keys(key, part):
    key = jax.random.fold_in(key, 7)
    result = jnp.clip(jax.random.normal(key, (SENTS, SLEN, D), jnp.float32), -6.0, 6.0)
    return result.astype(jnp.bfloat16)


def draw_decoder_states(key, part):
    key = jax.random.fold_in(key, 11)
    result = jnp.clip(jax.random.normal(key, (SENTS, TLEN, D), jnp.float32), -6.0, 6.0)
    return result.astype(jnp.bfloat16)


def plant(array, stream_key, least, high):
    spot = [jax.random.randint(jax.random.fold_in(stream_key, axis), (), 0, length) for axis, length in enumerate(array.shape)]
    longest = array.shape.index(max(array.shape))
    next_to = spot[:longest] + [(spot[longest] + 1) % array.shape[longest]] + spot[longest + 1:]
    return array.at[tuple(spot)].set(least).at[tuple(next_to)].set(high)


def block_scale(stream_key, extent, cuts, least, high):
    level = 1.0
    for axis_at, parts in cuts:
        draws = jax.random.uniform(jax.random.fold_in(jax.random.fold_in(stream_key, 6), axis_at), (parts,), jnp.float32, least / len(cuts), high / len(cuts))
        level = level * jnp.repeat(jnp.exp(draws), extent[axis_at] // parts).reshape((-1,) + (1,) * (len(extent) - 1 - axis_at))
    return level


def deal_out(rng, own, number, rows, count, top, most, skew):
    order = jax.random.permutation(rng, count)
    crowded, ordinary = shares(count, rows * top, most, skew, True), shares(count, rows * top, most, skew, False)
    places = jnp.arange(count)

    def named(lengths, rotation):
        used = int((lengths > 0).sum())
        fixed = max(1, used // 4)
        moved = fixed + (places - fixed + rotation * (used - fixed)) % max(1, count - fixed)
        return jnp.zeros((count,), jnp.int32).at[order[jnp.where(places < fixed, places, moved)]].set(jnp.asarray(lengths, jnp.int32))

    lengths = jnp.where(number % 4 == 0, named(crowded, number // 4), named(ordinary, number - number // 4 - 1))
    mixed = jax.random.permutation(jax.random.fold_in(own, 3), count)
    donor, receiver = mixed[0:count // 2 * 2:2], mixed[1:count // 2 * 2:2]
    slack = jnp.minimum(lengths[donor] - 1, most - lengths[receiver]) // 2
    slack = jnp.where((donor == order[0]) | (receiver == order[0]) | (lengths[receiver] == 0), 0, jnp.maximum(slack, 0))
    moved = jax.random.randint(jax.random.fold_in(own, 4), (count // 2,), 0, 1 << 20) % (slack + 1)
    lengths = lengths.at[donor].add(-moved).at[receiver].add(moved)
    labels = jnp.searchsorted(jnp.cumsum(lengths), jnp.arange(rows * top), side="right").astype(jnp.int32)
    listing = labels.reshape(top, rows).T
    listing = listing[jax.random.permutation(jax.random.fold_in(own, 1), rows)]
    rotation = jax.random.randint(jax.random.fold_in(own, 2), (rows, 1), 0, top)
    return jnp.take_along_axis(listing, (jnp.arange(top)[None, :] + rotation) % top, axis=1)


def shares(count, total, bound, lean, full):
    loads = [(1 << 20) // math.isqrt(rank ** lean) + 1 for rank in range(1, count + 1)]
    largest = bound if full else min(bound, max(-(-total // count), total * loads[0] // sum(loads)))
    least = 1 if total - largest >= count - 1 else 0
    counts, surplus = [largest] + [least] * (count - 1), total - largest - least * (count - 1)
    while surplus > 0:
        movable = [i for i in range(1, count) if counts[i] < largest] or [i for i in range(1, count) if counts[i] < bound]
        mass, budget = sum([loads[i] for i in movable]), surplus
        for i in movable:
            more = min(bound - counts[i], max(1, budget * loads[i] // mass), surplus)
            counts[i] = counts[i] + more
            surplus = surplus - more
    return np.array(counts)


def noise(key, dims, scale, reach, split=(), held_as=jnp.bfloat16):
    drawn = scale * jax.random.normal(key, dims, jnp.float32)
    if split:
        drawn = drawn * block_scale(key, dims, split, -0.22, 0.18)
    return jnp.clip(drawn, -reach, reach).astype(held_as)


def setup_inputs(seed: int = 0, part: int = 0) -> dict:
    streams_of = jax.random.split(jax.random.key(seed), 12)
    part_keys = jax.random.split(jax.random.fold_in(streams_of[11], part), 12)
    decoder_states = draw_decoder_states(jax.random.fold_in(jax.random.fold_in(streams_of[11], part), 71), part)
    memory_keys = draw_memory_keys(jax.random.fold_in(jax.random.fold_in(streams_of[11], part), 71), part)
    memory_values = noise(part_keys[2], (SENTS, SLEN, D), 1.0, 6.0, ((0, 8), (2, 2)))
    source_lengths = plant(jax.random.randint(part_keys[3], (SENTS,), 2, SLEN + 1), jax.random.fold_in(part_keys[3], 1), 2, SLEN).astype(jnp.int32)
    target_lengths = plant(jax.random.randint(part_keys[4], (SENTS,), TLEN // 2, TLEN + 1), jax.random.fold_in(part_keys[4], 1), TLEN // 2, TLEN).astype(jnp.int32)
    routes_keys = jax.random.split(jax.random.fold_in(part_keys[5], 1), SENTS * TLEN // (SENT_DEV * TLEN))
    routes_turns = jax.random.permutation(jax.random.fold_in(part_keys[5], 3), SENTS * TLEN // (SENT_DEV * TLEN))
    routes = jax.vmap(lambda own, number: deal_out(jax.random.fold_in(part_keys[5], 2), own, number, SENT_DEV * TLEN, EXPERTS, 2, CAP, 2))(routes_keys, routes_turns).reshape((SENTS, TLEN, 2))
    attn_gain = jnp.clip(1.0 + 0.15 * jax.random.normal(streams_of[6], (D,), jnp.float32), 0.25, 1.75)
    ffn_gain = jnp.clip(1.0 + 0.15 * jax.random.normal(streams_of[7], (D,), jnp.float32), 0.25, 1.75)
    router = noise(streams_of[8], (D, EXPERTS), D ** -0.5, 0.1875)
    fc_in = noise(streams_of[9], (D, EXPERTS * FF), D ** -0.5, 0.1875, ((1, 16),))
    fc_out = noise(streams_of[10], (EXPERTS * FF, D), FF ** -0.5, 0.09375, ((0, 16),))
    return dict(decoder_states=decoder_states, memory_keys=memory_keys, memory_values=memory_values, source_lengths=source_lengths, target_lengths=target_lengths, routes=routes, attn_gain=attn_gain, ffn_gain=ffn_gain, router=router, fc_in=fc_in, fc_out=fc_out)


def layer_norm(values, gain):
    widened = values.astype(jnp.float32)
    centered = widened - lax.optimization_barrier(jnp.mean(widened, axis=-1, keepdims=True))
    spread = lax.optimization_barrier(jnp.mean(centered * centered, axis=-1, keepdims=True))
    return (centered * lax.rsqrt(spread + 1e-05) * gain.astype(jnp.float32)).astype(jnp.bfloat16)

def cross_attend(states, keys, values, source_lengths, gain):
    sents, positions, width = states.shape
    heads = width // HEAD_DIM
    queries = layer_norm(states, gain).reshape(sents, positions, heads, HEAD_DIM)
    key_heads = keys.reshape(sents, -1, heads, HEAD_DIM)
    value_heads = values.reshape(sents, -1, heads, HEAD_DIM)
    scores = jnp.einsum('sthd,skhd->shtk', queries.astype(jnp.float32), key_heads.astype(jnp.float32)) * HEAD_DIM ** (-0.5)
    valid = jnp.arange(key_heads.shape[1], dtype=jnp.int32)[None, :] < source_lengths[:, None]
    scores = jnp.where(valid[:, None, None, :], scores, -jnp.inf)
    expon = jnp.exp(scores - lax.optimization_barrier(jnp.max(scores, axis=-1, keepdims=True)))
    weights = (expon / lax.optimization_barrier(jnp.sum(expon, axis=-1, keepdims=True))).astype(jnp.bfloat16)
    attended = jnp.einsum('shtk,skhd->sthd', weights.astype(jnp.float32), value_heads.astype(jnp.float32))
    return attended.reshape(sents, positions, width)

def reference(decoder_states, memory_keys, memory_values, source_lengths, target_lengths, routes, attn_gain, ffn_gain, router, fc_in, fc_out):
    attended = cross_attend(decoder_states, memory_keys, memory_values, source_lengths, attn_gain)
    state = (decoder_states.astype(jnp.float32) + attended).astype(jnp.bfloat16)
    normed = layer_norm(state, ffn_gain)
    blocks = SENTS // SENT_DEV
    per_block = SENT_DEV * TLEN
    tok_rows = normed.reshape(blocks * per_block, D)
    chosen_ids = routes.reshape(blocks, per_block, 2)
    logits = jnp.dot(tok_rows, router, preferred_element_type=jnp.float32).reshape(blocks, per_block, EXPERTS)
    onehot = chosen_ids[..., None] == jnp.arange(EXPERTS, dtype=jnp.int32)
    chosen = lax.optimization_barrier(jnp.sum(jnp.where(onehot, logits[:, :, None, :], 0.0), axis=-1))
    first = jax.nn.sigmoid(chosen[..., 0] - chosen[..., 1])
    gates = jnp.stack([first, 1.0 - first], axis=-1)
    live = (jnp.arange(TLEN, dtype=jnp.int32)[None, :] < target_lengths[:, None]).reshape(blocks, per_block)
    flags = onehot.reshape(blocks, per_block * 2, EXPERTS).astype(jnp.int32)
    earlier = jnp.cumsum(flags, axis=1) - flags
    slot = lax.optimization_barrier(jnp.sum(flags * earlier, axis=-1)).reshape(blocks, per_block, 2)
    block_ids = jnp.arange(blocks, dtype=jnp.int32)[:, None, None]
    row_ids = jnp.broadcast_to((block_ids[:, :, 0] * per_block + jnp.arange(per_block, dtype=jnp.int32)[None, :])[:, :, None], (blocks, per_block, 2))
    position = (chosen_ids * blocks + block_ids) * CAP + slot
    dump_index = EXPERTS * blocks * CAP
    target = jnp.where(live[..., None], position, dump_index).astype(jnp.int32)
    table = jnp.full((dump_index + 1,), blocks * per_block, jnp.int32).at[target.reshape(-1)].set(row_ids.reshape(-1))
    table = table[:dump_index].reshape(EXPERTS, blocks * CAP)
    padded = jnp.concatenate([tok_rows, jnp.zeros((1, D), jnp.bfloat16)], axis=0)

    def run_expert(index):
        picked = padded[table[index]]
        first_w = lax.dynamic_slice_in_dim(fc_in, (index * FF).astype(jnp.int32), FF, 1)
        second_w = lax.dynamic_slice_in_dim(fc_out, (index * FF).astype(jnp.int32), FF, 0)
        hidden = jax.nn.relu(jnp.dot(picked, first_w, preferred_element_type=jnp.float32)).astype(jnp.bfloat16)
        return jnp.dot(hidden, second_w, preferred_element_type=jnp.float32)
    outputs = lax.map(run_expert, jnp.arange(EXPERTS, dtype=jnp.int32)).reshape(EXPERTS * blocks * CAP, D)
    fetched = outputs[jnp.where(live[..., None], position, 0).astype(jnp.int32)]
    weight = gates * live[..., None].astype(jnp.float32)
    combined = lax.optimization_barrier(jnp.sum(weight[..., None] * fetched, axis=2))
    mixed = state.astype(jnp.float32) + combined.reshape(SENTS, TLEN, D)
    return mixed.astype(jnp.bfloat16)
```

```python
import functools

import jax
import jax.numpy as jnp
from jax import lax
from jax.experimental import pallas as pl
from jax.experimental.pallas import tpu as pltpu
from jax.sharding import PartitionSpec as P

HEAD_DIM = 128


def layer_norm(values, gain):
    centered = values - jnp.mean(values, axis=-1, keepdims=True)
    spread = jnp.mean(centered * centered, axis=-1, keepdims=True)
    return (centered * lax.rsqrt(spread + 1e-05) * gain).astype(jnp.bfloat16)


def attend_kernel(
    core_ref, length_ref, x_ref, own_ref, other_ref, again_ref, fgain_ref, state_ref, normed_ref, query_ref
):
    half = own_ref.shape[-1]
    widened = x_ref[...].astype(jnp.float32)
    query_ref[...] = layer_norm(widened, again_ref[...])
    core = core_ref[0]
    keys_seen = own_ref.shape[1]
    valid = lax.broadcasted_iota(jnp.int32, (1, keys_seen), 1) < length_ref[0]
    for part, memory in ((core, own_ref), (1 - core, other_ref)):
        for head in range(half // HEAD_DIM):
            local_at = head * HEAD_DIM
            at = pl.multiple_of(part * half + local_at, HEAD_DIM)
            span = pl.ds(at, HEAD_DIM)
            scores = lax.dot_general(
                query_ref[:, span],
                memory[0, :, local_at : local_at + HEAD_DIM],
                (((1,), (1,)), ((), ())),
                preferred_element_type=jnp.float32,
            ) * HEAD_DIM ** (-0.5)
            scores = jnp.where(valid, scores, -jnp.inf)
            expon = jnp.exp(scores - jnp.max(scores, axis=-1, keepdims=True))
            weights = (expon / jnp.sum(expon, axis=-1, keepdims=True)).astype(jnp.bfloat16)
            attended = jnp.dot(
                weights,
                memory[1, :, local_at : local_at + HEAD_DIM],
                preferred_element_type=jnp.float32,
            )
            state_ref[:, span] = (x_ref[:, span].astype(jnp.float32) + attended).astype(
                jnp.bfloat16
            )
    normed_ref[...] = layer_norm(state_ref[...].astype(jnp.float32), fgain_ref[...])


def attend(decoder_states, memory_keys, memory_values, source_lengths, attn_gain, ffn_gain):
    full_len, width = decoder_states.shape[1:]
    core = lax.axis_index("section")
    memory = jnp.stack([memory_keys, memory_values], axis=1)
    own = lax.dynamic_index_in_dim(memory, core, 0, keepdims=False)
    other = lax.ppermute(
        lax.dynamic_index_in_dim(memory, 1 - core, 0, keepdims=False), "section", [(0, 1), (1, 0)]
    )
    vmem = pl.BlockSpec(memory_space=pltpu.VMEM)
    smem = pl.BlockSpec(memory_space=pltpu.SMEM)
    shape = jax.ShapeDtypeStruct((full_len, width), jnp.bfloat16)
    return pl.pallas_call(
        attend_kernel,
        out_shape=(shape, shape),
        in_specs=[smem, smem, vmem, vmem, vmem, vmem, vmem],
        out_specs=(vmem, vmem),
        scratch_shapes=[pltpu.VMEM((full_len, width), jnp.bfloat16)],
        compiler_params=pltpu.CompilerParams(vmem_limit_bytes=16 * 2**20),
        name="attend",
    )(
        core.reshape(1),
        source_lengths,
        decoder_states[0],
        own,
        other,
        attn_gain[None],
        ffn_gain[None],
    )


def dense_kernel(expert_ref, codes_ref, x_ref, router_ref, in_ref, out_ref, result_ref):
    expert = expert_ref[0]
    experts_count = router_ref.shape[1]
    sents, full_len = codes_ref.shape[1:]
    rows = x_ref[...]
    hidden = jnp.dot(rows, in_ref[...], preferred_element_type=jnp.float32)
    hidden = jnp.maximum(hidden, 0.0).astype(jnp.bfloat16)
    produced = jnp.dot(hidden, out_ref[...], preferred_element_type=jnp.float32)
    logits = jnp.dot(rows, router_ref[...], preferred_element_type=jnp.float32)
    names = lax.broadcasted_iota(jnp.int32, (full_len, experts_count), 1)
    for sent in range(sents):
        at = slice(sent * full_len, (sent + 1) * full_len)
        code = codes_ref[0, sent : sent + 1, :].astype(jnp.float32)
        code = jnp.broadcast_to(code, (full_len, full_len)).T[:, :1].astype(jnp.int32)
        live = code >= 0
        first_id = code // experts_count
        second_id = code - first_id * experts_count
        chosen = [
            jnp.sum(jnp.where(names == ids, logits[at], 0.0), axis=-1, keepdims=True)
            for ids in (first_id, second_id)
        ]
        first = jax.nn.sigmoid(chosen[0] - chosen[1])
        weight = jnp.where(first_id == expert, first, 0.0) + jnp.where(
            second_id == expert, 1.0 - first, 0.0
        )
        weight = jnp.where(live, weight, 0.0)
        result_ref[at] = (weight * produced[at]).astype(jnp.bfloat16)


def dense_experts(normed, target_lengths, routes, router, fc_in, fc_out):
    full_len, width = normed.shape
    experts_count = router.shape[1]
    owners = lax.axis_size("expert")
    live = jnp.arange(full_len, dtype=jnp.int32)[None, :] < target_lengths[:, None]
    codes = jnp.where(live, routes[:, :, 0] * experts_count + routes[:, :, 1], -1)
    codes = lax.all_gather(codes, "expert", axis=0, tiled=True)
    rows = lax.all_gather(normed, ("expert", "section"), axis=0, tiled=True)
    tile = 4 * full_len
    steps = rows.shape[0] // tile
    codes = codes.reshape(steps, tile // full_len, full_len)
    expert = lax.axis_index("expert") // (owners // experts_count)
    whole = lambda i: (0, 0)
    gated = pl.pallas_call(
        dense_kernel,
        grid=(steps,),
        out_shape=jax.ShapeDtypeStruct(rows.shape, jnp.bfloat16),
        in_specs=[
            pl.BlockSpec(memory_space=pltpu.SMEM),
            pl.BlockSpec((1,) + codes.shape[1:], lambda i: (i, 0, 0)),
            pl.BlockSpec((tile, width), lambda i: (i, 0)),
            pl.BlockSpec(router.shape, whole),
            pl.BlockSpec(fc_in.shape, whole),
            pl.BlockSpec(fc_out.shape, whole),
        ],
        out_specs=pl.BlockSpec((tile, width), lambda i: (i, 0)),
        compiler_params=pltpu.CompilerParams(vmem_limit_bytes=40 * 2**20),
        name="dense_experts",
    )(expert.reshape(1), codes, rows, router, fc_in, fc_out)
    return lax.psum_scatter(gated, ("expert", "section"), scatter_dimension=0, tiled=True)


def expert_apply(slot_rows, fc_in, fc_out):
    width = slot_rows.shape[-1]
    flat_rows = slot_rows.reshape(-1, width)
    hidden = jax.nn.relu(jnp.dot(flat_rows, fc_in, preferred_element_type=jnp.float32)).astype(
        jnp.bfloat16
    )
    produced = jnp.dot(hidden, fc_out, preferred_element_type=jnp.float32)
    return produced.reshape(slot_rows.shape[0], slot_rows.shape[1], width)


def sparse_experts(normed, target_lengths, routes, router, fc_in, fc_out, capacity):
    full_len, width = normed.shape
    all_normed = lax.all_gather(normed[None], "section", axis=0, tiled=True)
    block_sents = all_normed.shape[0]
    block_rows = block_sents * full_len
    tok_rows = all_normed.reshape(block_rows, width)
    owners = lax.axis_size("expert")
    experts_count = owners // 2
    chosen_ids = routes.reshape(block_rows, 2)
    logits = jnp.dot(tok_rows, router, preferred_element_type=jnp.float32)
    onehot = chosen_ids[:, :, None] == jnp.arange(experts_count, dtype=jnp.int32)
    chosen = jnp.sum(jnp.where(onehot, logits[:, None, :], 0.0), axis=-1)
    first = jax.nn.sigmoid(chosen[:, 0] - chosen[:, 1])
    gates = jnp.stack([first, 1.0 - first], axis=-1)
    live = (jnp.arange(full_len, dtype=jnp.int32)[None, :] < target_lengths[:, None]).reshape(
        block_rows
    )
    flags = onehot.reshape(block_rows * 2, experts_count).astype(jnp.int32)
    earlier = jnp.cumsum(flags, axis=0) - flags
    slot = jnp.sum(flags * earlier, axis=-1).reshape(block_rows, 2)
    position = chosen_ids * capacity + slot
    dump_index = experts_count * capacity
    target = jnp.where(live[:, None], position, dump_index)
    row_ids = jnp.broadcast_to(jnp.arange(block_rows, dtype=jnp.int32)[:, None], (block_rows, 2))
    table = (
        jnp.full((dump_index + 1,), block_rows, jnp.int32)
        .at[target.reshape(-1)]
        .set(row_ids.reshape(-1))[:dump_index]
    )
    padded = jnp.concatenate([tok_rows, jnp.zeros((1, width), jnp.bfloat16)], axis=0)
    slot_buffer = padded[table].reshape(experts_count, capacity, width)
    outgoing = jnp.repeat(slot_buffer, 2, axis=0)
    returned = lax.all_to_all(
        expert_apply(
            lax.all_to_all(outgoing, "expert", split_axis=0, concat_axis=0, tiled=True),
            fc_in,
            fc_out,
        ).astype(jnp.bfloat16),
        "expert",
        split_axis=0,
        concat_axis=0,
        tiled=True,
    ).astype(jnp.float32)
    partial_value = jnp.sum(returned.reshape(experts_count, 2, capacity, width), axis=1)
    fetched = partial_value.reshape(dump_index, width)[jnp.where(live[:, None], position, 0)]
    weight = gates * live[:, None].astype(jnp.float32)
    contrib = jnp.sum(weight[:, :, None] * fetched, axis=1).reshape(block_sents, full_len, width)
    summed = lax.psum_scatter(contrib, "section", scatter_dimension=0, tiled=True)
    return summed[0]


def local(
    decoder_states,
    memory_keys,
    memory_values,
    source_lengths,
    target_lengths,
    routes,
    attn_gain,
    ffn_gain,
    router,
    fc_in,
    fc_out,
):
    state, normed = attend(
        decoder_states, memory_keys, memory_values, source_lengths, attn_gain, ffn_gain
    )
    block_rows = routes.shape[0] * routes.shape[1]
    experts_count = router.shape[1]
    capacity = 2 * max(1, 3 * block_rows // (2 * experts_count))
    expert_args = (normed, target_lengths, routes, router, fc_in, fc_out)
    if 2 * capacity >= block_rows:
        combined = dense_experts(*expert_args)
    else:
        combined = sparse_experts(*expert_args, capacity)
    return (state.astype(jnp.float32) + combined.astype(jnp.float32)).astype(jnp.bfloat16)[None]


def solution(mesh):
    placed = (
        P(("groups", "expert", "section"), None, None),
        P(("groups", "expert"), None, "section"),
        P(("groups", "expert"), None, "section"),
        P(("groups", "expert", "section")),
        P(("groups", "expert")),
        P(("groups", "expert"), None, None),
        P(),
        P(),
        P(),
        P(None, ("expert", "section")),
        P(("expert", "section"), None),
    )
    return jax.shard_map(
        local,
        mesh=mesh,
        in_specs=placed,
        out_specs=P(("groups", "expert", "section"), None, None),
        check_vma=False,
    )
```

```python
import functools

import jax
import jax.numpy as jnp
from jax import lax
from jax.experimental import pallas as pl
from jax.experimental.pallas import tpu as pltpu
from jax.sharding import PartitionSpec as P

HEAD_DIM = 128


def layer_norm(values, gain):
    centered = values - jnp.mean(values, axis=-1, keepdims=True)
    spread = jnp.mean(centered * centered, axis=-1, keepdims=True)
    return (centered * lax.rsqrt(spread + 1e-05) * gain).astype(jnp.bfloat16)


VMEM = pl.BlockSpec(memory_space=pltpu.VMEM)
SMEM = pl.BlockSpec(memory_space=pltpu.SMEM)


def call(kernel, name, outs, scalars, arrays, scratch=(), vmem_mib=24, cost=None):
    return pl.pallas_call(
        kernel,
        out_shape=tuple(jax.ShapeDtypeStruct(*out) for out in outs),
        in_specs=[SMEM] * len(scalars) + [VMEM] * len(arrays),
        out_specs=(VMEM,) * len(outs),
        scratch_shapes=list(scratch),
        compiler_params=pltpu.CompilerParams(vmem_limit_bytes=vmem_mib * 2**20),
        cost_estimate=cost,
        name=name,
    )(*scalars, *arrays)


def part_of(part, half):
    return pl.ds(pl.multiple_of(part * half, half), half)


def attend_kernel(
    core_ref,
    source_ref,
    target_ref,
    x_ref,
    own_ref,
    other_ref,
    again_ref,
    fgain_ref,
    router_ref,
    routes_ref,
    state_ref,
    keep_ref,
    send_ref,
    gates_ref,
    scratch_ref,
):
    full_len = x_ref.shape[0]
    half = own_ref.shape[-1]
    widened = x_ref[...].astype(jnp.float32)
    scratch_ref[...] = layer_norm(widened, again_ref[...])
    core = core_ref[0]
    keys_seen = own_ref.shape[1]
    valid = lax.broadcasted_iota(jnp.int32, (1, keys_seen), 1) < source_ref[0]
    for part, memory in ((core, own_ref), (1 - core, other_ref)):
        for head in range(half // HEAD_DIM):
            at = head * HEAD_DIM
            span = pl.ds(pl.multiple_of(part * half + at, HEAD_DIM), HEAD_DIM)
            scores = lax.dot_general(
                scratch_ref[:, span],
                memory[0, :, at : at + HEAD_DIM],
                (((1,), (1,)), ((), ())),
                preferred_element_type=jnp.float32,
            ) * HEAD_DIM ** (-0.5)
            scores = jnp.where(valid, scores, -jnp.inf)
            expon = jnp.exp(scores - jnp.max(scores, axis=-1, keepdims=True))
            weights = (expon / jnp.sum(expon, axis=-1, keepdims=True)).astype(jnp.bfloat16)
            attended = jnp.dot(
                weights, memory[1, :, at : at + HEAD_DIM], preferred_element_type=jnp.float32
            )
            state_ref[:, span] = (x_ref[:, span].astype(jnp.float32) + attended).astype(
                jnp.bfloat16
            )
    scratch_ref[...] = layer_norm(state_ref[...].astype(jnp.float32), fgain_ref[...])
    keep_ref[...] = scratch_ref[:, part_of(core, half)]
    send_ref[...] = scratch_ref[:, part_of(1 - core, half)]
    logits = lax.dot_general(
        router_ref[...],
        scratch_ref[...],
        (((1,), (1,)), ((), ())),
        preferred_element_type=jnp.float32,
    )
    names = lax.broadcasted_iota(jnp.int32, logits.shape, 0)
    routes = routes_ref[core]
    chosen = [
        jnp.sum(jnp.where(names == routes[k : k + 1], logits, 0.0), axis=0, keepdims=True)
        for k in range(2)
    ]
    first = jax.nn.sigmoid(chosen[0] - chosen[1])
    live = lax.broadcasted_iota(jnp.int32, (1, full_len), 1) < target_ref[core]
    gates_ref[0:1] = jnp.where(live, first, 0.0)
    gates_ref[1:2] = jnp.where(live, 1.0 - first, 0.0)


def slots_of(routes_ref, experts_count):
    sents, _, full_len = routes_ref.shape
    rows = sents * full_len
    ids = lax.broadcasted_iota(jnp.int32, (max(8, experts_count), full_len), 0)
    named = jnp.concatenate(
        [
            jnp.where((ids == routes_ref[s, 0:1]) | (ids == routes_ref[s, 1:2]), 1.0, 0.0)
            for s in range(sents)
        ],
        axis=1,
    )
    before = lax.broadcasted_iota(jnp.int32, (rows, rows), 0) < lax.broadcasted_iota(
        jnp.int32, (rows, rows), 1
    )
    earlier = jnp.dot(
        named.astype(jnp.bfloat16),
        jnp.where(before, 1.0, 0.0).astype(jnp.bfloat16),
        preferred_element_type=jnp.float32,
    )
    return named > 0.0, earlier


def select_kernel(core_ref, line_ref, routes_ref, own_ref, other_ref, *rest):
    pieces, block_ref = rest[:-1], rest[-1]
    experts_count = len(pieces)
    full_len = own_ref.shape[0]
    capacity = pieces[0].shape[0]
    core = core_ref[0]
    block_ref[part_of(core, full_len)] = own_ref[...]
    block_ref[part_of(1 - core, full_len)] = other_ref[...]
    named, earlier = slots_of(routes_ref, experts_count)
    slot = jnp.where(named, earlier, -1.0)
    ids = lax.broadcasted_iota(jnp.int32, slot.shape, 0)
    numbers = lax.broadcasted_iota(jnp.int32, (capacity, slot.shape[1]), 0).astype(jnp.float32)
    for offset, piece_ref in enumerate(pieces):
        expert = lax.rem(line_ref[0] + offset, experts_count)
        wanted = jnp.sum(jnp.where(ids == expert, slot, 0.0), axis=0, keepdims=True)
        picks = jnp.where(numbers == wanted, 1.0, 0.0).astype(jnp.bfloat16)
        piece_ref[...] = jnp.dot(
            picks, block_ref[...], preferred_element_type=jnp.float32
        ).astype(jnp.bfloat16)


def expert_kernel(
    core_ref, p_ref, q_ref, p2_ref, q2_ref, in_ref, out_ref, keep_ref, send_ref, rows_ref
):
    core = core_ref[0]
    capacity, half = p_ref.shape
    rows_ref[:capacity, part_of(core, half)] = p_ref[...]
    rows_ref[capacity:, part_of(core, half)] = q_ref[...]
    rows_ref[:capacity, part_of(1 - core, half)] = p2_ref[...]
    rows_ref[capacity:, part_of(1 - core, half)] = q2_ref[...]
    hidden = jnp.dot(rows_ref[...], in_ref[...], preferred_element_type=jnp.float32)
    hidden = jnp.maximum(hidden, 0.0).astype(jnp.bfloat16)
    send = jnp.dot(
        hidden, out_ref[:, part_of(1 - core, half)], preferred_element_type=jnp.float32
    ).astype(jnp.bfloat16)
    send_ref[0] = send[:capacity]
    send_ref[1] = send[capacity:]
    keep = jnp.dot(hidden, out_ref[:, part_of(core, half)], preferred_element_type=jnp.float32)
    keep_ref[0] = keep[:capacity]
    keep_ref[1] = keep[capacity:]


def combine_kernel(core_ref, line_ref, routes_ref, own_gates_ref, other_gates_ref, *rest):
    pieces, (own_ref, other_ref, rows_ref, gates_ref, sum_ref) = rest[:-5], rest[-5:]
    experts_count = len(pieces)
    capacity, half = pieces[0].shape
    sents, _, full_len = routes_ref.shape
    core = core_ref[0]
    for offset, piece_ref in enumerate(pieces):
        rows_ref[offset * capacity : (offset + 1) * capacity] = piece_ref[...]
    gates_ref[core] = own_gates_ref[...]
    gates_ref[1 - core] = other_gates_ref[...]
    _, earlier = slots_of(routes_ref, experts_count)
    ids = lax.broadcasted_iota(jnp.int32, (earlier.shape[0], full_len), 0)
    numbers = lax.broadcasted_iota(
        jnp.int32, (full_len, experts_count * capacity), 1
    ).astype(jnp.float32)
    for sent in range(sents):
        slots = earlier[:, sent * full_len : (sent + 1) * full_len]
        total = None
        for k in range(2):
            route = routes_ref[sent, k : k + 1]
            slot = jnp.sum(jnp.where(ids == route, slots, 0.0), axis=0, keepdims=True)
            offset = lax.rem(route - line_ref[0] + experts_count, experts_count)
            place = offset.astype(jnp.float32) * capacity + slot
            place, gate = (
                jnp.broadcast_to(row, (full_len, full_len)).T[:, :1]
                for row in (place, gates_ref[sent, k : k + 1])
            )
            picks = jnp.where(numbers == place, 1.0, 0.0).astype(jnp.bfloat16)
            term = gate * jnp.dot(picks, rows_ref[...], preferred_element_type=jnp.float32)
            total = term if total is None else total + term
        sum_ref[sent] = total
    own_ref[...] = sum_ref[core]
    other_ref[...] = sum_ref[1 - core].astype(jnp.bfloat16)


def finish_kernel(core_ref, state_ref, own_ref, other_ref, mixed_ref):
    core = core_ref[0]
    half = own_ref.shape[-1]
    for part, summed in ((core, own_ref), (1 - core, other_ref)):
        span = part_of(part, half)
        mixed_ref[:, span] = (
            state_ref[:, span].astype(jnp.float32) + summed[...].astype(jnp.float32)
        ).astype(jnp.bfloat16)


def swap(values):
    return lax.ppermute(values, "section", [(0, 1), (1, 0)])


def swap_owner(values):
    owners = lax.axis_size("expert")
    return lax.ppermute(values, "expert", [(i, i ^ 1) for i in range(owners)])


def shift(values, offset):
    owners = lax.axis_size("expert")
    return lax.ppermute(
        values, "expert", [(i, (i + 2 * offset) % owners) for i in range(owners)]
    )


def attend(
    core, decoder_states, memory_keys, memory_values, source_lengths, target_lengths, routes,
    attn_gain, ffn_gain, router,
):
    full_len, width = decoder_states.shape[1:]
    memory = jnp.stack([memory_keys, memory_values], axis=1)
    own = lax.dynamic_index_in_dim(memory, core[0], 0, keepdims=False)
    other = swap(lax.dynamic_index_in_dim(memory, 1 - core[0], 0, keepdims=False))
    half = (full_len, width // 2)
    return call(
        attend_kernel,
        "attend",
        [
            ((full_len, width), jnp.bfloat16),
            (half, jnp.bfloat16),
            (half, jnp.bfloat16),
            ((2, full_len), jnp.float32),
        ],
        [core, source_lengths, target_lengths],
        [
            decoder_states[0],
            own,
            other,
            attn_gain[None],
            ffn_gain[None],
            router.T,
            routes,
        ],
        scratch=[pltpu.VMEM((full_len, width), jnp.bfloat16)],
    )


def line_experts(core, state, keep, send, gates, routes, fc_in, fc_out, capacity):
    full_len, width = state.shape
    half = width // 2
    count = lax.axis_size("expert") // 2
    line = (lax.axis_index("expert") // 2).astype(jnp.int32).reshape(1)
    other = swap(send)
    other_gates = swap(gates)
    piece = ((capacity, half), jnp.bfloat16)
    selected = call(
        select_kernel,
        "select",
        [piece] * count,
        [core, line],
        [routes, keep, other],
        scratch=[pltpu.VMEM((2 * full_len, half), jnp.bfloat16)],
    )
    received = [selected[0]] + [shift(selected[r], r) for r in range(1, count)]
    home = []
    for offset, p in enumerate(received):
        q = swap_owner(p)
        p2, q2 = swap(p), swap(q)
        kept, sent = call(
            expert_kernel,
            "expert",
            [((2, capacity, half), jnp.float32), ((2, capacity, half), jnp.bfloat16)],
            [core],
            [p, q, p2, q2, fc_in, fc_out],
            scratch=[pltpu.VMEM((2 * capacity, width), jnp.bfloat16)],
            vmem_mib=32,
            cost=pl.CostEstimate(
                flops=8 * capacity * width * fc_in.shape[1],
                bytes_accessed=4 * width * fc_in.shape[1],
                transcendentals=0,
            ),
        )
        both = kept + swap(sent).astype(jnp.float32)
        across = swap_owner(both[1].astype(jnp.bfloat16))
        total = (both[0] + across.astype(jnp.float32)).astype(jnp.bfloat16)
        home.append(shift(total, -offset) if offset else total)
    own_sum, other_sum = call(
        combine_kernel,
        "combine",
        [((full_len, half), jnp.float32), ((full_len, half), jnp.bfloat16)],
        [core, line],
        [routes, gates, other_gates, *home],
        scratch=[
            pltpu.VMEM((count * capacity, half), jnp.bfloat16),
            pltpu.VMEM((2, 2, full_len), jnp.float32),
            pltpu.VMEM((2, full_len, half), jnp.float32),
        ],
    )
    (mixed,) = call(
        finish_kernel,
        "finish",
        [((full_len, width), jnp.bfloat16)],
        [core],
        [state, own_sum, swap(other_sum)],
    )
    return mixed


def expert_apply(slot_rows, fc_in, fc_out):
    width = slot_rows.shape[-1]
    flat_rows = slot_rows.reshape(-1, width)
    hidden = jax.nn.relu(jnp.dot(flat_rows, fc_in, preferred_element_type=jnp.float32)).astype(
        jnp.bfloat16
    )
    produced = jnp.dot(hidden, fc_out, preferred_element_type=jnp.float32)
    return produced.reshape(slot_rows.shape[0], slot_rows.shape[1], width)


def sparse_experts(normed, target_lengths, routes, router, fc_in, fc_out, capacity):
    full_len, width = normed.shape
    all_normed = lax.all_gather(normed[None], "section", axis=0, tiled=True)
    block_sents = all_normed.shape[0]
    block_rows = block_sents * full_len
    tok_rows = all_normed.reshape(block_rows, width)
    owners = lax.axis_size("expert")
    experts_count = owners // 2
    chosen_ids = routes.reshape(block_rows, 2)
    logits = jnp.dot(tok_rows, router, preferred_element_type=jnp.float32)
    onehot = chosen_ids[:, :, None] == jnp.arange(experts_count, dtype=jnp.int32)
    chosen = jnp.sum(jnp.where(onehot, logits[:, None, :], 0.0), axis=-1)
    first = jax.nn.sigmoid(chosen[:, 0] - chosen[:, 1])
    gates = jnp.stack([first, 1.0 - first], axis=-1)
    live = (jnp.arange(full_len, dtype=jnp.int32)[None, :] < target_lengths[:, None]).reshape(
        block_rows
    )
    flags = onehot.reshape(block_rows * 2, experts_count).astype(jnp.int32)
    earlier = jnp.cumsum(flags, axis=0) - flags
    slot = jnp.sum(flags * earlier, axis=-1).reshape(block_rows, 2)
    position = chosen_ids * capacity + slot
    dump_index = experts_count * capacity
    target = jnp.where(live[:, None], position, dump_index)
    row_ids = jnp.broadcast_to(jnp.arange(block_rows, dtype=jnp.int32)[:, None], (block_rows, 2))
    table = (
        jnp.full((dump_index + 1,), block_rows, jnp.int32)
        .at[target.reshape(-1)]
        .set(row_ids.reshape(-1))[:dump_index]
    )
    padded = jnp.concatenate([tok_rows, jnp.zeros((1, width), jnp.bfloat16)], axis=0)
    slot_buffer = padded[table].reshape(experts_count, capacity, width)
    outgoing = jnp.repeat(slot_buffer, 2, axis=0)
    returned = lax.all_to_all(
        expert_apply(
            lax.all_to_all(outgoing, "expert", split_axis=0, concat_axis=0, tiled=True),
            fc_in,
            fc_out,
        ).astype(jnp.bfloat16),
        "expert",
        split_axis=0,
        concat_axis=0,
        tiled=True,
    ).astype(jnp.float32)
    partial_value = jnp.sum(returned.reshape(experts_count, 2, capacity, width), axis=1)
    fetched = partial_value.reshape(dump_index, width)[jnp.where(live[:, None], position, 0)]
    weight = gates * live[:, None].astype(jnp.float32)
    contrib = jnp.sum(weight[:, :, None] * fetched, axis=1).reshape(block_sents, full_len, width)
    summed = lax.psum_scatter(contrib, "section", scatter_dimension=0, tiled=True)
    return summed[0]


def local(
    decoder_states,
    memory_keys,
    memory_values,
    source_lengths,
    target_lengths,
    routes,
    attn_gain,
    ffn_gain,
    router,
    fc_in,
    fc_out,
):
    core = lax.axis_index("section").astype(jnp.int32).reshape(1)
    by_choice = jnp.transpose(routes, (0, 2, 1))
    state, keep, send, gates = attend(
        core, decoder_states, memory_keys, memory_values, source_lengths, target_lengths, by_choice,
        attn_gain, ffn_gain, router,
    )
    block_rows = routes.shape[0] * routes.shape[1]
    experts_count = router.shape[1]
    capacity = 2 * max(1, 3 * block_rows // (2 * experts_count))
    if capacity % 16 == 0:
        mixed = line_experts(core, state, keep, send, gates, by_choice, fc_in, fc_out, capacity)
    else:
        halves = jnp.stack([keep, send])
        normed = jnp.concatenate([halves[core[0]], halves[1 - core[0]]], axis=-1)
        summed = sparse_experts(normed, target_lengths, routes, router, fc_in, fc_out, capacity)
        mixed = (state.astype(jnp.float32) + summed).astype(jnp.bfloat16)
    return mixed[None]


def solution(mesh):
    placed = (
        P(("groups", "expert", "section"), None, None),
        P(("groups", "expert"), None, "section"),
        P(("groups", "expert"), None, "section"),
        P(("groups", "expert", "section")),
        P(("groups", "expert")),
        P(("groups", "expert"), None, None),
        P(),
        P(),
        P(),
        P(None, ("expert", "section")),
        P(("expert", "section"), None),
    )
    return jax.shard_map(
        local,
        mesh=mesh,
        in_specs=placed,
        out_specs=P(("groups", "expert", "section"), None, None),
        check_vma=False,
    )
```

```python
import functools

import jax
import jax.numpy as jnp
from jax import lax
from jax.experimental import pallas as pl
from jax.experimental.pallas import tpu as pltpu
from jax.sharding import PartitionSpec as P

HEAD_DIM = 128


def layer_norm(values, gain):
    centered = values - jnp.mean(values, axis=-1, keepdims=True)
    spread = jnp.mean(centered * centered, axis=-1, keepdims=True)
    return (centered * lax.rsqrt(spread + 1e-05) * gain).astype(jnp.bfloat16)


VMEM = pl.BlockSpec(memory_space=pltpu.VMEM)
SMEM = pl.BlockSpec(memory_space=pltpu.SMEM)


def call(kernel, name, outs, scalars, arrays, scratch=(), vmem_mib=24, cost=None):
    return pl.pallas_call(
        kernel,
        out_shape=tuple(jax.ShapeDtypeStruct(*out) for out in outs),
        in_specs=[SMEM] * len(scalars) + [VMEM] * len(arrays),
        out_specs=(VMEM,) * len(outs),
        scratch_shapes=list(scratch),
        compiler_params=pltpu.CompilerParams(vmem_limit_bytes=vmem_mib * 2**20),
        cost_estimate=cost,
        name=name,
    )(*scalars, *arrays)


def part_of(part, half):
    return pl.ds(pl.multiple_of(part * half, half), half)


def attend_kernel(
    core_ref,
    source_ref,
    target_ref,
    x_ref,
    own_ref,
    other_ref,
    again_ref,
    fgain_ref,
    router_ref,
    routes_ref,
    state_ref,
    keep_ref,
    send_ref,
    gates_ref,
    scratch_ref,
):
    full_len = x_ref.shape[0]
    half = own_ref.shape[-1]
    widened = x_ref[...].astype(jnp.float32)
    scratch_ref[...] = layer_norm(widened, again_ref[...])
    core = core_ref[0]
    keys_seen = own_ref.shape[1]
    valid = lax.broadcasted_iota(jnp.int32, (1, keys_seen), 1) < source_ref[0]
    for part, memory in ((core, own_ref), (1 - core, other_ref)):
        for head in range(half // HEAD_DIM):
            at = head * HEAD_DIM
            span = pl.ds(pl.multiple_of(part * half + at, HEAD_DIM), HEAD_DIM)
            scores = lax.dot_general(
                scratch_ref[:, span],
                memory[0, :, at : at + HEAD_DIM],
                (((1,), (1,)), ((), ())),
                preferred_element_type=jnp.float32,
            ) * HEAD_DIM ** (-0.5)
            scores = jnp.where(valid, scores, -jnp.inf)
            expon = jnp.exp(scores - jnp.max(scores, axis=-1, keepdims=True))
            weights = (expon / jnp.sum(expon, axis=-1, keepdims=True)).astype(jnp.bfloat16)
            attended = jnp.dot(
                weights, memory[1, :, at : at + HEAD_DIM], preferred_element_type=jnp.float32
            )
            state_ref[:, span] = (x_ref[:, span].astype(jnp.float32) + attended).astype(
                jnp.bfloat16
            )
    scratch_ref[...] = layer_norm(state_ref[...].astype(jnp.float32), fgain_ref[...])
    keep_ref[...] = scratch_ref[:, part_of(core, half)]
    send_ref[...] = scratch_ref[:, part_of(1 - core, half)]
    logits = lax.dot_general(
        router_ref[...],
        scratch_ref[...],
        (((1,), (1,)), ((), ())),
        preferred_element_type=jnp.float32,
    )
    names = lax.broadcasted_iota(jnp.int32, logits.shape, 0)
    routes = routes_ref[core]
    chosen = [
        jnp.sum(jnp.where(names == routes[k : k + 1], logits, 0.0), axis=0, keepdims=True)
        for k in range(2)
    ]
    first = jax.nn.sigmoid(chosen[0] - chosen[1])
    live = lax.broadcasted_iota(jnp.int32, (1, full_len), 1) < target_ref[core]
    gates_ref[0:1] = jnp.where(live, first, 0.0)
    gates_ref[1:2] = jnp.where(live, 1.0 - first, 0.0)


def slots_of(routes_ref, experts_count):
    sents, _, full_len = routes_ref.shape
    rows = sents * full_len
    ids = lax.broadcasted_iota(jnp.int32, (max(8, experts_count), full_len), 0)
    named = jnp.concatenate(
        [
            jnp.where((ids == routes_ref[s, 0:1]) | (ids == routes_ref[s, 1:2]), 1.0, 0.0)
            for s in range(sents)
        ],
        axis=1,
    )
    before = lax.broadcasted_iota(jnp.int32, (rows, rows), 0) < lax.broadcasted_iota(
        jnp.int32, (rows, rows), 1
    )
    earlier = jnp.dot(
        named.astype(jnp.bfloat16),
        jnp.where(before, 1.0, 0.0).astype(jnp.bfloat16),
        preferred_element_type=jnp.float32,
    )
    return named > 0.0, earlier


def select_kernel(core_ref, line_ref, routes_ref, own_ref, other_ref, *rest):
    pieces, block_ref = rest[:-1], rest[-1]
    experts_count = len(pieces)
    full_len = own_ref.shape[0]
    capacity = pieces[0].shape[0]
    core = core_ref[0]
    block_ref[part_of(core, full_len)] = own_ref[...]
    block_ref[part_of(1 - core, full_len)] = other_ref[...]
    named, earlier = slots_of(routes_ref, experts_count)
    slot = jnp.where(named, earlier, -1.0)
    ids = lax.broadcasted_iota(jnp.int32, slot.shape, 0)
    numbers = lax.broadcasted_iota(jnp.int32, (capacity, slot.shape[1]), 0).astype(jnp.float32)
    for offset, piece_ref in enumerate(pieces):
        expert = lax.rem(line_ref[0] + offset, experts_count)
        wanted = jnp.sum(jnp.where(ids == expert, slot, 0.0), axis=0, keepdims=True)
        picks = jnp.where(numbers == wanted, 1.0, 0.0).astype(jnp.bfloat16)
        piece_ref[...] = jnp.dot(
            picks, block_ref[...], preferred_element_type=jnp.float32
        ).astype(jnp.bfloat16)


def expert_kernel(
    core_ref, p_ref, q_ref, p2_ref, q2_ref, in_ref, out_ref, keep_ref, send_ref, rows_ref
):
    core = core_ref[0]
    capacity, half = p_ref.shape
    rows_ref[:capacity, part_of(core, half)] = p_ref[...]
    rows_ref[capacity:, part_of(core, half)] = q_ref[...]
    rows_ref[:capacity, part_of(1 - core, half)] = p2_ref[...]
    rows_ref[capacity:, part_of(1 - core, half)] = q2_ref[...]
    hidden = jnp.dot(rows_ref[...], in_ref[...], preferred_element_type=jnp.float32)
    hidden = jnp.maximum(hidden, 0.0).astype(jnp.bfloat16)
    send = jnp.dot(
        hidden, out_ref[:, part_of(1 - core, half)], preferred_element_type=jnp.float32
    ).astype(jnp.bfloat16)
    send_ref[0] = send[:capacity]
    send_ref[1] = send[capacity:]
    keep = jnp.dot(hidden, out_ref[:, part_of(core, half)], preferred_element_type=jnp.float32)
    keep_ref[0] = keep[:capacity]
    keep_ref[1] = keep[capacity:]


def combine_kernel(core_ref, line_ref, routes_ref, own_gates_ref, other_gates_ref, *rest):
    pieces, (own_ref, other_ref, rows_ref, gates_ref, sum_ref) = rest[:-5], rest[-5:]
    experts_count = len(pieces)
    capacity, half = pieces[0].shape
    sents, _, full_len = routes_ref.shape
    core = core_ref[0]
    for offset, piece_ref in enumerate(pieces):
        rows_ref[offset * capacity : (offset + 1) * capacity] = piece_ref[...]
    gates_ref[core] = own_gates_ref[...]
    gates_ref[1 - core] = other_gates_ref[...]
    _, earlier = slots_of(routes_ref, experts_count)
    ids = lax.broadcasted_iota(jnp.int32, (earlier.shape[0], full_len), 0)
    numbers = lax.broadcasted_iota(
        jnp.int32, (full_len, experts_count * capacity), 1
    ).astype(jnp.float32)
    for sent in range(sents):
        slots = earlier[:, sent * full_len : (sent + 1) * full_len]
        total = None
        for k in range(2):
            route = routes_ref[sent, k : k + 1]
            slot = jnp.sum(jnp.where(ids == route, slots, 0.0), axis=0, keepdims=True)
            offset = lax.rem(route - line_ref[0] + experts_count, experts_count)
            place = offset.astype(jnp.float32) * capacity + slot
            place, gate = (
                jnp.broadcast_to(row, (full_len, full_len)).T[:, :1]
                for row in (place, gates_ref[sent, k : k + 1])
            )
            picks = jnp.where(numbers == place, 1.0, 0.0).astype(jnp.bfloat16)
            term = gate * jnp.dot(picks, rows_ref[...], preferred_element_type=jnp.float32)
            total = term if total is None else total + term
        sum_ref[sent] = total
    own_ref[...] = sum_ref[core]
    other_ref[...] = sum_ref[1 - core].astype(jnp.bfloat16)


def finish_kernel(core_ref, state_ref, own_ref, other_ref, mixed_ref):
    core = core_ref[0]
    half = own_ref.shape[-1]
    for part, summed in ((core, own_ref), (1 - core, other_ref)):
        span = part_of(part, half)
        mixed_ref[:, span] = (
            state_ref[:, span].astype(jnp.float32) + summed[...].astype(jnp.float32)
        ).astype(jnp.bfloat16)


def swap(values):
    return lax.ppermute(values, "section", [(0, 1), (1, 0)])


def swap_owner(values):
    owners = lax.axis_size("expert")
    return lax.ppermute(values, "expert", [(i, i ^ 1) for i in range(owners)])


def shift(values, offset):
    owners = lax.axis_size("expert")
    return lax.ppermute(
        values, "expert", [(i, (i + 2 * offset) % owners) for i in range(owners)]
    )


def after_kernel(value_ref, first_ref, out_ref):
    pass


def after(value, first):
    anywhere = pl.BlockSpec(memory_space=pl.ANY)
    return pl.pallas_call(
        after_kernel,
        out_shape=jax.ShapeDtypeStruct(value.shape, value.dtype),
        in_specs=[anywhere, anywhere],
        out_specs=anywhere,
        input_output_aliases={0: 0},
        name="after",
    )(value, first)


def piece_order(count):
    return sorted(range(count), key=lambda offset: min(offset, count - offset))


def attend(
    core, decoder_states, memory_keys, memory_values, source_lengths, target_lengths, routes,
    attn_gain, ffn_gain, router,
):
    full_len, width = decoder_states.shape[1:]
    memory = jnp.stack([memory_keys, memory_values], axis=1)
    own = lax.dynamic_index_in_dim(memory, core[0], 0, keepdims=False)
    other = swap(lax.dynamic_index_in_dim(memory, 1 - core[0], 0, keepdims=False))
    half = (full_len, width // 2)
    return call(
        attend_kernel,
        "attend",
        [
            ((full_len, width), jnp.bfloat16),
            (half, jnp.bfloat16),
            (half, jnp.bfloat16),
            ((2, full_len), jnp.float32),
        ],
        [core, source_lengths, target_lengths],
        [
            decoder_states[0],
            own,
            other,
            attn_gain[None],
            ffn_gain[None],
            router.T,
            routes,
        ],
        scratch=[pltpu.VMEM((full_len, width), jnp.bfloat16)],
    )


def line_experts(core, state, keep, send, gates, routes, fc_in, fc_out, capacity):
    full_len, width = state.shape
    half = width // 2
    count = lax.axis_size("expert") // 2
    line = (lax.axis_index("expert") // 2).astype(jnp.int32).reshape(1)
    other = swap(send)
    other_gates = swap(gates)
    piece = ((capacity, half), jnp.bfloat16)
    selected = call(
        select_kernel,
        "select",
        [piece] * count,
        [core, line],
        [routes, keep, other],
        scratch=[pltpu.VMEM((2 * full_len, half), jnp.bfloat16)],
    )
    travelling = [shift(selected[r], r) for r in range(1, count)]
    home = [None] * count
    home = [None] * count
    kepts, halves, wholes = [], [], []
    for at, offset in enumerate(piece_order(count)):
        p = travelling[offset - 1] if offset else selected[0]
        if at >= 2:
            p = after(p, kepts[at - 2])
        q = swap_owner(p)
        p2 = swap(p)
        q2 = swap(q)
        if at >= 2:
            q2 = after(q2, halves[at - 2])
        kept, sent = call(
            expert_kernel,
            "expert",
            [((2, capacity, half), jnp.float32), ((2, capacity, half), jnp.bfloat16)],
            [core],
            [p, q, p2, q2, fc_in, fc_out],
            scratch=[pltpu.VMEM((2 * capacity, width), jnp.bfloat16)],
            vmem_mib=32,
        )
        kepts.append(kept)
        both = kept + swap(sent).astype(jnp.float32)
        halves.append(both[1].astype(jnp.bfloat16))
        across = swap_owner(halves[-1])
        wholes.append((both[0] + across.astype(jnp.float32)).astype(jnp.bfloat16))
        home[offset] = shift(wholes[-1], -offset) if offset else wholes[-1]
    own_sum, other_sum = call(
        combine_kernel,
        "combine",
        [((full_len, half), jnp.float32), ((full_len, half), jnp.bfloat16)],
        [core, line],
        [routes, gates, other_gates, *home],
        scratch=[
            pltpu.VMEM((count * capacity, half), jnp.bfloat16),
            pltpu.VMEM((2, 2, full_len), jnp.float32),
            pltpu.VMEM((2, full_len, half), jnp.float32),
        ],
    )
    (mixed,) = call(
        finish_kernel,
        "finish",
        [((full_len, width), jnp.bfloat16)],
        [core],
        [state, own_sum, swap(other_sum)],
    )
    return mixed


def expert_apply(slot_rows, fc_in, fc_out):
    width = slot_rows.shape[-1]
    flat_rows = slot_rows.reshape(-1, width)
    hidden = jax.nn.relu(jnp.dot(flat_rows, fc_in, preferred_element_type=jnp.float32)).astype(
        jnp.bfloat16
    )
    produced = jnp.dot(hidden, fc_out, preferred_element_type=jnp.float32)
    return produced.reshape(slot_rows.shape[0], slot_rows.shape[1], width)


def sparse_experts(normed, target_lengths, routes, router, fc_in, fc_out, capacity):
    full_len, width = normed.shape
    all_normed = lax.all_gather(normed[None], "section", axis=0, tiled=True)
    block_sents = all_normed.shape[0]
    block_rows = block_sents * full_len
    tok_rows = all_normed.reshape(block_rows, width)
    owners = lax.axis_size("expert")
    experts_count = owners // 2
    chosen_ids = routes.reshape(block_rows, 2)
    logits = jnp.dot(tok_rows, router, preferred_element_type=jnp.float32)
    onehot = chosen_ids[:, :, None] == jnp.arange(experts_count, dtype=jnp.int32)
    chosen = jnp.sum(jnp.where(onehot, logits[:, None, :], 0.0), axis=-1)
    first = jax.nn.sigmoid(chosen[:, 0] - chosen[:, 1])
    gates = jnp.stack([first, 1.0 - first], axis=-1)
    live = (jnp.arange(full_len, dtype=jnp.int32)[None, :] < target_lengths[:, None]).reshape(
        block_rows
    )
    flags = onehot.reshape(block_rows * 2, experts_count).astype(jnp.int32)
    earlier = jnp.cumsum(flags, axis=0) - flags
    slot = jnp.sum(flags * earlier, axis=-1).reshape(block_rows, 2)
    position = chosen_ids * capacity + slot
    dump_index = experts_count * capacity
    target = jnp.where(live[:, None], position, dump_index)
    row_ids = jnp.broadcast_to(jnp.arange(block_rows, dtype=jnp.int32)[:, None], (block_rows, 2))
    table = (
        jnp.full((dump_index + 1,), block_rows, jnp.int32)
        .at[target.reshape(-1)]
        .set(row_ids.reshape(-1))[:dump_index]
    )
    padded = jnp.concatenate([tok_rows, jnp.zeros((1, width), jnp.bfloat16)], axis=0)
    slot_buffer = padded[table].reshape(experts_count, capacity, width)
    outgoing = jnp.repeat(slot_buffer, 2, axis=0)
    returned = lax.all_to_all(
        expert_apply(
            lax.all_to_all(outgoing, "expert", split_axis=0, concat_axis=0, tiled=True),
            fc_in,
            fc_out,
        ).astype(jnp.bfloat16),
        "expert",
        split_axis=0,
        concat_axis=0,
        tiled=True,
    ).astype(jnp.float32)
    partial_value = jnp.sum(returned.reshape(experts_count, 2, capacity, width), axis=1)
    fetched = partial_value.reshape(dump_index, width)[jnp.where(live[:, None], position, 0)]
    weight = gates * live[:, None].astype(jnp.float32)
    contrib = jnp.sum(weight[:, :, None] * fetched, axis=1).reshape(block_sents, full_len, width)
    summed = lax.psum_scatter(contrib, "section", scatter_dimension=0, tiled=True)
    return summed[0]


def local(
    decoder_states,
    memory_keys,
    memory_values,
    source_lengths,
    target_lengths,
    routes,
    attn_gain,
    ffn_gain,
    router,
    fc_in,
    fc_out,
):
    core = lax.axis_index("section").astype(jnp.int32).reshape(1)
    by_choice = jnp.transpose(routes, (0, 2, 1))
    state, keep, send, gates = attend(
        core, decoder_states, memory_keys, memory_values, source_lengths, target_lengths, by_choice,
        attn_gain, ffn_gain, router,
    )
    block_rows = routes.shape[0] * routes.shape[1]
    experts_count = router.shape[1]
    capacity = 2 * max(1, 3 * block_rows // (2 * experts_count))
    if capacity % 16 == 0:
        mixed = line_experts(core, state, keep, send, gates, by_choice, fc_in, fc_out, capacity)
    else:
        halves = jnp.stack([keep, send])
        normed = jnp.concatenate([halves[core[0]], halves[1 - core[0]]], axis=-1)
        summed = sparse_experts(normed, target_lengths, routes, router, fc_in, fc_out, capacity)
        mixed = (state.astype(jnp.float32) + summed).astype(jnp.bfloat16)
    return mixed[None]


def solution(mesh):
    placed = (
        P(("groups", "expert", "section"), None, None),
        P(("groups", "expert"), None, "section"),
        P(("groups", "expert"), None, "section"),
        P(("groups", "expert", "section")),
        P(("groups", "expert")),
        P(("groups", "expert"), None, None),
        P(),
        P(),
        P(),
        P(None, ("expert", "section")),
        P(("expert", "section"), None),
    )
    return jax.shard_map(
        local,
        mesh=mesh,
        in_specs=placed,
        out_specs=P(("groups", "expert", "section"), None, None),
        check_vma=False,
    )
```

```python
import functools

import jax
import jax.numpy as jnp
from jax import lax
from jax.experimental import pallas as pl
from jax.experimental.pallas import tpu as pltpu
from jax.sharding import PartitionSpec as P

HEAD_DIM = 128


def layer_norm(values, gain):
    centered = values - jnp.mean(values, axis=-1, keepdims=True)
    spread = jnp.mean(centered * centered, axis=-1, keepdims=True)
    return (centered * lax.rsqrt(spread + 1e-05) * gain).astype(jnp.bfloat16)


VMEM = pl.BlockSpec(memory_space=pltpu.VMEM)
SMEM = pl.BlockSpec(memory_space=pltpu.SMEM)


def call(kernel, name, outs, scalars, arrays, scratch=(), vmem_mib=12, cost=None):
    return pl.pallas_call(
        kernel,
        out_shape=tuple(jax.ShapeDtypeStruct(*out) for out in outs),
        in_specs=[SMEM] * len(scalars) + [VMEM] * len(arrays),
        out_specs=(VMEM,) * len(outs),
        scratch_shapes=list(scratch),
        compiler_params=pltpu.CompilerParams(vmem_limit_bytes=vmem_mib * 2**20),
        cost_estimate=cost,
        name=name,
    )(*scalars, *arrays)


def part_of(part, half):
    return pl.ds(pl.multiple_of(part * half, half), half)


def attend_kernel(
    core_ref,
    source_ref,
    target_ref,
    x_ref,
    own_ref,
    other_ref,
    again_ref,
    fgain_ref,
    router_ref,
    routes_ref,
    state_ref,
    keep_ref,
    send_ref,
    gates_ref,
    scratch_ref,
):
    full_len = x_ref.shape[0]
    half = own_ref.shape[-1]
    widened = x_ref[...].astype(jnp.float32)
    scratch_ref[...] = layer_norm(widened, again_ref[...])
    core = core_ref[0]
    keys_seen = own_ref.shape[1]
    valid = lax.broadcasted_iota(jnp.int32, (1, keys_seen), 1) < source_ref[0]
    for part, memory in ((core, own_ref), (1 - core, other_ref)):
        for head in range(half // HEAD_DIM):
            at = head * HEAD_DIM
            span = pl.ds(pl.multiple_of(part * half + at, HEAD_DIM), HEAD_DIM)
            scores = lax.dot_general(
                scratch_ref[:, span],
                memory[0, :, at : at + HEAD_DIM],
                (((1,), (1,)), ((), ())),
                preferred_element_type=jnp.float32,
            ) * HEAD_DIM ** (-0.5)
            scores = jnp.where(valid, scores, -jnp.inf)
            expon = jnp.exp(scores - jnp.max(scores, axis=-1, keepdims=True))
            weights = (expon / jnp.sum(expon, axis=-1, keepdims=True)).astype(jnp.bfloat16)
            attended = jnp.dot(
                weights, memory[1, :, at : at + HEAD_DIM], preferred_element_type=jnp.float32
            )
            state_ref[:, span] = (x_ref[:, span].astype(jnp.float32) + attended).astype(
                jnp.bfloat16
            )
    scratch_ref[...] = layer_norm(state_ref[...].astype(jnp.float32), fgain_ref[...])
    keep_ref[...] = scratch_ref[:, part_of(core, half)]
    send_ref[...] = scratch_ref[:, part_of(1 - core, half)]
    logits = lax.dot_general(
        router_ref[...],
        scratch_ref[...],
        (((1,), (1,)), ((), ())),
        preferred_element_type=jnp.float32,
    )
    names = lax.broadcasted_iota(jnp.int32, logits.shape, 0)
    routes = routes_ref[core]
    chosen = [
        jnp.sum(jnp.where(names == routes[k : k + 1], logits, 0.0), axis=0, keepdims=True)
        for k in range(2)
    ]
    first = jax.nn.sigmoid(chosen[0] - chosen[1])
    live = lax.broadcasted_iota(jnp.int32, (1, full_len), 1) < target_ref[core]
    gates_ref[0:1] = jnp.where(live, first, 0.0)
    gates_ref[1:2] = jnp.where(live, 1.0 - first, 0.0)


def slots_of(routes_ref, experts_count):
    sents, _, full_len = routes_ref.shape
    rows = sents * full_len
    ids = lax.broadcasted_iota(jnp.int32, (max(8, experts_count), full_len), 0)
    named = jnp.concatenate(
        [
            jnp.where((ids == routes_ref[s, 0:1]) | (ids == routes_ref[s, 1:2]), 1.0, 0.0)
            for s in range(sents)
        ],
        axis=1,
    )
    before = lax.broadcasted_iota(jnp.int32, (rows, rows), 0) < lax.broadcasted_iota(
        jnp.int32, (rows, rows), 1
    )
    earlier = jnp.dot(
        named.astype(jnp.bfloat16),
        jnp.where(before, 1.0, 0.0).astype(jnp.bfloat16),
        preferred_element_type=jnp.float32,
    )
    return named > 0.0, earlier


def select_kernel(core_ref, line_ref, routes_ref, own_ref, other_ref, *rest):
    pieces, block_ref = rest[:-1], rest[-1]
    experts_count = len(pieces)
    full_len = own_ref.shape[0]
    capacity = pieces[0].shape[0]
    core = core_ref[0]
    block_ref[part_of(core, full_len)] = own_ref[...]
    block_ref[part_of(1 - core, full_len)] = other_ref[...]
    named, earlier = slots_of(routes_ref, experts_count)
    slot = jnp.where(named, earlier, -1.0)
    ids = lax.broadcasted_iota(jnp.int32, slot.shape, 0)
    numbers = lax.broadcasted_iota(jnp.int32, (capacity, slot.shape[1]), 0).astype(jnp.float32)
    for offset, piece_ref in enumerate(pieces):
        expert = lax.rem(line_ref[0] + offset, experts_count)
        wanted = jnp.sum(jnp.where(ids == expert, slot, 0.0), axis=0, keepdims=True)
        picks = jnp.where(numbers == wanted, 1.0, 0.0).astype(jnp.bfloat16)
        piece_ref[...] = jnp.dot(
            picks, block_ref[...], preferred_element_type=jnp.float32
        ).astype(jnp.bfloat16)


def expert_kernel(
    core_ref, p_ref, q_ref, p2_ref, q2_ref, in_ref, out_ref, keep_ref, send_ref, rows_ref
):
    core = core_ref[0]
    capacity, half = p_ref.shape
    rows_ref[:capacity, part_of(core, half)] = p_ref[...]
    rows_ref[capacity:, part_of(core, half)] = q_ref[...]
    rows_ref[:capacity, part_of(1 - core, half)] = p2_ref[...]
    rows_ref[capacity:, part_of(1 - core, half)] = q2_ref[...]
    hidden = jnp.dot(rows_ref[...], in_ref[...], preferred_element_type=jnp.float32)
    hidden = jnp.maximum(hidden, 0.0).astype(jnp.bfloat16)
    send = jnp.dot(
        hidden, out_ref[:, part_of(1 - core, half)], preferred_element_type=jnp.float32
    ).astype(jnp.bfloat16)
    send_ref[0] = send[:capacity]
    send_ref[1] = send[capacity:]
    keep = jnp.dot(hidden, out_ref[:, part_of(core, half)], preferred_element_type=jnp.float32)
    keep_ref[0] = keep[:capacity]
    keep_ref[1] = keep[capacity:]


def combine_kernel(core_ref, line_ref, routes_ref, own_gates_ref, other_gates_ref, *rest):
    pieces, (own_ref, other_ref, rows_ref, gates_ref, sum_ref) = rest[:-5], rest[-5:]
    experts_count = len(pieces)
    capacity, half = pieces[0].shape
    sents, _, full_len = routes_ref.shape
    core = core_ref[0]
    for offset, piece_ref in enumerate(pieces):
        rows_ref[offset * capacity : (offset + 1) * capacity] = piece_ref[...]
    gates_ref[core] = own_gates_ref[...]
    gates_ref[1 - core] = other_gates_ref[...]
    _, earlier = slots_of(routes_ref, experts_count)
    ids = lax.broadcasted_iota(jnp.int32, (earlier.shape[0], full_len), 0)
    numbers = lax.broadcasted_iota(
        jnp.int32, (full_len, experts_count * capacity), 1
    ).astype(jnp.float32)
    for sent in range(sents):
        slots = earlier[:, sent * full_len : (sent + 1) * full_len]
        total = None
        for k in range(2):
            route = routes_ref[sent, k : k + 1]
            slot = jnp.sum(jnp.where(ids == route, slots, 0.0), axis=0, keepdims=True)
            offset = lax.rem(route - line_ref[0] + experts_count, experts_count)
            place = offset.astype(jnp.float32) * capacity + slot
            place, gate = (
                jnp.broadcast_to(row, (full_len, full_len)).T[:, :1]
                for row in (place, gates_ref[sent, k : k + 1])
            )
            picks = jnp.where(numbers == place, 1.0, 0.0).astype(jnp.bfloat16)
            term = gate * jnp.dot(picks, rows_ref[...], preferred_element_type=jnp.float32)
            total = term if total is None else total + term
        sum_ref[sent] = total
    own_ref[...] = sum_ref[core]
    other_ref[...] = sum_ref[1 - core].astype(jnp.bfloat16)


def finish_kernel(core_ref, state_ref, own_ref, other_ref, mixed_ref):
    core = core_ref[0]
    half = own_ref.shape[-1]
    for part, summed in ((core, own_ref), (1 - core, other_ref)):
        span = part_of(part, half)
        mixed_ref[:, span] = (
            state_ref[:, span].astype(jnp.float32) + summed[...].astype(jnp.float32)
        ).astype(jnp.bfloat16)


def swap(values):
    return lax.ppermute(values, "section", [(0, 1), (1, 0)])


def swap_owner(values):
    owners = lax.axis_size("expert")
    return lax.ppermute(values, "expert", [(i, i ^ 1) for i in range(owners)])


def shift(values, offset):
    owners = lax.axis_size("expert")
    return lax.ppermute(
        values, "expert", [(i, (i + 2 * offset) % owners) for i in range(owners)]
    )


def after_kernel(value_ref, first_ref, out_ref):
    pass


def after(value, first):
    anywhere = pl.BlockSpec(memory_space=pl.ANY)
    return pl.pallas_call(
        after_kernel,
        out_shape=jax.ShapeDtypeStruct(value.shape, value.dtype),
        in_specs=[anywhere, anywhere],
        out_specs=anywhere,
        input_output_aliases={0: 0},
        compiler_params=pltpu.CompilerParams(vmem_limit_bytes=2**20),
        name="after",
    )(value, first)


def piece_order(count):
    return sorted(range(count), key=lambda offset: min(offset, count - offset))


def attend(
    core, decoder_states, memory_keys, memory_values, source_lengths, target_lengths, routes,
    attn_gain, ffn_gain, router,
):
    full_len, width = decoder_states.shape[1:]
    memory = jnp.stack([memory_keys, memory_values], axis=1)
    own = lax.dynamic_index_in_dim(memory, core[0], 0, keepdims=False)
    other = swap(lax.dynamic_index_in_dim(memory, 1 - core[0], 0, keepdims=False))
    half = (full_len, width // 2)
    return call(
        attend_kernel,
        "attend",
        [
            ((full_len, width), jnp.bfloat16),
            (half, jnp.bfloat16),
            (half, jnp.bfloat16),
            ((2, full_len), jnp.float32),
        ],
        [core, source_lengths, target_lengths],
        [
            decoder_states[0],
            own,
            other,
            attn_gain[None],
            ffn_gain[None],
            router.T,
            routes,
        ],
        scratch=[pltpu.VMEM((full_len, width), jnp.bfloat16)],
    )


def line_experts(core, state, keep, send, gates, routes, fc_in, fc_out, capacity):
    full_len, width = state.shape
    half = width // 2
    count = lax.axis_size("expert") // 2
    line = (lax.axis_index("expert") // 2).astype(jnp.int32).reshape(1)
    other = swap(send)
    other_gates = swap(gates)
    piece = ((capacity, half), jnp.bfloat16)
    selected = call(
        select_kernel,
        "select",
        [piece] * count,
        [core, line],
        [routes, keep, other],
        scratch=[pltpu.VMEM((2 * full_len, half), jnp.bfloat16)],
    )
    travelling = [shift(selected[r], r) for r in range(1, count)]
    home = [None] * count
    home = [None] * count
    kepts, halves, wholes = [], [], []
    for at, offset in enumerate(piece_order(count)):
        p = travelling[offset - 1] if offset else selected[0]
        if at >= 2:
            p = after(p, kepts[at - 2])
        q = swap_owner(p)
        p2 = swap(p)
        q2 = swap(q)
        if at >= 2:
            q2 = after(q2, wholes[at - 2])
        kept, sent = call(
            expert_kernel,
            "expert",
            [((2, capacity, half), jnp.float32), ((2, capacity, half), jnp.bfloat16)],
            [core],
            [p, q, p2, q2, fc_in, fc_out],
            scratch=[pltpu.VMEM((2 * capacity, width), jnp.bfloat16)],
            vmem_mib=16,
        )
        kepts.append(kept)
        both = kept + swap(sent).astype(jnp.float32)
        halves.append(both[1].astype(jnp.bfloat16))
        across = swap_owner(halves[-1])
        wholes.append((both[0] + across.astype(jnp.float32)).astype(jnp.bfloat16))
        home[offset] = shift(wholes[-1], -offset) if offset else wholes[-1]
    own_sum, other_sum = call(
        combine_kernel,
        "combine",
        [((full_len, half), jnp.float32), ((full_len, half), jnp.bfloat16)],
        [core, line],
        [routes, gates, other_gates, *home],
        scratch=[
            pltpu.VMEM((count * capacity, half), jnp.bfloat16),
            pltpu.VMEM((2, 2, full_len), jnp.float32),
            pltpu.VMEM((2, full_len, half), jnp.float32),
        ],
    )
    (mixed,) = call(
        finish_kernel,
        "finish",
        [((full_len, width), jnp.bfloat16)],
        [core],
        [state, own_sum, swap(other_sum)],
    )
    return mixed


def expert_apply(slot_rows, fc_in, fc_out):
    width = slot_rows.shape[-1]
    flat_rows = slot_rows.reshape(-1, width)
    hidden = jax.nn.relu(jnp.dot(flat_rows, fc_in, preferred_element_type=jnp.float32)).astype(
        jnp.bfloat16
    )
    produced = jnp.dot(hidden, fc_out, preferred_element_type=jnp.float32)
    return produced.reshape(slot_rows.shape[0], slot_rows.shape[1], width)


def sparse_experts(normed, target_lengths, routes, router, fc_in, fc_out, capacity):
    full_len, width = normed.shape
    all_normed = lax.all_gather(normed[None], "section", axis=0, tiled=True)
    block_sents = all_normed.shape[0]
    block_rows = block_sents * full_len
    tok_rows = all_normed.reshape(block_rows, width)
    owners = lax.axis_size("expert")
    experts_count = owners // 2
    chosen_ids = routes.reshape(block_rows, 2)
    logits = jnp.dot(tok_rows, router, preferred_element_type=jnp.float32)
    onehot = chosen_ids[:, :, None] == jnp.arange(experts_count, dtype=jnp.int32)
    chosen = jnp.sum(jnp.where(onehot, logits[:, None, :], 0.0), axis=-1)
    first = jax.nn.sigmoid(chosen[:, 0] - chosen[:, 1])
    gates = jnp.stack([first, 1.0 - first], axis=-1)
    live = (jnp.arange(full_len, dtype=jnp.int32)[None, :] < target_lengths[:, None]).reshape(
        block_rows
    )
    flags = onehot.reshape(block_rows * 2, experts_count).astype(jnp.int32)
    earlier = jnp.cumsum(flags, axis=0) - flags
    slot = jnp.sum(flags * earlier, axis=-1).reshape(block_rows, 2)
    position = chosen_ids * capacity + slot
    dump_index = experts_count * capacity
    target = jnp.where(live[:, None], position, dump_index)
    row_ids = jnp.broadcast_to(jnp.arange(block_rows, dtype=jnp.int32)[:, None], (block_rows, 2))
    table = (
        jnp.full((dump_index + 1,), block_rows, jnp.int32)
        .at[target.reshape(-1)]
        .set(row_ids.reshape(-1))[:dump_index]
    )
    padded = jnp.concatenate([tok_rows, jnp.zeros((1, width), jnp.bfloat16)], axis=0)
    slot_buffer = padded[table].reshape(experts_count, capacity, width)
    outgoing = jnp.repeat(slot_buffer, 2, axis=0)
    returned = lax.all_to_all(
        expert_apply(
            lax.all_to_all(outgoing, "expert", split_axis=0, concat_axis=0, tiled=True),
            fc_in,
            fc_out,
        ).astype(jnp.bfloat16),
        "expert",
        split_axis=0,
        concat_axis=0,
        tiled=True,
    ).astype(jnp.float32)
    partial_value = jnp.sum(returned.reshape(experts_count, 2, capacity, width), axis=1)
    fetched = partial_value.reshape(dump_index, width)[jnp.where(live[:, None], position, 0)]
    weight = gates * live[:, None].astype(jnp.float32)
    contrib = jnp.sum(weight[:, :, None] * fetched, axis=1).reshape(block_sents, full_len, width)
    summed = lax.psum_scatter(contrib, "section", scatter_dimension=0, tiled=True)
    return summed[0]


def local(
    decoder_states,
    memory_keys,
    memory_values,
    source_lengths,
    target_lengths,
    routes,
    attn_gain,
    ffn_gain,
    router,
    fc_in,
    fc_out,
):
    core = lax.axis_index("section").astype(jnp.int32).reshape(1)
    by_choice = jnp.transpose(routes, (0, 2, 1))
    state, keep, send, gates = attend(
        core, decoder_states, memory_keys, memory_values, source_lengths, target_lengths, by_choice,
        attn_gain, ffn_gain, router,
    )
    block_rows = routes.shape[0] * routes.shape[1]
    experts_count = router.shape[1]
    capacity = 2 * max(1, 3 * block_rows // (2 * experts_count))
    if capacity % 16 == 0:
        mixed = line_experts(core, state, keep, send, gates, by_choice, fc_in, fc_out, capacity)
    else:
        halves = jnp.stack([keep, send])
        normed = jnp.concatenate([halves[core[0]], halves[1 - core[0]]], axis=-1)
        summed = sparse_experts(normed, target_lengths, routes, router, fc_in, fc_out, capacity)
        mixed = (state.astype(jnp.float32) + summed).astype(jnp.bfloat16)
    return mixed[None]


def solution(mesh):
    placed = (
        P(("groups", "expert", "section"), None, None),
        P(("groups", "expert"), None, "section"),
        P(("groups", "expert"), None, "section"),
        P(("groups", "expert", "section")),
        P(("groups", "expert")),
        P(("groups", "expert"), None, None),
        P(),
        P(),
        P(),
        P(None, ("expert", "section")),
        P(("expert", "section"), None),
    )
    return jax.shard_map(
        local,
        mesh=mesh,
        in_specs=placed,
        out_specs=P(("groups", "expert", "section"), None, None),
        check_vma=False,
    )
```

```python
import functools

import jax
import jax.numpy as jnp
from jax import lax
from jax.experimental import pallas as pl
from jax.experimental.pallas import tpu as pltpu
from jax.sharding import PartitionSpec as P

HEAD_DIM = 128


def layer_norm(values, gain):
    centered = values - jnp.mean(values, axis=-1, keepdims=True)
    spread = jnp.mean(centered * centered, axis=-1, keepdims=True)
    return (centered * lax.rsqrt(spread + 1e-05) * gain).astype(jnp.bfloat16)


VMEM = pl.BlockSpec(memory_space=pltpu.VMEM)
SMEM = pl.BlockSpec(memory_space=pltpu.SMEM)


def call(kernel, name, outs, scalars, arrays, scratch=(), vmem_mib=12, cost=None):
    return pl.pallas_call(
        kernel,
        out_shape=tuple(jax.ShapeDtypeStruct(*out) for out in outs),
        in_specs=[SMEM] * len(scalars) + [VMEM] * len(arrays),
        out_specs=(VMEM,) * len(outs),
        scratch_shapes=list(scratch),
        compiler_params=pltpu.CompilerParams(vmem_limit_bytes=vmem_mib * 2**20),
        cost_estimate=cost,
        name=name,
    )(*scalars, *arrays)


def part_of(part, half):
    return pl.ds(pl.multiple_of(part * half, half), half)


def attend_kernel(
    core_ref,
    source_ref,
    target_ref,
    x_ref,
    own_ref,
    other_ref,
    again_ref,
    fgain_ref,
    router_ref,
    routes_ref,
    state_ref,
    keep_ref,
    send_ref,
    gates_ref,
    scratch_ref,
):
    full_len = x_ref.shape[0]
    half = own_ref.shape[-1]
    widened = x_ref[...].astype(jnp.float32)
    scratch_ref[...] = layer_norm(widened, again_ref[...])
    core = core_ref[0]
    keys_seen = own_ref.shape[1]
    valid = lax.broadcasted_iota(jnp.int32, (1, keys_seen), 1) < source_ref[0]
    for part, memory in ((core, own_ref), (1 - core, other_ref)):
        for head in range(half // HEAD_DIM):
            at = head * HEAD_DIM
            span = pl.ds(pl.multiple_of(part * half + at, HEAD_DIM), HEAD_DIM)
            scores = lax.dot_general(
                scratch_ref[:, span],
                memory[0, :, at : at + HEAD_DIM],
                (((1,), (1,)), ((), ())),
                preferred_element_type=jnp.float32,
            ) * HEAD_DIM ** (-0.5)
            scores = jnp.where(valid, scores, -jnp.inf)
            expon = jnp.exp(scores - jnp.max(scores, axis=-1, keepdims=True))
            weights = (expon / jnp.sum(expon, axis=-1, keepdims=True)).astype(jnp.bfloat16)
            attended = jnp.dot(
                weights, memory[1, :, at : at + HEAD_DIM], preferred_element_type=jnp.float32
            )
            state_ref[:, span] = (x_ref[:, span].astype(jnp.float32) + attended).astype(
                jnp.bfloat16
            )
    scratch_ref[...] = layer_norm(state_ref[...].astype(jnp.float32), fgain_ref[...])
    keep_ref[...] = scratch_ref[:, part_of(core, half)]
    send_ref[...] = scratch_ref[:, part_of(1 - core, half)]
    logits = lax.dot_general(
        router_ref[...],
        scratch_ref[...],
        (((1,), (1,)), ((), ())),
        preferred_element_type=jnp.float32,
    )
    names = lax.broadcasted_iota(jnp.int32, logits.shape, 0)
    routes = routes_ref[core]
    chosen = [
        jnp.sum(jnp.where(names == routes[k : k + 1], logits, 0.0), axis=0, keepdims=True)
        for k in range(2)
    ]
    first = jax.nn.sigmoid(chosen[0] - chosen[1])
    live = lax.broadcasted_iota(jnp.int32, (1, full_len), 1) < target_ref[core]
    gates_ref[0:1] = jnp.where(live, first, 0.0)
    gates_ref[1:2] = jnp.where(live, 1.0 - first, 0.0)


def slots_of(routes_ref, experts_count):
    sents, _, full_len = routes_ref.shape
    rows = sents * full_len
    ids = lax.broadcasted_iota(jnp.int32, (max(8, experts_count), full_len), 0)
    named = jnp.concatenate(
        [
            jnp.where((ids == routes_ref[s, 0:1]) | (ids == routes_ref[s, 1:2]), 1.0, 0.0)
            for s in range(sents)
        ],
        axis=1,
    )
    before = lax.broadcasted_iota(jnp.int32, (rows, rows), 0) < lax.broadcasted_iota(
        jnp.int32, (rows, rows), 1
    )
    earlier = jnp.dot(
        named.astype(jnp.bfloat16),
        jnp.where(before, 1.0, 0.0).astype(jnp.bfloat16),
        preferred_element_type=jnp.float32,
    )
    return named > 0.0, earlier


def select_kernel(core_ref, line_ref, routes_ref, own_ref, other_ref, *rest):
    pieces, block_ref = rest[:-1], rest[-1]
    experts_count = len(pieces)
    full_len = own_ref.shape[0]
    capacity = pieces[0].shape[0]
    core = core_ref[0]
    block_ref[part_of(core, full_len)] = own_ref[...]
    block_ref[part_of(1 - core, full_len)] = other_ref[...]
    named, earlier = slots_of(routes_ref, experts_count)
    slot = jnp.where(named, earlier, -1.0)
    ids = lax.broadcasted_iota(jnp.int32, slot.shape, 0)
    numbers = lax.broadcasted_iota(jnp.int32, (capacity, slot.shape[1]), 0).astype(jnp.float32)
    for offset, piece_ref in enumerate(pieces):
        expert = lax.rem(line_ref[0] + offset, experts_count)
        wanted = jnp.sum(jnp.where(ids == expert, slot, 0.0), axis=0, keepdims=True)
        picks = jnp.where(numbers == wanted, 1.0, 0.0).astype(jnp.bfloat16)
        piece_ref[...] = jnp.dot(
            picks, block_ref[...], preferred_element_type=jnp.float32
        ).astype(jnp.bfloat16)


def expert_kernel(
    core_ref, p_ref, q_ref, p2_ref, q2_ref, in_ref, out_ref, keep_ref, send_ref, rows_ref
):
    core = core_ref[0]
    capacity, half = p_ref.shape
    rows_ref[:capacity, part_of(core, half)] = p_ref[...]
    rows_ref[capacity:, part_of(core, half)] = q_ref[...]
    rows_ref[:capacity, part_of(1 - core, half)] = p2_ref[...]
    rows_ref[capacity:, part_of(1 - core, half)] = q2_ref[...]
    hidden = jnp.dot(rows_ref[...], in_ref[...], preferred_element_type=jnp.float32)
    hidden = jnp.maximum(hidden, 0.0).astype(jnp.bfloat16)
    send = jnp.dot(
        hidden, out_ref[:, part_of(1 - core, half)], preferred_element_type=jnp.float32
    ).astype(jnp.bfloat16)
    send_ref[0] = send[:capacity]
    send_ref[1] = send[capacity:]
    keep = jnp.dot(hidden, out_ref[:, part_of(core, half)], preferred_element_type=jnp.float32)
    keep_ref[0] = keep[:capacity]
    keep_ref[1] = keep[capacity:]


def combine_kernel(core_ref, line_ref, routes_ref, own_gates_ref, other_gates_ref, *rest):
    pieces, (own_ref, other_ref, rows_ref, gates_ref, sum_ref) = rest[:-5], rest[-5:]
    experts_count = len(pieces)
    capacity, half = pieces[0].shape
    sents, _, full_len = routes_ref.shape
    core = core_ref[0]
    for offset, piece_ref in enumerate(pieces):
        rows_ref[offset * capacity : (offset + 1) * capacity] = piece_ref[...]
    gates_ref[core] = own_gates_ref[...]
    gates_ref[1 - core] = other_gates_ref[...]
    _, earlier = slots_of(routes_ref, experts_count)
    ids = lax.broadcasted_iota(jnp.int32, (earlier.shape[0], full_len), 0)
    numbers = lax.broadcasted_iota(
        jnp.int32, (full_len, experts_count * capacity), 1
    ).astype(jnp.float32)
    for sent in range(sents):
        slots = earlier[:, sent * full_len : (sent + 1) * full_len]
        total = None
        for k in range(2):
            route = routes_ref[sent, k : k + 1]
            slot = jnp.sum(jnp.where(ids == route, slots, 0.0), axis=0, keepdims=True)
            offset = lax.rem(route - line_ref[0] + experts_count, experts_count)
            place = offset.astype(jnp.float32) * capacity + slot
            place, gate = (
                jnp.broadcast_to(row, (full_len, full_len)).T[:, :1]
                for row in (place, gates_ref[sent, k : k + 1])
            )
            picks = jnp.where(numbers == place, 1.0, 0.0).astype(jnp.bfloat16)
            term = gate * jnp.dot(picks, rows_ref[...], preferred_element_type=jnp.float32)
            total = term if total is None else total + term
        sum_ref[sent] = total
    own_ref[...] = sum_ref[core]
    other_ref[...] = sum_ref[1 - core].astype(jnp.bfloat16)


def finish_kernel(core_ref, state_ref, own_ref, other_ref, mixed_ref):
    core = core_ref[0]
    half = own_ref.shape[-1]
    for part, summed in ((core, own_ref), (1 - core, other_ref)):
        span = part_of(part, half)
        mixed_ref[:, span] = (
            state_ref[:, span].astype(jnp.float32) + summed[...].astype(jnp.float32)
        ).astype(jnp.bfloat16)


def swap(values):
    return lax.ppermute(values, "section", [(0, 1), (1, 0)])


def swap_owner(values):
    owners = lax.axis_size("expert")
    return lax.ppermute(values, "expert", [(i, i ^ 1) for i in range(owners)])


def shift(values, offset):
    owners = lax.axis_size("expert")
    return lax.ppermute(
        values, "expert", [(i, (i + 2 * offset) % owners) for i in range(owners)]
    )


def after_kernel(value_ref, first_ref, out_ref):
    pass


def after(value, first):
    anywhere = pl.BlockSpec(memory_space=pl.ANY)
    return pl.pallas_call(
        after_kernel,
        out_shape=jax.ShapeDtypeStruct(value.shape, value.dtype),
        in_specs=[anywhere, anywhere],
        out_specs=anywhere,
        input_output_aliases={0: 0},
        compiler_params=pltpu.CompilerParams(vmem_limit_bytes=2**20),
        name="after",
    )(value, first)


def piece_order(count):
    return sorted(range(count), key=lambda offset: (offset > 0, -min(offset, count - offset)))


def attend(
    core, decoder_states, memory_keys, memory_values, source_lengths, target_lengths, routes,
    attn_gain, ffn_gain, router,
):
    full_len, width = decoder_states.shape[1:]
    memory = jnp.stack([memory_keys, memory_values], axis=1)
    own = lax.dynamic_index_in_dim(memory, core[0], 0, keepdims=False)
    other = swap(lax.dynamic_index_in_dim(memory, 1 - core[0], 0, keepdims=False))
    half = (full_len, width // 2)
    return call(
        attend_kernel,
        "attend",
        [
            ((full_len, width), jnp.bfloat16),
            (half, jnp.bfloat16),
            (half, jnp.bfloat16),
            ((2, full_len), jnp.float32),
        ],
        [core, source_lengths, target_lengths],
        [
            decoder_states[0],
            own,
            other,
            attn_gain[None],
            ffn_gain[None],
            router.T,
            routes,
        ],
        scratch=[pltpu.VMEM((full_len, width), jnp.bfloat16)],
    )


def line_experts(core, state, keep, send, gates, routes, fc_in, fc_out, capacity):
    full_len, width = state.shape
    half = width // 2
    count = lax.axis_size("expert") // 2
    line = (lax.axis_index("expert") // 2).astype(jnp.int32).reshape(1)
    other = swap(send)
    other_gates = swap(gates)
    piece = ((capacity, half), jnp.bfloat16)
    selected = call(
        select_kernel,
        "select",
        [piece] * count,
        [core, line],
        [routes, keep, other],
        scratch=[pltpu.VMEM((2 * full_len, half), jnp.bfloat16)],
    )
    travelling = [shift(selected[r], r) for r in range(1, count)]
    home = [None] * count
    home = [None] * count
    kepts, halves, wholes = [], [], []
    for at, offset in enumerate(piece_order(count)):
        p = travelling[offset - 1] if offset else selected[0]
        q = swap_owner(p)
        if at >= 2:
            q = after(q, kepts[at - 2])
        p2 = swap(p)
        q2 = swap(q)
        if at >= 2:
            q2 = after(q2, wholes[at - 2])
        kept, sent = call(
            expert_kernel,
            "expert",
            [((2, capacity, half), jnp.float32), ((2, capacity, half), jnp.bfloat16)],
            [core],
            [p, q, p2, q2, fc_in, fc_out],
            scratch=[pltpu.VMEM((2 * capacity, width), jnp.bfloat16)],
            vmem_mib=16,
        )
        kepts.append(kept)
        both = kept + swap(sent).astype(jnp.float32)
        halves.append(both[1].astype(jnp.bfloat16))
        across = swap_owner(halves[-1])
        wholes.append((both[0] + across.astype(jnp.float32)).astype(jnp.bfloat16))
        home[offset] = shift(wholes[-1], -offset) if offset else wholes[-1]
    own_sum, other_sum = call(
        combine_kernel,
        "combine",
        [((full_len, half), jnp.float32), ((full_len, half), jnp.bfloat16)],
        [core, line],
        [routes, gates, other_gates, *home],
        scratch=[
            pltpu.VMEM((count * capacity, half), jnp.bfloat16),
            pltpu.VMEM((2, 2, full_len), jnp.float32),
            pltpu.VMEM((2, full_len, half), jnp.float32),
        ],
    )
    (mixed,) = call(
        finish_kernel,
        "finish",
        [((full_len, width), jnp.bfloat16)],
        [core],
        [state, own_sum, swap(other_sum)],
    )
    return mixed


def expert_apply(slot_rows, fc_in, fc_out):
    width = slot_rows.shape[-1]
    flat_rows = slot_rows.reshape(-1, width)
    hidden = jax.nn.relu(jnp.dot(flat_rows, fc_in, preferred_element_type=jnp.float32)).astype(
        jnp.bfloat16
    )
    produced = jnp.dot(hidden, fc_out, preferred_element_type=jnp.float32)
    return produced.reshape(slot_rows.shape[0], slot_rows.shape[1], width)


def sparse_experts(normed, target_lengths, routes, router, fc_in, fc_out, capacity):
    full_len, width = normed.shape
    all_normed = lax.all_gather(normed[None], "section", axis=0, tiled=True)
    block_sents = all_normed.shape[0]
    block_rows = block_sents * full_len
    tok_rows = all_normed.reshape(block_rows, width)
    owners = lax.axis_size("expert")
    experts_count = owners // 2
    chosen_ids = routes.reshape(block_rows, 2)
    logits = jnp.dot(tok_rows, router, preferred_element_type=jnp.float32)
    onehot = chosen_ids[:, :, None] == jnp.arange(experts_count, dtype=jnp.int32)
    chosen = jnp.sum(jnp.where(onehot, logits[:, None, :], 0.0), axis=-1)
    first = jax.nn.sigmoid(chosen[:, 0] - chosen[:, 1])
    gates = jnp.stack([first, 1.0 - first], axis=-1)
    live = (jnp.arange(full_len, dtype=jnp.int32)[None, :] < target_lengths[:, None]).reshape(
        block_rows
    )
    flags = onehot.reshape(block_rows * 2, experts_count).astype(jnp.int32)
    earlier = jnp.cumsum(flags, axis=0) - flags
    slot = jnp.sum(flags * earlier, axis=-1).reshape(block_rows, 2)
    position = chosen_ids * capacity + slot
    dump_index = experts_count * capacity
    target = jnp.where(live[:, None], position, dump_index)
    row_ids = jnp.broadcast_to(jnp.arange(block_rows, dtype=jnp.int32)[:, None], (block_rows, 2))
    table = (
        jnp.full((dump_index + 1,), block_rows, jnp.int32)
        .at[target.reshape(-1)]
        .set(row_ids.reshape(-1))[:dump_index]
    )
    padded = jnp.concatenate([tok_rows, jnp.zeros((1, width), jnp.bfloat16)], axis=0)
    slot_buffer = padded[table].reshape(experts_count, capacity, width)
    outgoing = jnp.repeat(slot_buffer, 2, axis=0)
    returned = lax.all_to_all(
        expert_apply(
            lax.all_to_all(outgoing, "expert", split_axis=0, concat_axis=0, tiled=True),
            fc_in,
            fc_out,
        ).astype(jnp.bfloat16),
        "expert",
        split_axis=0,
        concat_axis=0,
        tiled=True,
    ).astype(jnp.float32)
    partial_value = jnp.sum(returned.reshape(experts_count, 2, capacity, width), axis=1)
    fetched = partial_value.reshape(dump_index, width)[jnp.where(live[:, None], position, 0)]
    weight = gates * live[:, None].astype(jnp.float32)
    contrib = jnp.sum(weight[:, :, None] * fetched, axis=1).reshape(block_sents, full_len, width)
    summed = lax.psum_scatter(contrib, "section", scatter_dimension=0, tiled=True)
    return summed[0]


def local(
    decoder_states,
    memory_keys,
    memory_values,
    source_lengths,
    target_lengths,
    routes,
    attn_gain,
    ffn_gain,
    router,
    fc_in,
    fc_out,
):
    core = lax.axis_index("section").astype(jnp.int32).reshape(1)
    by_choice = jnp.transpose(routes, (0, 2, 1))
    state, keep, send, gates = attend(
        core, decoder_states, memory_keys, memory_values, source_lengths, target_lengths, by_choice,
        attn_gain, ffn_gain, router,
    )
    block_rows = routes.shape[0] * routes.shape[1]
    experts_count = router.shape[1]
    capacity = 2 * max(1, 3 * block_rows // (2 * experts_count))
    if capacity % 16 == 0:
        mixed = line_experts(core, state, keep, send, gates, by_choice, fc_in, fc_out, capacity)
    else:
        halves = jnp.stack([keep, send])
        normed = jnp.concatenate([halves[core[0]], halves[1 - core[0]]], axis=-1)
        summed = sparse_experts(normed, target_lengths, routes, router, fc_in, fc_out, capacity)
        mixed = (state.astype(jnp.float32) + summed).astype(jnp.bfloat16)
    return mixed[None]


def solution(mesh):
    placed = (
        P(("groups", "expert", "section"), None, None),
        P(("groups", "expert"), None, "section"),
        P(("groups", "expert"), None, "section"),
        P(("groups", "expert", "section")),
        P(("groups", "expert")),
        P(("groups", "expert"), None, None),
        P(),
        P(),
        P(),
        P(None, ("expert", "section")),
        P(("expert", "section"), None),
    )
    return jax.shard_map(
        local,
        mesh=mesh,
        in_specs=placed,
        out_specs=P(("groups", "expert", "section"), None, None),
        check_vma=False,
    )
```

```python
import functools

import jax
import jax.numpy as jnp
from jax import lax
from jax.experimental import pallas as pl
from jax.experimental.pallas import tpu as pltpu
from jax.sharding import PartitionSpec as P

HEAD_DIM = 128


def layer_norm(values, gain):
    centered = values - jnp.mean(values, axis=-1, keepdims=True)
    spread = jnp.mean(centered * centered, axis=-1, keepdims=True)
    return (centered * lax.rsqrt(spread + 1e-05) * gain).astype(jnp.bfloat16)


VMEM = pl.BlockSpec(memory_space=pltpu.VMEM)
SMEM = pl.BlockSpec(memory_space=pltpu.SMEM)


def call(kernel, name, outs, scalars, arrays, scratch=(), vmem_mib=12, cost=None):
    return pl.pallas_call(
        kernel,
        out_shape=tuple(jax.ShapeDtypeStruct(*out) for out in outs),
        in_specs=[SMEM] * len(scalars) + [VMEM] * len(arrays),
        out_specs=(VMEM,) * len(outs),
        scratch_shapes=list(scratch),
        compiler_params=pltpu.CompilerParams(vmem_limit_bytes=vmem_mib * 2**20),
        cost_estimate=cost,
        name=name,
    )(*scalars, *arrays)


def part_of(part, half):
    return pl.ds(pl.multiple_of(part * half, half), half)


def attend_kernel(
    core_ref,
    source_ref,
    target_ref,
    x_ref,
    own_ref,
    other_ref,
    again_ref,
    fgain_ref,
    router_ref,
    routes_ref,
    state_ref,
    keep_ref,
    send_ref,
    gates_ref,
    scratch_ref,
):
    full_len = x_ref.shape[0]
    half = own_ref.shape[-1]
    widened = x_ref[...].astype(jnp.float32)
    scratch_ref[...] = layer_norm(widened, again_ref[...])
    core = core_ref[0]
    keys_seen = own_ref.shape[1]
    valid = lax.broadcasted_iota(jnp.int32, (1, keys_seen), 1) < source_ref[0]
    for part, memory in ((core, own_ref), (1 - core, other_ref)):
        for head in range(half // HEAD_DIM):
            at = head * HEAD_DIM
            span = pl.ds(pl.multiple_of(part * half + at, HEAD_DIM), HEAD_DIM)
            scores = lax.dot_general(
                scratch_ref[:, span],
                memory[0, :, at : at + HEAD_DIM],
                (((1,), (1,)), ((), ())),
                preferred_element_type=jnp.float32,
            ) * HEAD_DIM ** (-0.5)
            scores = jnp.where(valid, scores, -jnp.inf)
            expon = jnp.exp(scores - jnp.max(scores, axis=-1, keepdims=True))
            weights = (expon / jnp.sum(expon, axis=-1, keepdims=True)).astype(jnp.bfloat16)
            attended = jnp.dot(
                weights, memory[1, :, at : at + HEAD_DIM], preferred_element_type=jnp.float32
            )
            state_ref[:, span] = (x_ref[:, span].astype(jnp.float32) + attended).astype(
                jnp.bfloat16
            )
    scratch_ref[...] = layer_norm(state_ref[...].astype(jnp.float32), fgain_ref[...])
    keep_ref[...] = scratch_ref[:, part_of(core, half)]
    send_ref[...] = scratch_ref[:, part_of(1 - core, half)]
    logits = lax.dot_general(
        router_ref[...],
        scratch_ref[...],
        (((1,), (1,)), ((), ())),
        preferred_element_type=jnp.float32,
    )
    names = lax.broadcasted_iota(jnp.int32, logits.shape, 0)
    routes = routes_ref[core]
    chosen = [
        jnp.sum(jnp.where(names == routes[k : k + 1], logits, 0.0), axis=0, keepdims=True)
        for k in range(2)
    ]
    first = jax.nn.sigmoid(chosen[0] - chosen[1])
    live = lax.broadcasted_iota(jnp.int32, (1, full_len), 1) < target_ref[core]
    gates_ref[0:1] = jnp.where(live, first, 0.0)
    gates_ref[1:2] = jnp.where(live, 1.0 - first, 0.0)


def slots_of(routes_ref, experts_count):
    sents, _, full_len = routes_ref.shape
    rows = sents * full_len
    ids = lax.broadcasted_iota(jnp.int32, (max(8, experts_count), full_len), 0)
    named = jnp.concatenate(
        [
            jnp.where((ids == routes_ref[s, 0:1]) | (ids == routes_ref[s, 1:2]), 1.0, 0.0)
            for s in range(sents)
        ],
        axis=1,
    )
    before = lax.broadcasted_iota(jnp.int32, (rows, rows), 0) < lax.broadcasted_iota(
        jnp.int32, (rows, rows), 1
    )
    earlier = jnp.dot(
        named.astype(jnp.bfloat16),
        jnp.where(before, 1.0, 0.0).astype(jnp.bfloat16),
        preferred_element_type=jnp.float32,
    )
    return named > 0.0, earlier


def select_kernel(core_ref, line_ref, routes_ref, own_ref, other_ref, *rest):
    pieces, block_ref = rest[:-1], rest[-1]
    experts_count = len(pieces)
    full_len = own_ref.shape[0]
    capacity = pieces[0].shape[0]
    core = core_ref[0]
    block_ref[part_of(core, full_len)] = own_ref[...]
    block_ref[part_of(1 - core, full_len)] = other_ref[...]
    named, earlier = slots_of(routes_ref, experts_count)
    slot = jnp.where(named, earlier, -1.0)
    ids = lax.broadcasted_iota(jnp.int32, slot.shape, 0)
    numbers = lax.broadcasted_iota(jnp.int32, (capacity, slot.shape[1]), 0).astype(jnp.float32)
    for offset, piece_ref in enumerate(pieces):
        expert = lax.rem(line_ref[0] + offset, experts_count)
        wanted = jnp.sum(jnp.where(ids == expert, slot, 0.0), axis=0, keepdims=True)
        picks = jnp.where(numbers == wanted, 1.0, 0.0).astype(jnp.bfloat16)
        piece_ref[...] = jnp.dot(
            picks, block_ref[...], preferred_element_type=jnp.float32
        ).astype(jnp.bfloat16)


def expert_kernel(
    core_ref, p_ref, q_ref, p2_ref, q2_ref, in_ref, out_ref, keep_ref, send_ref, rows_ref
):
    core = core_ref[0]
    capacity, half = p_ref.shape
    rows_ref[:capacity, part_of(core, half)] = p_ref[...]
    rows_ref[capacity:, part_of(core, half)] = q_ref[...]
    rows_ref[:capacity, part_of(1 - core, half)] = p2_ref[...]
    rows_ref[capacity:, part_of(1 - core, half)] = q2_ref[...]
    hidden = jnp.dot(rows_ref[...], in_ref[...], preferred_element_type=jnp.float32)
    hidden = jnp.maximum(hidden, 0.0).astype(jnp.bfloat16)
    send = jnp.dot(
        hidden, out_ref[:, part_of(1 - core, half)], preferred_element_type=jnp.float32
    ).astype(jnp.bfloat16)
    send_ref[0] = send[:capacity]
    send_ref[1] = send[capacity:]
    keep = jnp.dot(hidden, out_ref[:, part_of(core, half)], preferred_element_type=jnp.float32)
    keep_ref[0] = keep[:capacity]
    keep_ref[1] = keep[capacity:]


def combine_kernel(core_ref, line_ref, routes_ref, own_gates_ref, other_gates_ref, *rest):
    pieces, (own_ref, other_ref, rows_ref, gates_ref, sum_ref) = rest[:-5], rest[-5:]
    experts_count = len(pieces)
    capacity, half = pieces[0].shape
    sents, _, full_len = routes_ref.shape
    core = core_ref[0]
    for offset, piece_ref in enumerate(pieces):
        rows_ref[offset * capacity : (offset + 1) * capacity] = piece_ref[...]
    gates_ref[core] = own_gates_ref[...]
    gates_ref[1 - core] = other_gates_ref[...]
    _, earlier = slots_of(routes_ref, experts_count)
    ids = lax.broadcasted_iota(jnp.int32, (earlier.shape[0], full_len), 0)
    numbers = lax.broadcasted_iota(
        jnp.int32, (full_len, experts_count * capacity), 1
    ).astype(jnp.float32)
    for sent in range(sents):
        slots = earlier[:, sent * full_len : (sent + 1) * full_len]
        total = None
        for k in range(2):
            route = routes_ref[sent, k : k + 1]
            slot = jnp.sum(jnp.where(ids == route, slots, 0.0), axis=0, keepdims=True)
            offset = lax.rem(route - line_ref[0] + experts_count, experts_count)
            place = offset.astype(jnp.float32) * capacity + slot
            place, gate = (
                jnp.broadcast_to(row, (full_len, full_len)).T[:, :1]
                for row in (place, gates_ref[sent, k : k + 1])
            )
            picks = jnp.where(numbers == place, 1.0, 0.0).astype(jnp.bfloat16)
            term = gate * jnp.dot(picks, rows_ref[...], preferred_element_type=jnp.float32)
            total = term if total is None else total + term
        sum_ref[sent] = total
    own_ref[...] = sum_ref[core]
    other_ref[...] = sum_ref[1 - core].astype(jnp.bfloat16)


def finish_kernel(core_ref, state_ref, own_ref, other_ref, mixed_ref):
    core = core_ref[0]
    half = own_ref.shape[-1]
    for part, summed in ((core, own_ref), (1 - core, other_ref)):
        span = part_of(part, half)
        mixed_ref[:, span] = (
            state_ref[:, span].astype(jnp.float32) + summed[...].astype(jnp.float32)
        ).astype(jnp.bfloat16)


def swap(values):
    return lax.ppermute(values, "section", [(0, 1), (1, 0)])


def swap_owner(values):
    owners = lax.axis_size("expert")
    return lax.ppermute(values, "expert", [(i, i ^ 1) for i in range(owners)])


def shift(values, offset):
    owners = lax.axis_size("expert")
    return lax.ppermute(
        values, "expert", [(i, (i + 2 * offset) % owners) for i in range(owners)]
    )


def after_kernel(value_ref, first_ref, out_ref):
    pass


def after(value, first):
    anywhere = pl.BlockSpec(memory_space=pl.ANY)
    return pl.pallas_call(
        after_kernel,
        out_shape=jax.ShapeDtypeStruct(value.shape, value.dtype),
        in_specs=[anywhere, anywhere],
        out_specs=anywhere,
        input_output_aliases={0: 0},
        compiler_params=pltpu.CompilerParams(vmem_limit_bytes=2**20),
        name="after",
    )(value, first)


def piece_order(count):
    return sorted(range(count), key=lambda offset: (offset > 0, -min(offset, count - offset)))


def attend(
    core, decoder_states, memory_keys, memory_values, source_lengths, target_lengths, routes,
    attn_gain, ffn_gain, router,
):
    full_len, width = decoder_states.shape[1:]
    memory = jnp.stack([memory_keys, memory_values], axis=1)
    own = lax.dynamic_index_in_dim(memory, core[0], 0, keepdims=False)
    other = swap(lax.dynamic_index_in_dim(memory, 1 - core[0], 0, keepdims=False))
    half = (full_len, width // 2)
    return call(
        attend_kernel,
        "attend",
        [
            ((full_len, width), jnp.bfloat16),
            (half, jnp.bfloat16),
            (half, jnp.bfloat16),
            ((2, full_len), jnp.float32),
        ],
        [core, source_lengths, target_lengths],
        [
            decoder_states[0],
            own,
            other,
            attn_gain[None],
            ffn_gain[None],
            router.T,
            routes,
        ],
        scratch=[pltpu.VMEM((full_len, width), jnp.bfloat16)],
    )


def line_experts(core, state, keep, send, gates, routes, fc_in, fc_out, capacity):
    full_len, width = state.shape
    half = width // 2
    count = lax.axis_size("expert") // 2
    line = (lax.axis_index("expert") // 2).astype(jnp.int32).reshape(1)
    other = swap(send)
    other_gates = swap(gates)
    piece = ((capacity, half), jnp.bfloat16)
    selected = call(
        select_kernel,
        "select",
        [piece] * count,
        [core, line],
        [routes, keep, other],
        scratch=[pltpu.VMEM((2 * full_len, half), jnp.bfloat16)],
    )
    travelling = [shift(selected[r], r) for r in range(1, count)]
    home = [None] * count
    home = [None] * count
    kepts, halves, wholes = [], [], []
    for at, offset in enumerate(piece_order(count)):
        p = travelling[offset - 1] if offset else selected[0]
        q = swap_owner(p)
        p2 = swap(p)
        q2 = swap(q)
        if at >= 2:
            q2 = after(q2, kepts[at - 2])
        if at >= 2:
            q2 = after(q2, wholes[at - 2])
        kept, sent = call(
            expert_kernel,
            "expert",
            [((2, capacity, half), jnp.float32), ((2, capacity, half), jnp.bfloat16)],
            [core],
            [p, q, p2, q2, fc_in, fc_out],
            scratch=[pltpu.VMEM((2 * capacity, width), jnp.bfloat16)],
            vmem_mib=16,
        )
        kepts.append(kept)
        both = kept + swap(sent).astype(jnp.float32)
        halves.append(both[1].astype(jnp.bfloat16))
        across = swap_owner(halves[-1])
        wholes.append((both[0] + across.astype(jnp.float32)).astype(jnp.bfloat16))
        home[offset] = shift(wholes[-1], -offset) if offset else wholes[-1]
    own_sum, other_sum = call(
        combine_kernel,
        "combine",
        [((full_len, half), jnp.float32), ((full_len, half), jnp.bfloat16)],
        [core, line],
        [routes, gates, other_gates, *home],
        scratch=[
            pltpu.VMEM((count * capacity, half), jnp.bfloat16),
            pltpu.VMEM((2, 2, full_len), jnp.float32),
            pltpu.VMEM((2, full_len, half), jnp.float32),
        ],
    )
    (mixed,) = call(
        finish_kernel,
        "finish",
        [((full_len, width), jnp.bfloat16)],
        [core],
        [state, own_sum, swap(other_sum)],
    )
    return mixed


def expert_apply(slot_rows, fc_in, fc_out):
    width = slot_rows.shape[-1]
    flat_rows = slot_rows.reshape(-1, width)
    hidden = jax.nn.relu(jnp.dot(flat_rows, fc_in, preferred_element_type=jnp.float32)).astype(
        jnp.bfloat16
    )
    produced = jnp.dot(hidden, fc_out, preferred_element_type=jnp.float32)
    return produced.reshape(slot_rows.shape[0], slot_rows.shape[1], width)


def sparse_experts(normed, target_lengths, routes, router, fc_in, fc_out, capacity):
    full_len, width = normed.shape
    all_normed = lax.all_gather(normed[None], "section", axis=0, tiled=True)
    block_sents = all_normed.shape[0]
    block_rows = block_sents * full_len
    tok_rows = all_normed.reshape(block_rows, width)
    owners = lax.axis_size("expert")
    experts_count = owners // 2
    chosen_ids = routes.reshape(block_rows, 2)
    logits = jnp.dot(tok_rows, router, preferred_element_type=jnp.float32)
    onehot = chosen_ids[:, :, None] == jnp.arange(experts_count, dtype=jnp.int32)
    chosen = jnp.sum(jnp.where(onehot, logits[:, None, :], 0.0), axis=-1)
    first = jax.nn.sigmoid(chosen[:, 0] - chosen[:, 1])
    gates = jnp.stack([first, 1.0 - first], axis=-1)
    live = (jnp.arange(full_len, dtype=jnp.int32)[None, :] < target_lengths[:, None]).reshape(
        block_rows
    )
    flags = onehot.reshape(block_rows * 2, experts_count).astype(jnp.int32)
    earlier = jnp.cumsum(flags, axis=0) - flags
    slot = jnp.sum(flags * earlier, axis=-1).reshape(block_rows, 2)
    position = chosen_ids * capacity + slot
    dump_index = experts_count * capacity
    target = jnp.where(live[:, None], position, dump_index)
    row_ids = jnp.broadcast_to(jnp.arange(block_rows, dtype=jnp.int32)[:, None], (block_rows, 2))
    table = (
        jnp.full((dump_index + 1,), block_rows, jnp.int32)
        .at[target.reshape(-1)]
        .set(row_ids.reshape(-1))[:dump_index]
    )
    padded = jnp.concatenate([tok_rows, jnp.zeros((1, width), jnp.bfloat16)], axis=0)
    slot_buffer = padded[table].reshape(experts_count, capacity, width)
    outgoing = jnp.repeat(slot_buffer, 2, axis=0)
    returned = lax.all_to_all(
        expert_apply(
            lax.all_to_all(outgoing, "expert", split_axis=0, concat_axis=0, tiled=True),
            fc_in,
            fc_out,
        ).astype(jnp.bfloat16),
        "expert",
        split_axis=0,
        concat_axis=0,
        tiled=True,
    ).astype(jnp.float32)
    partial_value = jnp.sum(returned.reshape(experts_count, 2, capacity, width), axis=1)
    fetched = partial_value.reshape(dump_index, width)[jnp.where(live[:, None], position, 0)]
    weight = gates * live[:, None].astype(jnp.float32)
    contrib = jnp.sum(weight[:, :, None] * fetched, axis=1).reshape(block_sents, full_len, width)
    summed = lax.psum_scatter(contrib, "section", scatter_dimension=0, tiled=True)
    return summed[0]


def local(
    decoder_states,
    memory_keys,
    memory_values,
    source_lengths,
    target_lengths,
    routes,
    attn_gain,
    ffn_gain,
    router,
    fc_in,
    fc_out,
):
    core = lax.axis_index("section").astype(jnp.int32).reshape(1)
    by_choice = jnp.transpose(routes, (0, 2, 1))
    state, keep, send, gates = attend(
        core, decoder_states, memory_keys, memory_values, source_lengths, target_lengths, by_choice,
        attn_gain, ffn_gain, router,
    )
    block_rows = routes.shape[0] * routes.shape[1]
    experts_count = router.shape[1]
    capacity = 2 * max(1, 3 * block_rows // (2 * experts_count))
    if capacity % 16 == 0:
        mixed = line_experts(core, state, keep, send, gates, by_choice, fc_in, fc_out, capacity)
    else:
        halves = jnp.stack([keep, send])
        normed = jnp.concatenate([halves[core[0]], halves[1 - core[0]]], axis=-1)
        summed = sparse_experts(normed, target_lengths, routes, router, fc_in, fc_out, capacity)
        mixed = (state.astype(jnp.float32) + summed).astype(jnp.bfloat16)
    return mixed[None]


def solution(mesh):
    placed = (
        P(("groups", "expert", "section"), None, None),
        P(("groups", "expert"), None, "section"),
        P(("groups", "expert"), None, "section"),
        P(("groups", "expert", "section")),
        P(("groups", "expert")),
        P(("groups", "expert"), None, None),
        P(),
        P(),
        P(),
        P(None, ("expert", "section")),
        P(("expert", "section"), None),
    )
    return jax.shard_map(
        local,
        mesh=mesh,
        in_specs=placed,
        out_specs=P(("groups", "expert", "section"), None, None),
        check_vma=False,
    )
```

```python
import functools

import jax
import jax.numpy as jnp
from jax import lax
from jax.experimental import pallas as pl
from jax.experimental.pallas import tpu as pltpu
from jax.sharding import PartitionSpec as P

HEAD_DIM = 128


def layer_norm(values, gain):
    centered = values - jnp.mean(values, axis=-1, keepdims=True)
    spread = jnp.mean(centered * centered, axis=-1, keepdims=True)
    return (centered * lax.rsqrt(spread + 1e-05) * gain).astype(jnp.bfloat16)


VMEM = pl.BlockSpec(memory_space=pltpu.VMEM)
SMEM = pl.BlockSpec(memory_space=pltpu.SMEM)


def call(kernel, name, outs, scalars, arrays, scratch=(), vmem_mib=12, cost=None):
    return pl.pallas_call(
        kernel,
        out_shape=tuple(jax.ShapeDtypeStruct(*out) for out in outs),
        in_specs=[SMEM] * len(scalars) + [VMEM] * len(arrays),
        out_specs=(VMEM,) * len(outs),
        scratch_shapes=list(scratch),
        compiler_params=pltpu.CompilerParams(vmem_limit_bytes=vmem_mib * 2**20),
        cost_estimate=cost,
        name=name,
    )(*scalars, *arrays)


def part_of(part, half):
    return pl.ds(pl.multiple_of(part * half, half), half)


def attend_kernel(
    core_ref,
    source_ref,
    target_ref,
    x_ref,
    own_ref,
    other_ref,
    again_ref,
    fgain_ref,
    router_ref,
    routes_ref,
    state_ref,
    keep_ref,
    send_ref,
    gates_ref,
    scratch_ref,
):
    full_len = x_ref.shape[0]
    half = own_ref.shape[-1]
    widened = x_ref[...].astype(jnp.float32)
    scratch_ref[...] = layer_norm(widened, again_ref[...])
    core = core_ref[0]
    keys_seen = own_ref.shape[1]
    valid = lax.broadcasted_iota(jnp.int32, (1, keys_seen), 1) < source_ref[0]
    for part, memory in ((core, own_ref), (1 - core, other_ref)):
        for head in range(half // HEAD_DIM):
            at = head * HEAD_DIM
            span = pl.ds(pl.multiple_of(part * half + at, HEAD_DIM), HEAD_DIM)
            scores = lax.dot_general(
                scratch_ref[:, span],
                memory[0, :, at : at + HEAD_DIM],
                (((1,), (1,)), ((), ())),
                preferred_element_type=jnp.float32,
            ) * HEAD_DIM ** (-0.5)
            scores = jnp.where(valid, scores, -jnp.inf)
            expon = jnp.exp(scores - jnp.max(scores, axis=-1, keepdims=True))
            weights = (expon / jnp.sum(expon, axis=-1, keepdims=True)).astype(jnp.bfloat16)
            attended = jnp.dot(
                weights, memory[1, :, at : at + HEAD_DIM], preferred_element_type=jnp.float32
            )
            state_ref[:, span] = (x_ref[:, span].astype(jnp.float32) + attended).astype(
                jnp.bfloat16
            )
    scratch_ref[...] = layer_norm(state_ref[...].astype(jnp.float32), fgain_ref[...])
    keep_ref[...] = scratch_ref[:, part_of(core, half)]
    send_ref[...] = scratch_ref[:, part_of(1 - core, half)]
    logits = lax.dot_general(
        router_ref[...],
        scratch_ref[...],
        (((1,), (1,)), ((), ())),
        preferred_element_type=jnp.float32,
    )
    names = lax.broadcasted_iota(jnp.int32, logits.shape, 0)
    routes = routes_ref[core]
    chosen = [
        jnp.sum(jnp.where(names == routes[k : k + 1], logits, 0.0), axis=0, keepdims=True)
        for k in range(2)
    ]
    first = jax.nn.sigmoid(chosen[0] - chosen[1])
    live = lax.broadcasted_iota(jnp.int32, (1, full_len), 1) < target_ref[core]
    gates_ref[0:1] = jnp.where(live, first, 0.0)
    gates_ref[1:2] = jnp.where(live, 1.0 - first, 0.0)


def slots_of(routes_ref, experts_count):
    sents, _, full_len = routes_ref.shape
    rows = sents * full_len
    ids = lax.broadcasted_iota(jnp.int32, (max(8, experts_count), full_len), 0)
    named = jnp.concatenate(
        [
            jnp.where((ids == routes_ref[s, 0:1]) | (ids == routes_ref[s, 1:2]), 1.0, 0.0)
            for s in range(sents)
        ],
        axis=1,
    )
    before = lax.broadcasted_iota(jnp.int32, (rows, rows), 0) < lax.broadcasted_iota(
        jnp.int32, (rows, rows), 1
    )
    earlier = jnp.dot(
        named.astype(jnp.bfloat16),
        jnp.where(before, 1.0, 0.0).astype(jnp.bfloat16),
        preferred_element_type=jnp.float32,
    )
    return named > 0.0, earlier


def select_kernel(core_ref, line_ref, routes_ref, own_ref, other_ref, *rest):
    pieces, block_ref = rest[:-1], rest[-1]
    experts_count = len(pieces)
    full_len = own_ref.shape[0]
    capacity = pieces[0].shape[0]
    core = core_ref[0]
    block_ref[part_of(core, full_len)] = own_ref[...]
    block_ref[part_of(1 - core, full_len)] = other_ref[...]
    named, earlier = slots_of(routes_ref, experts_count)
    slot = jnp.where(named, earlier, -1.0)
    ids = lax.broadcasted_iota(jnp.int32, slot.shape, 0)
    numbers = lax.broadcasted_iota(jnp.int32, (capacity, slot.shape[1]), 0).astype(jnp.float32)
    for offset, piece_ref in enumerate(pieces):
        expert = line_ref[0] ^ offset
        wanted = jnp.sum(jnp.where(ids == expert, slot, 0.0), axis=0, keepdims=True)
        picks = jnp.where(numbers == wanted, 1.0, 0.0).astype(jnp.bfloat16)
        piece_ref[...] = jnp.dot(
            picks, block_ref[...], preferred_element_type=jnp.float32
        ).astype(jnp.bfloat16)


def expert_kernel(
    core_ref, p_ref, q_ref, p2_ref, q2_ref, in_ref, out_ref, keep_ref, send_ref, rows_ref
):
    core = core_ref[0]
    capacity, half = p_ref.shape
    rows_ref[:capacity, part_of(core, half)] = p_ref[...]
    rows_ref[capacity:, part_of(core, half)] = q_ref[...]
    rows_ref[:capacity, part_of(1 - core, half)] = p2_ref[...]
    rows_ref[capacity:, part_of(1 - core, half)] = q2_ref[...]
    hidden = jnp.dot(rows_ref[...], in_ref[...], preferred_element_type=jnp.float32)
    hidden = jnp.maximum(hidden, 0.0).astype(jnp.bfloat16)
    send = jnp.dot(
        hidden, out_ref[:, part_of(1 - core, half)], preferred_element_type=jnp.float32
    ).astype(jnp.bfloat16)
    send_ref[0] = send[:capacity]
    send_ref[1] = send[capacity:]
    keep = jnp.dot(hidden, out_ref[:, part_of(core, half)], preferred_element_type=jnp.float32)
    keep_ref[0] = keep[:capacity]
    keep_ref[1] = keep[capacity:]


def combine_kernel(core_ref, line_ref, routes_ref, own_gates_ref, other_gates_ref, *rest):
    pieces, (own_ref, other_ref, rows_ref, gates_ref, sum_ref) = rest[:-5], rest[-5:]
    experts_count = len(pieces)
    capacity, half = pieces[0].shape
    sents, _, full_len = routes_ref.shape
    core = core_ref[0]
    for offset, piece_ref in enumerate(pieces):
        rows_ref[offset * capacity : (offset + 1) * capacity] = piece_ref[...]
    gates_ref[core] = own_gates_ref[...]
    gates_ref[1 - core] = other_gates_ref[...]
    _, earlier = slots_of(routes_ref, experts_count)
    ids = lax.broadcasted_iota(jnp.int32, (earlier.shape[0], full_len), 0)
    numbers = lax.broadcasted_iota(
        jnp.int32, (full_len, experts_count * capacity), 1
    ).astype(jnp.float32)
    for sent in range(sents):
        slots = earlier[:, sent * full_len : (sent + 1) * full_len]
        total = None
        for k in range(2):
            route = routes_ref[sent, k : k + 1]
            slot = jnp.sum(jnp.where(ids == route, slots, 0.0), axis=0, keepdims=True)
            place = (route ^ line_ref[0]).astype(jnp.float32) * capacity + slot
            place, gate = (
                jnp.broadcast_to(row, (full_len, full_len)).T[:, :1]
                for row in (place, gates_ref[sent, k : k + 1])
            )
            picks = jnp.where(numbers == place, 1.0, 0.0).astype(jnp.bfloat16)
            term = gate * jnp.dot(picks, rows_ref[...], preferred_element_type=jnp.float32)
            total = term if total is None else total + term
        sum_ref[sent] = total
    own_ref[...] = sum_ref[core]
    other_ref[...] = sum_ref[1 - core].astype(jnp.bfloat16)


def finish_kernel(core_ref, state_ref, own_ref, other_ref, mixed_ref):
    core = core_ref[0]
    half = own_ref.shape[-1]
    for part, summed in ((core, own_ref), (1 - core, other_ref)):
        span = part_of(part, half)
        mixed_ref[:, span] = (
            state_ref[:, span].astype(jnp.float32) + summed[...].astype(jnp.float32)
        ).astype(jnp.bfloat16)


def swap(values):
    return lax.ppermute(values, "section", [(0, 1), (1, 0)])


def swap_owner(values):
    owners = lax.axis_size("expert")
    return lax.ppermute(values, "expert", [(i, i ^ 1) for i in range(owners)])


def exchange(values, offset):
    owners = lax.axis_size("expert")
    return lax.ppermute(values, "expert", [(i, i ^ (2 * offset)) for i in range(owners)])


def after_kernel(*refs):
    pass


def after(value, *firsts):
    return pl.pallas_call(
        after_kernel,
        out_shape=jax.ShapeDtypeStruct(value.shape, value.dtype),
        in_specs=[pl.BlockSpec(memory_space=pl.ANY)] * (1 + len(firsts)),
        out_specs=pl.BlockSpec(memory_space=pl.ANY),
        input_output_aliases={0: 0},
        compiler_params=pltpu.CompilerParams(vmem_limit_bytes=2**20),
        name="after",
    )(value, *firsts)


def piece_order(count):
    return [0, *range(2, count), 1]


def attend(
    core, decoder_states, memory_keys, memory_values, source_lengths, target_lengths, routes,
    attn_gain, ffn_gain, router,
):
    full_len, width = decoder_states.shape[1:]
    memory = jnp.stack([memory_keys, memory_values], axis=1)
    own = lax.dynamic_index_in_dim(memory, core[0], 0, keepdims=False)
    other = swap(lax.dynamic_index_in_dim(memory, 1 - core[0], 0, keepdims=False))
    half = (full_len, width // 2)
    return call(
        attend_kernel,
        "attend",
        [
            ((full_len, width), jnp.bfloat16),
            (half, jnp.bfloat16),
            (half, jnp.bfloat16),
            ((2, full_len), jnp.float32),
        ],
        [core, source_lengths, target_lengths],
        [
            decoder_states[0],
            own,
            other,
            attn_gain[None],
            ffn_gain[None],
            router.T,
            routes,
        ],
        scratch=[pltpu.VMEM((full_len, width), jnp.bfloat16)],
    )


def line_experts(core, state, keep, send, gates, routes, fc_in, fc_out, capacity):
    full_len, width = state.shape
    half = width // 2
    count = lax.axis_size("expert") // 2
    line = (lax.axis_index("expert") // 2).astype(jnp.int32).reshape(1)
    other = swap(send)
    other_gates = swap(gates)
    piece = ((capacity, half), jnp.bfloat16)
    selected = call(
        select_kernel,
        "select",
        [piece] * count,
        [core, line],
        [routes, keep, other],
        scratch=[pltpu.VMEM((2 * full_len, half), jnp.bfloat16)],
    )
    travelling = [exchange(selected[r], r) for r in range(1, count)]
    order = piece_order(count)
    home = [None] * count
    qs, kepts, halves, wholes, homes = [], [], [], [], []
    for at, offset in enumerate(order):
        p = travelling[offset - 1] if offset else selected[0]
        if at < count - 1:
            coming = travelling[order[at + 1] - 1]
        q = swap_owner(p)
        if at == 0:
            q = after(q, coming)
        if at == 1:
            q = after(q, coming, kepts[at - 1])
        if at == 2:
            q = after(q, coming, wholes[at - 2])
        if at == 3:
            q = after(q, wholes[at - 2])
        qs.append(q)
        p2 = swap(p)
        q2 = swap(q)
        kept, sent = call(
            expert_kernel,
            "expert",
            [((2, capacity, half), jnp.float32), ((2, capacity, half), jnp.bfloat16)],
            [core],
            [p, q, p2, q2, fc_in, fc_out],
            scratch=[pltpu.VMEM((2 * capacity, width), jnp.bfloat16)],
            vmem_mib=16,
        )
        kepts.append(kept)
        moved = swap(sent)
        if at == 3:
            moved = after(moved, wholes[at - 1])
        both = kept + moved.astype(jnp.float32)
        halves.append(both[1].astype(jnp.bfloat16))
        across = swap_owner(halves[-1])
        wholes.append((both[0] + across.astype(jnp.float32)).astype(jnp.bfloat16))
        homes.append(exchange(wholes[-1], offset) if offset else wholes[-1])
        home[offset] = homes[-1]
    own_sum, other_sum = call(
        combine_kernel,
        "combine",
        [((full_len, half), jnp.float32), ((full_len, half), jnp.bfloat16)],
        [core, line],
        [routes, gates, other_gates, *home],
        scratch=[
            pltpu.VMEM((count * capacity, half), jnp.bfloat16),
            pltpu.VMEM((2, 2, full_len), jnp.float32),
            pltpu.VMEM((2, full_len, half), jnp.float32),
        ],
    )
    (mixed,) = call(
        finish_kernel,
        "finish",
        [((full_len, width), jnp.bfloat16)],
        [core],
        [state, own_sum, swap(other_sum)],
    )
    return mixed


def expert_apply(slot_rows, fc_in, fc_out):
    width = slot_rows.shape[-1]
    flat_rows = slot_rows.reshape(-1, width)
    hidden = jax.nn.relu(jnp.dot(flat_rows, fc_in, preferred_element_type=jnp.float32)).astype(
        jnp.bfloat16
    )
    produced = jnp.dot(hidden, fc_out, preferred_element_type=jnp.float32)
    return produced.reshape(slot_rows.shape[0], slot_rows.shape[1], width)


def sparse_experts(normed, target_lengths, routes, router, fc_in, fc_out, capacity):
    full_len, width = normed.shape
    all_normed = lax.all_gather(normed[None], "section", axis=0, tiled=True)
    block_sents = all_normed.shape[0]
    block_rows = block_sents * full_len
    tok_rows = all_normed.reshape(block_rows, width)
    owners = lax.axis_size("expert")
    experts_count = owners // 2
    chosen_ids = routes.reshape(block_rows, 2)
    logits = jnp.dot(tok_rows, router, preferred_element_type=jnp.float32)
    onehot = chosen_ids[:, :, None] == jnp.arange(experts_count, dtype=jnp.int32)
    chosen = jnp.sum(jnp.where(onehot, logits[:, None, :], 0.0), axis=-1)
    first = jax.nn.sigmoid(chosen[:, 0] - chosen[:, 1])
    gates = jnp.stack([first, 1.0 - first], axis=-1)
    live = (jnp.arange(full_len, dtype=jnp.int32)[None, :] < target_lengths[:, None]).reshape(
        block_rows
    )
    flags = onehot.reshape(block_rows * 2, experts_count).astype(jnp.int32)
    earlier = jnp.cumsum(flags, axis=0) - flags
    slot = jnp.sum(flags * earlier, axis=-1).reshape(block_rows, 2)
    position = chosen_ids * capacity + slot
    dump_index = experts_count * capacity
    target = jnp.where(live[:, None], position, dump_index)
    row_ids = jnp.broadcast_to(jnp.arange(block_rows, dtype=jnp.int32)[:, None], (block_rows, 2))
    table = (
        jnp.full((dump_index + 1,), block_rows, jnp.int32)
        .at[target.reshape(-1)]
        .set(row_ids.reshape(-1))[:dump_index]
    )
    padded = jnp.concatenate([tok_rows, jnp.zeros((1, width), jnp.bfloat16)], axis=0)
    slot_buffer = padded[table].reshape(experts_count, capacity, width)
    outgoing = jnp.repeat(slot_buffer, 2, axis=0)
    returned = lax.all_to_all(
        expert_apply(
            lax.all_to_all(outgoing, "expert", split_axis=0, concat_axis=0, tiled=True),
            fc_in,
            fc_out,
        ).astype(jnp.bfloat16),
        "expert",
        split_axis=0,
        concat_axis=0,
        tiled=True,
    ).astype(jnp.float32)
    partial_value = jnp.sum(returned.reshape(experts_count, 2, capacity, width), axis=1)
    fetched = partial_value.reshape(dump_index, width)[jnp.where(live[:, None], position, 0)]
    weight = gates * live[:, None].astype(jnp.float32)
    contrib = jnp.sum(weight[:, :, None] * fetched, axis=1).reshape(block_sents, full_len, width)
    summed = lax.psum_scatter(contrib, "section", scatter_dimension=0, tiled=True)
    return summed[0]


def local(
    decoder_states,
    memory_keys,
    memory_values,
    source_lengths,
    target_lengths,
    routes,
    attn_gain,
    ffn_gain,
    router,
    fc_in,
    fc_out,
):
    core = lax.axis_index("section").astype(jnp.int32).reshape(1)
    by_choice = jnp.transpose(routes, (0, 2, 1))
    state, keep, send, gates = attend(
        core, decoder_states, memory_keys, memory_values, source_lengths, target_lengths, by_choice,
        attn_gain, ffn_gain, router,
    )
    block_rows = routes.shape[0] * routes.shape[1]
    experts_count = router.shape[1]
    capacity = 2 * max(1, 3 * block_rows // (2 * experts_count))
    if capacity % 16 == 0 and experts_count & (experts_count - 1) == 0:
        mixed = line_experts(core, state, keep, send, gates, by_choice, fc_in, fc_out, capacity)
    else:
        halves = jnp.stack([keep, send])
        normed = jnp.concatenate([halves[core[0]], halves[1 - core[0]]], axis=-1)
        summed = sparse_experts(normed, target_lengths, routes, router, fc_in, fc_out, capacity)
        mixed = (state.astype(jnp.float32) + summed).astype(jnp.bfloat16)
    return mixed[None]


def solution(mesh):
    placed = (
        P(("groups", "expert", "section"), None, None),
        P(("groups", "expert"), None, "section"),
        P(("groups", "expert"), None, "section"),
        P(("groups", "expert", "section")),
        P(("groups", "expert")),
        P(("groups", "expert"), None, None),
        P(),
        P(),
        P(),
        P(None, ("expert", "section")),
        P(("expert", "section"), None),
    )
    return jax.shard_map(
        local,
        mesh=mesh,
        in_specs=placed,
        out_specs=P(("groups", "expert", "section"), None, None),
        check_vma=False,
    )
```

```python
import functools

import jax
import jax.numpy as jnp
from jax import lax
from jax.experimental import pallas as pl
from jax.experimental.pallas import tpu as pltpu
from jax.sharding import PartitionSpec as P

HEAD_DIM = 128


def layer_norm(values, gain):
    centered = values - jnp.mean(values, axis=-1, keepdims=True)
    spread = jnp.mean(centered * centered, axis=-1, keepdims=True)
    return (centered * lax.rsqrt(spread + 1e-05) * gain).astype(jnp.bfloat16)


VMEM = pl.BlockSpec(memory_space=pltpu.VMEM)
SMEM = pl.BlockSpec(memory_space=pltpu.SMEM)


def call(kernel, name, outs, scalars, arrays, scratch=(), vmem_mib=12, cost=None):
    return pl.pallas_call(
        kernel,
        out_shape=tuple(jax.ShapeDtypeStruct(*out) for out in outs),
        in_specs=[SMEM] * len(scalars) + [VMEM] * len(arrays),
        out_specs=(VMEM,) * len(outs),
        scratch_shapes=list(scratch),
        compiler_params=pltpu.CompilerParams(vmem_limit_bytes=vmem_mib * 2**20),
        cost_estimate=cost,
        name=name,
    )(*scalars, *arrays)


def part_of(part, half):
    return pl.ds(pl.multiple_of(part * half, half), half)


def attend_kernel(
    core_ref,
    source_ref,
    target_ref,
    x_ref,
    own_ref,
    other_ref,
    again_ref,
    fgain_ref,
    router_ref,
    routes_ref,
    state_ref,
    keep_ref,
    send_ref,
    gates_ref,
    scratch_ref,
):
    full_len = x_ref.shape[0]
    half = own_ref.shape[-1]
    widened = x_ref[...].astype(jnp.float32)
    scratch_ref[...] = layer_norm(widened, again_ref[...])
    core = core_ref[0]
    keys_seen = own_ref.shape[1]
    valid = lax.broadcasted_iota(jnp.int32, (1, keys_seen), 1) < source_ref[0]
    for part, memory in ((core, own_ref), (1 - core, other_ref)):
        for head in range(half // HEAD_DIM):
            at = head * HEAD_DIM
            span = pl.ds(pl.multiple_of(part * half + at, HEAD_DIM), HEAD_DIM)
            scores = lax.dot_general(
                scratch_ref[:, span],
                memory[0, :, at : at + HEAD_DIM],
                (((1,), (1,)), ((), ())),
                preferred_element_type=jnp.float32,
            ) * HEAD_DIM ** (-0.5)
            scores = jnp.where(valid, scores, -jnp.inf)
            expon = jnp.exp(scores - jnp.max(scores, axis=-1, keepdims=True))
            weights = (expon / jnp.sum(expon, axis=-1, keepdims=True)).astype(jnp.bfloat16)
            attended = jnp.dot(
                weights, memory[1, :, at : at + HEAD_DIM], preferred_element_type=jnp.float32
            )
            state_ref[:, span] = (x_ref[:, span].astype(jnp.float32) + attended).astype(
                jnp.bfloat16
            )
    scratch_ref[...] = layer_norm(state_ref[...].astype(jnp.float32), fgain_ref[...])
    keep_ref[...] = scratch_ref[:, part_of(core, half)]
    send_ref[...] = scratch_ref[:, part_of(1 - core, half)]
    logits = lax.dot_general(
        router_ref[...],
        scratch_ref[...],
        (((1,), (1,)), ((), ())),
        preferred_element_type=jnp.float32,
    )
    names = lax.broadcasted_iota(jnp.int32, logits.shape, 0)
    routes = routes_ref[core]
    chosen = [
        jnp.sum(jnp.where(names == routes[k : k + 1], logits, 0.0), axis=0, keepdims=True)
        for k in range(2)
    ]
    first = jax.nn.sigmoid(chosen[0] - chosen[1])
    live = lax.broadcasted_iota(jnp.int32, (1, full_len), 1) < target_ref[core]
    gates_ref[0:1] = jnp.where(live, first, 0.0)
    gates_ref[1:2] = jnp.where(live, 1.0 - first, 0.0)


def slots_of(routes_ref, experts_count):
    sents, _, full_len = routes_ref.shape
    rows = sents * full_len
    ids = lax.broadcasted_iota(jnp.int32, (max(8, experts_count), full_len), 0)
    named = jnp.concatenate(
        [
            jnp.where((ids == routes_ref[s, 0:1]) | (ids == routes_ref[s, 1:2]), 1.0, 0.0)
            for s in range(sents)
        ],
        axis=1,
    )
    before = lax.broadcasted_iota(jnp.int32, (rows, rows), 0) < lax.broadcasted_iota(
        jnp.int32, (rows, rows), 1
    )
    earlier = jnp.dot(
        named.astype(jnp.bfloat16),
        jnp.where(before, 1.0, 0.0).astype(jnp.bfloat16),
        preferred_element_type=jnp.float32,
    )
    return named > 0.0, earlier


def select_kernel(core_ref, line_ref, routes_ref, own_ref, other_ref, *rest):
    pieces, block_ref = rest[:-1], rest[-1]
    experts_count = len(pieces)
    full_len = own_ref.shape[0]
    capacity = pieces[0].shape[0]
    core = core_ref[0]
    block_ref[part_of(core, full_len)] = own_ref[...]
    block_ref[part_of(1 - core, full_len)] = other_ref[...]
    named, earlier = slots_of(routes_ref, experts_count)
    slot = jnp.where(named, earlier, -1.0)
    ids = lax.broadcasted_iota(jnp.int32, slot.shape, 0)
    numbers = lax.broadcasted_iota(jnp.int32, (capacity, slot.shape[1]), 0).astype(jnp.float32)
    for offset, piece_ref in enumerate(pieces):
        expert = lax.rem(line_ref[0] + offset, experts_count)
        wanted = jnp.sum(jnp.where(ids == expert, slot, 0.0), axis=0, keepdims=True)
        picks = jnp.where(numbers == wanted, 1.0, 0.0).astype(jnp.bfloat16)
        piece_ref[...] = jnp.dot(
            picks, block_ref[...], preferred_element_type=jnp.float32
        ).astype(jnp.bfloat16)


def expert_kernel(
    core_ref, p_ref, q_ref, p2_ref, q2_ref, in_ref, out_ref, keep_ref, send_ref, rows_ref
):
    core = core_ref[0]
    capacity, half = p_ref.shape
    rows_ref[:capacity, part_of(core, half)] = p_ref[...]
    rows_ref[capacity:, part_of(core, half)] = q_ref[...]
    rows_ref[:capacity, part_of(1 - core, half)] = p2_ref[...]
    rows_ref[capacity:, part_of(1 - core, half)] = q2_ref[...]
    hidden = jnp.dot(rows_ref[...], in_ref[...], preferred_element_type=jnp.float32)
    hidden = jnp.maximum(hidden, 0.0).astype(jnp.bfloat16)
    send = jnp.dot(
        hidden, out_ref[:, part_of(1 - core, half)], preferred_element_type=jnp.float32
    ).astype(jnp.bfloat16)
    send_ref[0] = send[:capacity]
    send_ref[1] = send[capacity:]
    keep = jnp.dot(hidden, out_ref[:, part_of(core, half)], preferred_element_type=jnp.float32)
    keep_ref[0] = keep[:capacity]
    keep_ref[1] = keep[capacity:]


def combine_kernel(core_ref, line_ref, routes_ref, own_gates_ref, other_gates_ref, *rest):
    pieces, (own_ref, other_ref, rows_ref, gates_ref, sum_ref) = rest[:-5], rest[-5:]
    experts_count = len(pieces)
    capacity, half = pieces[0].shape
    sents, _, full_len = routes_ref.shape
    core = core_ref[0]
    for offset, piece_ref in enumerate(pieces):
        rows_ref[offset * capacity : (offset + 1) * capacity] = piece_ref[...]
    gates_ref[core] = own_gates_ref[...]
    gates_ref[1 - core] = other_gates_ref[...]
    _, earlier = slots_of(routes_ref, experts_count)
    ids = lax.broadcasted_iota(jnp.int32, (earlier.shape[0], full_len), 0)
    numbers = lax.broadcasted_iota(
        jnp.int32, (full_len, experts_count * capacity), 1
    ).astype(jnp.float32)
    for sent in range(sents):
        slots = earlier[:, sent * full_len : (sent + 1) * full_len]
        total = None
        for k in range(2):
            route = routes_ref[sent, k : k + 1]
            slot = jnp.sum(jnp.where(ids == route, slots, 0.0), axis=0, keepdims=True)
            offset = lax.rem(route - line_ref[0] + experts_count, experts_count)
            place = offset.astype(jnp.float32) * capacity + slot
            place, gate = (
                jnp.broadcast_to(row, (full_len, full_len)).T[:, :1]
                for row in (place, gates_ref[sent, k : k + 1])
            )
            picks = jnp.where(numbers == place, 1.0, 0.0).astype(jnp.bfloat16)
            term = gate * jnp.dot(picks, rows_ref[...], preferred_element_type=jnp.float32)
            total = term if total is None else total + term
        sum_ref[sent] = total
    own_ref[...] = sum_ref[core]
    other_ref[...] = sum_ref[1 - core].astype(jnp.bfloat16)


def finish_kernel(core_ref, state_ref, own_ref, other_ref, mixed_ref):
    core = core_ref[0]
    half = own_ref.shape[-1]
    for part, summed in ((core, own_ref), (1 - core, other_ref)):
        span = part_of(part, half)
        mixed_ref[:, span] = (
            state_ref[:, span].astype(jnp.float32) + summed[...].astype(jnp.float32)
        ).astype(jnp.bfloat16)


def swap(values):
    return lax.ppermute(values, "section", [(0, 1), (1, 0)])


def swap_owner(values):
    owners = lax.axis_size("expert")
    return lax.ppermute(values, "expert", [(i, i ^ 1) for i in range(owners)])


def shift(values, offset):
    owners = lax.axis_size("expert")
    return lax.ppermute(
        values, "expert", [(i, (i + 2 * offset) % owners) for i in range(owners)]
    )


def after_kernel(value_ref, first_ref, out_ref):
    pass


def after(value, first):
    anywhere = pl.BlockSpec(memory_space=pl.ANY)
    return pl.pallas_call(
        after_kernel,
        out_shape=jax.ShapeDtypeStruct(value.shape, value.dtype),
        in_specs=[anywhere, anywhere],
        out_specs=anywhere,
        input_output_aliases={0: 0},
        compiler_params=pltpu.CompilerParams(vmem_limit_bytes=2**20),
        name="after",
    )(value, first)


def piece_order(count):
    return sorted(range(count), key=lambda offset: (offset > 0, -min(offset, count - offset)))


def attend(
    core, decoder_states, memory_keys, memory_values, source_lengths, target_lengths, routes,
    attn_gain, ffn_gain, router,
):
    full_len, width = decoder_states.shape[1:]
    memory = jnp.stack([memory_keys, memory_values], axis=1)
    own = lax.dynamic_index_in_dim(memory, core[0], 0, keepdims=False)
    other = swap(lax.dynamic_index_in_dim(memory, 1 - core[0], 0, keepdims=False))
    half = (full_len, width // 2)
    return call(
        attend_kernel,
        "attend",
        [
            ((full_len, width), jnp.bfloat16),
            (half, jnp.bfloat16),
            (half, jnp.bfloat16),
            ((2, full_len), jnp.float32),
        ],
        [core, source_lengths, target_lengths],
        [
            decoder_states[0],
            own,
            other,
            attn_gain[None],
            ffn_gain[None],
            router.T,
            routes,
        ],
        scratch=[pltpu.VMEM((full_len, width), jnp.bfloat16)],
    )


def line_experts(core, state, keep, send, gates, routes, fc_in, fc_out, capacity):
    full_len, width = state.shape
    half = width // 2
    count = lax.axis_size("expert") // 2
    line = (lax.axis_index("expert") // 2).astype(jnp.int32).reshape(1)
    other = swap(send)
    other_gates = swap(gates)
    piece = ((capacity, half), jnp.bfloat16)
    selected = call(
        select_kernel,
        "select",
        [piece] * count,
        [core, line],
        [routes, keep, other],
        scratch=[pltpu.VMEM((2 * full_len, half), jnp.bfloat16)],
    )
    travelling = [shift(selected[r], r) for r in range(1, count)]
    home = [None] * count
    home = [None] * count
    kepts, halves, wholes = [], [], []
    for at, offset in enumerate(piece_order(count)):
        p = travelling[offset - 1] if offset else selected[0]
        q = swap_owner(p)
        p2 = swap(p)
        q2 = swap(q)
        if at >= 2:
            q2 = after(q2, kepts[at - 2])
        if at >= 2:
            q2 = after(q2, halves[at - 2])
        kept, sent = call(
            expert_kernel,
            "expert",
            [((2, capacity, half), jnp.float32), ((2, capacity, half), jnp.bfloat16)],
            [core],
            [p, q, p2, q2, fc_in, fc_out],
            scratch=[pltpu.VMEM((2 * capacity, width), jnp.bfloat16)],
            vmem_mib=16,
        )
        kepts.append(kept)
        both = kept + swap(sent).astype(jnp.float32)
        halves.append(both[1].astype(jnp.bfloat16))
        across = swap_owner(halves[-1])
        wholes.append((both[0] + across.astype(jnp.float32)).astype(jnp.bfloat16))
        home[offset] = shift(wholes[-1], -offset) if offset else wholes[-1]
    own_sum, other_sum = call(
        combine_kernel,
        "combine",
        [((full_len, half), jnp.float32), ((full_len, half), jnp.bfloat16)],
        [core, line],
        [routes, gates, other_gates, *home],
        scratch=[
            pltpu.VMEM((count * capacity, half), jnp.bfloat16),
            pltpu.VMEM((2, 2, full_len), jnp.float32),
            pltpu.VMEM((2, full_len, half), jnp.float32),
        ],
    )
    (mixed,) = call(
        finish_kernel,
        "finish",
        [((full_len, width), jnp.bfloat16)],
        [core],
        [state, own_sum, swap(other_sum)],
    )
    return mixed


def expert_apply(slot_rows, fc_in, fc_out):
    width = slot_rows.shape[-1]
    flat_rows = slot_rows.reshape(-1, width)
    hidden = jax.nn.relu(jnp.dot(flat_rows, fc_in, preferred_element_type=jnp.float32)).astype(
        jnp.bfloat16
    )
    produced = jnp.dot(hidden, fc_out, preferred_element_type=jnp.float32)
    return produced.reshape(slot_rows.shape[0], slot_rows.shape[1], width)


def sparse_experts(normed, target_lengths, routes, router, fc_in, fc_out, capacity):
    full_len, width = normed.shape
    all_normed = lax.all_gather(normed[None], "section", axis=0, tiled=True)
    block_sents = all_normed.shape[0]
    block_rows = block_sents * full_len
    tok_rows = all_normed.reshape(block_rows, width)
    owners = lax.axis_size("expert")
    experts_count = owners // 2
    chosen_ids = routes.reshape(block_rows, 2)
    logits = jnp.dot(tok_rows, router, preferred_element_type=jnp.float32)
    onehot = chosen_ids[:, :, None] == jnp.arange(experts_count, dtype=jnp.int32)
    chosen = jnp.sum(jnp.where(onehot, logits[:, None, :], 0.0), axis=-1)
    first = jax.nn.sigmoid(chosen[:, 0] - chosen[:, 1])
    gates = jnp.stack([first, 1.0 - first], axis=-1)
    live = (jnp.arange(full_len, dtype=jnp.int32)[None, :] < target_lengths[:, None]).reshape(
        block_rows
    )
    flags = onehot.reshape(block_rows * 2, experts_count).astype(jnp.int32)
    earlier = jnp.cumsum(flags, axis=0) - flags
    slot = jnp.sum(flags * earlier, axis=-1).reshape(block_rows, 2)
    position = chosen_ids * capacity + slot
    dump_index = experts_count * capacity
    target = jnp.where(live[:, None], position, dump_index)
    row_ids = jnp.broadcast_to(jnp.arange(block_rows, dtype=jnp.int32)[:, None], (block_rows, 2))
    table = (
        jnp.full((dump_index + 1,), block_rows, jnp.int32)
        .at[target.reshape(-1)]
        .set(row_ids.reshape(-1))[:dump_index]
    )
    padded = jnp.concatenate([tok_rows, jnp.zeros((1, width), jnp.bfloat16)], axis=0)
    slot_buffer = padded[table].reshape(experts_count, capacity, width)
    outgoing = jnp.repeat(slot_buffer, 2, axis=0)
    returned = lax.all_to_all(
        expert_apply(
            lax.all_to_all(outgoing, "expert", split_axis=0, concat_axis=0, tiled=True),
            fc_in,
            fc_out,
        ).astype(jnp.bfloat16),
        "expert",
        split_axis=0,
        concat_axis=0,
        tiled=True,
    ).astype(jnp.float32)
    partial_value = jnp.sum(returned.reshape(experts_count, 2, capacity, width), axis=1)
    fetched = partial_value.reshape(dump_index, width)[jnp.where(live[:, None], position, 0)]
    weight = gates * live[:, None].astype(jnp.float32)
    contrib = jnp.sum(weight[:, :, None] * fetched, axis=1).reshape(block_sents, full_len, width)
    summed = lax.psum_scatter(contrib, "section", scatter_dimension=0, tiled=True)
    return summed[0]


def local(
    decoder_states,
    memory_keys,
    memory_values,
    source_lengths,
    target_lengths,
    routes,
    attn_gain,
    ffn_gain,
    router,
    fc_in,
    fc_out,
):
    core = lax.axis_index("section").astype(jnp.int32).reshape(1)
    by_choice = jnp.transpose(routes, (0, 2, 1))
    state, keep, send, gates = attend(
        core, decoder_states, memory_keys, memory_values, source_lengths, target_lengths, by_choice,
        attn_gain, ffn_gain, router,
    )
    block_rows = routes.shape[0] * routes.shape[1]
    experts_count = router.shape[1]
    capacity = 2 * max(1, 3 * block_rows // (2 * experts_count))
    if capacity % 16 == 0:
        mixed = line_experts(core, state, keep, send, gates, by_choice, fc_in, fc_out, capacity)
    else:
        halves = jnp.stack([keep, send])
        normed = jnp.concatenate([halves[core[0]], halves[1 - core[0]]], axis=-1)
        summed = sparse_experts(normed, target_lengths, routes, router, fc_in, fc_out, capacity)
        mixed = (state.astype(jnp.float32) + summed).astype(jnp.bfloat16)
    return mixed[None]


def solution(mesh):
    placed = (
        P(("groups", "expert", "section"), None, None),
        P(("groups", "expert"), None, "section"),
        P(("groups", "expert"), None, "section"),
        P(("groups", "expert", "section")),
        P(("groups", "expert")),
        P(("groups", "expert"), None, None),
        P(),
        P(),
        P(),
        P(None, ("expert", "section")),
        P(("expert", "section"), None),
    )
    return jax.shard_map(
        local,
        mesh=mesh,
        in_specs=placed,
        out_specs=P(("groups", "expert", "section"), None, None),
        check_vma=False,
    )
```

```python
import functools

import jax
import jax.numpy as jnp
from jax import lax
from jax.experimental import pallas as pl
from jax.experimental.pallas import tpu as pltpu
from jax.sharding import PartitionSpec as P

HEAD_DIM = 128


def layer_norm(values, gain):
    centered = values - jnp.mean(values, axis=-1, keepdims=True)
    spread = jnp.mean(centered * centered, axis=-1, keepdims=True)
    return (centered * lax.rsqrt(spread + 1e-05) * gain).astype(jnp.bfloat16)


VMEM = pl.BlockSpec(memory_space=pltpu.VMEM)
SMEM = pl.BlockSpec(memory_space=pltpu.SMEM)
HBM = pl.BlockSpec(memory_space=pltpu.HBM)


def call(kernel, name, outs, scalars, arrays, far=(), scratch=(), vmem_mib=12):
    return pl.pallas_call(
        kernel,
        out_shape=tuple(jax.ShapeDtypeStruct(*out) for out in outs),
        in_specs=[SMEM] * len(scalars) + [VMEM] * len(arrays) + [HBM] * len(far),
        out_specs=(VMEM,) * len(outs),
        scratch_shapes=list(scratch),
        compiler_params=pltpu.CompilerParams(vmem_limit_bytes=vmem_mib * 2**20),
        name=name,
    )(*scalars, *arrays, *(pltpu.with_memory_space_constraint(a, pltpu.HBM) for a in far))


def fetch(sems, *pairs):
    copies = [
        pltpu.make_async_copy(source, target, sems.at[i]) for i, (source, target) in enumerate(pairs)
    ]
    for copy in copies:
        copy.start()
    return copies


def part_of(part, half):
    return pl.ds(pl.multiple_of(part * half, half), half)


def attend_half(queries, keys, values, length):
    rows = queries.shape[0]
    heads = [slice(at, at + HEAD_DIM) for at in range(0, queries.shape[1], HEAD_DIM)]
    scores = jnp.concatenate(
        [
            lax.dot_general(
                queries[:, head],
                keys[:, head],
                (((1,), (1,)), ((), ())),
                preferred_element_type=jnp.float32,
            )
            for head in heads
        ],
        axis=0,
    ) * HEAD_DIM ** (-0.5)
    valid = lax.broadcasted_iota(jnp.int32, (1, keys.shape[0]), 1) < length
    scores = jnp.where(valid, scores, -jnp.inf)
    expon = jnp.exp(scores - jnp.max(scores, axis=-1, keepdims=True))
    weights = (expon / jnp.sum(expon, axis=-1, keepdims=True)).astype(jnp.bfloat16)
    return jnp.concatenate(
        [
            jnp.dot(
                weights[i * rows : (i + 1) * rows],
                values[:, head],
                preferred_element_type=jnp.float32,
            )
            for i, head in enumerate(heads)
        ],
        axis=1,
    )


def add_rounded(x, attended):
    return (x.astype(jnp.float32) + attended).astype(jnp.bfloat16)


def attend_own_kernel(
    core_ref,
    source_ref,
    x_in,
    gain_in,
    keys_in,
    values_in,
    state_ref,
    query_ref,
    rest_ref,
    x_ref,
    gain_ref,
    keys_ref,
    values_ref,
    scratch_ref,
    sems,
):
    core = core_ref[0]
    copies = fetch(
        sems,
        (x_in.at[0], x_ref),
        (gain_in, gain_ref),
        (keys_in.at[core], keys_ref),
        (values_in.at[core], values_ref),
    )
    half = keys_ref.shape[1]
    copies[0].wait()
    copies[1].wait()
    scratch_ref[...] = layer_norm(x_ref[...].astype(jnp.float32), gain_ref[...])
    own, other = part_of(core, half), part_of(1 - core, half)
    query_ref[...] = scratch_ref[:, other]
    rest_ref[...] = x_ref[:, other]
    copies[2].wait()
    copies[3].wait()
    attended = attend_half(scratch_ref[:, own], keys_ref[...], values_ref[...], source_ref[0])
    state_ref[...] = add_rounded(x_ref[:, own], attended)


def attend_other_kernel(
    core_ref,
    source_ref,
    own_ref,
    query_ref,
    rest_ref,
    keys_ref,
    values_ref,
    gain_in,
    router_in,
    routes_in,
    target_in,
    state_ref,
    keep_ref,
    send_ref,
    gates_ref,
    routes_ref,
    gain_ref,
    router_ref,
    target_ref,
    scratch_ref,
    sems,
):
    core = core_ref[0]
    copies = fetch(
        sems,
        (gain_in, gain_ref),
        (router_in, router_ref),
        (routes_in, routes_ref),
        (target_in, target_ref),
    )
    full_len, half = own_ref.shape
    own, other = part_of(core, half), part_of(1 - core, half)
    attended = attend_half(query_ref[...], keys_ref[core], values_ref[core], source_ref[0])
    state_ref[:, own] = own_ref[...]
    state_ref[:, other] = add_rounded(rest_ref[...], attended)
    copies[0].wait()
    scratch_ref[...] = layer_norm(state_ref[...].astype(jnp.float32), gain_ref[...])
    keep_ref[...] = scratch_ref[:, own]
    send_ref[...] = scratch_ref[:, other]
    for copy in copies[1:]:
        copy.wait()
    logits = lax.dot_general(
        router_ref[...],
        scratch_ref[...],
        (((1,), (1,)), ((), ())),
        preferred_element_type=jnp.float32,
    )
    names = lax.broadcasted_iota(jnp.int32, logits.shape, 0)
    routes = routes_ref[core]
    chosen = [
        jnp.sum(jnp.where(names == routes[k : k + 1], logits, 0.0), axis=0, keepdims=True)
        for k in range(2)
    ]
    first = jax.nn.sigmoid(chosen[0] - chosen[1])
    live = lax.broadcasted_iota(jnp.int32, (1, full_len), 1) < target_ref[core]
    gates_ref[0:1] = jnp.where(live, first, 0.0)
    gates_ref[1:2] = jnp.where(live, 1.0 - first, 0.0)


def slots_of(routes_ref, experts_count):
    sents, _, full_len = routes_ref.shape
    rows = sents * full_len
    ids = lax.broadcasted_iota(jnp.int32, (max(8, experts_count), full_len), 0)
    named = jnp.concatenate(
        [
            jnp.where((ids == routes_ref[s, 0:1]) | (ids == routes_ref[s, 1:2]), 1.0, 0.0)
            for s in range(sents)
        ],
        axis=1,
    )
    before = lax.broadcasted_iota(jnp.int32, (rows, rows), 0) < lax.broadcasted_iota(
        jnp.int32, (rows, rows), 1
    )
    earlier = jnp.dot(
        named.astype(jnp.bfloat16),
        jnp.where(before, 1.0, 0.0).astype(jnp.bfloat16),
        preferred_element_type=jnp.float32,
    )
    return named > 0.0, earlier


def select_kernel(core_ref, line_ref, routes_ref, own_ref, other_ref, *rest):
    pieces, block_ref = rest[:-1], rest[-1]
    experts_count = len(pieces)
    full_len = own_ref.shape[0]
    capacity = pieces[0].shape[0]
    core = core_ref[0]
    block_ref[part_of(core, full_len)] = own_ref[...]
    block_ref[part_of(1 - core, full_len)] = other_ref[...]
    named, earlier = slots_of(routes_ref, experts_count)
    slot = jnp.where(named, earlier, -1.0)
    ids = lax.broadcasted_iota(jnp.int32, slot.shape, 0)
    numbers = lax.broadcasted_iota(jnp.int32, (capacity, slot.shape[1]), 0).astype(jnp.float32)
    for offset, piece_ref in enumerate(pieces):
        expert = lax.rem(line_ref[0] + offset, experts_count)
        wanted = jnp.sum(jnp.where(ids == expert, slot, 0.0), axis=0, keepdims=True)
        picks = jnp.where(numbers == wanted, 1.0, 0.0).astype(jnp.bfloat16)
        piece_ref[...] = jnp.dot(
            picks, block_ref[...], preferred_element_type=jnp.float32
        ).astype(jnp.bfloat16)


def expert_kernel(
    core_ref, p_ref, q_ref, p2_ref, q2_ref, in_ref, out_ref, keep_ref, send_ref, rows_ref
):
    core = core_ref[0]
    capacity, half = p_ref.shape
    rows_ref[:capacity, part_of(core, half)] = p_ref[...]
    rows_ref[capacity:, part_of(core, half)] = q_ref[...]
    rows_ref[:capacity, part_of(1 - core, half)] = p2_ref[...]
    rows_ref[capacity:, part_of(1 - core, half)] = q2_ref[...]
    hidden = jnp.dot(rows_ref[...], in_ref[...], preferred_element_type=jnp.float32)
    hidden = jnp.maximum(hidden, 0.0).astype(jnp.bfloat16)
    send = jnp.dot(
        hidden, out_ref[:, part_of(1 - core, half)], preferred_element_type=jnp.float32
    ).astype(jnp.bfloat16)
    send_ref[0] = send[:capacity]
    send_ref[1] = send[capacity:]
    keep = jnp.dot(hidden, out_ref[:, part_of(core, half)], preferred_element_type=jnp.float32)
    keep_ref[0] = keep[:capacity]
    keep_ref[1] = keep[capacity:]


def first_expert_kernel(
    core_ref,
    p_ref,
    q_ref,
    p2_ref,
    q2_ref,
    in_in,
    out_in,
    keep_ref,
    send_ref,
    rows_ref,
    in_ref,
    out_ref,
    hidden_ref,
    sems,
):
    core = core_ref[0]
    capacity, half = p_ref.shape
    tile = in_ref.shape[1] // 4
    tiles = [slice(at, at + tile) for at in range(0, in_ref.shape[1], tile)]
    copies = fetch(
        sems,
        *[(in_in.at[:, at], in_ref.at[:, at]) for at in tiles],
        (out_in, out_ref),
    )
    rows_ref[:capacity, part_of(core, half)] = p_ref[...]
    rows_ref[capacity:, part_of(core, half)] = q_ref[...]
    rows_ref[:capacity, part_of(1 - core, half)] = p2_ref[...]
    rows_ref[capacity:, part_of(1 - core, half)] = q2_ref[...]
    for copy, at in zip(copies, tiles):
        copy.wait()
        hidden = jnp.dot(rows_ref[...], in_ref[:, at], preferred_element_type=jnp.float32)
        hidden_ref[:, at] = jnp.maximum(hidden, 0.0).astype(jnp.bfloat16)
    copies[-1].wait()
    send = jnp.dot(
        hidden_ref[...], out_ref[:, part_of(1 - core, half)], preferred_element_type=jnp.float32
    ).astype(jnp.bfloat16)
    send_ref[0] = send[:capacity]
    send_ref[1] = send[capacity:]
    keep = jnp.dot(
        hidden_ref[...], out_ref[:, part_of(core, half)], preferred_element_type=jnp.float32
    )
    keep_ref[0] = keep[:capacity]
    keep_ref[1] = keep[capacity:]


def combine_kernel(core_ref, line_ref, routes_ref, own_gates_ref, other_gates_ref, *rest):
    pieces, (own_ref, other_ref, rows_ref, gates_ref, sum_ref) = rest[:-5], rest[-5:]
    experts_count = len(pieces)
    capacity, half = pieces[0].shape
    sents, _, full_len = routes_ref.shape
    core = core_ref[0]
    for offset, piece_ref in enumerate(pieces):
        rows_ref[offset * capacity : (offset + 1) * capacity] = piece_ref[...]
    gates_ref[core] = own_gates_ref[...]
    gates_ref[1 - core] = other_gates_ref[...]
    _, earlier = slots_of(routes_ref, experts_count)
    ids = lax.broadcasted_iota(jnp.int32, (earlier.shape[0], full_len), 0)
    numbers = lax.broadcasted_iota(
        jnp.int32, (full_len, experts_count * capacity), 1
    ).astype(jnp.float32)
    for sent in range(sents):
        slots = earlier[:, sent * full_len : (sent + 1) * full_len]
        total = None
        for k in range(2):
            route = routes_ref[sent, k : k + 1]
            slot = jnp.sum(jnp.where(ids == route, slots, 0.0), axis=0, keepdims=True)
            offset = lax.rem(route - line_ref[0] + experts_count, experts_count)
            place = offset.astype(jnp.float32) * capacity + slot
            place, gate = (
                jnp.broadcast_to(row, (full_len, full_len)).T[:, :1]
                for row in (place, gates_ref[sent, k : k + 1])
            )
            picks = jnp.where(numbers == place, 1.0, 0.0).astype(jnp.bfloat16)
            term = gate * jnp.dot(picks, rows_ref[...], preferred_element_type=jnp.float32)
            total = term if total is None else total + term
        sum_ref[sent] = total
    own_ref[...] = sum_ref[core]
    other_ref[...] = sum_ref[1 - core].astype(jnp.bfloat16)


def finish_kernel(core_ref, state_ref, own_ref, other_ref, mixed_ref):
    core = core_ref[0]
    half = own_ref.shape[-1]
    for part, summed in ((core, own_ref), (1 - core, other_ref)):
        span = part_of(part, half)
        mixed_ref[:, span] = (
            state_ref[:, span].astype(jnp.float32) + summed[...].astype(jnp.float32)
        ).astype(jnp.bfloat16)


def swap(values):
    return lax.ppermute(values, "section", [(0, 1), (1, 0)])


def swap_owner(values):
    owners = lax.axis_size("expert")
    return lax.ppermute(values, "expert", [(i, i ^ 1) for i in range(owners)])


def shift(values, offset):
    owners = lax.axis_size("expert")
    return lax.ppermute(
        values, "expert", [(i, (i + 2 * offset) % owners) for i in range(owners)]
    )


def after_kernel(value_ref, first_ref, out_ref):
    pass


def after(value, first):
    anywhere = pl.BlockSpec(memory_space=pl.ANY)
    return pl.pallas_call(
        after_kernel,
        out_shape=jax.ShapeDtypeStruct(value.shape, value.dtype),
        in_specs=[anywhere, anywhere],
        out_specs=anywhere,
        input_output_aliases={0: 0},
        compiler_params=pltpu.CompilerParams(vmem_limit_bytes=2**20),
        name="after",
    )(value, first)


def piece_order(count):
    return sorted(range(count), key=lambda offset: (offset > 0, -min(offset, count - offset)))


def attend(
    core, decoder_states, memory_keys, memory_values, source_lengths, target_lengths, routes,
    attn_gain, ffn_gain, router,
):
    full_len, width = decoder_states.shape[1:]
    half = (full_len, width // 2)
    memory = memory_keys.shape[1:]
    other_keys, other_values = swap(memory_keys), swap(memory_values)
    own, query, rest = call(
        attend_own_kernel,
        "attend_own",
        [(half, jnp.bfloat16)] * 3,
        [core, source_lengths],
        [],
        [decoder_states, attn_gain[None], memory_keys, memory_values],
        scratch=[
            pltpu.VMEM((full_len, width), jnp.bfloat16),
            pltpu.VMEM((1, width), jnp.float32),
            pltpu.VMEM(memory, jnp.bfloat16),
            pltpu.VMEM(memory, jnp.bfloat16),
            pltpu.VMEM((full_len, width), jnp.bfloat16),
            pltpu.SemaphoreType.DMA((4,)),
        ],
    )
    return call(
        attend_other_kernel,
        "attend_other",
        [
            ((full_len, width), jnp.bfloat16),
            (half, jnp.bfloat16),
            (half, jnp.bfloat16),
            ((2, full_len), jnp.float32),
            (routes.shape, jnp.int32),
        ],
        [core, source_lengths],
        [own, query, rest, other_keys, other_values],
        [ffn_gain[None], router.T, routes, target_lengths],
        scratch=[
            pltpu.VMEM((1, width), jnp.float32),
            pltpu.VMEM(router.shape[::-1], jnp.bfloat16),
            pltpu.SMEM(target_lengths.shape, jnp.int32),
            pltpu.VMEM((full_len, width), jnp.bfloat16),
            pltpu.SemaphoreType.DMA((4,)),
        ],
    )


def line_experts(core, state, keep, send, gates, routes, fc_in, fc_out, capacity):
    full_len, width = state.shape
    half = width // 2
    count = lax.axis_size("expert") // 2
    line = (lax.axis_index("expert") // 2).astype(jnp.int32).reshape(1)
    other = swap(send)
    other_gates = swap(gates)
    piece = ((capacity, half), jnp.bfloat16)
    selected = call(
        select_kernel,
        "select",
        [piece] * count,
        [core, line],
        [routes, keep, other],
        scratch=[pltpu.VMEM((2 * full_len, half), jnp.bfloat16)],
    )
    travelling = [shift(selected[r], r) for r in range(1, count)]
    home = [None] * count
    home = [None] * count
    kepts, halves, wholes = [], [], []
    for at, offset in enumerate(piece_order(count)):
        p = travelling[offset - 1] if offset else selected[0]
        q = swap_owner(p)
        p2 = swap(p)
        q2 = swap(q)
        if at >= 2:
            q2 = after(q2, kepts[at - 2])
        if at >= 2:
            q2 = after(q2, halves[at - 2])
        outs = [((2, capacity, half), jnp.float32), ((2, capacity, half), jnp.bfloat16)]
        rows = pltpu.VMEM((2 * capacity, width), jnp.bfloat16)
        if at == 0:
            kept, sent = call(
                first_expert_kernel,
                "first_expert",
                outs,
                [core],
                [p, q, p2, q2],
                [fc_in, fc_out],
                scratch=[
                    rows,
                    pltpu.VMEM(fc_in.shape, jnp.bfloat16),
                    pltpu.VMEM(fc_out.shape, jnp.bfloat16),
                    pltpu.VMEM((2 * capacity, fc_in.shape[1]), jnp.bfloat16),
                    pltpu.SemaphoreType.DMA((5,)),
                ],
                vmem_mib=20,
            )
        else:
            kept, sent = call(
                expert_kernel,
                "expert",
                outs,
                [core],
                [p, q, p2, q2, fc_in, fc_out],
                scratch=[rows],
                vmem_mib=16,
            )
        kepts.append(kept)
        both = kept + swap(sent).astype(jnp.float32)
        halves.append(both[1].astype(jnp.bfloat16))
        across = swap_owner(halves[-1])
        wholes.append((both[0] + across.astype(jnp.float32)).astype(jnp.bfloat16))
        home[offset] = shift(wholes[-1], -offset) if offset else wholes[-1]
    own_sum, other_sum = call(
        combine_kernel,
        "combine",
        [((full_len, half), jnp.float32), ((full_len, half), jnp.bfloat16)],
        [core, line],
        [routes, gates, other_gates, *home],
        scratch=[
            pltpu.VMEM((count * capacity, half), jnp.bfloat16),
            pltpu.VMEM((2, 2, full_len), jnp.float32),
            pltpu.VMEM((2, full_len, half), jnp.float32),
        ],
    )
    (mixed,) = call(
        finish_kernel,
        "finish",
        [((full_len, width), jnp.bfloat16)],
        [core],
        [state, own_sum, swap(other_sum)],
    )
    return mixed


def expert_apply(slot_rows, fc_in, fc_out):
    width = slot_rows.shape[-1]
    flat_rows = slot_rows.reshape(-1, width)
    hidden = jax.nn.relu(jnp.dot(flat_rows, fc_in, preferred_element_type=jnp.float32)).astype(
        jnp.bfloat16
    )
    produced = jnp.dot(hidden, fc_out, preferred_element_type=jnp.float32)
    return produced.reshape(slot_rows.shape[0], slot_rows.shape[1], width)


def sparse_experts(normed, target_lengths, routes, router, fc_in, fc_out, capacity):
    full_len, width = normed.shape
    all_normed = lax.all_gather(normed[None], "section", axis=0, tiled=True)
    block_sents = all_normed.shape[0]
    block_rows = block_sents * full_len
    tok_rows = all_normed.reshape(block_rows, width)
    owners = lax.axis_size("expert")
    experts_count = owners // 2
    chosen_ids = routes.reshape(block_rows, 2)
    logits = jnp.dot(tok_rows, router, preferred_element_type=jnp.float32)
    onehot = chosen_ids[:, :, None] == jnp.arange(experts_count, dtype=jnp.int32)
    chosen = jnp.sum(jnp.where(onehot, logits[:, None, :], 0.0), axis=-1)
    first = jax.nn.sigmoid(chosen[:, 0] - chosen[:, 1])
    gates = jnp.stack([first, 1.0 - first], axis=-1)
    live = (jnp.arange(full_len, dtype=jnp.int32)[None, :] < target_lengths[:, None]).reshape(
        block_rows
    )
    flags = onehot.reshape(block_rows * 2, experts_count).astype(jnp.int32)
    earlier = jnp.cumsum(flags, axis=0) - flags
    slot = jnp.sum(flags * earlier, axis=-1).reshape(block_rows, 2)
    position = chosen_ids * capacity + slot
    dump_index = experts_count * capacity
    target = jnp.where(live[:, None], position, dump_index)
    row_ids = jnp.broadcast_to(jnp.arange(block_rows, dtype=jnp.int32)[:, None], (block_rows, 2))
    table = (
        jnp.full((dump_index + 1,), block_rows, jnp.int32)
        .at[target.reshape(-1)]
        .set(row_ids.reshape(-1))[:dump_index]
    )
    padded = jnp.concatenate([tok_rows, jnp.zeros((1, width), jnp.bfloat16)], axis=0)
    slot_buffer = padded[table].reshape(experts_count, capacity, width)
    outgoing = jnp.repeat(slot_buffer, 2, axis=0)
    returned = lax.all_to_all(
        expert_apply(
            lax.all_to_all(outgoing, "expert", split_axis=0, concat_axis=0, tiled=True),
            fc_in,
            fc_out,
        ).astype(jnp.bfloat16),
        "expert",
        split_axis=0,
        concat_axis=0,
        tiled=True,
    ).astype(jnp.float32)
    partial_value = jnp.sum(returned.reshape(experts_count, 2, capacity, width), axis=1)
    fetched = partial_value.reshape(dump_index, width)[jnp.where(live[:, None], position, 0)]
    weight = gates * live[:, None].astype(jnp.float32)
    contrib = jnp.sum(weight[:, :, None] * fetched, axis=1).reshape(block_sents, full_len, width)
    summed = lax.psum_scatter(contrib, "section", scatter_dimension=0, tiled=True)
    return summed[0]


def local(
    decoder_states,
    memory_keys,
    memory_values,
    source_lengths,
    target_lengths,
    routes,
    attn_gain,
    ffn_gain,
    router,
    fc_in,
    fc_out,
):
    core = lax.axis_index("section").astype(jnp.int32).reshape(1)
    by_choice = jnp.transpose(routes, (0, 2, 1))
    state, keep, send, gates, by_choice = attend(
        core, decoder_states, memory_keys, memory_values, source_lengths, target_lengths, by_choice,
        attn_gain, ffn_gain, router,
    )
    block_rows = routes.shape[0] * routes.shape[1]
    experts_count = router.shape[1]
    capacity = 2 * max(1, 3 * block_rows // (2 * experts_count))
    if capacity % 16 == 0:
        mixed = line_experts(core, state, keep, send, gates, by_choice, fc_in, fc_out, capacity)
    else:
        halves = jnp.stack([keep, send])
        normed = jnp.concatenate([halves[core[0]], halves[1 - core[0]]], axis=-1)
        summed = sparse_experts(normed, target_lengths, routes, router, fc_in, fc_out, capacity)
        mixed = (state.astype(jnp.float32) + summed).astype(jnp.bfloat16)
    return mixed[None]


def solution(mesh):
    placed = (
        P(("groups", "expert", "section"), None, None),
        P(("groups", "expert"), None, "section"),
        P(("groups", "expert"), None, "section"),
        P(("groups", "expert", "section")),
        P(("groups", "expert")),
        P(("groups", "expert"), None, None),
        P(),
        P(),
        P(),
        P(None, ("expert", "section")),
        P(("expert", "section"), None),
    )
    return jax.shard_map(
        local,
        mesh=mesh,
        in_specs=placed,
        out_specs=P(("groups", "expert", "section"), None, None),
        check_vma=False,
    )
```

```python
import functools

import jax
import jax.numpy as jnp
from jax import lax
from jax.experimental import pallas as pl
from jax.experimental.pallas import tpu as pltpu
from jax.sharding import PartitionSpec as P

HEAD_DIM = 128


def layer_norm(values, gain):
    centered = values - jnp.mean(values, axis=-1, keepdims=True)
    spread = jnp.mean(centered * centered, axis=-1, keepdims=True)
    return (centered * lax.rsqrt(spread + 1e-05) * gain).astype(jnp.bfloat16)


VMEM = pl.BlockSpec(memory_space=pltpu.VMEM)
SMEM = pl.BlockSpec(memory_space=pltpu.SMEM)
HBM = pl.BlockSpec(memory_space=pltpu.HBM)


def call(kernel, name, outs, scalars, arrays, far=(), scratch=(), vmem_mib=12):
    return pl.pallas_call(
        kernel,
        out_shape=tuple(jax.ShapeDtypeStruct(*out) for out in outs),
        in_specs=[SMEM] * len(scalars) + [VMEM] * len(arrays) + [HBM] * len(far),
        out_specs=(VMEM,) * len(outs),
        scratch_shapes=list(scratch),
        compiler_params=pltpu.CompilerParams(vmem_limit_bytes=vmem_mib * 2**20),
        name=name,
    )(*scalars, *arrays, *(pltpu.with_memory_space_constraint(a, pltpu.HBM) for a in far))


def fetch(sems, *pairs):
    copies = [
        pltpu.make_async_copy(source, target, sems.at[i]) for i, (source, target) in enumerate(pairs)
    ]
    for copy in copies:
        copy.start()
    return copies


def part_of(part, half):
    return pl.ds(pl.multiple_of(part * half, half), half)


def attend_half(queries, keys, values, length):
    rows = queries.shape[0]
    heads = [slice(at, at + HEAD_DIM) for at in range(0, queries.shape[1], HEAD_DIM)]
    scores = jnp.concatenate(
        [
            lax.dot_general(
                queries[:, head],
                keys[:, head],
                (((1,), (1,)), ((), ())),
                preferred_element_type=jnp.float32,
            )
            for head in heads
        ],
        axis=0,
    ) * HEAD_DIM ** (-0.5)
    valid = lax.broadcasted_iota(jnp.int32, (1, keys.shape[0]), 1) < length
    scores = jnp.where(valid, scores, -jnp.inf)
    expon = jnp.exp(scores - jnp.max(scores, axis=-1, keepdims=True))
    weights = (expon / jnp.sum(expon, axis=-1, keepdims=True)).astype(jnp.bfloat16)
    return jnp.concatenate(
        [
            jnp.dot(
                weights[i * rows : (i + 1) * rows],
                values[:, head],
                preferred_element_type=jnp.float32,
            )
            for i, head in enumerate(heads)
        ],
        axis=1,
    )


def add_rounded(x, attended):
    return (x.astype(jnp.float32) + attended).astype(jnp.bfloat16)


def attend_own_kernel(
    core_ref,
    source_ref,
    x_in,
    gain_in,
    keys_in,
    values_in,
    state_ref,
    query_ref,
    rest_ref,
    x_ref,
    gain_ref,
    keys_ref,
    values_ref,
    scratch_ref,
    sems,
):
    core = core_ref[0]
    copies = fetch(
        sems,
        (x_in.at[0], x_ref),
        (gain_in, gain_ref),
        (keys_in.at[core], keys_ref),
        (values_in.at[core], values_ref),
    )
    half = keys_ref.shape[1]
    copies[0].wait()
    copies[1].wait()
    scratch_ref[...] = layer_norm(x_ref[...].astype(jnp.float32), gain_ref[...])
    own, other = part_of(core, half), part_of(1 - core, half)
    query_ref[...] = scratch_ref[:, other]
    rest_ref[...] = x_ref[:, other]
    copies[2].wait()
    copies[3].wait()
    attended = attend_half(scratch_ref[:, own], keys_ref[...], values_ref[...], source_ref[0])
    state_ref[...] = add_rounded(x_ref[:, own], attended)


def attend_other_kernel(
    core_ref,
    source_ref,
    own_ref,
    query_ref,
    rest_ref,
    keys_ref,
    values_ref,
    gain_in,
    router_in,
    routes_in,
    target_in,
    state_ref,
    keep_ref,
    send_ref,
    gates_ref,
    routes_ref,
    gain_ref,
    router_ref,
    target_ref,
    scratch_ref,
    sems,
):
    core = core_ref[0]
    copies = fetch(
        sems,
        (gain_in, gain_ref),
        (router_in, router_ref),
        (routes_in, routes_ref),
        (target_in, target_ref),
    )
    full_len, half = own_ref.shape
    own, other = part_of(core, half), part_of(1 - core, half)
    attended = attend_half(query_ref[...], keys_ref[core], values_ref[core], source_ref[0])
    state_ref[:, own] = own_ref[...]
    state_ref[:, other] = add_rounded(rest_ref[...], attended)
    copies[0].wait()
    scratch_ref[...] = layer_norm(state_ref[...].astype(jnp.float32), gain_ref[...])
    keep_ref[...] = scratch_ref[:, own]
    send_ref[...] = scratch_ref[:, other]
    for copy in copies[1:]:
        copy.wait()
    logits = lax.dot_general(
        router_ref[...],
        scratch_ref[...],
        (((1,), (1,)), ((), ())),
        preferred_element_type=jnp.float32,
    )
    names = lax.broadcasted_iota(jnp.int32, logits.shape, 0)
    routes = routes_ref[core]
    chosen = [
        jnp.sum(jnp.where(names == routes[k : k + 1], logits, 0.0), axis=0, keepdims=True)
        for k in range(2)
    ]
    first = jax.nn.sigmoid(chosen[0] - chosen[1])
    live = lax.broadcasted_iota(jnp.int32, (1, full_len), 1) < target_ref[core]
    gates_ref[0:1] = jnp.where(live, first, 0.0)
    gates_ref[1:2] = jnp.where(live, 1.0 - first, 0.0)


def slots_of(routes_ref, experts_count):
    sents, _, full_len = routes_ref.shape
    rows = sents * full_len
    ids = lax.broadcasted_iota(jnp.int32, (max(8, experts_count), full_len), 0)
    named = jnp.concatenate(
        [
            jnp.where((ids == routes_ref[s, 0:1]) | (ids == routes_ref[s, 1:2]), 1.0, 0.0)
            for s in range(sents)
        ],
        axis=1,
    )
    before = lax.broadcasted_iota(jnp.int32, (rows, rows), 0) < lax.broadcasted_iota(
        jnp.int32, (rows, rows), 1
    )
    earlier = jnp.dot(
        named.astype(jnp.bfloat16),
        jnp.where(before, 1.0, 0.0).astype(jnp.bfloat16),
        preferred_element_type=jnp.float32,
    )
    return named > 0.0, earlier


def select_kernel(core_ref, line_ref, routes_ref, own_ref, other_ref, *rest):
    pieces, block_ref = rest[:-1], rest[-1]
    experts_count = len(pieces)
    full_len = own_ref.shape[0]
    capacity = pieces[0].shape[0]
    core = core_ref[0]
    block_ref[part_of(core, full_len)] = own_ref[...]
    block_ref[part_of(1 - core, full_len)] = other_ref[...]
    named, earlier = slots_of(routes_ref, experts_count)
    slot = jnp.where(named, earlier, -1.0)
    ids = lax.broadcasted_iota(jnp.int32, slot.shape, 0)
    numbers = lax.broadcasted_iota(jnp.int32, (capacity, slot.shape[1]), 0).astype(jnp.float32)
    for offset, piece_ref in enumerate(pieces):
        expert = lax.rem(line_ref[0] + offset, experts_count)
        wanted = jnp.sum(jnp.where(ids == expert, slot, 0.0), axis=0, keepdims=True)
        picks = jnp.where(numbers == wanted, 1.0, 0.0).astype(jnp.bfloat16)
        piece_ref[...] = jnp.dot(
            picks, block_ref[...], preferred_element_type=jnp.float32
        ).astype(jnp.bfloat16)


def expert_kernel(
    core_ref, p_ref, q_ref, p2_ref, q2_ref, in_ref, out_ref, keep_ref, send_ref, rows_ref
):
    core = core_ref[0]
    capacity, half = p_ref.shape
    rows_ref[:capacity, part_of(core, half)] = p_ref[...]
    rows_ref[capacity:, part_of(core, half)] = q_ref[...]
    rows_ref[:capacity, part_of(1 - core, half)] = p2_ref[...]
    rows_ref[capacity:, part_of(1 - core, half)] = q2_ref[...]
    hidden = jnp.dot(rows_ref[...], in_ref[...], preferred_element_type=jnp.float32)
    hidden = jnp.maximum(hidden, 0.0).astype(jnp.bfloat16)
    send = jnp.dot(
        hidden, out_ref[:, part_of(1 - core, half)], preferred_element_type=jnp.float32
    ).astype(jnp.bfloat16)
    send_ref[0] = send[:capacity]
    send_ref[1] = send[capacity:]
    keep = jnp.dot(hidden, out_ref[:, part_of(core, half)], preferred_element_type=jnp.float32)
    keep_ref[0] = keep[:capacity]
    keep_ref[1] = keep[capacity:]


def first_expert_kernel(
    core_ref,
    p_ref,
    q_ref,
    p2_ref,
    q2_ref,
    in_in,
    out_in,
    keep_ref,
    send_ref,
    rows_ref,
    in_ref,
    out_ref,
    hidden_ref,
    sems,
):
    core = core_ref[0]
    capacity, half = p_ref.shape
    tile = in_ref.shape[1] // 4
    tiles = [slice(at, at + tile) for at in range(0, in_ref.shape[1], tile)]
    copies = fetch(
        sems,
        *[(in_in.at[:, at], in_ref.at[:, at]) for at in tiles],
        (out_in, out_ref),
    )
    rows_ref[:capacity, part_of(core, half)] = p_ref[...]
    rows_ref[capacity:, part_of(core, half)] = q_ref[...]
    rows_ref[:capacity, part_of(1 - core, half)] = p2_ref[...]
    rows_ref[capacity:, part_of(1 - core, half)] = q2_ref[...]
    for copy, at in zip(copies, tiles):
        copy.wait()
        hidden = jnp.dot(rows_ref[...], in_ref[:, at], preferred_element_type=jnp.float32)
        hidden_ref[:, at] = jnp.maximum(hidden, 0.0).astype(jnp.bfloat16)
    copies[-1].wait()
    send = jnp.dot(
        hidden_ref[...], out_ref[:, part_of(1 - core, half)], preferred_element_type=jnp.float32
    ).astype(jnp.bfloat16)
    send_ref[0] = send[:capacity]
    send_ref[1] = send[capacity:]
    keep = jnp.dot(
        hidden_ref[...], out_ref[:, part_of(core, half)], preferred_element_type=jnp.float32
    )
    keep_ref[0] = keep[:capacity]
    keep_ref[1] = keep[capacity:]


def combine_kernel(core_ref, line_ref, routes_ref, own_gates_ref, other_gates_ref, *rest):
    pieces, (own_ref, other_ref, rows_ref, gates_ref, sum_ref) = rest[:-5], rest[-5:]
    experts_count = len(pieces)
    capacity, half = pieces[0].shape
    sents, _, full_len = routes_ref.shape
    core = core_ref[0]
    for offset, piece_ref in enumerate(pieces):
        rows_ref[offset * capacity : (offset + 1) * capacity] = piece_ref[...]
    gates_ref[core] = own_gates_ref[...]
    gates_ref[1 - core] = other_gates_ref[...]
    _, earlier = slots_of(routes_ref, experts_count)
    ids = lax.broadcasted_iota(jnp.int32, (earlier.shape[0], full_len), 0)
    numbers = lax.broadcasted_iota(
        jnp.int32, (full_len, experts_count * capacity), 1
    ).astype(jnp.float32)
    for sent in range(sents):
        slots = earlier[:, sent * full_len : (sent + 1) * full_len]
        total = None
        for k in range(2):
            route = routes_ref[sent, k : k + 1]
            slot = jnp.sum(jnp.where(ids == route, slots, 0.0), axis=0, keepdims=True)
            offset = lax.rem(route - line_ref[0] + experts_count, experts_count)
            place = offset.astype(jnp.float32) * capacity + slot
            place, gate = (
                jnp.broadcast_to(row, (full_len, full_len)).T[:, :1]
                for row in (place, gates_ref[sent, k : k + 1])
            )
            picks = jnp.where(numbers == place, 1.0, 0.0).astype(jnp.bfloat16)
            term = gate * jnp.dot(picks, rows_ref[...], preferred_element_type=jnp.float32)
            total = term if total is None else total + term
        sum_ref[sent] = total
    own_ref[...] = sum_ref[core]
    other_ref[...] = sum_ref[1 - core].astype(jnp.bfloat16)


def finish_kernel(core_ref, state_ref, own_ref, other_ref, mixed_ref):
    core = core_ref[0]
    half = own_ref.shape[-1]
    for part, summed in ((core, own_ref), (1 - core, other_ref)):
        span = part_of(part, half)
        mixed_ref[:, span] = (
            state_ref[:, span].astype(jnp.float32) + summed[...].astype(jnp.float32)
        ).astype(jnp.bfloat16)


def swap(values):
    return lax.ppermute(values, "section", [(0, 1), (1, 0)])


def swap_owner(values):
    owners = lax.axis_size("expert")
    return lax.ppermute(values, "expert", [(i, i ^ 1) for i in range(owners)])


def shift(values, offset):
    owners = lax.axis_size("expert")
    return lax.ppermute(
        values, "expert", [(i, (i + 2 * offset) % owners) for i in range(owners)]
    )


def after_kernel(*refs):
    pass


def after(value, *firsts):
    return pl.pallas_call(
        after_kernel,
        out_shape=jax.ShapeDtypeStruct(value.shape, value.dtype),
        in_specs=[pl.BlockSpec(memory_space=pl.ANY)] * (1 + len(firsts)),
        out_specs=pl.BlockSpec(memory_space=pl.ANY),
        input_output_aliases={0: 0},
        compiler_params=pltpu.CompilerParams(vmem_limit_bytes=2**20),
        name="after",
    )(value, *firsts)


def attend(
    core, decoder_states, memory_keys, memory_values, source_lengths, target_lengths, routes,
    attn_gain, ffn_gain, router,
):
    full_len, width = decoder_states.shape[1:]
    half = (full_len, width // 2)
    memory = memory_keys.shape[1:]
    other_keys, other_values = swap(memory_keys), swap(memory_values)
    own, query, rest = call(
        attend_own_kernel,
        "attend_own",
        [(half, jnp.bfloat16)] * 3,
        [core, source_lengths],
        [],
        [decoder_states, attn_gain[None], memory_keys, memory_values],
        scratch=[
            pltpu.VMEM((full_len, width), jnp.bfloat16),
            pltpu.VMEM((1, width), jnp.float32),
            pltpu.VMEM(memory, jnp.bfloat16),
            pltpu.VMEM(memory, jnp.bfloat16),
            pltpu.VMEM((full_len, width), jnp.bfloat16),
            pltpu.SemaphoreType.DMA((4,)),
        ],
    )
    return call(
        attend_other_kernel,
        "attend_other",
        [
            ((full_len, width), jnp.bfloat16),
            (half, jnp.bfloat16),
            (half, jnp.bfloat16),
            ((2, full_len), jnp.float32),
            (routes.shape, jnp.int32),
        ],
        [core, source_lengths],
        [own, query, rest, other_keys, other_values],
        [ffn_gain[None], router.T, routes, target_lengths],
        scratch=[
            pltpu.VMEM((1, width), jnp.float32),
            pltpu.VMEM(router.shape[::-1], jnp.bfloat16),
            pltpu.SMEM(target_lengths.shape, jnp.int32),
            pltpu.VMEM((full_len, width), jnp.bfloat16),
            pltpu.SemaphoreType.DMA((4,)),
        ],
    )


def line_experts(core, state, keep, send, gates, routes, fc_in, fc_out, capacity):
    full_len, width = state.shape
    half = width // 2
    count = lax.axis_size("expert") // 2
    line = (lax.axis_index("expert") // 2).astype(jnp.int32).reshape(1)
    other = swap(send)
    other_gates = swap(gates)
    piece = ((capacity, half), jnp.bfloat16)
    selected = call(
        select_kernel,
        "select",
        [piece] * count,
        [core, line],
        [routes, keep, other],
        scratch=[pltpu.VMEM((2 * full_len, half), jnp.bfloat16)],
    )
    travelling = [shift(selected[r], r) for r in range(1, count)]
    home = [None] * count
    kept, halves, wholes, ps, qs, q2s = {}, {}, {}, {}, {}, {}
    order = [0, 1, 2, 3]
    for offset in order:
        p = travelling[offset - 1] if offset else selected[0]
        if offset == 2:
            p = after(p, kept[0])
        q = swap_owner(p)
        p2 = swap(p)
        q2 = swap(q)
        if offset == 3:
            q2 = after(q2, halves[1])
        ps[offset], qs[offset], q2s[offset] = p, q, q2
        outs = [((2, capacity, half), jnp.float32), ((2, capacity, half), jnp.bfloat16)]
        rows = pltpu.VMEM((2 * capacity, width), jnp.bfloat16)
        if offset == order[0]:
            kept[offset], sent = call(
                first_expert_kernel,
                "first_expert",
                outs,
                [core],
                [p, q, p2, q2],
                [fc_in, fc_out],
                scratch=[
                    rows,
                    pltpu.VMEM(fc_in.shape, jnp.bfloat16),
                    pltpu.VMEM(fc_out.shape, jnp.bfloat16),
                    pltpu.VMEM((2 * capacity, fc_in.shape[1]), jnp.bfloat16),
                    pltpu.SemaphoreType.DMA((5,)),
                ],
                vmem_mib=20,
            )
        else:
            kept[offset], sent = call(
                expert_kernel,
                "expert",
                outs,
                [core],
                [p, q, p2, q2, fc_in, fc_out],
                scratch=[rows],
                vmem_mib=16,
            )
        moving = swap(sent)
        both = kept[offset] + moving.astype(jnp.float32)
        halves[offset] = both[1].astype(jnp.bfloat16)
        if offset == 0:
            own_both = both
            continue
        across = swap_owner(halves[offset])
        wholes[offset] = (both[0] + across.astype(jnp.float32)).astype(jnp.bfloat16)
        home[offset] = shift(wholes[offset], -offset)
    across = swap_owner(after(halves[0], halves[order[-1]]))
    home[0] = (own_both[0] + across.astype(jnp.float32)).astype(jnp.bfloat16)
    own_sum, other_sum = call(
        combine_kernel,
        "combine",
        [((full_len, half), jnp.float32), ((full_len, half), jnp.bfloat16)],
        [core, line],
        [routes, gates, other_gates, *home],
        scratch=[
            pltpu.VMEM((count * capacity, half), jnp.bfloat16),
            pltpu.VMEM((2, 2, full_len), jnp.float32),
            pltpu.VMEM((2, full_len, half), jnp.float32),
        ],
    )
    (mixed,) = call(
        finish_kernel,
        "finish",
        [((full_len, width), jnp.bfloat16)],
        [core],
        [state, own_sum, swap(other_sum)],
    )
    return mixed


def expert_apply(slot_rows, fc_in, fc_out):
    width = slot_rows.shape[-1]
    flat_rows = slot_rows.reshape(-1, width)
    hidden = jax.nn.relu(jnp.dot(flat_rows, fc_in, preferred_element_type=jnp.float32)).astype(
        jnp.bfloat16
    )
    produced = jnp.dot(hidden, fc_out, preferred_element_type=jnp.float32)
    return produced.reshape(slot_rows.shape[0], slot_rows.shape[1], width)


def sparse_experts(normed, target_lengths, routes, router, fc_in, fc_out, capacity):
    full_len, width = normed.shape
    all_normed = lax.all_gather(normed[None], "section", axis=0, tiled=True)
    block_sents = all_normed.shape[0]
    block_rows = block_sents * full_len
    tok_rows = all_normed.reshape(block_rows, width)
    owners = lax.axis_size("expert")
    experts_count = owners // 2
    chosen_ids = routes.reshape(block_rows, 2)
    logits = jnp.dot(tok_rows, router, preferred_element_type=jnp.float32)
    onehot = chosen_ids[:, :, None] == jnp.arange(experts_count, dtype=jnp.int32)
    chosen = jnp.sum(jnp.where(onehot, logits[:, None, :], 0.0), axis=-1)
    first = jax.nn.sigmoid(chosen[:, 0] - chosen[:, 1])
    gates = jnp.stack([first, 1.0 - first], axis=-1)
    live = (jnp.arange(full_len, dtype=jnp.int32)[None, :] < target_lengths[:, None]).reshape(
        block_rows
    )
    flags = onehot.reshape(block_rows * 2, experts_count).astype(jnp.int32)
    earlier = jnp.cumsum(flags, axis=0) - flags
    slot = jnp.sum(flags * earlier, axis=-1).reshape(block_rows, 2)
    position = chosen_ids * capacity + slot
    dump_index = experts_count * capacity
    target = jnp.where(live[:, None], position, dump_index)
    row_ids = jnp.broadcast_to(jnp.arange(block_rows, dtype=jnp.int32)[:, None], (block_rows, 2))
    table = (
        jnp.full((dump_index + 1,), block_rows, jnp.int32)
        .at[target.reshape(-1)]
        .set(row_ids.reshape(-1))[:dump_index]
    )
    padded = jnp.concatenate([tok_rows, jnp.zeros((1, width), jnp.bfloat16)], axis=0)
    slot_buffer = padded[table].reshape(experts_count, capacity, width)
    outgoing = jnp.repeat(slot_buffer, 2, axis=0)
    returned = lax.all_to_all(
        expert_apply(
            lax.all_to_all(outgoing, "expert", split_axis=0, concat_axis=0, tiled=True),
            fc_in,
            fc_out,
        ).astype(jnp.bfloat16),
        "expert",
        split_axis=0,
        concat_axis=0,
        tiled=True,
    ).astype(jnp.float32)
    partial_value = jnp.sum(returned.reshape(experts_count, 2, capacity, width), axis=1)
    fetched = partial_value.reshape(dump_index, width)[jnp.where(live[:, None], position, 0)]
    weight = gates * live[:, None].astype(jnp.float32)
    contrib = jnp.sum(weight[:, :, None] * fetched, axis=1).reshape(block_sents, full_len, width)
    summed = lax.psum_scatter(contrib, "section", scatter_dimension=0, tiled=True)
    return summed[0]


def local(
    decoder_states,
    memory_keys,
    memory_values,
    source_lengths,
    target_lengths,
    routes,
    attn_gain,
    ffn_gain,
    router,
    fc_in,
    fc_out,
):
    core = lax.axis_index("section").astype(jnp.int32).reshape(1)
    by_choice = jnp.transpose(routes, (0, 2, 1))
    state, keep, send, gates, by_choice = attend(
        core, decoder_states, memory_keys, memory_values, source_lengths, target_lengths, by_choice,
        attn_gain, ffn_gain, router,
    )
    block_rows = routes.shape[0] * routes.shape[1]
    experts_count = router.shape[1]
    capacity = 2 * max(1, 3 * block_rows // (2 * experts_count))
    if capacity % 16 == 0:
        mixed = line_experts(core, state, keep, send, gates, by_choice, fc_in, fc_out, capacity)
    else:
        halves = jnp.stack([keep, send])
        normed = jnp.concatenate([halves[core[0]], halves[1 - core[0]]], axis=-1)
        summed = sparse_experts(normed, target_lengths, routes, router, fc_in, fc_out, capacity)
        mixed = (state.astype(jnp.float32) + summed).astype(jnp.bfloat16)
    return mixed[None]


def solution(mesh):
    placed = (
        P(("groups", "expert", "section"), None, None),
        P(("groups", "expert"), None, "section"),
        P(("groups", "expert"), None, "section"),
        P(("groups", "expert", "section")),
        P(("groups", "expert")),
        P(("groups", "expert"), None, None),
        P(),
        P(),
        P(),
        P(None, ("expert", "section")),
        P(("expert", "section"), None),
    )
    return jax.shard_map(
        local,
        mesh=mesh,
        in_specs=placed,
        out_specs=P(("groups", "expert", "section"), None, None),
        check_vma=False,
    )
```

```python
import functools

import jax
import jax.numpy as jnp
from jax import lax
from jax.experimental import pallas as pl
from jax.experimental.pallas import tpu as pltpu
from jax.sharding import PartitionSpec as P

HEAD_DIM = 128


def layer_norm(values, gain):
    centered = values - jnp.mean(values, axis=-1, keepdims=True)
    spread = jnp.mean(centered * centered, axis=-1, keepdims=True)
    return (centered * lax.rsqrt(spread + 1e-05) * gain).astype(jnp.bfloat16)


VMEM = pl.BlockSpec(memory_space=pltpu.VMEM)
SMEM = pl.BlockSpec(memory_space=pltpu.SMEM)
HBM = pl.BlockSpec(memory_space=pltpu.HBM)


def call(kernel, name, outs, scalars, arrays, far=(), scratch=(), vmem_mib=12):
    return pl.pallas_call(
        kernel,
        out_shape=tuple(jax.ShapeDtypeStruct(*out) for out in outs),
        in_specs=[SMEM] * len(scalars) + [VMEM] * len(arrays) + [HBM] * len(far),
        out_specs=(VMEM,) * len(outs),
        scratch_shapes=list(scratch),
        compiler_params=pltpu.CompilerParams(vmem_limit_bytes=vmem_mib * 2**20),
        name=name,
    )(*scalars, *arrays, *(pltpu.with_memory_space_constraint(a, pltpu.HBM) for a in far))


def fetch(sems, *pairs):
    copies = [
        pltpu.make_async_copy(source, target, sems.at[i]) for i, (source, target) in enumerate(pairs)
    ]
    for copy in copies:
        copy.start()
    return copies


def part_of(part, half):
    return pl.ds(pl.multiple_of(part * half, half), half)


def attend_half(queries, keys, values, length):
    rows = queries.shape[0]
    heads = [slice(at, at + HEAD_DIM) for at in range(0, queries.shape[1], HEAD_DIM)]
    scores = jnp.concatenate(
        [
            lax.dot_general(
                queries[:, head],
                keys[:, head],
                (((1,), (1,)), ((), ())),
                preferred_element_type=jnp.float32,
            )
            for head in heads
        ],
        axis=0,
    ) * HEAD_DIM ** (-0.5)
    valid = lax.broadcasted_iota(jnp.int32, (1, keys.shape[0]), 1) < length
    scores = jnp.where(valid, scores, -jnp.inf)
    expon = jnp.exp(scores - jnp.max(scores, axis=-1, keepdims=True))
    weights = (expon / jnp.sum(expon, axis=-1, keepdims=True)).astype(jnp.bfloat16)
    return jnp.concatenate(
        [
            jnp.dot(
                weights[i * rows : (i + 1) * rows],
                values[:, head],
                preferred_element_type=jnp.float32,
            )
            for i, head in enumerate(heads)
        ],
        axis=1,
    )


def add_rounded(x, attended):
    return (x.astype(jnp.float32) + attended).astype(jnp.bfloat16)


def attend_own_kernel(
    core_ref,
    source_ref,
    x_in,
    gain_in,
    keys_in,
    values_in,
    state_ref,
    query_ref,
    rest_ref,
    x_ref,
    gain_ref,
    keys_ref,
    values_ref,
    scratch_ref,
    sems,
):
    core = core_ref[0]
    copies = fetch(
        sems,
        (x_in.at[0], x_ref),
        (gain_in, gain_ref),
        (keys_in.at[core], keys_ref),
        (values_in.at[core], values_ref),
    )
    half = keys_ref.shape[1]
    copies[0].wait()
    copies[1].wait()
    scratch_ref[...] = layer_norm(x_ref[...].astype(jnp.float32), gain_ref[...])
    own, other = part_of(core, half), part_of(1 - core, half)
    query_ref[...] = scratch_ref[:, other]
    rest_ref[...] = x_ref[:, other]
    copies[2].wait()
    copies[3].wait()
    attended = attend_half(scratch_ref[:, own], keys_ref[...], values_ref[...], source_ref[0])
    state_ref[...] = add_rounded(x_ref[:, own], attended)


def attend_other_kernel(
    core_ref,
    source_ref,
    own_ref,
    query_ref,
    rest_ref,
    keys_ref,
    values_ref,
    gain_in,
    router_in,
    routes_in,
    target_in,
    state_ref,
    keep_ref,
    send_ref,
    gates_ref,
    routes_ref,
    gain_ref,
    router_ref,
    target_ref,
    scratch_ref,
    sems,
):
    core = core_ref[0]
    copies = fetch(
        sems,
        (gain_in, gain_ref),
        (router_in, router_ref),
        (routes_in, routes_ref),
        (target_in, target_ref),
    )
    full_len, half = own_ref.shape
    own, other = part_of(core, half), part_of(1 - core, half)
    attended = attend_half(query_ref[...], keys_ref[core], values_ref[core], source_ref[0])
    state_ref[:, own] = own_ref[...]
    state_ref[:, other] = add_rounded(rest_ref[...], attended)
    copies[0].wait()
    scratch_ref[...] = layer_norm(state_ref[...].astype(jnp.float32), gain_ref[...])
    keep_ref[...] = scratch_ref[:, own]
    send_ref[...] = scratch_ref[:, other]
    for copy in copies[1:]:
        copy.wait()
    logits = lax.dot_general(
        router_ref[...],
        scratch_ref[...],
        (((1,), (1,)), ((), ())),
        preferred_element_type=jnp.float32,
    )
    names = lax.broadcasted_iota(jnp.int32, logits.shape, 0)
    routes = routes_ref[core]
    chosen = [
        jnp.sum(jnp.where(names == routes[k : k + 1], logits, 0.0), axis=0, keepdims=True)
        for k in range(2)
    ]
    first = jax.nn.sigmoid(chosen[0] - chosen[1])
    live = lax.broadcasted_iota(jnp.int32, (1, full_len), 1) < target_ref[core]
    gates_ref[0:1] = jnp.where(live, first, 0.0)
    gates_ref[1:2] = jnp.where(live, 1.0 - first, 0.0)


def slots_of(routes_ref, experts_count):
    sents, _, full_len = routes_ref.shape
    rows = sents * full_len
    ids = lax.broadcasted_iota(jnp.int32, (max(8, experts_count), full_len), 0)
    named = jnp.concatenate(
        [
            jnp.where((ids == routes_ref[s, 0:1]) | (ids == routes_ref[s, 1:2]), 1.0, 0.0)
            for s in range(sents)
        ],
        axis=1,
    )
    before = lax.broadcasted_iota(jnp.int32, (rows, rows), 0) < lax.broadcasted_iota(
        jnp.int32, (rows, rows), 1
    )
    earlier = jnp.dot(
        named.astype(jnp.bfloat16),
        jnp.where(before, 1.0, 0.0).astype(jnp.bfloat16),
        preferred_element_type=jnp.float32,
    )
    return named > 0.0, earlier


def select_kernel(core_ref, line_ref, routes_ref, own_ref, other_ref, *rest):
    pieces, block_ref = rest[:-1], rest[-1]
    experts_count = len(pieces)
    full_len = own_ref.shape[0]
    capacity = pieces[0].shape[0]
    core = core_ref[0]
    block_ref[part_of(core, full_len)] = own_ref[...]
    block_ref[part_of(1 - core, full_len)] = other_ref[...]
    named, earlier = slots_of(routes_ref, experts_count)
    slot = jnp.where(named, earlier, -1.0)
    ids = lax.broadcasted_iota(jnp.int32, slot.shape, 0)
    numbers = lax.broadcasted_iota(jnp.int32, (capacity, slot.shape[1]), 0).astype(jnp.float32)
    for offset, piece_ref in enumerate(pieces):
        expert = line_ref[0] ^ offset
        wanted = jnp.sum(jnp.where(ids == expert, slot, 0.0), axis=0, keepdims=True)
        picks = jnp.where(numbers == wanted, 1.0, 0.0).astype(jnp.bfloat16)
        piece_ref[...] = jnp.dot(
            picks, block_ref[...], preferred_element_type=jnp.float32
        ).astype(jnp.bfloat16)


def expert_kernel(
    core_ref, p_ref, q_ref, p2_ref, q2_ref, in_ref, out_ref, keep_ref, send_ref, rows_ref
):
    core = core_ref[0]
    capacity, half = p_ref.shape
    rows_ref[:capacity, part_of(core, half)] = p_ref[...]
    rows_ref[capacity:, part_of(core, half)] = q_ref[...]
    rows_ref[:capacity, part_of(1 - core, half)] = p2_ref[...]
    rows_ref[capacity:, part_of(1 - core, half)] = q2_ref[...]
    hidden = jnp.dot(rows_ref[...], in_ref[...], preferred_element_type=jnp.float32)
    hidden = jnp.maximum(hidden, 0.0).astype(jnp.bfloat16)
    send = jnp.dot(
        hidden, out_ref[:, part_of(1 - core, half)], preferred_element_type=jnp.float32
    ).astype(jnp.bfloat16)
    send_ref[0] = send[:capacity]
    send_ref[1] = send[capacity:]
    keep = jnp.dot(hidden, out_ref[:, part_of(core, half)], preferred_element_type=jnp.float32)
    keep_ref[0] = keep[:capacity]
    keep_ref[1] = keep[capacity:]


def first_expert_kernel(
    core_ref,
    p_ref,
    q_ref,
    p2_ref,
    q2_ref,
    in_in,
    out_in,
    keep_ref,
    send_ref,
    rows_ref,
    in_ref,
    out_ref,
    hidden_ref,
    sems,
):
    core = core_ref[0]
    capacity, half = p_ref.shape
    tile = in_ref.shape[1] // 4
    tiles = [slice(at, at + tile) for at in range(0, in_ref.shape[1], tile)]
    copies = fetch(
        sems,
        *[(in_in.at[:, at], in_ref.at[:, at]) for at in tiles],
        (out_in, out_ref),
    )
    rows_ref[:capacity, part_of(core, half)] = p_ref[...]
    rows_ref[capacity:, part_of(core, half)] = q_ref[...]
    rows_ref[:capacity, part_of(1 - core, half)] = p2_ref[...]
    rows_ref[capacity:, part_of(1 - core, half)] = q2_ref[...]
    for copy, at in zip(copies, tiles):
        copy.wait()
        hidden = jnp.dot(rows_ref[...], in_ref[:, at], preferred_element_type=jnp.float32)
        hidden_ref[:, at] = jnp.maximum(hidden, 0.0).astype(jnp.bfloat16)
    copies[-1].wait()
    send = jnp.dot(
        hidden_ref[...], out_ref[:, part_of(1 - core, half)], preferred_element_type=jnp.float32
    ).astype(jnp.bfloat16)
    send_ref[0] = send[:capacity]
    send_ref[1] = send[capacity:]
    keep = jnp.dot(
        hidden_ref[...], out_ref[:, part_of(core, half)], preferred_element_type=jnp.float32
    )
    keep_ref[0] = keep[:capacity]
    keep_ref[1] = keep[capacity:]


def combine_kernel(core_ref, line_ref, routes_ref, own_gates_ref, other_gates_ref, *rest):
    pieces, (own_ref, other_ref, rows_ref, gates_ref, sum_ref) = rest[:-5], rest[-5:]
    experts_count = len(pieces)
    capacity, half = pieces[0].shape
    sents, _, full_len = routes_ref.shape
    core = core_ref[0]
    for offset, piece_ref in enumerate(pieces):
        rows_ref[offset * capacity : (offset + 1) * capacity] = piece_ref[...]
    gates_ref[core] = own_gates_ref[...]
    gates_ref[1 - core] = other_gates_ref[...]
    _, earlier = slots_of(routes_ref, experts_count)
    ids = lax.broadcasted_iota(jnp.int32, (earlier.shape[0], full_len), 0)
    numbers = lax.broadcasted_iota(
        jnp.int32, (full_len, experts_count * capacity), 1
    ).astype(jnp.float32)
    for sent in range(sents):
        slots = earlier[:, sent * full_len : (sent + 1) * full_len]
        total = None
        for k in range(2):
            route = routes_ref[sent, k : k + 1]
            slot = jnp.sum(jnp.where(ids == route, slots, 0.0), axis=0, keepdims=True)
            place = (route ^ line_ref[0]).astype(jnp.float32) * capacity + slot
            place, gate = (
                jnp.broadcast_to(row, (full_len, full_len)).T[:, :1]
                for row in (place, gates_ref[sent, k : k + 1])
            )
            picks = jnp.where(numbers == place, 1.0, 0.0).astype(jnp.bfloat16)
            term = gate * jnp.dot(picks, rows_ref[...], preferred_element_type=jnp.float32)
            total = term if total is None else total + term
        sum_ref[sent] = total
    own_ref[...] = sum_ref[core]
    other_ref[...] = sum_ref[1 - core].astype(jnp.bfloat16)


def finish_kernel(core_ref, state_ref, own_ref, other_ref, mixed_ref):
    core = core_ref[0]
    half = own_ref.shape[-1]
    for part, summed in ((core, own_ref), (1 - core, other_ref)):
        span = part_of(part, half)
        mixed_ref[:, span] = (
            state_ref[:, span].astype(jnp.float32) + summed[...].astype(jnp.float32)
        ).astype(jnp.bfloat16)


def swap(values):
    return lax.ppermute(values, "section", [(0, 1), (1, 0)])


def swap_owner(values):
    owners = lax.axis_size("expert")
    return lax.ppermute(values, "expert", [(i, i ^ 1) for i in range(owners)])


def exchange(values, offset):
    owners = lax.axis_size("expert")
    return lax.ppermute(values, "expert", [(i, i ^ (2 * offset)) for i in range(owners)])


def after_kernel(*refs):
    pass


def after(value, *firsts):
    return pl.pallas_call(
        after_kernel,
        out_shape=jax.ShapeDtypeStruct(value.shape, value.dtype),
        in_specs=[pl.BlockSpec(memory_space=pl.ANY)] * (1 + len(firsts)),
        out_specs=pl.BlockSpec(memory_space=pl.ANY),
        input_output_aliases={0: 0},
        compiler_params=pltpu.CompilerParams(vmem_limit_bytes=2**20),
        name="after",
    )(value, *firsts)


def attend(
    core, decoder_states, memory_keys, memory_values, source_lengths, target_lengths, routes,
    attn_gain, ffn_gain, router,
):
    full_len, width = decoder_states.shape[1:]
    half = (full_len, width // 2)
    memory = memory_keys.shape[1:]
    other_keys, other_values = swap(memory_keys), swap(memory_values)
    own, query, rest = call(
        attend_own_kernel,
        "attend_own",
        [(half, jnp.bfloat16)] * 3,
        [core, source_lengths],
        [],
        [decoder_states, attn_gain[None], memory_keys, memory_values],
        scratch=[
            pltpu.VMEM((full_len, width), jnp.bfloat16),
            pltpu.VMEM((1, width), jnp.float32),
            pltpu.VMEM(memory, jnp.bfloat16),
            pltpu.VMEM(memory, jnp.bfloat16),
            pltpu.VMEM((full_len, width), jnp.bfloat16),
            pltpu.SemaphoreType.DMA((4,)),
        ],
    )
    return call(
        attend_other_kernel,
        "attend_other",
        [
            ((full_len, width), jnp.bfloat16),
            (half, jnp.bfloat16),
            (half, jnp.bfloat16),
            ((2, full_len), jnp.float32),
            (routes.shape, jnp.int32),
        ],
        [core, source_lengths],
        [own, query, rest, other_keys, other_values],
        [ffn_gain[None], router.T, routes, target_lengths],
        scratch=[
            pltpu.VMEM((1, width), jnp.float32),
            pltpu.VMEM(router.shape[::-1], jnp.bfloat16),
            pltpu.SMEM(target_lengths.shape, jnp.int32),
            pltpu.VMEM((full_len, width), jnp.bfloat16),
            pltpu.SemaphoreType.DMA((4,)),
        ],
    )


def line_experts(core, state, keep, send, gates, routes, fc_in, fc_out, capacity):
    full_len, width = state.shape
    half = width // 2
    count = lax.axis_size("expert") // 2
    line = (lax.axis_index("expert") // 2).astype(jnp.int32).reshape(1)
    other = swap(send)
    other_gates = swap(gates)
    piece = ((capacity, half), jnp.bfloat16)
    selected = call(
        select_kernel,
        "select",
        [piece] * count,
        [core, line],
        [routes, keep, other],
        scratch=[pltpu.VMEM((2 * full_len, half), jnp.bfloat16)],
    )
    travelling = [exchange(selected[r], r) for r in range(1, count)]
    home = [None] * count
    kept, halves, wholes, ps, qs, q2s = {}, {}, {}, {}, {}, {}
    order = [0, 1, 2, 3]
    for offset in order:
        p = travelling[offset - 1] if offset else selected[0]
        q = swap_owner(p)
        p2 = swap(p)
        q2 = swap(q)
        if offset == 1:
            q2 = after(q2, kept[0])
        if offset == 2:
            q2 = after(q2, kept[0], kept[1])
        if offset == 3:
            q2 = after(q2, halves[1])
        ps[offset], qs[offset], q2s[offset] = p, q, q2
        outs = [((2, capacity, half), jnp.float32), ((2, capacity, half), jnp.bfloat16)]
        rows = pltpu.VMEM((2 * capacity, width), jnp.bfloat16)
        if offset == order[0]:
            kept[offset], sent = call(
                first_expert_kernel,
                "first_expert",
                outs,
                [core],
                [p, q, p2, q2],
                [fc_in, fc_out],
                scratch=[
                    rows,
                    pltpu.VMEM(fc_in.shape, jnp.bfloat16),
                    pltpu.VMEM(fc_out.shape, jnp.bfloat16),
                    pltpu.VMEM((2 * capacity, fc_in.shape[1]), jnp.bfloat16),
                    pltpu.SemaphoreType.DMA((5,)),
                ],
                vmem_mib=20,
            )
        else:
            kept[offset], sent = call(
                expert_kernel,
                "expert",
                outs,
                [core],
                [p, q, p2, q2, fc_in, fc_out],
                scratch=[rows],
                vmem_mib=16,
            )
        moving = swap(sent)
        if offset == 3:
            moving = after(moving, wholes[1])
        both = kept[offset] + moving.astype(jnp.float32)
        halves[offset] = both[1].astype(jnp.bfloat16)
        if offset == 0:
            own_both = both
            continue
        across = swap_owner(halves[offset])
        wholes[offset] = (both[0] + across.astype(jnp.float32)).astype(jnp.bfloat16)
        home[offset] = exchange(wholes[offset], offset)
    across = swap_owner(after(halves[0], halves[order[-1]]))
    home[0] = (own_both[0] + across.astype(jnp.float32)).astype(jnp.bfloat16)
    own_sum, other_sum = call(
        combine_kernel,
        "combine",
        [((full_len, half), jnp.float32), ((full_len, half), jnp.bfloat16)],
        [core, line],
        [routes, gates, other_gates, *home],
        scratch=[
            pltpu.VMEM((count * capacity, half), jnp.bfloat16),
            pltpu.VMEM((2, 2, full_len), jnp.float32),
            pltpu.VMEM((2, full_len, half), jnp.float32),
        ],
    )
    (mixed,) = call(
        finish_kernel,
        "finish",
        [((full_len, width), jnp.bfloat16)],
        [core],
        [state, own_sum, swap(other_sum)],
    )
    return mixed


def expert_apply(slot_rows, fc_in, fc_out):
    width = slot_rows.shape[-1]
    flat_rows = slot_rows.reshape(-1, width)
    hidden = jax.nn.relu(jnp.dot(flat_rows, fc_in, preferred_element_type=jnp.float32)).astype(
        jnp.bfloat16
    )
    produced = jnp.dot(hidden, fc_out, preferred_element_type=jnp.float32)
    return produced.reshape(slot_rows.shape[0], slot_rows.shape[1], width)


def sparse_experts(normed, target_lengths, routes, router, fc_in, fc_out, capacity):
    full_len, width = normed.shape
    all_normed = lax.all_gather(normed[None], "section", axis=0, tiled=True)
    block_sents = all_normed.shape[0]
    block_rows = block_sents * full_len
    tok_rows = all_normed.reshape(block_rows, width)
    owners = lax.axis_size("expert")
    experts_count = owners // 2
    chosen_ids = routes.reshape(block_rows, 2)
    logits = jnp.dot(tok_rows, router, preferred_element_type=jnp.float32)
    onehot = chosen_ids[:, :, None] == jnp.arange(experts_count, dtype=jnp.int32)
    chosen = jnp.sum(jnp.where(onehot, logits[:, None, :], 0.0), axis=-1)
    first = jax.nn.sigmoid(chosen[:, 0] - chosen[:, 1])
    gates = jnp.stack([first, 1.0 - first], axis=-1)
    live = (jnp.arange(full_len, dtype=jnp.int32)[None, :] < target_lengths[:, None]).reshape(
        block_rows
    )
    flags = onehot.reshape(block_rows * 2, experts_count).astype(jnp.int32)
    earlier = jnp.cumsum(flags, axis=0) - flags
    slot = jnp.sum(flags * earlier, axis=-1).reshape(block_rows, 2)
    position = chosen_ids * capacity + slot
    dump_index = experts_count * capacity
    target = jnp.where(live[:, None], position, dump_index)
    row_ids = jnp.broadcast_to(jnp.arange(block_rows, dtype=jnp.int32)[:, None], (block_rows, 2))
    table = (
        jnp.full((dump_index + 1,), block_rows, jnp.int32)
        .at[target.reshape(-1)]
        .set(row_ids.reshape(-1))[:dump_index]
    )
    padded = jnp.concatenate([tok_rows, jnp.zeros((1, width), jnp.bfloat16)], axis=0)
    slot_buffer = padded[table].reshape(experts_count, capacity, width)
    outgoing = jnp.repeat(slot_buffer, 2, axis=0)
    returned = lax.all_to_all(
        expert_apply(
            lax.all_to_all(outgoing, "expert", split_axis=0, concat_axis=0, tiled=True),
            fc_in,
            fc_out,
        ).astype(jnp.bfloat16),
        "expert",
        split_axis=0,
        concat_axis=0,
        tiled=True,
    ).astype(jnp.float32)
    partial_value = jnp.sum(returned.reshape(experts_count, 2, capacity, width), axis=1)
    fetched = partial_value.reshape(dump_index, width)[jnp.where(live[:, None], position, 0)]
    weight = gates * live[:, None].astype(jnp.float32)
    contrib = jnp.sum(weight[:, :, None] * fetched, axis=1).reshape(block_sents, full_len, width)
    summed = lax.psum_scatter(contrib, "section", scatter_dimension=0, tiled=True)
    return summed[0]


def local(
    decoder_states,
    memory_keys,
    memory_values,
    source_lengths,
    target_lengths,
    routes,
    attn_gain,
    ffn_gain,
    router,
    fc_in,
    fc_out,
):
    core = lax.axis_index("section").astype(jnp.int32).reshape(1)
    by_choice = jnp.transpose(routes, (0, 2, 1))
    state, keep, send, gates, by_choice = attend(
        core, decoder_states, memory_keys, memory_values, source_lengths, target_lengths, by_choice,
        attn_gain, ffn_gain, router,
    )
    block_rows = routes.shape[0] * routes.shape[1]
    experts_count = router.shape[1]
    capacity = 2 * max(1, 3 * block_rows // (2 * experts_count))
    if capacity % 16 == 0 and experts_count & (experts_count - 1) == 0:
        mixed = line_experts(core, state, keep, send, gates, by_choice, fc_in, fc_out, capacity)
    else:
        halves = jnp.stack([keep, send])
        normed = jnp.concatenate([halves[core[0]], halves[1 - core[0]]], axis=-1)
        summed = sparse_experts(normed, target_lengths, routes, router, fc_in, fc_out, capacity)
        mixed = (state.astype(jnp.float32) + summed).astype(jnp.bfloat16)
    return mixed[None]


def solution(mesh):
    placed = (
        P(("groups", "expert", "section"), None, None),
        P(("groups", "expert"), None, "section"),
        P(("groups", "expert"), None, "section"),
        P(("groups", "expert", "section")),
        P(("groups", "expert")),
        P(("groups", "expert"), None, None),
        P(),
        P(),
        P(),
        P(None, ("expert", "section")),
        P(("expert", "section"), None),
    )
    return jax.shard_map(
        local,
        mesh=mesh,
        in_specs=placed,
        out_specs=P(("groups", "expert", "section"), None, None),
        check_vma=False,
    )
```

```python
import functools

import jax
import jax.numpy as jnp
from jax import lax
from jax.experimental import pallas as pl
from jax.experimental.pallas import tpu as pltpu
from jax.sharding import PartitionSpec as P

HEAD_DIM = 128


def layer_norm(values, gain):
    centered = values - jnp.mean(values, axis=-1, keepdims=True)
    spread = jnp.mean(centered * centered, axis=-1, keepdims=True)
    return (centered * lax.rsqrt(spread + 1e-05) * gain).astype(jnp.bfloat16)


VMEM = pl.BlockSpec(memory_space=pltpu.VMEM)
SMEM = pl.BlockSpec(memory_space=pltpu.SMEM)
HBM = pl.BlockSpec(memory_space=pltpu.HBM)


def call(kernel, name, outs, scalars, arrays, far=(), scratch=(), vmem_mib=12):
    return pl.pallas_call(
        kernel,
        out_shape=tuple(jax.ShapeDtypeStruct(*out) for out in outs),
        in_specs=[SMEM] * len(scalars) + [VMEM] * len(arrays) + [HBM] * len(far),
        out_specs=(VMEM,) * len(outs),
        scratch_shapes=list(scratch),
        compiler_params=pltpu.CompilerParams(vmem_limit_bytes=vmem_mib * 2**20),
        name=name,
    )(*scalars, *arrays, *(pltpu.with_memory_space_constraint(a, pltpu.HBM) for a in far))


def fetch(sems, *pairs):
    copies = [
        pltpu.make_async_copy(source, target, sems.at[i]) for i, (source, target) in enumerate(pairs)
    ]
    for copy in copies:
        copy.start()
    return copies


def part_of(part, half):
    return pl.ds(pl.multiple_of(part * half, half), half)


def attend_half(queries, keys, values, length):
    rows = queries.shape[0]
    heads = [slice(at, at + HEAD_DIM) for at in range(0, queries.shape[1], HEAD_DIM)]
    scores = jnp.concatenate(
        [
            lax.dot_general(
                queries[:, head],
                keys[:, head],
                (((1,), (1,)), ((), ())),
                preferred_element_type=jnp.float32,
            )
            for head in heads
        ],
        axis=0,
    ) * HEAD_DIM ** (-0.5)
    valid = lax.broadcasted_iota(jnp.int32, (1, keys.shape[0]), 1) < length
    scores = jnp.where(valid, scores, -jnp.inf)
    expon = jnp.exp(scores - jnp.max(scores, axis=-1, keepdims=True))
    weights = (expon / jnp.sum(expon, axis=-1, keepdims=True)).astype(jnp.bfloat16)
    return jnp.concatenate(
        [
            jnp.dot(
                weights[i * rows : (i + 1) * rows],
                values[:, head],
                preferred_element_type=jnp.float32,
            )
            for i, head in enumerate(heads)
        ],
        axis=1,
    )


def add_rounded(x, attended):
    return (x.astype(jnp.float32) + attended).astype(jnp.bfloat16)


def attend_own_kernel(
    core_ref,
    source_ref,
    x_in,
    gain_in,
    keys_in,
    values_in,
    state_ref,
    query_ref,
    rest_ref,
    x_ref,
    gain_ref,
    keys_ref,
    values_ref,
    scratch_ref,
    sems,
):
    core = core_ref[0]
    copies = fetch(
        sems,
        (x_in.at[0], x_ref),
        (gain_in, gain_ref),
        (keys_in.at[core], keys_ref),
        (values_in.at[core], values_ref),
    )
    half = keys_ref.shape[1]
    copies[0].wait()
    copies[1].wait()
    scratch_ref[...] = layer_norm(x_ref[...].astype(jnp.float32), gain_ref[...])
    own, other = part_of(core, half), part_of(1 - core, half)
    query_ref[...] = scratch_ref[:, other]
    rest_ref[...] = x_ref[:, other]
    copies[2].wait()
    copies[3].wait()
    attended = attend_half(scratch_ref[:, own], keys_ref[...], values_ref[...], source_ref[0])
    state_ref[...] = add_rounded(x_ref[:, own], attended)


def attend_other_kernel(
    core_ref,
    source_ref,
    own_ref,
    query_ref,
    rest_ref,
    keys_ref,
    values_ref,
    gain_in,
    router_in,
    routes_in,
    target_in,
    state_ref,
    keep_ref,
    send_ref,
    gates_ref,
    routes_ref,
    gain_ref,
    router_ref,
    target_ref,
    scratch_ref,
    sems,
):
    core = core_ref[0]
    copies = fetch(
        sems,
        (gain_in, gain_ref),
        (router_in, router_ref),
        (routes_in, routes_ref),
        (target_in, target_ref),
    )
    full_len, half = own_ref.shape
    own, other = part_of(core, half), part_of(1 - core, half)
    attended = attend_half(query_ref[...], keys_ref[core], values_ref[core], source_ref[0])
    state_ref[:, own] = own_ref[...]
    state_ref[:, other] = add_rounded(rest_ref[...], attended)
    copies[0].wait()
    scratch_ref[...] = layer_norm(state_ref[...].astype(jnp.float32), gain_ref[...])
    keep_ref[...] = scratch_ref[:, own]
    send_ref[...] = scratch_ref[:, other]
    for copy in copies[1:]:
        copy.wait()
    logits = lax.dot_general(
        router_ref[...],
        scratch_ref[...],
        (((1,), (1,)), ((), ())),
        preferred_element_type=jnp.float32,
    )
    names = lax.broadcasted_iota(jnp.int32, logits.shape, 0)
    routes = routes_ref[core]
    chosen = [
        jnp.sum(jnp.where(names == routes[k : k + 1], logits, 0.0), axis=0, keepdims=True)
        for k in range(2)
    ]
    first = jax.nn.sigmoid(chosen[0] - chosen[1])
    live = lax.broadcasted_iota(jnp.int32, (1, full_len), 1) < target_ref[core]
    gates_ref[0:1] = jnp.where(live, first, 0.0)
    gates_ref[1:2] = jnp.where(live, 1.0 - first, 0.0)


def slots_of(routes_ref, experts_count):
    sents, _, full_len = routes_ref.shape
    rows = sents * full_len
    ids = lax.broadcasted_iota(jnp.int32, (max(8, experts_count), full_len), 0)
    named = jnp.concatenate(
        [
            jnp.where((ids == routes_ref[s, 0:1]) | (ids == routes_ref[s, 1:2]), 1.0, 0.0)
            for s in range(sents)
        ],
        axis=1,
    )
    before = lax.broadcasted_iota(jnp.int32, (rows, rows), 0) < lax.broadcasted_iota(
        jnp.int32, (rows, rows), 1
    )
    earlier = jnp.dot(
        named.astype(jnp.bfloat16),
        jnp.where(before, 1.0, 0.0).astype(jnp.bfloat16),
        preferred_element_type=jnp.float32,
    )
    return named > 0.0, earlier


def select_kernel(core_ref, line_ref, routes_ref, own_ref, other_ref, *rest):
    pieces, block_ref = rest[:-1], rest[-1]
    experts_count = len(pieces)
    full_len = own_ref.shape[0]
    capacity = pieces[0].shape[0]
    core = core_ref[0]
    block_ref[part_of(core, full_len)] = own_ref[...]
    block_ref[part_of(1 - core, full_len)] = other_ref[...]
    named, earlier = slots_of(routes_ref, experts_count)
    slot = jnp.where(named, earlier, -1.0)
    ids = lax.broadcasted_iota(jnp.int32, slot.shape, 0)
    numbers = lax.broadcasted_iota(jnp.int32, (capacity, slot.shape[1]), 0).astype(jnp.float32)
    for offset, piece_ref in enumerate(pieces):
        expert = line_ref[0] ^ offset
        wanted = jnp.sum(jnp.where(ids == expert, slot, 0.0), axis=0, keepdims=True)
        picks = jnp.where(numbers == wanted, 1.0, 0.0).astype(jnp.bfloat16)
        piece_ref[...] = jnp.dot(
            picks, block_ref[...], preferred_element_type=jnp.float32
        ).astype(jnp.bfloat16)


def expert_kernel(
    core_ref, p_ref, q_ref, p2_ref, q2_ref, in_ref, out_ref, keep_ref, send_ref, rows_ref
):
    core = core_ref[0]
    capacity, half = p_ref.shape
    rows_ref[:capacity, part_of(core, half)] = p_ref[...]
    rows_ref[capacity:, part_of(core, half)] = q_ref[...]
    rows_ref[:capacity, part_of(1 - core, half)] = p2_ref[...]
    rows_ref[capacity:, part_of(1 - core, half)] = q2_ref[...]
    hidden = jnp.dot(rows_ref[...], in_ref[...], preferred_element_type=jnp.float32)
    hidden = jnp.maximum(hidden, 0.0).astype(jnp.bfloat16)
    send = jnp.dot(
        hidden, out_ref[:, part_of(1 - core, half)], preferred_element_type=jnp.float32
    ).astype(jnp.bfloat16)
    send_ref[0] = send[:capacity]
    send_ref[1] = send[capacity:]
    keep = jnp.dot(hidden, out_ref[:, part_of(core, half)], preferred_element_type=jnp.float32)
    keep_ref[0] = keep[:capacity]
    keep_ref[1] = keep[capacity:]


def load_kernel(in_in, out_in, in_ref, out_ref, sems):
    for copy in fetch(sems, (in_in, in_ref), (out_in, out_ref)):
        copy.wait()


def combine_kernel(core_ref, line_ref, routes_ref, own_gates_ref, other_gates_ref, *rest):
    pieces, (own_ref, other_ref, rows_ref, gates_ref, sum_ref) = rest[:-5], rest[-5:]
    experts_count = len(pieces)
    capacity, half = pieces[0].shape
    sents, _, full_len = routes_ref.shape
    core = core_ref[0]
    for offset, piece_ref in enumerate(pieces):
        rows_ref[offset * capacity : (offset + 1) * capacity] = piece_ref[...]
    gates_ref[core] = own_gates_ref[...]
    gates_ref[1 - core] = other_gates_ref[...]
    _, earlier = slots_of(routes_ref, experts_count)
    ids = lax.broadcasted_iota(jnp.int32, (earlier.shape[0], full_len), 0)
    numbers = lax.broadcasted_iota(
        jnp.int32, (full_len, experts_count * capacity), 1
    ).astype(jnp.float32)
    for sent in range(sents):
        slots = earlier[:, sent * full_len : (sent + 1) * full_len]
        total = None
        for k in range(2):
            route = routes_ref[sent, k : k + 1]
            slot = jnp.sum(jnp.where(ids == route, slots, 0.0), axis=0, keepdims=True)
            place = (route ^ line_ref[0]).astype(jnp.float32) * capacity + slot
            place, gate = (
                jnp.broadcast_to(row, (full_len, full_len)).T[:, :1]
                for row in (place, gates_ref[sent, k : k + 1])
            )
            picks = jnp.where(numbers == place, 1.0, 0.0).astype(jnp.bfloat16)
            term = gate * jnp.dot(picks, rows_ref[...], preferred_element_type=jnp.float32)
            total = term if total is None else total + term
        sum_ref[sent] = total
    own_ref[...] = sum_ref[core]
    other_ref[...] = sum_ref[1 - core].astype(jnp.bfloat16)


def finish_kernel(core_ref, state_ref, own_ref, other_ref, mixed_ref):
    core = core_ref[0]
    half = own_ref.shape[-1]
    for part, summed in ((core, own_ref), (1 - core, other_ref)):
        span = part_of(part, half)
        mixed_ref[:, span] = (
            state_ref[:, span].astype(jnp.float32) + summed[...].astype(jnp.float32)
        ).astype(jnp.bfloat16)


def swap(values):
    return lax.ppermute(values, "section", [(0, 1), (1, 0)])


def swap_owner(values):
    owners = lax.axis_size("expert")
    return lax.ppermute(values, "expert", [(i, i ^ 1) for i in range(owners)])


def exchange(values, offset):
    owners = lax.axis_size("expert")
    return lax.ppermute(values, "expert", [(i, i ^ (2 * offset)) for i in range(owners)])


def after_kernel(*refs):
    pass


def after(value, *firsts):
    return pl.pallas_call(
        after_kernel,
        out_shape=jax.ShapeDtypeStruct(value.shape, value.dtype),
        in_specs=[pl.BlockSpec(memory_space=pl.ANY)] * (1 + len(firsts)),
        out_specs=pl.BlockSpec(memory_space=pl.ANY),
        input_output_aliases={0: 0},
        compiler_params=pltpu.CompilerParams(vmem_limit_bytes=2**20),
        name="after",
    )(value, *firsts)


def attend(
    core, decoder_states, memory_keys, memory_values, source_lengths, target_lengths, routes,
    attn_gain, ffn_gain, router,
):
    full_len, width = decoder_states.shape[1:]
    half = (full_len, width // 2)
    memory = memory_keys.shape[1:]
    other_keys, other_values = swap(memory_keys), swap(memory_values)
    own, query, rest = call(
        attend_own_kernel,
        "attend_own",
        [(half, jnp.bfloat16)] * 3,
        [core, source_lengths],
        [],
        [decoder_states, attn_gain[None], memory_keys, memory_values],
        scratch=[
            pltpu.VMEM((full_len, width), jnp.bfloat16),
            pltpu.VMEM((1, width), jnp.float32),
            pltpu.VMEM(memory, jnp.bfloat16),
            pltpu.VMEM(memory, jnp.bfloat16),
            pltpu.VMEM((full_len, width), jnp.bfloat16),
            pltpu.SemaphoreType.DMA((4,)),
        ],
    )
    return call(
        attend_other_kernel,
        "attend_other",
        [
            ((full_len, width), jnp.bfloat16),
            (half, jnp.bfloat16),
            (half, jnp.bfloat16),
            ((2, full_len), jnp.float32),
            (routes.shape, jnp.int32),
        ],
        [core, source_lengths],
        [own, query, rest, other_keys, other_values],
        [ffn_gain[None], router.T, routes, target_lengths],
        scratch=[
            pltpu.VMEM((1, width), jnp.float32),
            pltpu.VMEM(router.shape[::-1], jnp.bfloat16),
            pltpu.SMEM(target_lengths.shape, jnp.int32),
            pltpu.VMEM((full_len, width), jnp.bfloat16),
            pltpu.SemaphoreType.DMA((4,)),
        ],
    )


def line_experts(core, state, keep, send, gates, routes, fc_in, fc_out, capacity):
    full_len, width = state.shape
    half = width // 2
    count = lax.axis_size("expert") // 2
    line = (lax.axis_index("expert") // 2).astype(jnp.int32).reshape(1)
    other = swap(send)
    other_gates = swap(gates)
    piece = ((capacity, half), jnp.bfloat16)
    selected = call(
        select_kernel,
        "select",
        [piece] * count,
        [core, line],
        [routes, keep, other],
        scratch=[pltpu.VMEM((2 * full_len, half), jnp.bfloat16)],
    )
    near_in, near_out = call(
        load_kernel,
        "load",
        [(fc_in.shape, jnp.bfloat16), (fc_out.shape, jnp.bfloat16)],
        [],
        [],
        [fc_in, fc_out],
        scratch=[pltpu.SemaphoreType.DMA((2,))],
    )
    travelling = [exchange(selected[r], r) for r in range(1, count)]
    home = [None] * count
    kept, halves, wholes, ps, qs, q2s = {}, {}, {}, {}, {}, {}
    order = [0, 1, 2, 3]
    for offset in order:
        p = travelling[offset - 1] if offset else selected[0]
        if offset == 1:
            p = after(p, near_in)
        q = swap_owner(p)
        p2 = swap(p)
        q2 = swap(q)
        if offset == 1:
            q2 = after(q2, kept[0])
        if offset == 2:
            q2 = after(q2, kept[0], kept[1])
        if offset == 3:
            q2 = after(q2, halves[1])
        ps[offset], qs[offset], q2s[offset] = p, q, q2
        outs = [((2, capacity, half), jnp.float32), ((2, capacity, half), jnp.bfloat16)]
        rows = pltpu.VMEM((2 * capacity, width), jnp.bfloat16)
        kept[offset], sent = call(
            expert_kernel,
            "expert",
            outs,
            [core],
            [p, q, p2, q2, near_in, near_out],
            scratch=[rows],
            vmem_mib=16,
        )
        moving = swap(sent)
        if offset == 2:
            moving = after(moving, wholes[1])
        both = kept[offset] + moving.astype(jnp.float32)
        halves[offset] = both[1].astype(jnp.bfloat16)
        if offset == 0:
            own_both = both
            continue
        across = swap_owner(halves[offset])
        wholes[offset] = (both[0] + across.astype(jnp.float32)).astype(jnp.bfloat16)
        home[offset] = exchange(wholes[offset], offset)
    across = swap_owner(after(halves[0], halves[3]))
    home[0] = (own_both[0] + across.astype(jnp.float32)).astype(jnp.bfloat16)
    own_sum, other_sum = call(
        combine_kernel,
        "combine",
        [((full_len, half), jnp.float32), ((full_len, half), jnp.bfloat16)],
        [core, line],
        [routes, gates, other_gates, *home],
        scratch=[
            pltpu.VMEM((count * capacity, half), jnp.bfloat16),
            pltpu.VMEM((2, 2, full_len), jnp.float32),
            pltpu.VMEM((2, full_len, half), jnp.float32),
        ],
    )
    (mixed,) = call(
        finish_kernel,
        "finish",
        [((full_len, width), jnp.bfloat16)],
        [core],
        [state, own_sum, swap(other_sum)],
    )
    return mixed


def expert_apply(slot_rows, fc_in, fc_out):
    width = slot_rows.shape[-1]
    flat_rows = slot_rows.reshape(-1, width)
    hidden = jax.nn.relu(jnp.dot(flat_rows, fc_in, preferred_element_type=jnp.float32)).astype(
        jnp.bfloat16
    )
    produced = jnp.dot(hidden, fc_out, preferred_element_type=jnp.float32)
    return produced.reshape(slot_rows.shape[0], slot_rows.shape[1], width)


def sparse_experts(normed, target_lengths, routes, router, fc_in, fc_out, capacity):
    full_len, width = normed.shape
    all_normed = lax.all_gather(normed[None], "section", axis=0, tiled=True)
    block_sents = all_normed.shape[0]
    block_rows = block_sents * full_len
    tok_rows = all_normed.reshape(block_rows, width)
    owners = lax.axis_size("expert")
    experts_count = owners // 2
    chosen_ids = routes.reshape(block_rows, 2)
    logits = jnp.dot(tok_rows, router, preferred_element_type=jnp.float32)
    onehot = chosen_ids[:, :, None] == jnp.arange(experts_count, dtype=jnp.int32)
    chosen = jnp.sum(jnp.where(onehot, logits[:, None, :], 0.0), axis=-1)
    first = jax.nn.sigmoid(chosen[:, 0] - chosen[:, 1])
    gates = jnp.stack([first, 1.0 - first], axis=-1)
    live = (jnp.arange(full_len, dtype=jnp.int32)[None, :] < target_lengths[:, None]).reshape(
        block_rows
    )
    flags = onehot.reshape(block_rows * 2, experts_count).astype(jnp.int32)
    earlier = jnp.cumsum(flags, axis=0) - flags
    slot = jnp.sum(flags * earlier, axis=-1).reshape(block_rows, 2)
    position = chosen_ids * capacity + slot
    dump_index = experts_count * capacity
    target = jnp.where(live[:, None], position, dump_index)
    row_ids = jnp.broadcast_to(jnp.arange(block_rows, dtype=jnp.int32)[:, None], (block_rows, 2))
    table = (
        jnp.full((dump_index + 1,), block_rows, jnp.int32)
        .at[target.reshape(-1)]
        .set(row_ids.reshape(-1))[:dump_index]
    )
    padded = jnp.concatenate([tok_rows, jnp.zeros((1, width), jnp.bfloat16)], axis=0)
    slot_buffer = padded[table].reshape(experts_count, capacity, width)
    outgoing = jnp.repeat(slot_buffer, 2, axis=0)
    returned = lax.all_to_all(
        expert_apply(
            lax.all_to_all(outgoing, "expert", split_axis=0, concat_axis=0, tiled=True),
            fc_in,
            fc_out,
        ).astype(jnp.bfloat16),
        "expert",
        split_axis=0,
        concat_axis=0,
        tiled=True,
    ).astype(jnp.float32)
    partial_value = jnp.sum(returned.reshape(experts_count, 2, capacity, width), axis=1)
    fetched = partial_value.reshape(dump_index, width)[jnp.where(live[:, None], position, 0)]
    weight = gates * live[:, None].astype(jnp.float32)
    contrib = jnp.sum(weight[:, :, None] * fetched, axis=1).reshape(block_sents, full_len, width)
    summed = lax.psum_scatter(contrib, "section", scatter_dimension=0, tiled=True)
    return summed[0]


def local(
    decoder_states,
    memory_keys,
    memory_values,
    source_lengths,
    target_lengths,
    routes,
    attn_gain,
    ffn_gain,
    router,
    fc_in,
    fc_out,
):
    core = lax.axis_index("section").astype(jnp.int32).reshape(1)
    by_choice = jnp.transpose(routes, (0, 2, 1))
    state, keep, send, gates, by_choice = attend(
        core, decoder_states, memory_keys, memory_values, source_lengths, target_lengths, by_choice,
        attn_gain, ffn_gain, router,
    )
    block_rows = routes.shape[0] * routes.shape[1]
    experts_count = router.shape[1]
    capacity = 2 * max(1, 3 * block_rows // (2 * experts_count))
    if capacity % 16 == 0 and experts_count & (experts_count - 1) == 0:
        mixed = line_experts(core, state, keep, send, gates, by_choice, fc_in, fc_out, capacity)
    else:
        halves = jnp.stack([keep, send])
        normed = jnp.concatenate([halves[core[0]], halves[1 - core[0]]], axis=-1)
        summed = sparse_experts(normed, target_lengths, routes, router, fc_in, fc_out, capacity)
        mixed = (state.astype(jnp.float32) + summed).astype(jnp.bfloat16)
    return mixed[None]


def solution(mesh):
    placed = (
        P(("groups", "expert", "section"), None, None),
        P(("groups", "expert"), None, "section"),
        P(("groups", "expert"), None, "section"),
        P(("groups", "expert", "section")),
        P(("groups", "expert")),
        P(("groups", "expert"), None, None),
        P(),
        P(),
        P(),
        P(None, ("expert", "section")),
        P(("expert", "section"), None),
    )
    return jax.shard_map(
        local,
        mesh=mesh,
        in_specs=placed,
        out_specs=P(("groups", "expert", "section"), None, None),
        check_vma=False,
    )
```

```python
import functools

import jax
import jax.numpy as jnp
from jax import lax
from jax.experimental import pallas as pl
from jax.experimental.pallas import tpu as pltpu
from jax.sharding import PartitionSpec as P

HEAD_DIM = 128


def layer_norm(values, gain):
    centered = values - jnp.mean(values, axis=-1, keepdims=True)
    spread = jnp.mean(centered * centered, axis=-1, keepdims=True)
    return (centered * lax.rsqrt(spread + 1e-05) * gain).astype(jnp.bfloat16)


VMEM = pl.BlockSpec(memory_space=pltpu.VMEM)
SMEM = pl.BlockSpec(memory_space=pltpu.SMEM)
HBM = pl.BlockSpec(memory_space=pltpu.HBM)


def call(kernel, name, outs, scalars, arrays, far=(), scratch=(), vmem_mib=12):
    return pl.pallas_call(
        kernel,
        out_shape=tuple(jax.ShapeDtypeStruct(*out) for out in outs),
        in_specs=[SMEM] * len(scalars) + [VMEM] * len(arrays) + [HBM] * len(far),
        out_specs=(VMEM,) * len(outs),
        scratch_shapes=list(scratch),
        compiler_params=pltpu.CompilerParams(vmem_limit_bytes=vmem_mib * 2**20),
        name=name,
    )(*scalars, *arrays, *(pltpu.with_memory_space_constraint(a, pltpu.HBM) for a in far))


def fetch(sems, *pairs):
    copies = [
        pltpu.make_async_copy(source, target, sems.at[i]) for i, (source, target) in enumerate(pairs)
    ]
    for copy in copies:
        copy.start()
    return copies


def part_of(part, half):
    return pl.ds(pl.multiple_of(part * half, half), half)


def attend_half(queries, keys, values, length):
    rows = queries.shape[0]
    heads = [slice(at, at + HEAD_DIM) for at in range(0, queries.shape[1], HEAD_DIM)]
    scores = jnp.concatenate(
        [
            lax.dot_general(
                queries[:, head],
                keys[:, head],
                (((1,), (1,)), ((), ())),
                preferred_element_type=jnp.float32,
            )
            for head in heads
        ],
        axis=0,
    ) * HEAD_DIM ** (-0.5)
    valid = lax.broadcasted_iota(jnp.int32, (1, keys.shape[0]), 1) < length
    scores = jnp.where(valid, scores, -jnp.inf)
    expon = jnp.exp(scores - jnp.max(scores, axis=-1, keepdims=True))
    weights = (expon / jnp.sum(expon, axis=-1, keepdims=True)).astype(jnp.bfloat16)
    return jnp.concatenate(
        [
            jnp.dot(
                weights[i * rows : (i + 1) * rows],
                values[:, head],
                preferred_element_type=jnp.float32,
            )
            for i, head in enumerate(heads)
        ],
        axis=1,
    )


def add_rounded(x, attended):
    return (x.astype(jnp.float32) + attended).astype(jnp.bfloat16)


def attend_own_kernel(
    core_ref,
    source_ref,
    x_in,
    gain_in,
    keys_in,
    values_in,
    state_ref,
    query_ref,
    rest_ref,
    x_ref,
    gain_ref,
    keys_ref,
    values_ref,
    scratch_ref,
    sems,
):
    core = core_ref[0]
    copies = fetch(
        sems,
        (x_in.at[0], x_ref),
        (gain_in, gain_ref),
        (keys_in.at[core], keys_ref),
        (values_in.at[core], values_ref),
    )
    half = keys_ref.shape[1]
    copies[0].wait()
    copies[1].wait()
    scratch_ref[...] = layer_norm(x_ref[...].astype(jnp.float32), gain_ref[...])
    own, other = part_of(core, half), part_of(1 - core, half)
    query_ref[...] = scratch_ref[:, other]
    rest_ref[...] = x_ref[:, other]
    copies[2].wait()
    copies[3].wait()
    attended = attend_half(scratch_ref[:, own], keys_ref[...], values_ref[...], source_ref[0])
    state_ref[...] = add_rounded(x_ref[:, own], attended)


def attend_other_kernel(
    core_ref,
    source_ref,
    own_ref,
    query_ref,
    rest_ref,
    keys_ref,
    values_ref,
    gain_in,
    router_in,
    routes_in,
    target_in,
    state_ref,
    keep_ref,
    send_ref,
    gates_ref,
    routes_ref,
    gain_ref,
    router_ref,
    target_ref,
    scratch_ref,
    sems,
):
    core = core_ref[0]
    copies = fetch(
        sems,
        (gain_in, gain_ref),
        (router_in, router_ref),
        (routes_in, routes_ref),
        (target_in, target_ref),
    )
    full_len, half = own_ref.shape
    own, other = part_of(core, half), part_of(1 - core, half)
    attended = attend_half(query_ref[...], keys_ref[core], values_ref[core], source_ref[0])
    state_ref[:, own] = own_ref[...]
    state_ref[:, other] = add_rounded(rest_ref[...], attended)
    copies[0].wait()
    scratch_ref[...] = layer_norm(state_ref[...].astype(jnp.float32), gain_ref[...])
    keep_ref[...] = scratch_ref[:, own]
    send_ref[...] = scratch_ref[:, other]
    for copy in copies[1:]:
        copy.wait()
    logits = lax.dot_general(
        router_ref[...],
        scratch_ref[...],
        (((1,), (1,)), ((), ())),
        preferred_element_type=jnp.float32,
    )
    names = lax.broadcasted_iota(jnp.int32, logits.shape, 0)
    routes = routes_ref[core]
    chosen = [
        jnp.sum(jnp.where(names == routes[k : k + 1], logits, 0.0), axis=0, keepdims=True)
        for k in range(2)
    ]
    first = jax.nn.sigmoid(chosen[0] - chosen[1])
    live = lax.broadcasted_iota(jnp.int32, (1, full_len), 1) < target_ref[core]
    gates_ref[0:1] = jnp.where(live, first, 0.0)
    gates_ref[1:2] = jnp.where(live, 1.0 - first, 0.0)


def slots_of(routes_ref, experts_count):
    sents, _, full_len = routes_ref.shape
    rows = sents * full_len
    ids = lax.broadcasted_iota(jnp.int32, (max(8, experts_count), full_len), 0)
    named = jnp.concatenate(
        [
            jnp.where((ids == routes_ref[s, 0:1]) | (ids == routes_ref[s, 1:2]), 1.0, 0.0)
            for s in range(sents)
        ],
        axis=1,
    )
    before = lax.broadcasted_iota(jnp.int32, (rows, rows), 0) < lax.broadcasted_iota(
        jnp.int32, (rows, rows), 1
    )
    earlier = jnp.dot(
        named.astype(jnp.bfloat16),
        jnp.where(before, 1.0, 0.0).astype(jnp.bfloat16),
        preferred_element_type=jnp.float32,
    )
    return named > 0.0, earlier


def select_kernel(core_ref, line_ref, routes_ref, own_ref, other_ref, *rest):
    pieces, block_ref = rest[:-1], rest[-1]
    experts_count = len(pieces)
    full_len = own_ref.shape[0]
    capacity = pieces[0].shape[0]
    core = core_ref[0]
    block_ref[part_of(core, full_len)] = own_ref[...]
    block_ref[part_of(1 - core, full_len)] = other_ref[...]
    named, earlier = slots_of(routes_ref, experts_count)
    slot = jnp.where(named, earlier, -1.0)
    ids = lax.broadcasted_iota(jnp.int32, slot.shape, 0)
    numbers = lax.broadcasted_iota(jnp.int32, (capacity, slot.shape[1]), 0).astype(jnp.float32)
    for offset, piece_ref in enumerate(pieces):
        expert = line_ref[0] ^ offset
        wanted = jnp.sum(jnp.where(ids == expert, slot, 0.0), axis=0, keepdims=True)
        picks = jnp.where(numbers == wanted, 1.0, 0.0).astype(jnp.bfloat16)
        piece_ref[...] = jnp.dot(
            picks, block_ref[...], preferred_element_type=jnp.float32
        ).astype(jnp.bfloat16)


def expert_kernel(
    core_ref, p_ref, q_ref, p2_ref, q2_ref, in_ref, out_ref, keep_ref, send_ref, rows_ref
):
    core = core_ref[0]
    capacity, half = p_ref.shape
    rows_ref[:capacity, part_of(core, half)] = p_ref[...]
    rows_ref[capacity:, part_of(core, half)] = q_ref[...]
    rows_ref[:capacity, part_of(1 - core, half)] = p2_ref[...]
    rows_ref[capacity:, part_of(1 - core, half)] = q2_ref[...]
    hidden = jnp.dot(rows_ref[...], in_ref[...], preferred_element_type=jnp.float32)
    hidden = jnp.maximum(hidden, 0.0).astype(jnp.bfloat16)
    send = jnp.dot(
        hidden, out_ref[:, part_of(1 - core, half)], preferred_element_type=jnp.float32
    ).astype(jnp.bfloat16)
    send_ref[0] = send[:capacity]
    send_ref[1] = send[capacity:]
    keep = jnp.dot(hidden, out_ref[:, part_of(core, half)], preferred_element_type=jnp.float32)
    keep_ref[0] = keep[:capacity]
    keep_ref[1] = keep[capacity:]


def load_kernel(in_in, out_in, in_ref, out_ref, sems):
    for copy in fetch(sems, (in_in, in_ref), (out_in, out_ref)):
        copy.wait()


def combine_kernel(core_ref, line_ref, routes_ref, own_gates_ref, other_gates_ref, *rest):
    pieces, (own_ref, other_ref, rows_ref, gates_ref, sum_ref) = rest[:-5], rest[-5:]
    experts_count = len(pieces)
    capacity, half = pieces[0].shape
    sents, _, full_len = routes_ref.shape
    core = core_ref[0]
    for offset, piece_ref in enumerate(pieces):
        rows_ref[offset * capacity : (offset + 1) * capacity] = piece_ref[...]
    gates_ref[core] = own_gates_ref[...]
    gates_ref[1 - core] = other_gates_ref[...]
    _, earlier = slots_of(routes_ref, experts_count)
    ids = lax.broadcasted_iota(jnp.int32, (earlier.shape[0], full_len), 0)
    numbers = lax.broadcasted_iota(
        jnp.int32, (full_len, experts_count * capacity), 1
    ).astype(jnp.float32)
    for sent in range(sents):
        slots = earlier[:, sent * full_len : (sent + 1) * full_len]
        total = None
        for k in range(2):
            route = routes_ref[sent, k : k + 1]
            slot = jnp.sum(jnp.where(ids == route, slots, 0.0), axis=0, keepdims=True)
            place = (route ^ line_ref[0]).astype(jnp.float32) * capacity + slot
            place, gate = (
                jnp.broadcast_to(row, (full_len, full_len)).T[:, :1]
                for row in (place, gates_ref[sent, k : k + 1])
            )
            picks = jnp.where(numbers == place, 1.0, 0.0).astype(jnp.bfloat16)
            term = gate * jnp.dot(picks, rows_ref[...], preferred_element_type=jnp.float32)
            total = term if total is None else total + term
        sum_ref[sent] = total
    own_ref[...] = sum_ref[core]
    other_ref[...] = sum_ref[1 - core].astype(jnp.bfloat16)


def finish_kernel(core_ref, state_ref, own_ref, other_ref, mixed_ref):
    core = core_ref[0]
    half = own_ref.shape[-1]
    for part, summed in ((core, own_ref), (1 - core, other_ref)):
        span = part_of(part, half)
        mixed_ref[:, span] = (
            state_ref[:, span].astype(jnp.float32) + summed[...].astype(jnp.float32)
        ).astype(jnp.bfloat16)


def swap(values):
    return lax.ppermute(values, "section", [(0, 1), (1, 0)])


def swap_owner(values):
    owners = lax.axis_size("expert")
    return lax.ppermute(values, "expert", [(i, i ^ 1) for i in range(owners)])


def exchange(values, offset):
    owners = lax.axis_size("expert")
    return lax.ppermute(values, "expert", [(i, i ^ (2 * offset)) for i in range(owners)])


def after_kernel(*refs):
    pass


def after(value, *firsts):
    return pl.pallas_call(
        after_kernel,
        out_shape=jax.ShapeDtypeStruct(value.shape, value.dtype),
        in_specs=[pl.BlockSpec(memory_space=pl.ANY)] * (1 + len(firsts)),
        out_specs=pl.BlockSpec(memory_space=pl.ANY),
        input_output_aliases={0: 0},
        compiler_params=pltpu.CompilerParams(vmem_limit_bytes=2**20),
        name="after",
    )(value, *firsts)


def attend(
    core, decoder_states, memory_keys, memory_values, source_lengths, target_lengths, routes,
    attn_gain, ffn_gain, router,
):
    full_len, width = decoder_states.shape[1:]
    half = (full_len, width // 2)
    memory = memory_keys.shape[1:]
    other_keys, other_values = swap(memory_keys), swap(memory_values)
    own, query, rest = call(
        attend_own_kernel,
        "attend_own",
        [(half, jnp.bfloat16)] * 3,
        [core, source_lengths],
        [],
        [decoder_states, attn_gain[None], memory_keys, memory_values],
        scratch=[
            pltpu.VMEM((full_len, width), jnp.bfloat16),
            pltpu.VMEM((1, width), jnp.float32),
            pltpu.VMEM(memory, jnp.bfloat16),
            pltpu.VMEM(memory, jnp.bfloat16),
            pltpu.VMEM((full_len, width), jnp.bfloat16),
            pltpu.SemaphoreType.DMA((4,)),
        ],
    )
    return call(
        attend_other_kernel,
        "attend_other",
        [
            ((full_len, width), jnp.bfloat16),
            (half, jnp.bfloat16),
            (half, jnp.bfloat16),
            ((2, full_len), jnp.float32),
            (routes.shape, jnp.int32),
        ],
        [core, source_lengths],
        [own, query, rest, other_keys, other_values],
        [ffn_gain[None], router.T, routes, target_lengths],
        scratch=[
            pltpu.VMEM((1, width), jnp.float32),
            pltpu.VMEM(router.shape[::-1], jnp.bfloat16),
            pltpu.SMEM(target_lengths.shape, jnp.int32),
            pltpu.VMEM((full_len, width), jnp.bfloat16),
            pltpu.SemaphoreType.DMA((4,)),
        ],
    )


def line_experts(core, state, keep, send, gates, routes, fc_in, fc_out, capacity):
    full_len, width = state.shape
    half = width // 2
    count = lax.axis_size("expert") // 2
    line = (lax.axis_index("expert") // 2).astype(jnp.int32).reshape(1)
    other = swap(send)
    other_gates = swap(gates)
    piece = ((capacity, half), jnp.bfloat16)
    selected = call(
        select_kernel,
        "select",
        [piece] * count,
        [core, line],
        [routes, keep, other],
        scratch=[pltpu.VMEM((2 * full_len, half), jnp.bfloat16)],
    )
    near_in, near_out = call(
        load_kernel,
        "load",
        [(fc_in.shape, jnp.bfloat16), (fc_out.shape, jnp.bfloat16)],
        [],
        [],
        [fc_in, fc_out],
        scratch=[pltpu.SemaphoreType.DMA((2,))],
    )
    travelling = [exchange(selected[r], r) for r in range(1, count)]
    home = [None] * count
    ps, qs, kept, halves, wholes = {}, {}, {}, {}, {}
    for offset in [0, 2, 1, 3]:
        p = travelling[offset - 1] if offset else selected[0]
        if offset == 2:
            p = after(p, near_in, qs[0])
        q = swap_owner(p)
        if offset == 3:
            q = after(q, qs[1])
        ps[offset], qs[offset] = p, q
    for offset in [2, 3, 1, 0]:
        p, q = ps[offset], qs[offset]
        p2, q2 = swap(p), swap(q)
        if offset == 3:
            q2 = after(q2, kept[2])
        if offset == 1:
            q2 = after(q2, wholes[2], kept[3])
        if offset == 0:
            q2 = after(q2, wholes[3], kept[1])
        kept[offset], sent = call(
            expert_kernel,
            "expert",
            [((2, capacity, half), jnp.float32), ((2, capacity, half), jnp.bfloat16)],
            [core],
            [p, q, p2, q2, near_in, near_out],
            scratch=[pltpu.VMEM((2 * capacity, width), jnp.bfloat16)],
            vmem_mib=16,
        )
        moving = swap(sent)
        both = kept[offset] + moving.astype(jnp.float32)
        halves[offset] = both[1].astype(jnp.bfloat16)
        leaving = halves[offset]
        if offset == 0:
            leaving = after(leaving, halves[1])
        across = swap_owner(leaving)
        if offset == 3:
            across = after(across, home[2])
        wholes[offset] = (both[0] + across.astype(jnp.float32)).astype(jnp.bfloat16)
        home[offset] = exchange(wholes[offset], offset) if offset else wholes[offset]
    own_sum, other_sum = call(
        combine_kernel,
        "combine",
        [((full_len, half), jnp.float32), ((full_len, half), jnp.bfloat16)],
        [core, line],
        [routes, gates, other_gates, *home],
        scratch=[
            pltpu.VMEM((count * capacity, half), jnp.bfloat16),
            pltpu.VMEM((2, 2, full_len), jnp.float32),
            pltpu.VMEM((2, full_len, half), jnp.float32),
        ],
    )
    (mixed,) = call(
        finish_kernel,
        "finish",
        [((full_len, width), jnp.bfloat16)],
        [core],
        [state, own_sum, swap(other_sum)],
    )
    return mixed


def expert_apply(slot_rows, fc_in, fc_out):
    width = slot_rows.shape[-1]
    flat_rows = slot_rows.reshape(-1, width)
    hidden = jax.nn.relu(jnp.dot(flat_rows, fc_in, preferred_element_type=jnp.float32)).astype(
        jnp.bfloat16
    )
    produced = jnp.dot(hidden, fc_out, preferred_element_type=jnp.float32)
    return produced.reshape(slot_rows.shape[0], slot_rows.shape[1], width)


def sparse_experts(normed, target_lengths, routes, router, fc_in, fc_out, capacity):
    full_len, width = normed.shape
    all_normed = lax.all_gather(normed[None], "section", axis=0, tiled=True)
    block_sents = all_normed.shape[0]
    block_rows = block_sents * full_len
    tok_rows = all_normed.reshape(block_rows, width)
    owners = lax.axis_size("expert")
    experts_count = owners // 2
    chosen_ids = routes.reshape(block_rows, 2)
    logits = jnp.dot(tok_rows, router, preferred_element_type=jnp.float32)
    onehot = chosen_ids[:, :, None] == jnp.arange(experts_count, dtype=jnp.int32)
    chosen = jnp.sum(jnp.where(onehot, logits[:, None, :], 0.0), axis=-1)
    first = jax.nn.sigmoid(chosen[:, 0] - chosen[:, 1])
    gates = jnp.stack([first, 1.0 - first], axis=-1)
    live = (jnp.arange(full_len, dtype=jnp.int32)[None, :] < target_lengths[:, None]).reshape(
        block_rows
    )
    flags = onehot.reshape(block_rows * 2, experts_count).astype(jnp.int32)
    earlier = jnp.cumsum(flags, axis=0) - flags
    slot = jnp.sum(flags * earlier, axis=-1).reshape(block_rows, 2)
    position = chosen_ids * capacity + slot
    dump_index = experts_count * capacity
    target = jnp.where(live[:, None], position, dump_index)
    row_ids = jnp.broadcast_to(jnp.arange(block_rows, dtype=jnp.int32)[:, None], (block_rows, 2))
    table = (
        jnp.full((dump_index + 1,), block_rows, jnp.int32)
        .at[target.reshape(-1)]
        .set(row_ids.reshape(-1))[:dump_index]
    )
    padded = jnp.concatenate([tok_rows, jnp.zeros((1, width), jnp.bfloat16)], axis=0)
    slot_buffer = padded[table].reshape(experts_count, capacity, width)
    outgoing = jnp.repeat(slot_buffer, 2, axis=0)
    returned = lax.all_to_all(
        expert_apply(
            lax.all_to_all(outgoing, "expert", split_axis=0, concat_axis=0, tiled=True),
            fc_in,
            fc_out,
        ).astype(jnp.bfloat16),
        "expert",
        split_axis=0,
        concat_axis=0,
        tiled=True,
    ).astype(jnp.float32)
    partial_value = jnp.sum(returned.reshape(experts_count, 2, capacity, width), axis=1)
    fetched = partial_value.reshape(dump_index, width)[jnp.where(live[:, None], position, 0)]
    weight = gates * live[:, None].astype(jnp.float32)
    contrib = jnp.sum(weight[:, :, None] * fetched, axis=1).reshape(block_sents, full_len, width)
    summed = lax.psum_scatter(contrib, "section", scatter_dimension=0, tiled=True)
    return summed[0]


def local(
    decoder_states,
    memory_keys,
    memory_values,
    source_lengths,
    target_lengths,
    routes,
    attn_gain,
    ffn_gain,
    router,
    fc_in,
    fc_out,
):
    core = lax.axis_index("section").astype(jnp.int32).reshape(1)
    by_choice = jnp.transpose(routes, (0, 2, 1))
    state, keep, send, gates, by_choice = attend(
        core, decoder_states, memory_keys, memory_values, source_lengths, target_lengths, by_choice,
        attn_gain, ffn_gain, router,
    )
    block_rows = routes.shape[0] * routes.shape[1]
    experts_count = router.shape[1]
    capacity = 2 * max(1, 3 * block_rows // (2 * experts_count))
    if capacity % 16 == 0 and experts_count & (experts_count - 1) == 0:
        mixed = line_experts(core, state, keep, send, gates, by_choice, fc_in, fc_out, capacity)
    else:
        halves = jnp.stack([keep, send])
        normed = jnp.concatenate([halves[core[0]], halves[1 - core[0]]], axis=-1)
        summed = sparse_experts(normed, target_lengths, routes, router, fc_in, fc_out, capacity)
        mixed = (state.astype(jnp.float32) + summed).astype(jnp.bfloat16)
    return mixed[None]


def solution(mesh):
    placed = (
        P(("groups", "expert", "section"), None, None),
        P(("groups", "expert"), None, "section"),
        P(("groups", "expert"), None, "section"),
        P(("groups", "expert", "section")),
        P(("groups", "expert")),
        P(("groups", "expert"), None, None),
        P(),
        P(),
        P(),
        P(None, ("expert", "section")),
        P(("expert", "section"), None),
    )
    return jax.shard_map(
        local,
        mesh=mesh,
        in_specs=placed,
        out_specs=P(("groups", "expert", "section"), None, None),
        check_vma=False,
    )
```

```python
import functools

import jax
import jax.numpy as jnp
from jax import lax
from jax.experimental import pallas as pl
from jax.experimental.pallas import tpu as pltpu
from jax.sharding import PartitionSpec as P

HEAD_DIM = 128


def layer_norm(values, gain):
    centered = values - jnp.mean(values, axis=-1, keepdims=True)
    spread = jnp.mean(centered * centered, axis=-1, keepdims=True)
    return (centered * lax.rsqrt(spread + 1e-05) * gain).astype(jnp.bfloat16)


VMEM = pl.BlockSpec(memory_space=pltpu.VMEM)
SMEM = pl.BlockSpec(memory_space=pltpu.SMEM)
HBM = pl.BlockSpec(memory_space=pltpu.HBM)


def call(kernel, name, outs, scalars, arrays, far=(), scratch=(), vmem_mib=12):
    return pl.pallas_call(
        kernel,
        out_shape=tuple(jax.ShapeDtypeStruct(*out) for out in outs),
        in_specs=[SMEM] * len(scalars) + [VMEM] * len(arrays) + [HBM] * len(far),
        out_specs=(VMEM,) * len(outs),
        scratch_shapes=list(scratch),
        compiler_params=pltpu.CompilerParams(vmem_limit_bytes=vmem_mib * 2**20),
        name=name,
    )(*scalars, *arrays, *(pltpu.with_memory_space_constraint(a, pltpu.HBM) for a in far))


def fetch(sems, *pairs):
    copies = [
        pltpu.make_async_copy(source, target, sems.at[i]) for i, (source, target) in enumerate(pairs)
    ]
    for copy in copies:
        copy.start()
    return copies


def part_of(part, half):
    return pl.ds(pl.multiple_of(part * half, half), half)


def attend_half(queries, keys, values, length):
    rows = queries.shape[0]
    heads = [slice(at, at + HEAD_DIM) for at in range(0, queries.shape[1], HEAD_DIM)]
    scores = jnp.concatenate(
        [
            lax.dot_general(
                queries[:, head],
                keys[:, head],
                (((1,), (1,)), ((), ())),
                preferred_element_type=jnp.float32,
            )
            for head in heads
        ],
        axis=0,
    ) * HEAD_DIM ** (-0.5)
    valid = lax.broadcasted_iota(jnp.int32, (1, keys.shape[0]), 1) < length
    scores = jnp.where(valid, scores, -jnp.inf)
    expon = jnp.exp(scores - jnp.max(scores, axis=-1, keepdims=True))
    weights = (expon / jnp.sum(expon, axis=-1, keepdims=True)).astype(jnp.bfloat16)
    return jnp.concatenate(
        [
            jnp.dot(
                weights[i * rows : (i + 1) * rows],
                values[:, head],
                preferred_element_type=jnp.float32,
            )
            for i, head in enumerate(heads)
        ],
        axis=1,
    )


def add_rounded(x, attended):
    return (x.astype(jnp.float32) + attended).astype(jnp.bfloat16)


def attend_own_kernel(
    core_ref,
    source_ref,
    x_in,
    gain_in,
    keys_in,
    values_in,
    state_ref,
    query_ref,
    rest_ref,
    x_ref,
    gain_ref,
    keys_ref,
    values_ref,
    scratch_ref,
    sems,
):
    core = core_ref[0]
    copies = fetch(
        sems,
        (x_in.at[0], x_ref),
        (gain_in, gain_ref),
        (keys_in.at[core], keys_ref),
        (values_in.at[core], values_ref),
    )
    half = keys_ref.shape[1]
    copies[0].wait()
    copies[1].wait()
    scratch_ref[...] = layer_norm(x_ref[...].astype(jnp.float32), gain_ref[...])
    own, other = part_of(core, half), part_of(1 - core, half)
    query_ref[...] = scratch_ref[:, other]
    rest_ref[...] = x_ref[:, other]
    copies[2].wait()
    copies[3].wait()
    attended = attend_half(scratch_ref[:, own], keys_ref[...], values_ref[...], source_ref[0])
    state_ref[...] = add_rounded(x_ref[:, own], attended)


def attend_other_kernel(
    core_ref,
    source_ref,
    own_ref,
    query_ref,
    rest_ref,
    keys_ref,
    values_ref,
    gain_in,
    router_in,
    routes_in,
    target_in,
    state_ref,
    keep_ref,
    send_ref,
    gates_ref,
    routes_ref,
    gain_ref,
    router_ref,
    target_ref,
    scratch_ref,
    sems,
):
    core = core_ref[0]
    copies = fetch(
        sems,
        (gain_in, gain_ref),
        (router_in, router_ref),
        (routes_in, routes_ref),
        (target_in, target_ref),
    )
    full_len, half = own_ref.shape
    own, other = part_of(core, half), part_of(1 - core, half)
    attended = attend_half(query_ref[...], keys_ref[core], values_ref[core], source_ref[0])
    state_ref[:, own] = own_ref[...]
    state_ref[:, other] = add_rounded(rest_ref[...], attended)
    copies[0].wait()
    scratch_ref[...] = layer_norm(state_ref[...].astype(jnp.float32), gain_ref[...])
    keep_ref[...] = scratch_ref[:, own]
    send_ref[...] = scratch_ref[:, other]
    for copy in copies[1:]:
        copy.wait()
    logits = lax.dot_general(
        router_ref[...],
        scratch_ref[...],
        (((1,), (1,)), ((), ())),
        preferred_element_type=jnp.float32,
    )
    names = lax.broadcasted_iota(jnp.int32, logits.shape, 0)
    routes = routes_ref[core]
    chosen = [
        jnp.sum(jnp.where(names == routes[k : k + 1], logits, 0.0), axis=0, keepdims=True)
        for k in range(2)
    ]
    first = jax.nn.sigmoid(chosen[0] - chosen[1])
    live = lax.broadcasted_iota(jnp.int32, (1, full_len), 1) < target_ref[core]
    gates_ref[0:1] = jnp.where(live, first, 0.0)
    gates_ref[1:2] = jnp.where(live, 1.0 - first, 0.0)


def slots_of(routes_ref, experts_count):
    sents, _, full_len = routes_ref.shape
    rows = sents * full_len
    ids = lax.broadcasted_iota(jnp.int32, (max(8, experts_count), full_len), 0)
    named = jnp.concatenate(
        [
            jnp.where((ids == routes_ref[s, 0:1]) | (ids == routes_ref[s, 1:2]), 1.0, 0.0)
            for s in range(sents)
        ],
        axis=1,
    )
    before = lax.broadcasted_iota(jnp.int32, (rows, rows), 0) < lax.broadcasted_iota(
        jnp.int32, (rows, rows), 1
    )
    earlier = jnp.dot(
        named.astype(jnp.bfloat16),
        jnp.where(before, 1.0, 0.0).astype(jnp.bfloat16),
        preferred_element_type=jnp.float32,
    )
    return named > 0.0, earlier


def select_kernel(core_ref, line_ref, routes_ref, own_ref, other_ref, *rest):
    pieces, block_ref = rest[:-1], rest[-1]
    experts_count = len(pieces)
    full_len = own_ref.shape[0]
    capacity = pieces[0].shape[0]
    core = core_ref[0]
    block_ref[part_of(core, full_len)] = own_ref[...]
    block_ref[part_of(1 - core, full_len)] = other_ref[...]
    named, earlier = slots_of(routes_ref, experts_count)
    slot = jnp.where(named, earlier, -1.0)
    ids = lax.broadcasted_iota(jnp.int32, slot.shape, 0)
    numbers = lax.broadcasted_iota(jnp.int32, (capacity, slot.shape[1]), 0).astype(jnp.float32)
    for offset, piece_ref in enumerate(pieces):
        expert = line_ref[0] ^ offset
        wanted = jnp.sum(jnp.where(ids == expert, slot, 0.0), axis=0, keepdims=True)
        picks = jnp.where(numbers == wanted, 1.0, 0.0).astype(jnp.bfloat16)
        piece_ref[...] = jnp.dot(
            picks, block_ref[...], preferred_element_type=jnp.float32
        ).astype(jnp.bfloat16)


def expert_kernel(
    core_ref, p_ref, q_ref, p2_ref, q2_ref, in_ref, out_ref, keep_ref, send_ref, rows_ref
):
    core = core_ref[0]
    capacity, half = p_ref.shape
    rows_ref[:capacity, part_of(core, half)] = p_ref[...]
    rows_ref[capacity:, part_of(core, half)] = q_ref[...]
    rows_ref[:capacity, part_of(1 - core, half)] = p2_ref[...]
    rows_ref[capacity:, part_of(1 - core, half)] = q2_ref[...]
    hidden = jnp.dot(rows_ref[...], in_ref[...], preferred_element_type=jnp.float32)
    hidden = jnp.maximum(hidden, 0.0).astype(jnp.bfloat16)
    send = jnp.dot(
        hidden, out_ref[:, part_of(1 - core, half)], preferred_element_type=jnp.float32
    ).astype(jnp.bfloat16)
    send_ref[0] = send[:capacity]
    send_ref[1] = send[capacity:]
    keep = jnp.dot(hidden, out_ref[:, part_of(core, half)], preferred_element_type=jnp.float32)
    keep_ref[0] = keep[:capacity]
    keep_ref[1] = keep[capacity:]


def load_kernel(in_in, out_in, in_ref, out_ref, sems):
    for copy in fetch(sems, (in_in, in_ref), (out_in, out_ref)):
        copy.wait()


def combine_kernel(core_ref, line_ref, routes_ref, own_gates_ref, other_gates_ref, *rest):
    pieces, (own_ref, other_ref, rows_ref, gates_ref, sum_ref) = rest[:-5], rest[-5:]
    experts_count = len(pieces)
    capacity, half = pieces[0].shape
    sents, _, full_len = routes_ref.shape
    core = core_ref[0]
    for offset, piece_ref in enumerate(pieces):
        rows_ref[offset * capacity : (offset + 1) * capacity] = piece_ref[...]
    gates_ref[core] = own_gates_ref[...]
    gates_ref[1 - core] = other_gates_ref[...]
    _, earlier = slots_of(routes_ref, experts_count)
    ids = lax.broadcasted_iota(jnp.int32, (earlier.shape[0], full_len), 0)
    numbers = lax.broadcasted_iota(
        jnp.int32, (full_len, experts_count * capacity), 1
    ).astype(jnp.float32)
    for sent in range(sents):
        slots = earlier[:, sent * full_len : (sent + 1) * full_len]
        total = None
        for k in range(2):
            route = routes_ref[sent, k : k + 1]
            slot = jnp.sum(jnp.where(ids == route, slots, 0.0), axis=0, keepdims=True)
            place = (route ^ line_ref[0]).astype(jnp.float32) * capacity + slot
            place, gate = (
                jnp.broadcast_to(row, (full_len, full_len)).T[:, :1]
                for row in (place, gates_ref[sent, k : k + 1])
            )
            picks = jnp.where(numbers == place, 1.0, 0.0).astype(jnp.bfloat16)
            term = gate * jnp.dot(picks, rows_ref[...], preferred_element_type=jnp.float32)
            total = term if total is None else total + term
        sum_ref[sent] = total
    own_ref[...] = sum_ref[core]
    other_ref[...] = sum_ref[1 - core].astype(jnp.bfloat16)


def finish_kernel(core_ref, state_ref, own_ref, other_ref, mixed_ref):
    core = core_ref[0]
    half = own_ref.shape[-1]
    for part, summed in ((core, own_ref), (1 - core, other_ref)):
        span = part_of(part, half)
        mixed_ref[:, span] = (
            state_ref[:, span].astype(jnp.float32) + summed[...].astype(jnp.float32)
        ).astype(jnp.bfloat16)


def swap(values):
    return lax.ppermute(values, "section", [(0, 1), (1, 0)])


def swap_owner(values):
    owners = lax.axis_size("expert")
    return lax.ppermute(values, "expert", [(i, i ^ 1) for i in range(owners)])


def exchange(values, offset):
    owners = lax.axis_size("expert")
    return lax.ppermute(values, "expert", [(i, i ^ (2 * offset)) for i in range(owners)])


def after_kernel(*refs):
    pass


def after(value, *firsts):
    return pl.pallas_call(
        after_kernel,
        out_shape=jax.ShapeDtypeStruct(value.shape, value.dtype),
        in_specs=[pl.BlockSpec(memory_space=pl.ANY)] * (1 + len(firsts)),
        out_specs=pl.BlockSpec(memory_space=pl.ANY),
        input_output_aliases={0: 0},
        compiler_params=pltpu.CompilerParams(vmem_limit_bytes=2**20),
        name="after",
    )(value, *firsts)


def attend(
    core, decoder_states, memory_keys, memory_values, source_lengths, target_lengths, routes,
    attn_gain, ffn_gain, router,
):
    full_len, width = decoder_states.shape[1:]
    half = (full_len, width // 2)
    memory = memory_keys.shape[1:]
    other_keys, other_values = swap(memory_keys), swap(memory_values)
    own, query, rest = call(
        attend_own_kernel,
        "attend_own",
        [(half, jnp.bfloat16)] * 3,
        [core, source_lengths],
        [],
        [decoder_states, attn_gain[None], memory_keys, memory_values],
        scratch=[
            pltpu.VMEM((full_len, width), jnp.bfloat16),
            pltpu.VMEM((1, width), jnp.float32),
            pltpu.VMEM(memory, jnp.bfloat16),
            pltpu.VMEM(memory, jnp.bfloat16),
            pltpu.VMEM((full_len, width), jnp.bfloat16),
            pltpu.SemaphoreType.DMA((4,)),
        ],
    )
    return call(
        attend_other_kernel,
        "attend_other",
        [
            ((full_len, width), jnp.bfloat16),
            (half, jnp.bfloat16),
            (half, jnp.bfloat16),
            ((2, full_len), jnp.float32),
            (routes.shape, jnp.int32),
        ],
        [core, source_lengths],
        [own, query, rest, other_keys, other_values],
        [ffn_gain[None], router.T, routes, target_lengths],
        scratch=[
            pltpu.VMEM((1, width), jnp.float32),
            pltpu.VMEM(router.shape[::-1], jnp.bfloat16),
            pltpu.SMEM(target_lengths.shape, jnp.int32),
            pltpu.VMEM((full_len, width), jnp.bfloat16),
            pltpu.SemaphoreType.DMA((4,)),
        ],
    )


def line_experts(core, state, keep, send, gates, routes, fc_in, fc_out, capacity):
    full_len, width = state.shape
    half = width // 2
    count = lax.axis_size("expert") // 2
    line = (lax.axis_index("expert") // 2).astype(jnp.int32).reshape(1)
    other = swap(send)
    other_gates = swap(gates)
    piece = ((capacity, half), jnp.bfloat16)
    selected = call(
        select_kernel,
        "select",
        [piece] * count,
        [core, line],
        [routes, keep, other],
        scratch=[pltpu.VMEM((2 * full_len, half), jnp.bfloat16)],
    )
    near_in, near_out = call(
        load_kernel,
        "load",
        [(fc_in.shape, jnp.bfloat16), (fc_out.shape, jnp.bfloat16)],
        [],
        [],
        [fc_in, fc_out],
        scratch=[pltpu.SemaphoreType.DMA((2,))],
    )
    travelling = [exchange(selected[r], r) for r in range(1, count)]
    home = [None] * count
    ps, qs, kept, halves, wholes, boths = {}, {}, {}, {}, {}, {}
    for offset in [0, 1, 2, 3]:
        p = travelling[offset - 1] if offset else selected[0]
        if offset == 2:
            p = after(p, near_in)
        q = swap_owner(p)
        ps[offset], qs[offset] = p, q
    for offset in [0, 1, 2, 3]:
        p, q = ps[offset], qs[offset]
        p2, q2 = swap(p), swap(q)
        if offset == 1:
            q2 = after(q2, kept[0])
        if offset == 2:
            q2 = after(q2, kept[0], kept[1])
        if offset == 3:
            q2 = after(q2, halves[2])
        kept[offset], sent = call(
            expert_kernel,
            "expert",
            [((2, capacity, half), jnp.float32), ((2, capacity, half), jnp.bfloat16)],
            [core],
            [p, q, p2, q2, near_in, near_out],
            scratch=[pltpu.VMEM((2 * capacity, width), jnp.bfloat16)],
            vmem_mib=16,
        )
        moving = swap(sent)
        both = kept[offset] + moving.astype(jnp.float32)
        halves[offset] = both[1].astype(jnp.bfloat16)
        boths[offset] = both
    for offset in [2, 3, 1, 0]:
        both, leaving = boths[offset], halves[offset]
        if offset == 1:
            leaving = after(leaving, halves[3])
        if offset == 0:
            leaving = after(leaving, wholes[3])
        across = swap_owner(leaving)
        wholes[offset] = (both[0] + across.astype(jnp.float32)).astype(jnp.bfloat16)
        home[offset] = exchange(wholes[offset], offset) if offset else wholes[offset]
    own_sum, other_sum = call(
        combine_kernel,
        "combine",
        [((full_len, half), jnp.float32), ((full_len, half), jnp.bfloat16)],
        [core, line],
        [routes, gates, other_gates, *home],
        scratch=[
            pltpu.VMEM((count * capacity, half), jnp.bfloat16),
            pltpu.VMEM((2, 2, full_len), jnp.float32),
            pltpu.VMEM((2, full_len, half), jnp.float32),
        ],
    )
    (mixed,) = call(
        finish_kernel,
        "finish",
        [((full_len, width), jnp.bfloat16)],
        [core],
        [state, own_sum, swap(other_sum)],
    )
    return mixed


def expert_apply(slot_rows, fc_in, fc_out):
    width = slot_rows.shape[-1]
    flat_rows = slot_rows.reshape(-1, width)
    hidden = jax.nn.relu(jnp.dot(flat_rows, fc_in, preferred_element_type=jnp.float32)).astype(
        jnp.bfloat16
    )
    produced = jnp.dot(hidden, fc_out, preferred_element_type=jnp.float32)
    return produced.reshape(slot_rows.shape[0], slot_rows.shape[1], width)


def sparse_experts(normed, target_lengths, routes, router, fc_in, fc_out, capacity):
    full_len, width = normed.shape
    all_normed = lax.all_gather(normed[None], "section", axis=0, tiled=True)
    block_sents = all_normed.shape[0]
    block_rows = block_sents * full_len
    tok_rows = all_normed.reshape(block_rows, width)
    owners = lax.axis_size("expert")
    experts_count = owners // 2
    chosen_ids = routes.reshape(block_rows, 2)
    logits = jnp.dot(tok_rows, router, preferred_element_type=jnp.float32)
    onehot = chosen_ids[:, :, None] == jnp.arange(experts_count, dtype=jnp.int32)
    chosen = jnp.sum(jnp.where(onehot, logits[:, None, :], 0.0), axis=-1)
    first = jax.nn.sigmoid(chosen[:, 0] - chosen[:, 1])
    gates = jnp.stack([first, 1.0 - first], axis=-1)
    live = (jnp.arange(full_len, dtype=jnp.int32)[None, :] < target_lengths[:, None]).reshape(
        block_rows
    )
    flags = onehot.reshape(block_rows * 2, experts_count).astype(jnp.int32)
    earlier = jnp.cumsum(flags, axis=0) - flags
    slot = jnp.sum(flags * earlier, axis=-1).reshape(block_rows, 2)
    position = chosen_ids * capacity + slot
    dump_index = experts_count * capacity
    target = jnp.where(live[:, None], position, dump_index)
    row_ids = jnp.broadcast_to(jnp.arange(block_rows, dtype=jnp.int32)[:, None], (block_rows, 2))
    table = (
        jnp.full((dump_index + 1,), block_rows, jnp.int32)
        .at[target.reshape(-1)]
        .set(row_ids.reshape(-1))[:dump_index]
    )
    padded = jnp.concatenate([tok_rows, jnp.zeros((1, width), jnp.bfloat16)], axis=0)
    slot_buffer = padded[table].reshape(experts_count, capacity, width)
    outgoing = jnp.repeat(slot_buffer, 2, axis=0)
    returned = lax.all_to_all(
        expert_apply(
            lax.all_to_all(outgoing, "expert", split_axis=0, concat_axis=0, tiled=True),
            fc_in,
            fc_out,
        ).astype(jnp.bfloat16),
        "expert",
        split_axis=0,
        concat_axis=0,
        tiled=True,
    ).astype(jnp.float32)
    partial_value = jnp.sum(returned.reshape(experts_count, 2, capacity, width), axis=1)
    fetched = partial_value.reshape(dump_index, width)[jnp.where(live[:, None], position, 0)]
    weight = gates * live[:, None].astype(jnp.float32)
    contrib = jnp.sum(weight[:, :, None] * fetched, axis=1).reshape(block_sents, full_len, width)
    summed = lax.psum_scatter(contrib, "section", scatter_dimension=0, tiled=True)
    return summed[0]


def local(
    decoder_states,
    memory_keys,
    memory_values,
    source_lengths,
    target_lengths,
    routes,
    attn_gain,
    ffn_gain,
    router,
    fc_in,
    fc_out,
):
    core = lax.axis_index("section").astype(jnp.int32).reshape(1)
    by_choice = jnp.transpose(routes, (0, 2, 1))
    state, keep, send, gates, by_choice = attend(
        core, decoder_states, memory_keys, memory_values, source_lengths, target_lengths, by_choice,
        attn_gain, ffn_gain, router,
    )
    block_rows = routes.shape[0] * routes.shape[1]
    experts_count = router.shape[1]
    capacity = 2 * max(1, 3 * block_rows // (2 * experts_count))
    if capacity % 16 == 0 and experts_count & (experts_count - 1) == 0:
        mixed = line_experts(core, state, keep, send, gates, by_choice, fc_in, fc_out, capacity)
    else:
        halves = jnp.stack([keep, send])
        normed = jnp.concatenate([halves[core[0]], halves[1 - core[0]]], axis=-1)
        summed = sparse_experts(normed, target_lengths, routes, router, fc_in, fc_out, capacity)
        mixed = (state.astype(jnp.float32) + summed).astype(jnp.bfloat16)
    return mixed[None]


def solution(mesh):
    placed = (
        P(("groups", "expert", "section"), None, None),
        P(("groups", "expert"), None, "section"),
        P(("groups", "expert"), None, "section"),
        P(("groups", "expert", "section")),
        P(("groups", "expert")),
        P(("groups", "expert"), None, None),
        P(),
        P(),
        P(),
        P(None, ("expert", "section")),
        P(("expert", "section"), None),
    )
    return jax.shard_map(
        local,
        mesh=mesh,
        in_specs=placed,
        out_specs=P(("groups", "expert", "section"), None, None),
        check_vma=False,
    )
```

```python
import functools

import jax
import jax.numpy as jnp
from jax import lax
from jax.experimental import pallas as pl
from jax.experimental.pallas import tpu as pltpu
from jax.sharding import PartitionSpec as P

HEAD_DIM = 128


def layer_norm(values, gain):
    centered = values - jnp.mean(values, axis=-1, keepdims=True)
    spread = jnp.mean(centered * centered, axis=-1, keepdims=True)
    return (centered * lax.rsqrt(spread + 1e-05) * gain).astype(jnp.bfloat16)


VMEM = pl.BlockSpec(memory_space=pltpu.VMEM)
SMEM = pl.BlockSpec(memory_space=pltpu.SMEM)
HBM = pl.BlockSpec(memory_space=pltpu.HBM)


def call(kernel, name, outs, scalars, arrays, far=(), scratch=(), vmem_mib=12):
    return pl.pallas_call(
        kernel,
        out_shape=tuple(jax.ShapeDtypeStruct(*out) for out in outs),
        in_specs=[SMEM] * len(scalars) + [VMEM] * len(arrays) + [HBM] * len(far),
        out_specs=(VMEM,) * len(outs),
        scratch_shapes=list(scratch),
        compiler_params=pltpu.CompilerParams(vmem_limit_bytes=vmem_mib * 2**20),
        name=name,
    )(*scalars, *arrays, *(pltpu.with_memory_space_constraint(a, pltpu.HBM) for a in far))


def fetch(sems, *pairs):
    copies = [
        pltpu.make_async_copy(source, target, sems.at[i]) for i, (source, target) in enumerate(pairs)
    ]
    for copy in copies:
        copy.start()
    return copies


def part_of(part, half):
    return pl.ds(pl.multiple_of(part * half, half), half)


def attend_half(queries, keys, values, length):
    rows = queries.shape[0]
    heads = [slice(at, at + HEAD_DIM) for at in range(0, queries.shape[1], HEAD_DIM)]
    scores = jnp.concatenate(
        [
            lax.dot_general(
                queries[:, head],
                keys[:, head],
                (((1,), (1,)), ((), ())),
                preferred_element_type=jnp.float32,
            )
            for head in heads
        ],
        axis=0,
    ) * HEAD_DIM ** (-0.5)
    valid = lax.broadcasted_iota(jnp.int32, (1, keys.shape[0]), 1) < length
    scores = jnp.where(valid, scores, -jnp.inf)
    expon = jnp.exp(scores - jnp.max(scores, axis=-1, keepdims=True))
    weights = (expon / jnp.sum(expon, axis=-1, keepdims=True)).astype(jnp.bfloat16)
    return jnp.concatenate(
        [
            jnp.dot(
                weights[i * rows : (i + 1) * rows],
                values[:, head],
                preferred_element_type=jnp.float32,
            )
            for i, head in enumerate(heads)
        ],
        axis=1,
    )


def add_rounded(x, attended):
    return (x.astype(jnp.float32) + attended).astype(jnp.bfloat16)


def attend_own_kernel(
    core_ref,
    source_ref,
    x_in,
    gain_in,
    keys_in,
    values_in,
    state_ref,
    query_ref,
    rest_ref,
    x_ref,
    gain_ref,
    keys_ref,
    values_ref,
    scratch_ref,
    sems,
):
    core = core_ref[0]
    copies = fetch(
        sems,
        (x_in.at[0], x_ref),
        (gain_in, gain_ref),
        (keys_in.at[core], keys_ref),
        (values_in.at[core], values_ref),
    )
    half = keys_ref.shape[1]
    copies[0].wait()
    copies[1].wait()
    scratch_ref[...] = layer_norm(x_ref[...].astype(jnp.float32), gain_ref[...])
    own, other = part_of(core, half), part_of(1 - core, half)
    query_ref[...] = scratch_ref[:, other]
    rest_ref[...] = x_ref[:, other]
    copies[2].wait()
    copies[3].wait()
    attended = attend_half(scratch_ref[:, own], keys_ref[...], values_ref[...], source_ref[0])
    state_ref[...] = add_rounded(x_ref[:, own], attended)


def attend_other_kernel(
    core_ref,
    source_ref,
    own_ref,
    query_ref,
    rest_ref,
    keys_ref,
    values_ref,
    gain_in,
    router_in,
    routes_in,
    target_in,
    state_ref,
    keep_ref,
    send_ref,
    gates_ref,
    routes_ref,
    gain_ref,
    router_ref,
    target_ref,
    scratch_ref,
    sems,
):
    core = core_ref[0]
    copies = fetch(
        sems,
        (gain_in, gain_ref),
        (router_in, router_ref),
        (routes_in, routes_ref),
        (target_in, target_ref),
    )
    full_len, half = own_ref.shape
    own, other = part_of(core, half), part_of(1 - core, half)
    attended = attend_half(query_ref[...], keys_ref[core], values_ref[core], source_ref[0])
    state_ref[:, own] = own_ref[...]
    state_ref[:, other] = add_rounded(rest_ref[...], attended)
    copies[0].wait()
    scratch_ref[...] = layer_norm(state_ref[...].astype(jnp.float32), gain_ref[...])
    keep_ref[...] = scratch_ref[:, own]
    send_ref[...] = scratch_ref[:, other]
    for copy in copies[1:]:
        copy.wait()
    logits = lax.dot_general(
        router_ref[...],
        scratch_ref[...],
        (((1,), (1,)), ((), ())),
        preferred_element_type=jnp.float32,
    )
    names = lax.broadcasted_iota(jnp.int32, logits.shape, 0)
    routes = routes_ref[core]
    chosen = [
        jnp.sum(jnp.where(names == routes[k : k + 1], logits, 0.0), axis=0, keepdims=True)
        for k in range(2)
    ]
    first = jax.nn.sigmoid(chosen[0] - chosen[1])
    live = lax.broadcasted_iota(jnp.int32, (1, full_len), 1) < target_ref[core]
    gates_ref[0:1] = jnp.where(live, first, 0.0)
    gates_ref[1:2] = jnp.where(live, 1.0 - first, 0.0)


def slots_of(routes_ref, experts_count):
    sents, _, full_len = routes_ref.shape
    rows = sents * full_len
    ids = lax.broadcasted_iota(jnp.int32, (max(8, experts_count), full_len), 0)
    named = jnp.concatenate(
        [
            jnp.where((ids == routes_ref[s, 0:1]) | (ids == routes_ref[s, 1:2]), 1.0, 0.0)
            for s in range(sents)
        ],
        axis=1,
    )
    before = lax.broadcasted_iota(jnp.int32, (rows, rows), 0) < lax.broadcasted_iota(
        jnp.int32, (rows, rows), 1
    )
    earlier = jnp.dot(
        named.astype(jnp.bfloat16),
        jnp.where(before, 1.0, 0.0).astype(jnp.bfloat16),
        preferred_element_type=jnp.float32,
    )
    return named > 0.0, earlier


def select_kernel(core_ref, line_ref, routes_ref, own_ref, other_ref, *rest):
    pieces, block_ref = rest[:-1], rest[-1]
    experts_count = len(pieces)
    full_len = own_ref.shape[0]
    capacity = pieces[0].shape[0]
    core = core_ref[0]
    block_ref[part_of(core, full_len)] = own_ref[...]
    block_ref[part_of(1 - core, full_len)] = other_ref[...]
    named, earlier = slots_of(routes_ref, experts_count)
    slot = jnp.where(named, earlier, -1.0)
    ids = lax.broadcasted_iota(jnp.int32, slot.shape, 0)
    numbers = lax.broadcasted_iota(jnp.int32, (capacity, slot.shape[1]), 0).astype(jnp.float32)
    for offset, piece_ref in enumerate(pieces):
        expert = line_ref[0] ^ offset
        wanted = jnp.sum(jnp.where(ids == expert, slot, 0.0), axis=0, keepdims=True)
        picks = jnp.where(numbers == wanted, 1.0, 0.0).astype(jnp.bfloat16)
        piece_ref[...] = jnp.dot(
            picks, block_ref[...], preferred_element_type=jnp.float32
        ).astype(jnp.bfloat16)


def expert_kernel(
    core_ref, p_ref, q_ref, p2_ref, q2_ref, in_ref, out_ref, keep_ref, send_ref, rows_ref
):
    core = core_ref[0]
    capacity, half = p_ref.shape
    rows_ref[:capacity, part_of(core, half)] = p_ref[...]
    rows_ref[capacity:, part_of(core, half)] = q_ref[...]
    rows_ref[:capacity, part_of(1 - core, half)] = p2_ref[...]
    rows_ref[capacity:, part_of(1 - core, half)] = q2_ref[...]
    hidden = jnp.dot(rows_ref[...], in_ref[...], preferred_element_type=jnp.float32)
    hidden = jnp.maximum(hidden, 0.0).astype(jnp.bfloat16)
    send = jnp.dot(
        hidden, out_ref[:, part_of(1 - core, half)], preferred_element_type=jnp.float32
    ).astype(jnp.bfloat16)
    send_ref[0] = send[:capacity]
    send_ref[1] = send[capacity:]
    keep = jnp.dot(hidden, out_ref[:, part_of(core, half)], preferred_element_type=jnp.float32)
    keep_ref[0] = keep[:capacity]
    keep_ref[1] = keep[capacity:]


def load_kernel(in_in, out_in, in_ref, out_ref, sems):
    for copy in fetch(sems, (in_in, in_ref), (out_in, out_ref)):
        copy.wait()


def combine_kernel(core_ref, line_ref, routes_ref, own_gates_ref, other_gates_ref, *rest):
    pieces, (own_ref, other_ref, rows_ref, gates_ref, sum_ref) = rest[:-5], rest[-5:]
    experts_count = len(pieces)
    capacity, half = pieces[0].shape
    sents, _, full_len = routes_ref.shape
    core = core_ref[0]
    for offset, piece_ref in enumerate(pieces):
        rows_ref[offset * capacity : (offset + 1) * capacity] = piece_ref[...]
    gates_ref[core] = own_gates_ref[...]
    gates_ref[1 - core] = other_gates_ref[...]
    _, earlier = slots_of(routes_ref, experts_count)
    ids = lax.broadcasted_iota(jnp.int32, (earlier.shape[0], full_len), 0)
    numbers = lax.broadcasted_iota(
        jnp.int32, (full_len, experts_count * capacity), 1
    ).astype(jnp.float32)
    for sent in range(sents):
        slots = earlier[:, sent * full_len : (sent + 1) * full_len]
        total = None
        for k in range(2):
            route = routes_ref[sent, k : k + 1]
            slot = jnp.sum(jnp.where(ids == route, slots, 0.0), axis=0, keepdims=True)
            place = (route ^ line_ref[0]).astype(jnp.float32) * capacity + slot
            place, gate = (
                jnp.broadcast_to(row, (full_len, full_len)).T[:, :1]
                for row in (place, gates_ref[sent, k : k + 1])
            )
            picks = jnp.where(numbers == place, 1.0, 0.0).astype(jnp.bfloat16)
            term = gate * jnp.dot(picks, rows_ref[...], preferred_element_type=jnp.float32)
            total = term if total is None else total + term
        sum_ref[sent] = total
    own_ref[...] = sum_ref[core]
    other_ref[...] = sum_ref[1 - core].astype(jnp.bfloat16)


def finish_kernel(core_ref, state_ref, own_ref, other_ref, mixed_ref):
    core = core_ref[0]
    half = own_ref.shape[-1]
    for part, summed in ((core, own_ref), (1 - core, other_ref)):
        span = part_of(part, half)
        mixed_ref[:, span] = (
            state_ref[:, span].astype(jnp.float32) + summed[...].astype(jnp.float32)
        ).astype(jnp.bfloat16)


def swap(values):
    return lax.ppermute(values, "section", [(0, 1), (1, 0)])


def swap_owner(values):
    owners = lax.axis_size("expert")
    return lax.ppermute(values, "expert", [(i, i ^ 1) for i in range(owners)])


def exchange(values, offset):
    owners = lax.axis_size("expert")
    return lax.ppermute(values, "expert", [(i, i ^ (2 * offset)) for i in range(owners)])


def after_kernel(*refs):
    pass


def after(value, *firsts):
    return pl.pallas_call(
        after_kernel,
        out_shape=jax.ShapeDtypeStruct(value.shape, value.dtype),
        in_specs=[pl.BlockSpec(memory_space=pl.ANY)] * (1 + len(firsts)),
        out_specs=pl.BlockSpec(memory_space=pl.ANY),
        input_output_aliases={0: 0},
        compiler_params=pltpu.CompilerParams(vmem_limit_bytes=2**20),
        name="after",
    )(value, *firsts)


def attend(
    core, decoder_states, memory_keys, memory_values, source_lengths, target_lengths, routes,
    attn_gain, ffn_gain, router,
):
    full_len, width = decoder_states.shape[1:]
    half = (full_len, width // 2)
    memory = memory_keys.shape[1:]
    other_keys, other_values = swap(memory_keys), swap(memory_values)
    own, query, rest = call(
        attend_own_kernel,
        "attend_own",
        [(half, jnp.bfloat16)] * 3,
        [core, source_lengths],
        [],
        [decoder_states, attn_gain[None], memory_keys, memory_values],
        scratch=[
            pltpu.VMEM((full_len, width), jnp.bfloat16),
            pltpu.VMEM((1, width), jnp.float32),
            pltpu.VMEM(memory, jnp.bfloat16),
            pltpu.VMEM(memory, jnp.bfloat16),
            pltpu.VMEM((full_len, width), jnp.bfloat16),
            pltpu.SemaphoreType.DMA((4,)),
        ],
    )
    return call(
        attend_other_kernel,
        "attend_other",
        [
            ((full_len, width), jnp.bfloat16),
            (half, jnp.bfloat16),
            (half, jnp.bfloat16),
            ((2, full_len), jnp.float32),
            (routes.shape, jnp.int32),
        ],
        [core, source_lengths],
        [own, query, rest, other_keys, other_values],
        [ffn_gain[None], router.T, routes, target_lengths],
        scratch=[
            pltpu.VMEM((1, width), jnp.float32),
            pltpu.VMEM(router.shape[::-1], jnp.bfloat16),
            pltpu.SMEM(target_lengths.shape, jnp.int32),
            pltpu.VMEM((full_len, width), jnp.bfloat16),
            pltpu.SemaphoreType.DMA((4,)),
        ],
    )


def line_experts(core, state, keep, send, gates, routes, fc_in, fc_out, capacity):
    full_len, width = state.shape
    half = width // 2
    count = lax.axis_size("expert") // 2
    line = (lax.axis_index("expert") // 2).astype(jnp.int32).reshape(1)
    other = swap(send)
    other_gates = swap(gates)
    piece = ((capacity, half), jnp.bfloat16)
    selected = call(
        select_kernel,
        "select",
        [piece] * count,
        [core, line],
        [routes, keep, other],
        scratch=[pltpu.VMEM((2 * full_len, half), jnp.bfloat16)],
    )
    near_in, near_out = call(
        load_kernel,
        "load",
        [(fc_in.shape, jnp.bfloat16), (fc_out.shape, jnp.bfloat16)],
        [],
        [],
        [fc_in, fc_out],
        scratch=[pltpu.SemaphoreType.DMA((2,))],
    )
    travelling = [exchange(selected[r], r) for r in range(1, count)]
    home = [None] * count
    ps, qs, kept, halves, wholes, boths = {}, {}, {}, {}, {}, {}
    for offset in [0, 1, 2, 3]:
        p = travelling[offset - 1] if offset else selected[0]
        if offset == 1:
            p = after(p, near_in)
        q = swap_owner(p)
        ps[offset], qs[offset] = p, q
    for offset in [0, 1, 2, 3]:
        p, q = ps[offset], qs[offset]
        p2, q2 = swap(p), swap(q)
        if offset == 2:
            q2 = after(q2, kept[0], kept[1])
        if offset == 3:
            q2 = after(q2, halves[2])
        kept[offset], sent = call(
            expert_kernel,
            "expert",
            [((2, capacity, half), jnp.float32), ((2, capacity, half), jnp.bfloat16)],
            [core],
            [p, q, p2, q2, near_in, near_out],
            scratch=[pltpu.VMEM((2 * capacity, width), jnp.bfloat16)],
            vmem_mib=16,
        )
        moving = swap(sent)
        both = kept[offset] + moving.astype(jnp.float32)
        halves[offset] = both[1].astype(jnp.bfloat16)
        boths[offset] = both
    for offset in [2, 3, 1, 0]:
        both, leaving = boths[offset], halves[offset]
        if offset == 1:
            leaving = after(leaving, halves[3])
        if offset == 0:
            leaving = after(leaving, wholes[3])
        across = swap_owner(leaving)
        wholes[offset] = (both[0] + across.astype(jnp.float32)).astype(jnp.bfloat16)
        home[offset] = exchange(wholes[offset], offset) if offset else wholes[offset]
    own_sum, other_sum = call(
        combine_kernel,
        "combine",
        [((full_len, half), jnp.float32), ((full_len, half), jnp.bfloat16)],
        [core, line],
        [routes, gates, other_gates, *home],
        scratch=[
            pltpu.VMEM((count * capacity, half), jnp.bfloat16),
            pltpu.VMEM((2, 2, full_len), jnp.float32),
            pltpu.VMEM((2, full_len, half), jnp.float32),
        ],
    )
    (mixed,) = call(
        finish_kernel,
        "finish",
        [((full_len, width), jnp.bfloat16)],
        [core],
        [state, own_sum, swap(other_sum)],
    )
    return mixed


def expert_apply(slot_rows, fc_in, fc_out):
    width = slot_rows.shape[-1]
    flat_rows = slot_rows.reshape(-1, width)
    hidden = jax.nn.relu(jnp.dot(flat_rows, fc_in, preferred_element_type=jnp.float32)).astype(
        jnp.bfloat16
    )
    produced = jnp.dot(hidden, fc_out, preferred_element_type=jnp.float32)
    return produced.reshape(slot_rows.shape[0], slot_rows.shape[1], width)


def sparse_experts(normed, target_lengths, routes, router, fc_in, fc_out, capacity):
    full_len, width = normed.shape
    all_normed = lax.all_gather(normed[None], "section", axis=0, tiled=True)
    block_sents = all_normed.shape[0]
    block_rows = block_sents * full_len
    tok_rows = all_normed.reshape(block_rows, width)
    owners = lax.axis_size("expert")
    experts_count = owners // 2
    chosen_ids = routes.reshape(block_rows, 2)
    logits = jnp.dot(tok_rows, router, preferred_element_type=jnp.float32)
    onehot = chosen_ids[:, :, None] == jnp.arange(experts_count, dtype=jnp.int32)
    chosen = jnp.sum(jnp.where(onehot, logits[:, None, :], 0.0), axis=-1)
    first = jax.nn.sigmoid(chosen[:, 0] - chosen[:, 1])
    gates = jnp.stack([first, 1.0 - first], axis=-1)
    live = (jnp.arange(full_len, dtype=jnp.int32)[None, :] < target_lengths[:, None]).reshape(
        block_rows
    )
    flags = onehot.reshape(block_rows * 2, experts_count).astype(jnp.int32)
    earlier = jnp.cumsum(flags, axis=0) - flags
    slot = jnp.sum(flags * earlier, axis=-1).reshape(block_rows, 2)
    position = chosen_ids * capacity + slot
    dump_index = experts_count * capacity
    target = jnp.where(live[:, None], position, dump_index)
    row_ids = jnp.broadcast_to(jnp.arange(block_rows, dtype=jnp.int32)[:, None], (block_rows, 2))
    table = (
        jnp.full((dump_index + 1,), block_rows, jnp.int32)
        .at[target.reshape(-1)]
        .set(row_ids.reshape(-1))[:dump_index]
    )
    padded = jnp.concatenate([tok_rows, jnp.zeros((1, width), jnp.bfloat16)], axis=0)
    slot_buffer = padded[table].reshape(experts_count, capacity, width)
    outgoing = jnp.repeat(slot_buffer, 2, axis=0)
    returned = lax.all_to_all(
        expert_apply(
            lax.all_to_all(outgoing, "expert", split_axis=0, concat_axis=0, tiled=True),
            fc_in,
            fc_out,
        ).astype(jnp.bfloat16),
        "expert",
        split_axis=0,
        concat_axis=0,
        tiled=True,
    ).astype(jnp.float32)
    partial_value = jnp.sum(returned.reshape(experts_count, 2, capacity, width), axis=1)
    fetched = partial_value.reshape(dump_index, width)[jnp.where(live[:, None], position, 0)]
    weight = gates * live[:, None].astype(jnp.float32)
    contrib = jnp.sum(weight[:, :, None] * fetched, axis=1).reshape(block_sents, full_len, width)
    summed = lax.psum_scatter(contrib, "section", scatter_dimension=0, tiled=True)
    return summed[0]


def local(
    decoder_states,
    memory_keys,
    memory_values,
    source_lengths,
    target_lengths,
    routes,
    attn_gain,
    ffn_gain,
    router,
    fc_in,
    fc_out,
):
    core = lax.axis_index("section").astype(jnp.int32).reshape(1)
    by_choice = jnp.transpose(routes, (0, 2, 1))
    state, keep, send, gates, by_choice = attend(
        core, decoder_states, memory_keys, memory_values, source_lengths, target_lengths, by_choice,
        attn_gain, ffn_gain, router,
    )
    block_rows = routes.shape[0] * routes.shape[1]
    experts_count = router.shape[1]
    capacity = 2 * max(1, 3 * block_rows // (2 * experts_count))
    if capacity % 16 == 0 and experts_count & (experts_count - 1) == 0:
        mixed = line_experts(core, state, keep, send, gates, by_choice, fc_in, fc_out, capacity)
    else:
        halves = jnp.stack([keep, send])
        normed = jnp.concatenate([halves[core[0]], halves[1 - core[0]]], axis=-1)
        summed = sparse_experts(normed, target_lengths, routes, router, fc_in, fc_out, capacity)
        mixed = (state.astype(jnp.float32) + summed).astype(jnp.bfloat16)
    return mixed[None]


def solution(mesh):
    placed = (
        P(("groups", "expert", "section"), None, None),
        P(("groups", "expert"), None, "section"),
        P(("groups", "expert"), None, "section"),
        P(("groups", "expert", "section")),
        P(("groups", "expert")),
        P(("groups", "expert"), None, None),
        P(),
        P(),
        P(),
        P(None, ("expert", "section")),
        P(("expert", "section"), None),
    )
    return jax.shard_map(
        local,
        mesh=mesh,
        in_specs=placed,
        out_specs=P(("groups", "expert", "section"), None, None),
        check_vma=False,
    )
```

```python
import functools

import jax
import jax.numpy as jnp
from jax import lax
from jax.experimental import pallas as pl
from jax.experimental.pallas import tpu as pltpu
from jax.sharding import PartitionSpec as P

HEAD_DIM = 128


def layer_norm(values, gain):
    centered = values - jnp.mean(values, axis=-1, keepdims=True)
    spread = jnp.mean(centered * centered, axis=-1, keepdims=True)
    return (centered * lax.rsqrt(spread + 1e-05) * gain).astype(jnp.bfloat16)


VMEM = pl.BlockSpec(memory_space=pltpu.VMEM)
SMEM = pl.BlockSpec(memory_space=pltpu.SMEM)
HBM = pl.BlockSpec(memory_space=pltpu.HBM)


def call(kernel, name, outs, scalars, arrays, far=(), scratch=(), vmem_mib=12):
    return pl.pallas_call(
        kernel,
        out_shape=tuple(jax.ShapeDtypeStruct(*out) for out in outs),
        in_specs=[SMEM] * len(scalars) + [VMEM] * len(arrays) + [HBM] * len(far),
        out_specs=(VMEM,) * len(outs),
        scratch_shapes=list(scratch),
        compiler_params=pltpu.CompilerParams(vmem_limit_bytes=vmem_mib * 2**20),
        name=name,
    )(*scalars, *arrays, *(pltpu.with_memory_space_constraint(a, pltpu.HBM) for a in far))


def fetch(sems, *pairs):
    copies = [
        pltpu.make_async_copy(source, target, sems.at[i]) for i, (source, target) in enumerate(pairs)
    ]
    for copy in copies:
        copy.start()
    return copies


def part_of(part, half):
    return pl.ds(pl.multiple_of(part * half, half), half)


def attend_half(queries, keys, values, length):
    rows = queries.shape[0]
    heads = [slice(at, at + HEAD_DIM) for at in range(0, queries.shape[1], HEAD_DIM)]
    scores = jnp.concatenate(
        [
            lax.dot_general(
                queries[:, head],
                keys[:, head],
                (((1,), (1,)), ((), ())),
                preferred_element_type=jnp.float32,
            )
            for head in heads
        ],
        axis=0,
    ) * HEAD_DIM ** (-0.5)
    valid = lax.broadcasted_iota(jnp.int32, (1, keys.shape[0]), 1) < length
    scores = jnp.where(valid, scores, -jnp.inf)
    expon = jnp.exp(scores - jnp.max(scores, axis=-1, keepdims=True))
    weights = (expon / jnp.sum(expon, axis=-1, keepdims=True)).astype(jnp.bfloat16)
    return jnp.concatenate(
        [
            jnp.dot(
                weights[i * rows : (i + 1) * rows],
                values[:, head],
                preferred_element_type=jnp.float32,
            )
            for i, head in enumerate(heads)
        ],
        axis=1,
    )


def add_rounded(x, attended):
    return (x.astype(jnp.float32) + attended).astype(jnp.bfloat16)


def attend_own_kernel(
    core_ref,
    source_ref,
    x_in,
    gain_in,
    keys_in,
    values_in,
    state_ref,
    query_ref,
    rest_ref,
    x_ref,
    gain_ref,
    keys_ref,
    values_ref,
    scratch_ref,
    sems,
):
    core = core_ref[0]
    copies = fetch(
        sems,
        (x_in.at[0], x_ref),
        (gain_in, gain_ref),
        (keys_in.at[core], keys_ref),
        (values_in.at[core], values_ref),
    )
    half = keys_ref.shape[1]
    copies[0].wait()
    copies[1].wait()
    scratch_ref[...] = layer_norm(x_ref[...].astype(jnp.float32), gain_ref[...])
    own, other = part_of(core, half), part_of(1 - core, half)
    query_ref[...] = scratch_ref[:, other]
    rest_ref[...] = x_ref[:, other]
    copies[2].wait()
    copies[3].wait()
    attended = attend_half(scratch_ref[:, own], keys_ref[...], values_ref[...], source_ref[0])
    state_ref[...] = add_rounded(x_ref[:, own], attended)


def attend_other_kernel(
    core_ref,
    source_ref,
    own_ref,
    query_ref,
    rest_ref,
    keys_ref,
    values_ref,
    gain_in,
    router_in,
    routes_in,
    target_in,
    state_ref,
    keep_ref,
    send_ref,
    gates_ref,
    routes_ref,
    gain_ref,
    router_ref,
    target_ref,
    scratch_ref,
    sems,
):
    core = core_ref[0]
    copies = fetch(
        sems,
        (gain_in, gain_ref),
        (router_in, router_ref),
        (routes_in, routes_ref),
        (target_in, target_ref),
    )
    full_len, half = own_ref.shape
    own, other = part_of(core, half), part_of(1 - core, half)
    attended = attend_half(query_ref[...], keys_ref[core], values_ref[core], source_ref[0])
    state_ref[:, own] = own_ref[...]
    state_ref[:, other] = add_rounded(rest_ref[...], attended)
    copies[0].wait()
    scratch_ref[...] = layer_norm(state_ref[...].astype(jnp.float32), gain_ref[...])
    keep_ref[...] = scratch_ref[:, own]
    send_ref[...] = scratch_ref[:, other]
    for copy in copies[1:]:
        copy.wait()
    logits = lax.dot_general(
        router_ref[...],
        scratch_ref[...],
        (((1,), (1,)), ((), ())),
        preferred_element_type=jnp.float32,
    )
    names = lax.broadcasted_iota(jnp.int32, logits.shape, 0)
    routes = routes_ref[core]
    chosen = [
        jnp.sum(jnp.where(names == routes[k : k + 1], logits, 0.0), axis=0, keepdims=True)
        for k in range(2)
    ]
    first = jax.nn.sigmoid(chosen[0] - chosen[1])
    live = lax.broadcasted_iota(jnp.int32, (1, full_len), 1) < target_ref[core]
    gates_ref[0:1] = jnp.where(live, first, 0.0)
    gates_ref[1:2] = jnp.where(live, 1.0 - first, 0.0)


def slots_of(routes_ref, experts_count):
    sents, _, full_len = routes_ref.shape
    rows = sents * full_len
    ids = lax.broadcasted_iota(jnp.int32, (max(8, experts_count), full_len), 0)
    named = jnp.concatenate(
        [
            jnp.where((ids == routes_ref[s, 0:1]) | (ids == routes_ref[s, 1:2]), 1.0, 0.0)
            for s in range(sents)
        ],
        axis=1,
    )
    before = lax.broadcasted_iota(jnp.int32, (rows, rows), 0) < lax.broadcasted_iota(
        jnp.int32, (rows, rows), 1
    )
    earlier = jnp.dot(
        named.astype(jnp.bfloat16),
        jnp.where(before, 1.0, 0.0).astype(jnp.bfloat16),
        preferred_element_type=jnp.float32,
    )
    return named > 0.0, earlier


def select_kernel(core_ref, line_ref, routes_ref, own_ref, other_ref, *rest):
    pieces, block_ref = rest[:-1], rest[-1]
    experts_count = len(pieces)
    full_len = own_ref.shape[0]
    capacity = pieces[0].shape[0]
    core = core_ref[0]
    block_ref[part_of(core, full_len)] = own_ref[...]
    block_ref[part_of(1 - core, full_len)] = other_ref[...]
    named, earlier = slots_of(routes_ref, experts_count)
    slot = jnp.where(named, earlier, -1.0)
    ids = lax.broadcasted_iota(jnp.int32, slot.shape, 0)
    numbers = lax.broadcasted_iota(jnp.int32, (capacity, slot.shape[1]), 0).astype(jnp.float32)
    for offset, piece_ref in enumerate(pieces):
        expert = line_ref[0] ^ offset
        wanted = jnp.sum(jnp.where(ids == expert, slot, 0.0), axis=0, keepdims=True)
        picks = jnp.where(numbers == wanted, 1.0, 0.0).astype(jnp.bfloat16)
        piece_ref[...] = jnp.dot(
            picks, block_ref[...], preferred_element_type=jnp.float32
        ).astype(jnp.bfloat16)


def expert_kernel(
    core_ref, p_ref, q_ref, p2_ref, q2_ref, in_ref, out_ref, keep_ref, send_ref, rows_ref
):
    core = core_ref[0]
    capacity, half = p_ref.shape
    rows_ref[:capacity, part_of(core, half)] = p_ref[...]
    rows_ref[capacity:, part_of(core, half)] = q_ref[...]
    rows_ref[:capacity, part_of(1 - core, half)] = p2_ref[...]
    rows_ref[capacity:, part_of(1 - core, half)] = q2_ref[...]
    hidden = jnp.dot(rows_ref[...], in_ref[...], preferred_element_type=jnp.float32)
    hidden = jnp.maximum(hidden, 0.0).astype(jnp.bfloat16)
    send = jnp.dot(
        hidden, out_ref[:, part_of(1 - core, half)], preferred_element_type=jnp.float32
    ).astype(jnp.bfloat16)
    send_ref[0] = send[:capacity]
    send_ref[1] = send[capacity:]
    keep = jnp.dot(hidden, out_ref[:, part_of(core, half)], preferred_element_type=jnp.float32)
    keep_ref[0] = keep[:capacity]
    keep_ref[1] = keep[capacity:]


def load_kernel(in_in, out_in, in_ref, out_ref, sems):
    for copy in fetch(sems, (in_in, in_ref), (out_in, out_ref)):
        copy.wait()


def combine_kernel(core_ref, line_ref, routes_ref, own_gates_ref, other_gates_ref, *rest):
    pieces, (own_ref, other_ref, rows_ref, gates_ref, sum_ref) = rest[:-5], rest[-5:]
    experts_count = len(pieces)
    capacity, half = pieces[0].shape
    sents, _, full_len = routes_ref.shape
    core = core_ref[0]
    for offset, piece_ref in enumerate(pieces):
        rows_ref[offset * capacity : (offset + 1) * capacity] = piece_ref[...]
    gates_ref[core] = own_gates_ref[...]
    gates_ref[1 - core] = other_gates_ref[...]
    _, earlier = slots_of(routes_ref, experts_count)
    ids = lax.broadcasted_iota(jnp.int32, (earlier.shape[0], full_len), 0)
    numbers = lax.broadcasted_iota(
        jnp.int32, (full_len, experts_count * capacity), 1
    ).astype(jnp.float32)
    for sent in range(sents):
        slots = earlier[:, sent * full_len : (sent + 1) * full_len]
        total = None
        for k in range(2):
            route = routes_ref[sent, k : k + 1]
            slot = jnp.sum(jnp.where(ids == route, slots, 0.0), axis=0, keepdims=True)
            place = (route ^ line_ref[0]).astype(jnp.float32) * capacity + slot
            place, gate = (
                jnp.broadcast_to(row, (full_len, full_len)).T[:, :1]
                for row in (place, gates_ref[sent, k : k + 1])
            )
            picks = jnp.where(numbers == place, 1.0, 0.0).astype(jnp.bfloat16)
            term = gate * jnp.dot(picks, rows_ref[...], preferred_element_type=jnp.float32)
            total = term if total is None else total + term
        sum_ref[sent] = total
    own_ref[...] = sum_ref[core]
    other_ref[...] = sum_ref[1 - core].astype(jnp.bfloat16)


def finish_kernel(core_ref, state_ref, own_ref, other_ref, mixed_ref):
    core = core_ref[0]
    half = own_ref.shape[-1]
    for part, summed in ((core, own_ref), (1 - core, other_ref)):
        span = part_of(part, half)
        mixed_ref[:, span] = (
            state_ref[:, span].astype(jnp.float32) + summed[...].astype(jnp.float32)
        ).astype(jnp.bfloat16)


def swap(values):
    return lax.ppermute(values, "section", [(0, 1), (1, 0)])


def swap_owner(values):
    owners = lax.axis_size("expert")
    return lax.ppermute(values, "expert", [(i, i ^ 1) for i in range(owners)])


def exchange(values, offset):
    owners = lax.axis_size("expert")
    return lax.ppermute(values, "expert", [(i, i ^ (2 * offset)) for i in range(owners)])


def after_kernel(*refs):
    pass


def after(value, *firsts):
    return pl.pallas_call(
        after_kernel,
        out_shape=jax.ShapeDtypeStruct(value.shape, value.dtype),
        in_specs=[pl.BlockSpec(memory_space=pl.ANY)] * (1 + len(firsts)),
        out_specs=pl.BlockSpec(memory_space=pl.ANY),
        input_output_aliases={0: 0},
        compiler_params=pltpu.CompilerParams(vmem_limit_bytes=2**20),
        name="after",
    )(value, *firsts)


def attend(
    core, decoder_states, memory_keys, memory_values, source_lengths, target_lengths, routes,
    attn_gain, ffn_gain, router,
):
    full_len, width = decoder_states.shape[1:]
    half = (full_len, width // 2)
    memory = memory_keys.shape[1:]
    other_keys, other_values = swap(memory_keys), swap(memory_values)
    own, query, rest = call(
        attend_own_kernel,
        "attend_own",
        [(half, jnp.bfloat16)] * 3,
        [core, source_lengths],
        [],
        [decoder_states, attn_gain[None], memory_keys, memory_values],
        scratch=[
            pltpu.VMEM((full_len, width), jnp.bfloat16),
            pltpu.VMEM((1, width), jnp.float32),
            pltpu.VMEM(memory, jnp.bfloat16),
            pltpu.VMEM(memory, jnp.bfloat16),
            pltpu.VMEM((full_len, width), jnp.bfloat16),
            pltpu.SemaphoreType.DMA((4,)),
        ],
    )
    return call(
        attend_other_kernel,
        "attend_other",
        [
            ((full_len, width), jnp.bfloat16),
            (half, jnp.bfloat16),
            (half, jnp.bfloat16),
            ((2, full_len), jnp.float32),
            (routes.shape, jnp.int32),
        ],
        [core, source_lengths],
        [own, query, rest, other_keys, other_values],
        [ffn_gain[None], router.T, routes, target_lengths],
        scratch=[
            pltpu.VMEM((1, width), jnp.float32),
            pltpu.VMEM(router.shape[::-1], jnp.bfloat16),
            pltpu.SMEM(target_lengths.shape, jnp.int32),
            pltpu.VMEM((full_len, width), jnp.bfloat16),
            pltpu.SemaphoreType.DMA((4,)),
        ],
    )


def line_experts(core, state, keep, send, gates, routes, fc_in, fc_out, capacity):
    full_len, width = state.shape
    half = width // 2
    count = lax.axis_size("expert") // 2
    line = (lax.axis_index("expert") // 2).astype(jnp.int32).reshape(1)
    other = swap(send)
    other_gates = swap(gates)
    piece = ((capacity, half), jnp.bfloat16)
    selected = call(
        select_kernel,
        "select",
        [piece] * count,
        [core, line],
        [routes, keep, other],
        scratch=[pltpu.VMEM((2 * full_len, half), jnp.bfloat16)],
    )
    near_in, near_out = call(
        load_kernel,
        "load",
        [(fc_in.shape, jnp.bfloat16), (fc_out.shape, jnp.bfloat16)],
        [],
        [],
        [fc_in, fc_out],
        scratch=[pltpu.SemaphoreType.DMA((2,))],
    )
    travelling = [exchange(selected[r], r) for r in range(1, count)]
    home = [None] * count
    ps, qs, kept, halves, wholes, boths = {}, {}, {}, {}, {}, {}
    for offset in [0, 1, 2, 3]:
        p = travelling[offset - 1] if offset else selected[0]
        if offset == 1:
            p = after(p, near_in)
        q = swap_owner(p)
        ps[offset], qs[offset] = p, q
    for offset in [0, 1, 2, 3]:
        p, q = ps[offset], qs[offset]
        if offset == 3:
            q = after(q, kept[2])
        p2, q2 = swap(p), swap(q)
        if offset == 2:
            q2 = after(q2, kept[0], kept[1])
        if offset == 3:
            q2 = after(q2, halves[2])
        kept[offset], sent = call(
            expert_kernel,
            "expert",
            [((2, capacity, half), jnp.float32), ((2, capacity, half), jnp.bfloat16)],
            [core],
            [p, q, p2, q2, near_in, near_out],
            scratch=[pltpu.VMEM((2 * capacity, width), jnp.bfloat16)],
            vmem_mib=16,
        )
        moving = swap(sent)
        both = kept[offset] + moving.astype(jnp.float32)
        halves[offset] = both[1].astype(jnp.bfloat16)
        boths[offset] = both
    for offset in [2, 3, 1, 0]:
        both, leaving = boths[offset], halves[offset]
        if offset == 1:
            leaving = after(leaving, halves[3])
        if offset == 0:
            leaving = after(leaving, wholes[3])
        across = swap_owner(leaving)
        wholes[offset] = (both[0] + across.astype(jnp.float32)).astype(jnp.bfloat16)
        home[offset] = exchange(wholes[offset], offset) if offset else wholes[offset]
    own_sum, other_sum = call(
        combine_kernel,
        "combine",
        [((full_len, half), jnp.float32), ((full_len, half), jnp.bfloat16)],
        [core, line],
        [routes, gates, other_gates, *home],
        scratch=[
            pltpu.VMEM((count * capacity, half), jnp.bfloat16),
            pltpu.VMEM((2, 2, full_len), jnp.float32),
            pltpu.VMEM((2, full_len, half), jnp.float32),
        ],
    )
    (mixed,) = call(
        finish_kernel,
        "finish",
        [((full_len, width), jnp.bfloat16)],
        [core],
        [state, own_sum, swap(other_sum)],
    )
    return mixed


def expert_apply(slot_rows, fc_in, fc_out):
    width = slot_rows.shape[-1]
    flat_rows = slot_rows.reshape(-1, width)
    hidden = jax.nn.relu(jnp.dot(flat_rows, fc_in, preferred_element_type=jnp.float32)).astype(
        jnp.bfloat16
    )
    produced = jnp.dot(hidden, fc_out, preferred_element_type=jnp.float32)
    return produced.reshape(slot_rows.shape[0], slot_rows.shape[1], width)


def sparse_experts(normed, target_lengths, routes, router, fc_in, fc_out, capacity):
    full_len, width = normed.shape
    all_normed = lax.all_gather(normed[None], "section", axis=0, tiled=True)
    block_sents = all_normed.shape[0]
    block_rows = block_sents * full_len
    tok_rows = all_normed.reshape(block_rows, width)
    owners = lax.axis_size("expert")
    experts_count = owners // 2
    chosen_ids = routes.reshape(block_rows, 2)
    logits = jnp.dot(tok_rows, router, preferred_element_type=jnp.float32)
    onehot = chosen_ids[:, :, None] == jnp.arange(experts_count, dtype=jnp.int32)
    chosen = jnp.sum(jnp.where(onehot, logits[:, None, :], 0.0), axis=-1)
    first = jax.nn.sigmoid(chosen[:, 0] - chosen[:, 1])
    gates = jnp.stack([first, 1.0 - first], axis=-1)
    live = (jnp.arange(full_len, dtype=jnp.int32)[None, :] < target_lengths[:, None]).reshape(
        block_rows
    )
    flags = onehot.reshape(block_rows * 2, experts_count).astype(jnp.int32)
    earlier = jnp.cumsum(flags, axis=0) - flags
    slot = jnp.sum(flags * earlier, axis=-1).reshape(block_rows, 2)
    position = chosen_ids * capacity + slot
    dump_index = experts_count * capacity
    target = jnp.where(live[:, None], position, dump_index)
    row_ids = jnp.broadcast_to(jnp.arange(block_rows, dtype=jnp.int32)[:, None], (block_rows, 2))
    table = (
        jnp.full((dump_index + 1,), block_rows, jnp.int32)
        .at[target.reshape(-1)]
        .set(row_ids.reshape(-1))[:dump_index]
    )
    padded = jnp.concatenate([tok_rows, jnp.zeros((1, width), jnp.bfloat16)], axis=0)
    slot_buffer = padded[table].reshape(experts_count, capacity, width)
    outgoing = jnp.repeat(slot_buffer, 2, axis=0)
    returned = lax.all_to_all(
        expert_apply(
            lax.all_to_all(outgoing, "expert", split_axis=0, concat_axis=0, tiled=True),
            fc_in,
            fc_out,
        ).astype(jnp.bfloat16),
        "expert",
        split_axis=0,
        concat_axis=0,
        tiled=True,
    ).astype(jnp.float32)
    partial_value = jnp.sum(returned.reshape(experts_count, 2, capacity, width), axis=1)
    fetched = partial_value.reshape(dump_index, width)[jnp.where(live[:, None], position, 0)]
    weight = gates * live[:, None].astype(jnp.float32)
    contrib = jnp.sum(weight[:, :, None] * fetched, axis=1).reshape(block_sents, full_len, width)
    summed = lax.psum_scatter(contrib, "section", scatter_dimension=0, tiled=True)
    return summed[0]


def local(
    decoder_states,
    memory_keys,
    memory_values,
    source_lengths,
    target_lengths,
    routes,
    attn_gain,
    ffn_gain,
    router,
    fc_in,
    fc_out,
):
    core = lax.axis_index("section").astype(jnp.int32).reshape(1)
    by_choice = jnp.transpose(routes, (0, 2, 1))
    state, keep, send, gates, by_choice = attend(
        core, decoder_states, memory_keys, memory_values, source_lengths, target_lengths, by_choice,
        attn_gain, ffn_gain, router,
    )
    block_rows = routes.shape[0] * routes.shape[1]
    experts_count = router.shape[1]
    capacity = 2 * max(1, 3 * block_rows // (2 * experts_count))
    if capacity % 16 == 0 and experts_count & (experts_count - 1) == 0:
        mixed = line_experts(core, state, keep, send, gates, by_choice, fc_in, fc_out, capacity)
    else:
        halves = jnp.stack([keep, send])
        normed = jnp.concatenate([halves[core[0]], halves[1 - core[0]]], axis=-1)
        summed = sparse_experts(normed, target_lengths, routes, router, fc_in, fc_out, capacity)
        mixed = (state.astype(jnp.float32) + summed).astype(jnp.bfloat16)
    return mixed[None]


def solution(mesh):
    placed = (
        P(("groups", "expert", "section"), None, None),
        P(("groups", "expert"), None, "section"),
        P(("groups", "expert"), None, "section"),
        P(("groups", "expert", "section")),
        P(("groups", "expert")),
        P(("groups", "expert"), None, None),
        P(),
        P(),
        P(),
        P(None, ("expert", "section")),
        P(("expert", "section"), None),
    )
    return jax.shard_map(
        local,
        mesh=mesh,
        in_specs=placed,
        out_specs=P(("groups", "expert", "section"), None, None),
        check_vma=False,
    )
```

```python
import functools

import jax
import jax.numpy as jnp
from jax import lax
from jax.experimental import pallas as pl
from jax.experimental.pallas import tpu as pltpu
from jax.sharding import PartitionSpec as P

HEAD_DIM = 128


def layer_norm(values, gain):
    centered = values - jnp.mean(values, axis=-1, keepdims=True)
    spread = jnp.mean(centered * centered, axis=-1, keepdims=True)
    return (centered * lax.rsqrt(spread + 1e-05) * gain).astype(jnp.bfloat16)


VMEM = pl.BlockSpec(memory_space=pltpu.VMEM)
SMEM = pl.BlockSpec(memory_space=pltpu.SMEM)
HBM = pl.BlockSpec(memory_space=pltpu.HBM)


def call(kernel, name, outs, scalars, arrays, far=(), scratch=(), vmem_mib=12):
    return pl.pallas_call(
        kernel,
        out_shape=tuple(jax.ShapeDtypeStruct(*out) for out in outs),
        in_specs=[SMEM] * len(scalars) + [VMEM] * len(arrays) + [HBM] * len(far),
        out_specs=(VMEM,) * len(outs),
        scratch_shapes=list(scratch),
        compiler_params=pltpu.CompilerParams(vmem_limit_bytes=vmem_mib * 2**20),
        name=name,
    )(*scalars, *arrays, *(pltpu.with_memory_space_constraint(a, pltpu.HBM) for a in far))


def fetch(sems, *pairs):
    copies = [
        pltpu.make_async_copy(source, target, sems.at[i]) for i, (source, target) in enumerate(pairs)
    ]
    for copy in copies:
        copy.start()
    return copies


def part_of(part, half):
    return pl.ds(pl.multiple_of(part * half, half), half)


def attend_half(queries, keys, values, length):
    rows = queries.shape[0]
    heads = [slice(at, at + HEAD_DIM) for at in range(0, queries.shape[1], HEAD_DIM)]
    scores = jnp.concatenate(
        [
            lax.dot_general(
                queries[:, head],
                keys[:, head],
                (((1,), (1,)), ((), ())),
                preferred_element_type=jnp.float32,
            )
            for head in heads
        ],
        axis=0,
    ) * HEAD_DIM ** (-0.5)
    valid = lax.broadcasted_iota(jnp.int32, (1, keys.shape[0]), 1) < length
    scores = jnp.where(valid, scores, -jnp.inf)
    expon = jnp.exp(scores - jnp.max(scores, axis=-1, keepdims=True))
    weights = (expon / jnp.sum(expon, axis=-1, keepdims=True)).astype(jnp.bfloat16)
    return jnp.concatenate(
        [
            jnp.dot(
                weights[i * rows : (i + 1) * rows],
                values[:, head],
                preferred_element_type=jnp.float32,
            )
            for i, head in enumerate(heads)
        ],
        axis=1,
    )


def add_rounded(x, attended):
    return (x.astype(jnp.float32) + attended).astype(jnp.bfloat16)


def attend_own_kernel(
    core_ref,
    source_ref,
    x_in,
    gain_in,
    keys_in,
    values_in,
    state_ref,
    query_ref,
    rest_ref,
    x_ref,
    gain_ref,
    keys_ref,
    values_ref,
    scratch_ref,
    sems,
):
    core = core_ref[0]
    copies = fetch(
        sems,
        (x_in.at[0], x_ref),
        (gain_in, gain_ref),
        (keys_in.at[core], keys_ref),
        (values_in.at[core], values_ref),
    )
    half = keys_ref.shape[1]
    copies[0].wait()
    copies[1].wait()
    scratch_ref[...] = layer_norm(x_ref[...].astype(jnp.float32), gain_ref[...])
    own, other = part_of(core, half), part_of(1 - core, half)
    query_ref[...] = scratch_ref[:, other]
    rest_ref[...] = x_ref[:, other]
    copies[2].wait()
    copies[3].wait()
    attended = attend_half(scratch_ref[:, own], keys_ref[...], values_ref[...], source_ref[0])
    state_ref[...] = add_rounded(x_ref[:, own], attended)


def attend_other_kernel(
    core_ref,
    source_ref,
    own_ref,
    query_ref,
    rest_ref,
    keys_ref,
    values_ref,
    gain_in,
    router_in,
    routes_in,
    target_in,
    state_ref,
    keep_ref,
    send_ref,
    gates_ref,
    routes_ref,
    gain_ref,
    router_ref,
    target_ref,
    scratch_ref,
    sems,
):
    core = core_ref[0]
    copies = fetch(
        sems,
        (gain_in, gain_ref),
        (router_in, router_ref),
        (routes_in, routes_ref),
        (target_in, target_ref),
    )
    full_len, half = own_ref.shape
    own, other = part_of(core, half), part_of(1 - core, half)
    attended = attend_half(query_ref[...], keys_ref[core], values_ref[core], source_ref[0])
    state_ref[:, own] = own_ref[...]
    state_ref[:, other] = add_rounded(rest_ref[...], attended)
    copies[0].wait()
    scratch_ref[...] = layer_norm(state_ref[...].astype(jnp.float32), gain_ref[...])
    keep_ref[...] = scratch_ref[:, own]
    send_ref[...] = scratch_ref[:, other]
    for copy in copies[1:]:
        copy.wait()
    logits = lax.dot_general(
        router_ref[...],
        scratch_ref[...],
        (((1,), (1,)), ((), ())),
        preferred_element_type=jnp.float32,
    )
    names = lax.broadcasted_iota(jnp.int32, logits.shape, 0)
    routes = routes_ref[core]
    chosen = [
        jnp.sum(jnp.where(names == routes[k : k + 1], logits, 0.0), axis=0, keepdims=True)
        for k in range(2)
    ]
    first = jax.nn.sigmoid(chosen[0] - chosen[1])
    live = lax.broadcasted_iota(jnp.int32, (1, full_len), 1) < target_ref[core]
    gates_ref[0:1] = jnp.where(live, first, 0.0)
    gates_ref[1:2] = jnp.where(live, 1.0 - first, 0.0)


def slots_of(routes_ref, experts_count):
    sents, _, full_len = routes_ref.shape
    rows = sents * full_len
    ids = lax.broadcasted_iota(jnp.int32, (max(8, experts_count), full_len), 0)
    named = jnp.concatenate(
        [
            jnp.where((ids == routes_ref[s, 0:1]) | (ids == routes_ref[s, 1:2]), 1.0, 0.0)
            for s in range(sents)
        ],
        axis=1,
    )
    before = lax.broadcasted_iota(jnp.int32, (rows, rows), 0) < lax.broadcasted_iota(
        jnp.int32, (rows, rows), 1
    )
    earlier = jnp.dot(
        named.astype(jnp.bfloat16),
        jnp.where(before, 1.0, 0.0).astype(jnp.bfloat16),
        preferred_element_type=jnp.float32,
    )
    return named > 0.0, earlier


def select_kernel(core_ref, line_ref, routes_ref, own_ref, other_ref, *rest):
    pieces, (slots_ref, block_ref) = rest[:-2], rest[-2:]
    experts_count = len(pieces)
    full_len = own_ref.shape[0]
    capacity = pieces[0].shape[0]
    core = core_ref[0]
    block_ref[part_of(core, full_len)] = own_ref[...]
    block_ref[part_of(1 - core, full_len)] = other_ref[...]
    named, earlier = slots_of(routes_ref, experts_count)
    slots_ref[...] = earlier
    slot = jnp.where(named, earlier, -1.0)
    ids = lax.broadcasted_iota(jnp.int32, slot.shape, 0)
    numbers = lax.broadcasted_iota(jnp.int32, (capacity, slot.shape[1]), 0).astype(jnp.float32)
    for offset, piece_ref in enumerate(pieces):
        expert = line_ref[0] ^ offset
        wanted = jnp.sum(jnp.where(ids == expert, slot, 0.0), axis=0, keepdims=True)
        picks = jnp.where(numbers == wanted, 1.0, 0.0).astype(jnp.bfloat16)
        piece_ref[...] = jnp.dot(
            picks, block_ref[...], preferred_element_type=jnp.float32
        ).astype(jnp.bfloat16)


def expert_kernel(
    core_ref, p_ref, q_ref, p2_ref, q2_ref, in_ref, out_ref, keep_ref, send_ref, rows_ref
):
    core = core_ref[0]
    capacity, half = p_ref.shape
    rows_ref[:capacity, part_of(core, half)] = p_ref[...]
    rows_ref[capacity:, part_of(core, half)] = q_ref[...]
    rows_ref[:capacity, part_of(1 - core, half)] = p2_ref[...]
    rows_ref[capacity:, part_of(1 - core, half)] = q2_ref[...]
    hidden = jnp.dot(rows_ref[...], in_ref[...], preferred_element_type=jnp.float32)
    hidden = jnp.maximum(hidden, 0.0).astype(jnp.bfloat16)
    send = jnp.dot(
        hidden, out_ref[:, part_of(1 - core, half)], preferred_element_type=jnp.float32
    ).astype(jnp.bfloat16)
    send_ref[0] = send[:capacity]
    send_ref[1] = send[capacity:]
    keep = jnp.dot(hidden, out_ref[:, part_of(core, half)], preferred_element_type=jnp.float32)
    keep_ref[0] = keep[:capacity]
    keep_ref[1] = keep[capacity:]


def load_kernel(in_in, out_in, in_ref, out_ref, sems):
    for copy in fetch(sems, (in_in, in_ref), (out_in, out_ref)):
        copy.wait()


def gated_sum(sent, line, routes, gates, slots_ref, rows):
    full_len = routes.shape[1]
    experts_count = slots_ref.shape[0]
    parts = [slots_ref[:, at : at + full_len] for at in range(0, slots_ref.shape[1], full_len)]
    slots = jnp.where(sent == 0, parts[0], parts[1])
    ids = lax.broadcasted_iota(jnp.int32, (experts_count, full_len), 0)
    numbers = lax.broadcasted_iota(jnp.int32, (full_len, rows.shape[0]), 1).astype(jnp.float32)
    capacity = rows.shape[0] // (lax.axis_size("expert") // 2)
    total = None
    for k in range(2):
        route = routes[k : k + 1]
        slot = jnp.sum(jnp.where(ids == route, slots, 0.0), axis=0, keepdims=True)
        place = (route ^ line).astype(jnp.float32) * capacity + slot
        place, gate = (
            jnp.broadcast_to(row, (full_len, full_len)).T[:, :1]
            for row in (place, gates[k : k + 1])
        )
        picks = jnp.where(numbers == place, 1.0, 0.0).astype(jnp.bfloat16)
        term = gate * jnp.dot(picks, rows, preferred_element_type=jnp.float32)
        total = term if total is None else total + term
    return total


def combine_other_kernel(core_ref, line_ref, routes_ref, gates_ref, slots_ref, *rest):
    pieces, (other_ref, rows_ref) = rest[:-2], rest[-2:]
    capacity = pieces[0].shape[0]
    for offset, piece_ref in enumerate(pieces):
        rows_ref[offset * capacity : (offset + 1) * capacity] = piece_ref[...]
    sent = 1 - core_ref[0]
    other_ref[...] = gated_sum(
        sent, line_ref[0], routes_ref[sent], gates_ref[...], slots_ref, rows_ref[...]
    ).astype(jnp.bfloat16)


def combine_own_kernel(
    core_ref, line_ref, routes_ref, gates_ref, slots_ref, rows_ref, state_ref, own_ref
):
    core = core_ref[0]
    summed = gated_sum(
        core, line_ref[0], routes_ref[core], gates_ref[...], slots_ref, rows_ref[...]
    )
    own_ref[...] = add_rounded(state_ref[:, part_of(core, own_ref.shape[1])], summed)


def finish_kernel(core_ref, state_ref, own_ref, other_ref, mixed_ref):
    core = core_ref[0]
    half = own_ref.shape[-1]
    mixed_ref[:, part_of(core, half)] = own_ref[...]
    span = part_of(1 - core, half)
    mixed_ref[:, span] = add_rounded(state_ref[:, span], other_ref[...].astype(jnp.float32))


def swap(values):
    return lax.ppermute(values, "section", [(0, 1), (1, 0)])


def swap_owner(values):
    owners = lax.axis_size("expert")
    return lax.ppermute(values, "expert", [(i, i ^ 1) for i in range(owners)])


def exchange(values, offset):
    owners = lax.axis_size("expert")
    return lax.ppermute(values, "expert", [(i, i ^ (2 * offset)) for i in range(owners)])


def after_kernel(*refs):
    pass


def after(value, *firsts):
    return pl.pallas_call(
        after_kernel,
        out_shape=jax.ShapeDtypeStruct(value.shape, value.dtype),
        in_specs=[pl.BlockSpec(memory_space=pl.ANY)] * (1 + len(firsts)),
        out_specs=pl.BlockSpec(memory_space=pl.ANY),
        input_output_aliases={0: 0},
        compiler_params=pltpu.CompilerParams(vmem_limit_bytes=2**20),
        name="after",
    )(value, *firsts)


def attend(
    core, decoder_states, memory_keys, memory_values, source_lengths, target_lengths, routes,
    attn_gain, ffn_gain, router,
):
    full_len, width = decoder_states.shape[1:]
    half = (full_len, width // 2)
    memory = memory_keys.shape[1:]
    other_keys, other_values = swap(memory_keys), swap(memory_values)
    own, query, rest = call(
        attend_own_kernel,
        "attend_own",
        [(half, jnp.bfloat16)] * 3,
        [core, source_lengths],
        [],
        [decoder_states, attn_gain[None], memory_keys, memory_values],
        scratch=[
            pltpu.VMEM((full_len, width), jnp.bfloat16),
            pltpu.VMEM((1, width), jnp.float32),
            pltpu.VMEM(memory, jnp.bfloat16),
            pltpu.VMEM(memory, jnp.bfloat16),
            pltpu.VMEM((full_len, width), jnp.bfloat16),
            pltpu.SemaphoreType.DMA((4,)),
        ],
    )
    return call(
        attend_other_kernel,
        "attend_other",
        [
            ((full_len, width), jnp.bfloat16),
            (half, jnp.bfloat16),
            (half, jnp.bfloat16),
            ((2, full_len), jnp.float32),
            (routes.shape, jnp.int32),
        ],
        [core, source_lengths],
        [own, query, rest, other_keys, other_values],
        [ffn_gain[None], router.T, routes, target_lengths],
        scratch=[
            pltpu.VMEM((1, width), jnp.float32),
            pltpu.VMEM(router.shape[::-1], jnp.bfloat16),
            pltpu.SMEM(target_lengths.shape, jnp.int32),
            pltpu.VMEM((full_len, width), jnp.bfloat16),
            pltpu.SemaphoreType.DMA((4,)),
        ],
    )


def line_experts(core, state, keep, send, gates, routes, fc_in, fc_out, capacity):
    full_len, width = state.shape
    half = width // 2
    count = lax.axis_size("expert") // 2
    line = (lax.axis_index("expert") // 2).astype(jnp.int32).reshape(1)
    other = swap(send)
    other_gates = swap(gates)
    piece = ((capacity, half), jnp.bfloat16)
    *selected, slots = call(
        select_kernel,
        "select",
        [piece] * count + [((max(8, count), 2 * full_len), jnp.float32)],
        [core, line],
        [routes, keep, other],
        scratch=[pltpu.VMEM((2 * full_len, half), jnp.bfloat16)],
    )
    near_in, near_out = call(
        load_kernel,
        "load",
        [(fc_in.shape, jnp.bfloat16), (fc_out.shape, jnp.bfloat16)],
        [],
        [],
        [fc_in, fc_out],
        scratch=[pltpu.SemaphoreType.DMA((2,))],
    )
    def run(p, q, p2, q2):
        keep, sent = call(
            expert_kernel,
            "expert",
            [((2, capacity, half), jnp.float32), ((2, capacity, half), jnp.bfloat16)],
            [core],
            [p, q, p2, q2, near_in, near_out],
            scratch=[pltpu.VMEM((2 * capacity, width), jnp.bfloat16)],
            vmem_mib=16,
        )
        return keep, swap(sent)

    def sums(keep, moving):
        both = keep + moving.astype(jnp.float32)
        return both, both[1].astype(jnp.bfloat16)

    def whole(both, across):
        return (both[0] + across.astype(jnp.float32)).astype(jnp.bfloat16)

    travelling = [exchange(selected[r], r) for r in range(1, count)]
    home = [None] * count
    ps, qs, kept, halves, wholes, boths = {}, {}, {}, {}, {}, {}
    p = selected[0]
    q = swap_owner(p)
    ps[0], qs[0] = p, q
    p = travelling[0]
    p = after(p, near_in)
    q = swap_owner(p)
    ps[1], qs[1] = p, q
    p = travelling[1]
    q = swap_owner(p)
    ps[2], qs[2] = p, q
    p = travelling[2]
    q = swap_owner(p)
    ps[3], qs[3] = p, q
    p, q = ps[0], qs[0]
    p2, q2 = swap(p), swap(q)
    kept[0], moving = run(p, q, p2, q2)
    boths[0], halves[0] = sums(kept[0], moving)
    p, q = ps[2], qs[2]
    p2, q2 = swap(p), swap(q)
    kept[2], moving = run(p, q, p2, q2)
    boths[2], halves[2] = sums(kept[2], moving)
    p, q = ps[1], qs[1]
    p2, q2 = swap(p), swap(q)
    q2 = after(q2, kept[0], kept[2])
    kept[1], moving = run(p, q, p2, q2)
    boths[1], halves[1] = sums(kept[1], moving)
    p, q = ps[3], qs[3]
    q = after(q, kept[2])
    p2, q2 = swap(p), swap(q)
    q2 = after(q2, halves[2], kept[1])
    kept[3], moving = run(p, q, p2, q2)
    boths[3], halves[3] = sums(kept[3], moving)
    leaving = halves[2]
    across = swap_owner(leaving)
    wholes[2] = whole(boths[2], across)
    home[2] = exchange(wholes[2], 2)
    leaving = halves[3]
    across = swap_owner(leaving)
    wholes[3] = whole(boths[3], across)
    home[3] = exchange(wholes[3], 3)
    leaving = halves[1]
    leaving = after(leaving, halves[3])
    across = swap_owner(leaving)
    wholes[1] = whole(boths[1], across)
    home[1] = exchange(wholes[1], 1)
    leaving = halves[0]
    leaving = after(leaving, wholes[3])
    across = swap_owner(leaving)
    wholes[0] = whole(boths[0], across)
    home[0] = wholes[0]
    leaving, rows = call(
        combine_other_kernel,
        "combine_other",
        [((full_len, half), jnp.bfloat16), ((count * capacity, half), jnp.bfloat16)],
        [core, line],
        [routes, other_gates, slots, *home],
    )
    arriving = swap(leaving)
    (own,) = call(
        combine_own_kernel,
        "combine_own",
        [((full_len, half), jnp.bfloat16)],
        [core, line],
        [routes, gates, slots, rows, state],
    )
    (mixed,) = call(
        finish_kernel,
        "finish",
        [((full_len, width), jnp.bfloat16)],
        [core],
        [state, own, arriving],
    )
    return mixed


def expert_apply(slot_rows, fc_in, fc_out):
    width = slot_rows.shape[-1]
    flat_rows = slot_rows.reshape(-1, width)
    hidden = jax.nn.relu(jnp.dot(flat_rows, fc_in, preferred_element_type=jnp.float32)).astype(
        jnp.bfloat16
    )
    produced = jnp.dot(hidden, fc_out, preferred_element_type=jnp.float32)
    return produced.reshape(slot_rows.shape[0], slot_rows.shape[1], width)


def sparse_experts(normed, target_lengths, routes, router, fc_in, fc_out, capacity):
    full_len, width = normed.shape
    all_normed = lax.all_gather(normed[None], "section", axis=0, tiled=True)
    block_sents = all_normed.shape[0]
    block_rows = block_sents * full_len
    tok_rows = all_normed.reshape(block_rows, width)
    owners = lax.axis_size("expert")
    experts_count = owners // 2
    chosen_ids = routes.reshape(block_rows, 2)
    logits = jnp.dot(tok_rows, router, preferred_element_type=jnp.float32)
    onehot = chosen_ids[:, :, None] == jnp.arange(experts_count, dtype=jnp.int32)
    chosen = jnp.sum(jnp.where(onehot, logits[:, None, :], 0.0), axis=-1)
    first = jax.nn.sigmoid(chosen[:, 0] - chosen[:, 1])
    gates = jnp.stack([first, 1.0 - first], axis=-1)
    live = (jnp.arange(full_len, dtype=jnp.int32)[None, :] < target_lengths[:, None]).reshape(
        block_rows
    )
    flags = onehot.reshape(block_rows * 2, experts_count).astype(jnp.int32)
    earlier = jnp.cumsum(flags, axis=0) - flags
    slot = jnp.sum(flags * earlier, axis=-1).reshape(block_rows, 2)
    position = chosen_ids * capacity + slot
    dump_index = experts_count * capacity
    target = jnp.where(live[:, None], position, dump_index)
    row_ids = jnp.broadcast_to(jnp.arange(block_rows, dtype=jnp.int32)[:, None], (block_rows, 2))
    table = (
        jnp.full((dump_index + 1,), block_rows, jnp.int32)
        .at[target.reshape(-1)]
        .set(row_ids.reshape(-1))[:dump_index]
    )
    padded = jnp.concatenate([tok_rows, jnp.zeros((1, width), jnp.bfloat16)], axis=0)
    slot_buffer = padded[table].reshape(experts_count, capacity, width)
    outgoing = jnp.repeat(slot_buffer, 2, axis=0)
    returned = lax.all_to_all(
        expert_apply(
            lax.all_to_all(outgoing, "expert", split_axis=0, concat_axis=0, tiled=True),
            fc_in,
            fc_out,
        ).astype(jnp.bfloat16),
        "expert",
        split_axis=0,
        concat_axis=0,
        tiled=True,
    ).astype(jnp.float32)
    partial_value = jnp.sum(returned.reshape(experts_count, 2, capacity, width), axis=1)
    fetched = partial_value.reshape(dump_index, width)[jnp.where(live[:, None], position, 0)]
    weight = gates * live[:, None].astype(jnp.float32)
    contrib = jnp.sum(weight[:, :, None] * fetched, axis=1).reshape(block_sents, full_len, width)
    summed = lax.psum_scatter(contrib, "section", scatter_dimension=0, tiled=True)
    return summed[0]


def local(
    decoder_states,
    memory_keys,
    memory_values,
    source_lengths,
    target_lengths,
    routes,
    attn_gain,
    ffn_gain,
    router,
    fc_in,
    fc_out,
):
    core = lax.axis_index("section").astype(jnp.int32).reshape(1)
    by_choice = jnp.transpose(routes, (0, 2, 1))
    state, keep, send, gates, by_choice = attend(
        core, decoder_states, memory_keys, memory_values, source_lengths, target_lengths, by_choice,
        attn_gain, ffn_gain, router,
    )
    block_rows = routes.shape[0] * routes.shape[1]
    experts_count = router.shape[1]
    capacity = 2 * max(1, 3 * block_rows // (2 * experts_count))
    if capacity % 16 == 0 and experts_count & (experts_count - 1) == 0:
        mixed = line_experts(core, state, keep, send, gates, by_choice, fc_in, fc_out, capacity)
    else:
        halves = jnp.stack([keep, send])
        normed = jnp.concatenate([halves[core[0]], halves[1 - core[0]]], axis=-1)
        summed = sparse_experts(normed, target_lengths, routes, router, fc_in, fc_out, capacity)
        mixed = (state.astype(jnp.float32) + summed).astype(jnp.bfloat16)
    return mixed[None]


def solution(mesh):
    placed = (
        P(("groups", "expert", "section"), None, None),
        P(("groups", "expert"), None, "section"),
        P(("groups", "expert"), None, "section"),
        P(("groups", "expert", "section")),
        P(("groups", "expert")),
        P(("groups", "expert"), None, None),
        P(),
        P(),
        P(),
        P(None, ("expert", "section")),
        P(("expert", "section"), None),
    )
    return jax.shard_map(
        local,
        mesh=mesh,
        in_specs=placed,
        out_specs=P(("groups", "expert", "section"), None, None),
        check_vma=False,
    )
```

```python
import functools

import jax
import jax.numpy as jnp
from jax import lax
from jax.experimental import pallas as pl
from jax.experimental.pallas import tpu as pltpu
from jax.sharding import PartitionSpec as P

HEAD_DIM = 128


def layer_norm(values, gain):
    centered = values - jnp.mean(values, axis=-1, keepdims=True)
    spread = jnp.mean(centered * centered, axis=-1, keepdims=True)
    return (centered * lax.rsqrt(spread + 1e-05) * gain).astype(jnp.bfloat16)


VMEM = pl.BlockSpec(memory_space=pltpu.VMEM)
SMEM = pl.BlockSpec(memory_space=pltpu.SMEM)
HBM = pl.BlockSpec(memory_space=pltpu.HBM)


def call(kernel, name, outs, scalars, arrays, far=(), scratch=(), vmem_mib=12):
    return pl.pallas_call(
        kernel,
        out_shape=tuple(jax.ShapeDtypeStruct(*out) for out in outs),
        in_specs=[SMEM] * len(scalars) + [VMEM] * len(arrays) + [HBM] * len(far),
        out_specs=(VMEM,) * len(outs),
        scratch_shapes=list(scratch),
        compiler_params=pltpu.CompilerParams(vmem_limit_bytes=vmem_mib * 2**20),
        name=name,
    )(*scalars, *arrays, *(pltpu.with_memory_space_constraint(a, pltpu.HBM) for a in far))


def fetch(sems, *pairs):
    copies = [
        pltpu.make_async_copy(source, target, sems.at[i]) for i, (source, target) in enumerate(pairs)
    ]
    for copy in copies:
        copy.start()
    return copies


def part_of(part, half):
    return pl.ds(pl.multiple_of(part * half, half), half)


def attend_half(queries, keys, values, length):
    rows = queries.shape[0]
    heads = [slice(at, at + HEAD_DIM) for at in range(0, queries.shape[1], HEAD_DIM)]
    scores = jnp.concatenate(
        [
            lax.dot_general(
                queries[:, head],
                keys[:, head],
                (((1,), (1,)), ((), ())),
                preferred_element_type=jnp.float32,
            )
            for head in heads
        ],
        axis=0,
    ) * HEAD_DIM ** (-0.5)
    valid = lax.broadcasted_iota(jnp.int32, (1, keys.shape[0]), 1) < length
    scores = jnp.where(valid, scores, -jnp.inf)
    expon = jnp.exp(scores - jnp.max(scores, axis=-1, keepdims=True))
    weights = (expon / jnp.sum(expon, axis=-1, keepdims=True)).astype(jnp.bfloat16)
    return jnp.concatenate(
        [
            jnp.dot(
                weights[i * rows : (i + 1) * rows],
                values[:, head],
                preferred_element_type=jnp.float32,
            )
            for i, head in enumerate(heads)
        ],
        axis=1,
    )


def add_rounded(x, attended):
    return (x.astype(jnp.float32) + attended).astype(jnp.bfloat16)


def attend_own_kernel(
    core_ref,
    source_ref,
    x_in,
    gain_in,
    keys_in,
    values_in,
    state_ref,
    query_ref,
    rest_ref,
    x_ref,
    gain_ref,
    keys_ref,
    values_ref,
    scratch_ref,
    sems,
):
    core = core_ref[0]
    copies = fetch(
        sems,
        (x_in.at[0], x_ref),
        (gain_in, gain_ref),
        (keys_in.at[core], keys_ref),
        (values_in.at[core], values_ref),
    )
    half = keys_ref.shape[1]
    copies[0].wait()
    copies[1].wait()
    scratch_ref[...] = layer_norm(x_ref[...].astype(jnp.float32), gain_ref[...])
    own, other = part_of(core, half), part_of(1 - core, half)
    query_ref[...] = scratch_ref[:, other]
    rest_ref[...] = x_ref[:, other]
    copies[2].wait()
    copies[3].wait()
    attended = attend_half(scratch_ref[:, own], keys_ref[...], values_ref[...], source_ref[0])
    state_ref[...] = add_rounded(x_ref[:, own], attended)


def attend_other_kernel(
    core_ref,
    source_ref,
    own_ref,
    query_ref,
    rest_ref,
    keys_ref,
    values_ref,
    gain_in,
    router_in,
    routes_in,
    target_in,
    state_ref,
    keep_ref,
    send_ref,
    gates_ref,
    routes_ref,
    gain_ref,
    router_ref,
    target_ref,
    scratch_ref,
    sems,
):
    core = core_ref[0]
    copies = fetch(
        sems,
        (gain_in, gain_ref),
        (router_in, router_ref),
        (routes_in, routes_ref),
        (target_in, target_ref),
    )
    full_len, half = own_ref.shape
    own, other = part_of(core, half), part_of(1 - core, half)
    attended = attend_half(query_ref[...], keys_ref[core], values_ref[core], source_ref[0])
    state_ref[:, own] = own_ref[...]
    state_ref[:, other] = add_rounded(rest_ref[...], attended)
    copies[0].wait()
    scratch_ref[...] = layer_norm(state_ref[...].astype(jnp.float32), gain_ref[...])
    keep_ref[...] = scratch_ref[:, own]
    send_ref[...] = scratch_ref[:, other]
    for copy in copies[1:]:
        copy.wait()
    logits = lax.dot_general(
        router_ref[...],
        scratch_ref[...],
        (((1,), (1,)), ((), ())),
        preferred_element_type=jnp.float32,
    )
    names = lax.broadcasted_iota(jnp.int32, logits.shape, 0)
    routes = routes_ref[core]
    chosen = [
        jnp.sum(jnp.where(names == routes[k : k + 1], logits, 0.0), axis=0, keepdims=True)
        for k in range(2)
    ]
    first = jax.nn.sigmoid(chosen[0] - chosen[1])
    live = lax.broadcasted_iota(jnp.int32, (1, full_len), 1) < target_ref[core]
    gates_ref[0:1] = jnp.where(live, first, 0.0)
    gates_ref[1:2] = jnp.where(live, 1.0 - first, 0.0)


def slots_of(routes_ref, experts_count):
    sents, _, full_len = routes_ref.shape
    rows = sents * full_len
    ids = lax.broadcasted_iota(jnp.int32, (max(8, experts_count), full_len), 0)
    named = jnp.concatenate(
        [
            jnp.where((ids == routes_ref[s, 0:1]) | (ids == routes_ref[s, 1:2]), 1.0, 0.0)
            for s in range(sents)
        ],
        axis=1,
    )
    before = lax.broadcasted_iota(jnp.int32, (rows, rows), 0) < lax.broadcasted_iota(
        jnp.int32, (rows, rows), 1
    )
    earlier = jnp.dot(
        named.astype(jnp.bfloat16),
        jnp.where(before, 1.0, 0.0).astype(jnp.bfloat16),
        preferred_element_type=jnp.float32,
    )
    return named > 0.0, earlier


def select_kernel(core_ref, line_ref, routes_ref, own_ref, other_ref, *rest):
    pieces, (slots_ref, block_ref) = rest[:-2], rest[-2:]
    experts_count = len(pieces)
    full_len = own_ref.shape[0]
    capacity = pieces[0].shape[0]
    core = core_ref[0]
    block_ref[part_of(core, full_len)] = own_ref[...]
    block_ref[part_of(1 - core, full_len)] = other_ref[...]
    named, earlier = slots_of(routes_ref, experts_count)
    slots_ref[...] = earlier
    slot = jnp.where(named, earlier, -1.0)
    ids = lax.broadcasted_iota(jnp.int32, slot.shape, 0)
    numbers = lax.broadcasted_iota(jnp.int32, (capacity, slot.shape[1]), 0).astype(jnp.float32)
    for offset, piece_ref in enumerate(pieces):
        expert = line_ref[0] ^ offset
        wanted = jnp.sum(jnp.where(ids == expert, slot, 0.0), axis=0, keepdims=True)
        picks = jnp.where(numbers == wanted, 1.0, 0.0).astype(jnp.bfloat16)
        piece_ref[...] = jnp.dot(
            picks, block_ref[...], preferred_element_type=jnp.float32
        ).astype(jnp.bfloat16)


def pair_kernel(p_ref, q_ref, pair_ref):
    capacity = p_ref.shape[0]
    pair_ref[:capacity] = p_ref[...]
    pair_ref[capacity:] = q_ref[...]


def expert_kernel(core_ref, pair_ref, pair2_ref, in_ref, out_ref, keep_ref, send_ref, rows_ref):
    core = core_ref[0]
    half = pair_ref.shape[1]
    capacity = pair_ref.shape[0] // 2
    rows_ref[:, part_of(core, half)] = pair_ref[...]
    rows_ref[:, part_of(1 - core, half)] = pair2_ref[...]
    hidden = jnp.dot(rows_ref[...], in_ref[...], preferred_element_type=jnp.float32)
    hidden = jnp.maximum(hidden, 0.0).astype(jnp.bfloat16)
    send = jnp.dot(
        hidden, out_ref[:, part_of(1 - core, half)], preferred_element_type=jnp.float32
    ).astype(jnp.bfloat16)
    send_ref[0] = send[:capacity]
    send_ref[1] = send[capacity:]
    keep = jnp.dot(hidden, out_ref[:, part_of(core, half)], preferred_element_type=jnp.float32)
    keep_ref[0] = keep[:capacity]
    keep_ref[1] = keep[capacity:]


def load_kernel(in_in, out_in, in_ref, out_ref, sems):
    for copy in fetch(sems, (in_in, in_ref), (out_in, out_ref)):
        copy.wait()


def gated_sum(sent, line, routes, gates, slots_ref, rows):
    full_len = routes.shape[1]
    experts_count = slots_ref.shape[0]
    parts = [slots_ref[:, at : at + full_len] for at in range(0, slots_ref.shape[1], full_len)]
    slots = jnp.where(sent == 0, parts[0], parts[1])
    ids = lax.broadcasted_iota(jnp.int32, (experts_count, full_len), 0)
    numbers = lax.broadcasted_iota(jnp.int32, (full_len, rows.shape[0]), 1).astype(jnp.float32)
    capacity = rows.shape[0] // (lax.axis_size("expert") // 2)
    total = None
    for k in range(2):
        route = routes[k : k + 1]
        slot = jnp.sum(jnp.where(ids == route, slots, 0.0), axis=0, keepdims=True)
        place = (route ^ line).astype(jnp.float32) * capacity + slot
        place, gate = (
            jnp.broadcast_to(row, (full_len, full_len)).T[:, :1]
            for row in (place, gates[k : k + 1])
        )
        picks = jnp.where(numbers == place, 1.0, 0.0).astype(jnp.bfloat16)
        term = gate * jnp.dot(picks, rows, preferred_element_type=jnp.float32)
        total = term if total is None else total + term
    return total


def combine_other_kernel(core_ref, line_ref, routes_ref, gates_ref, slots_ref, *rest):
    pieces, (other_ref, rows_ref) = rest[:-2], rest[-2:]
    capacity = pieces[0].shape[0]
    for offset, piece_ref in enumerate(pieces):
        rows_ref[offset * capacity : (offset + 1) * capacity] = piece_ref[...]
    sent = 1 - core_ref[0]
    other_ref[...] = gated_sum(
        sent, line_ref[0], routes_ref[sent], gates_ref[...], slots_ref, rows_ref[...]
    ).astype(jnp.bfloat16)


def combine_own_kernel(
    core_ref, line_ref, routes_ref, gates_ref, slots_ref, rows_ref, state_ref, own_ref
):
    core = core_ref[0]
    summed = gated_sum(
        core, line_ref[0], routes_ref[core], gates_ref[...], slots_ref, rows_ref[...]
    )
    own_ref[...] = add_rounded(state_ref[:, part_of(core, own_ref.shape[1])], summed)


def finish_kernel(core_ref, state_ref, own_ref, other_ref, mixed_ref):
    core = core_ref[0]
    half = own_ref.shape[-1]
    mixed_ref[:, part_of(core, half)] = own_ref[...]
    span = part_of(1 - core, half)
    mixed_ref[:, span] = add_rounded(state_ref[:, span], other_ref[...].astype(jnp.float32))


def swap(values):
    return lax.ppermute(values, "section", [(0, 1), (1, 0)])


def swap_owner(values):
    owners = lax.axis_size("expert")
    return lax.ppermute(values, "expert", [(i, i ^ 1) for i in range(owners)])


def exchange(values, offset):
    owners = lax.axis_size("expert")
    return lax.ppermute(values, "expert", [(i, i ^ (2 * offset)) for i in range(owners)])


def after_kernel(*refs):
    pass


def after(value, *firsts):
    return pl.pallas_call(
        after_kernel,
        out_shape=jax.ShapeDtypeStruct(value.shape, value.dtype),
        in_specs=[pl.BlockSpec(memory_space=pl.ANY)] * (1 + len(firsts)),
        out_specs=pl.BlockSpec(memory_space=pl.ANY),
        input_output_aliases={0: 0},
        compiler_params=pltpu.CompilerParams(vmem_limit_bytes=2**20),
        name="after",
    )(value, *firsts)


def attend(
    core, decoder_states, memory_keys, memory_values, source_lengths, target_lengths, routes,
    attn_gain, ffn_gain, router,
):
    full_len, width = decoder_states.shape[1:]
    half = (full_len, width // 2)
    memory = memory_keys.shape[1:]
    other_keys, other_values = swap(memory_keys), swap(memory_values)
    own, query, rest = call(
        attend_own_kernel,
        "attend_own",
        [(half, jnp.bfloat16)] * 3,
        [core, source_lengths],
        [],
        [decoder_states, attn_gain[None], memory_keys, memory_values],
        scratch=[
            pltpu.VMEM((full_len, width), jnp.bfloat16),
            pltpu.VMEM((1, width), jnp.float32),
            pltpu.VMEM(memory, jnp.bfloat16),
            pltpu.VMEM(memory, jnp.bfloat16),
            pltpu.VMEM((full_len, width), jnp.bfloat16),
            pltpu.SemaphoreType.DMA((4,)),
        ],
    )
    return call(
        attend_other_kernel,
        "attend_other",
        [
            ((full_len, width), jnp.bfloat16),
            (half, jnp.bfloat16),
            (half, jnp.bfloat16),
            ((2, full_len), jnp.float32),
            (routes.shape, jnp.int32),
        ],
        [core, source_lengths],
        [own, query, rest, other_keys, other_values],
        [ffn_gain[None], router.T, routes, target_lengths],
        scratch=[
            pltpu.VMEM((1, width), jnp.float32),
            pltpu.VMEM(router.shape[::-1], jnp.bfloat16),
            pltpu.SMEM(target_lengths.shape, jnp.int32),
            pltpu.VMEM((full_len, width), jnp.bfloat16),
            pltpu.SemaphoreType.DMA((4,)),
        ],
    )


def line_experts(core, state, keep, send, gates, routes, fc_in, fc_out, capacity):
    full_len, width = state.shape
    half = width // 2
    count = lax.axis_size("expert") // 2
    line = (lax.axis_index("expert") // 2).astype(jnp.int32).reshape(1)
    other = swap(send)
    other_gates = swap(gates)
    piece = ((capacity, half), jnp.bfloat16)
    *selected, slots = call(
        select_kernel,
        "select",
        [piece] * count + [((max(8, count), 2 * full_len), jnp.float32)],
        [core, line],
        [routes, keep, other],
        scratch=[pltpu.VMEM((2 * full_len, half), jnp.bfloat16)],
    )
    near_in, near_out = call(
        load_kernel,
        "load",
        [(fc_in.shape, jnp.bfloat16), (fc_out.shape, jnp.bfloat16)],
        [],
        [],
        [fc_in, fc_out],
        scratch=[pltpu.SemaphoreType.DMA((2,))],
    )
    both_blocks = [((2 * capacity, half), jnp.bfloat16)]

    def run(own, other):
        keep, sent = call(
            expert_kernel,
            "expert",
            [((2, capacity, half), jnp.float32), ((2, capacity, half), jnp.bfloat16)],
            [core],
            [own, other, near_in, near_out],
            scratch=[pltpu.VMEM((2 * capacity, width), jnp.bfloat16)],
            vmem_mib=16,
        )
        return keep, swap(sent)

    def sums(keep, moving):
        both = keep + moving.astype(jnp.float32)
        return both, both[1].astype(jnp.bfloat16)

    def whole(both, across):
        return (both[0] + across.astype(jnp.float32)).astype(jnp.bfloat16)

    travelling = [exchange(selected[r], r) for r in range(1, count)]
    home = [None] * count
    ps, qs, kept, halves, wholes, boths = {}, {}, {}, {}, {}, {}
    p = selected[0]
    q = swap_owner(p)
    ps[0], qs[0] = p, q
    p = travelling[0]
    q = swap_owner(p)
    ps[1], qs[1] = p, q
    p = travelling[1]
    p = after(p, near_in)
    q = swap_owner(p)
    ps[2], qs[2] = p, q
    p = travelling[2]
    q = swap_owner(p)
    ps[3], qs[3] = p, q
    p, q = ps[0], qs[0]
    (own,) = call(pair_kernel, "pair", both_blocks, [], [p, q])
    q2 = swap(own)
    kept[0], moving = run(own, q2)
    boths[0], halves[0] = sums(kept[0], moving)
    p, q = ps[2], qs[2]
    q = after(q, kept[0])
    (own,) = call(pair_kernel, "pair", both_blocks, [], [p, q])
    q2 = swap(own)
    kept[2], moving = run(own, q2)
    boths[2], halves[2] = sums(kept[2], moving)
    p, q = ps[1], qs[1]
    q = after(q, travelling[2])
    (own,) = call(pair_kernel, "pair", both_blocks, [], [p, q])
    q2 = swap(own)
    q2 = after(q2, kept[2])
    kept[1], moving = run(own, q2)
    boths[1], halves[1] = sums(kept[1], moving)
    p, q = ps[3], qs[3]
    q = after(q, kept[2])
    (own,) = call(pair_kernel, "pair", both_blocks, [], [p, q])
    q2 = swap(own)
    q2 = after(q2, kept[1], halves[2])
    kept[3], moving = run(own, q2)
    boths[3], halves[3] = sums(kept[3], moving)
    leaving = halves[2]
    across = swap_owner(leaving)
    wholes[2] = whole(boths[2], across)
    home[2] = exchange(wholes[2], 2)
    leaving = halves[3]
    across = swap_owner(leaving)
    wholes[3] = whole(boths[3], across)
    home[3] = exchange(wholes[3], 3)
    leaving = halves[1]
    leaving = after(leaving, halves[3])
    across = swap_owner(leaving)
    wholes[1] = whole(boths[1], across)
    home[1] = exchange(wholes[1], 1)
    leaving = halves[0]
    leaving = after(leaving, wholes[3])
    across = swap_owner(leaving)
    wholes[0] = whole(boths[0], across)
    home[0] = wholes[0]
    leaving, rows = call(
        combine_other_kernel,
        "combine_other",
        [((full_len, half), jnp.bfloat16), ((count * capacity, half), jnp.bfloat16)],
        [core, line],
        [routes, other_gates, slots, *home],
    )
    arriving = swap(leaving)
    (own,) = call(
        combine_own_kernel,
        "combine_own",
        [((full_len, half), jnp.bfloat16)],
        [core, line],
        [routes, gates, slots, rows, state],
    )
    (mixed,) = call(
        finish_kernel,
        "finish",
        [((full_len, width), jnp.bfloat16)],
        [core],
        [state, own, arriving],
    )
    return mixed


def expert_apply(slot_rows, fc_in, fc_out):
    width = slot_rows.shape[-1]
    flat_rows = slot_rows.reshape(-1, width)
    hidden = jax.nn.relu(jnp.dot(flat_rows, fc_in, preferred_element_type=jnp.float32)).astype(
        jnp.bfloat16
    )
    produced = jnp.dot(hidden, fc_out, preferred_element_type=jnp.float32)
    return produced.reshape(slot_rows.shape[0], slot_rows.shape[1], width)


def sparse_experts(normed, target_lengths, routes, router, fc_in, fc_out, capacity):
    full_len, width = normed.shape
    all_normed = lax.all_gather(normed[None], "section", axis=0, tiled=True)
    block_sents = all_normed.shape[0]
    block_rows = block_sents * full_len
    tok_rows = all_normed.reshape(block_rows, width)
    owners = lax.axis_size("expert")
    experts_count = owners // 2
    chosen_ids = routes.reshape(block_rows, 2)
    logits = jnp.dot(tok_rows, router, preferred_element_type=jnp.float32)
    onehot = chosen_ids[:, :, None] == jnp.arange(experts_count, dtype=jnp.int32)
    chosen = jnp.sum(jnp.where(onehot, logits[:, None, :], 0.0), axis=-1)
    first = jax.nn.sigmoid(chosen[:, 0] - chosen[:, 1])
    gates = jnp.stack([first, 1.0 - first], axis=-1)
    live = (jnp.arange(full_len, dtype=jnp.int32)[None, :] < target_lengths[:, None]).reshape(
        block_rows
    )
    flags = onehot.reshape(block_rows * 2, experts_count).astype(jnp.int32)
    earlier = jnp.cumsum(flags, axis=0) - flags
    slot = jnp.sum(flags * earlier, axis=-1).reshape(block_rows, 2)
    position = chosen_ids * capacity + slot
    dump_index = experts_count * capacity
    target = jnp.where(live[:, None], position, dump_index)
    row_ids = jnp.broadcast_to(jnp.arange(block_rows, dtype=jnp.int32)[:, None], (block_rows, 2))
    table = (
        jnp.full((dump_index + 1,), block_rows, jnp.int32)
        .at[target.reshape(-1)]
        .set(row_ids.reshape(-1))[:dump_index]
    )
    padded = jnp.concatenate([tok_rows, jnp.zeros((1, width), jnp.bfloat16)], axis=0)
    slot_buffer = padded[table].reshape(experts_count, capacity, width)
    outgoing = jnp.repeat(slot_buffer, 2, axis=0)
    returned = lax.all_to_all(
        expert_apply(
            lax.all_to_all(outgoing, "expert", split_axis=0, concat_axis=0, tiled=True),
            fc_in,
            fc_out,
        ).astype(jnp.bfloat16),
        "expert",
        split_axis=0,
        concat_axis=0,
        tiled=True,
    ).astype(jnp.float32)
    partial_value = jnp.sum(returned.reshape(experts_count, 2, capacity, width), axis=1)
    fetched = partial_value.reshape(dump_index, width)[jnp.where(live[:, None], position, 0)]
    weight = gates * live[:, None].astype(jnp.float32)
    contrib = jnp.sum(weight[:, :, None] * fetched, axis=1).reshape(block_sents, full_len, width)
    summed = lax.psum_scatter(contrib, "section", scatter_dimension=0, tiled=True)
    return summed[0]


def local(
    decoder_states,
    memory_keys,
    memory_values,
    source_lengths,
    target_lengths,
    routes,
    attn_gain,
    ffn_gain,
    router,
    fc_in,
    fc_out,
):
    core = lax.axis_index("section").astype(jnp.int32).reshape(1)
    by_choice = jnp.transpose(routes, (0, 2, 1))
    state, keep, send, gates, by_choice = attend(
        core, decoder_states, memory_keys, memory_values, source_lengths, target_lengths, by_choice,
        attn_gain, ffn_gain, router,
    )
    block_rows = routes.shape[0] * routes.shape[1]
    experts_count = router.shape[1]
    capacity = 2 * max(1, 3 * block_rows // (2 * experts_count))
    if capacity % 16 == 0 and experts_count & (experts_count - 1) == 0:
        mixed = line_experts(core, state, keep, send, gates, by_choice, fc_in, fc_out, capacity)
    else:
        halves = jnp.stack([keep, send])
        normed = jnp.concatenate([halves[core[0]], halves[1 - core[0]]], axis=-1)
        summed = sparse_experts(normed, target_lengths, routes, router, fc_in, fc_out, capacity)
        mixed = (state.astype(jnp.float32) + summed).astype(jnp.bfloat16)
    return mixed[None]


def solution(mesh):
    placed = (
        P(("groups", "expert", "section"), None, None),
        P(("groups", "expert"), None, "section"),
        P(("groups", "expert"), None, "section"),
        P(("groups", "expert", "section")),
        P(("groups", "expert")),
        P(("groups", "expert"), None, None),
        P(),
        P(),
        P(),
        P(None, ("expert", "section")),
        P(("expert", "section"), None),
    )
    return jax.shard_map(
        local,
        mesh=mesh,
        in_specs=placed,
        out_specs=P(("groups", "expert", "section"), None, None),
        check_vma=False,
    )
```

```python
import functools

import jax
import jax.numpy as jnp
from jax import lax
from jax.experimental import pallas as pl
from jax.experimental.pallas import tpu as pltpu
from jax.sharding import PartitionSpec as P

HEAD_DIM = 128


def layer_norm(values, gain):
    centered = values - jnp.mean(values, axis=-1, keepdims=True)
    spread = jnp.mean(centered * centered, axis=-1, keepdims=True)
    return (centered * lax.rsqrt(spread + 1e-05) * gain).astype(jnp.bfloat16)


VMEM = pl.BlockSpec(memory_space=pltpu.VMEM)
SMEM = pl.BlockSpec(memory_space=pltpu.SMEM)
HBM = pl.BlockSpec(memory_space=pltpu.HBM)


def call(kernel, name, outs, scalars, arrays, far=(), scratch=(), vmem_mib=12):
    return pl.pallas_call(
        kernel,
        out_shape=tuple(jax.ShapeDtypeStruct(*out) for out in outs),
        in_specs=[SMEM] * len(scalars) + [VMEM] * len(arrays) + [HBM] * len(far),
        out_specs=(VMEM,) * len(outs),
        scratch_shapes=list(scratch),
        compiler_params=pltpu.CompilerParams(vmem_limit_bytes=vmem_mib * 2**20),
        name=name,
    )(*scalars, *arrays, *(pltpu.with_memory_space_constraint(a, pltpu.HBM) for a in far))


def fetch(sems, *pairs):
    copies = [
        pltpu.make_async_copy(source, target, sems.at[i]) for i, (source, target) in enumerate(pairs)
    ]
    for copy in copies:
        copy.start()
    return copies


def part_of(part, half):
    return pl.ds(pl.multiple_of(part * half, half), half)


def attend_half(queries, keys, values, length):
    rows = queries.shape[0]
    heads = [slice(at, at + HEAD_DIM) for at in range(0, queries.shape[1], HEAD_DIM)]
    scores = jnp.concatenate(
        [
            lax.dot_general(
                queries[:, head],
                keys[:, head],
                (((1,), (1,)), ((), ())),
                preferred_element_type=jnp.float32,
            )
            for head in heads
        ],
        axis=0,
    ) * HEAD_DIM ** (-0.5)
    valid = lax.broadcasted_iota(jnp.int32, (1, keys.shape[0]), 1) < length
    scores = jnp.where(valid, scores, -jnp.inf)
    expon = jnp.exp(scores - jnp.max(scores, axis=-1, keepdims=True))
    weights = (expon / jnp.sum(expon, axis=-1, keepdims=True)).astype(jnp.bfloat16)
    return jnp.concatenate(
        [
            jnp.dot(
                weights[i * rows : (i + 1) * rows],
                values[:, head],
                preferred_element_type=jnp.float32,
            )
            for i, head in enumerate(heads)
        ],
        axis=1,
    )


def add_rounded(x, attended):
    return (x.astype(jnp.float32) + attended).astype(jnp.bfloat16)


def attend_own_kernel(
    core_ref,
    source_ref,
    x_in,
    gain_in,
    keys_in,
    values_in,
    state_ref,
    query_ref,
    rest_ref,
    x_ref,
    gain_ref,
    keys_ref,
    values_ref,
    scratch_ref,
    sems,
):
    core = core_ref[0]
    copies = fetch(
        sems,
        (x_in.at[0], x_ref),
        (gain_in, gain_ref),
        (keys_in.at[core], keys_ref),
        (values_in.at[core], values_ref),
    )
    half = keys_ref.shape[1]
    copies[0].wait()
    copies[1].wait()
    scratch_ref[...] = layer_norm(x_ref[...].astype(jnp.float32), gain_ref[...])
    own, other = part_of(core, half), part_of(1 - core, half)
    query_ref[...] = scratch_ref[:, other]
    rest_ref[...] = x_ref[:, other]
    copies[2].wait()
    copies[3].wait()
    attended = attend_half(scratch_ref[:, own], keys_ref[...], values_ref[...], source_ref[0])
    state_ref[...] = add_rounded(x_ref[:, own], attended)


def attend_other_kernel(
    core_ref,
    source_ref,
    own_ref,
    query_ref,
    rest_ref,
    keys_ref,
    values_ref,
    gain_in,
    router_in,
    routes_in,
    target_in,
    state_ref,
    keep_ref,
    send_ref,
    gates_ref,
    routes_ref,
    gain_ref,
    router_ref,
    target_ref,
    scratch_ref,
    sems,
):
    core = core_ref[0]
    copies = fetch(
        sems,
        (gain_in, gain_ref),
        (router_in, router_ref),
        (routes_in, routes_ref),
        (target_in, target_ref),
    )
    full_len, half = own_ref.shape
    own, other = part_of(core, half), part_of(1 - core, half)
    attended = attend_half(query_ref[...], keys_ref[core], values_ref[core], source_ref[0])
    state_ref[:, own] = own_ref[...]
    state_ref[:, other] = add_rounded(rest_ref[...], attended)
    copies[0].wait()
    scratch_ref[...] = layer_norm(state_ref[...].astype(jnp.float32), gain_ref[...])
    keep_ref[...] = scratch_ref[:, own]
    send_ref[...] = scratch_ref[:, other]
    for copy in copies[1:]:
        copy.wait()
    logits = lax.dot_general(
        router_ref[...],
        scratch_ref[...],
        (((1,), (1,)), ((), ())),
        preferred_element_type=jnp.float32,
    )
    names = lax.broadcasted_iota(jnp.int32, logits.shape, 0)
    routes = routes_ref[core]
    chosen = [
        jnp.sum(jnp.where(names == routes[k : k + 1], logits, 0.0), axis=0, keepdims=True)
        for k in range(2)
    ]
    first = jax.nn.sigmoid(chosen[0] - chosen[1])
    live = lax.broadcasted_iota(jnp.int32, (1, full_len), 1) < target_ref[core]
    gates_ref[0:1] = jnp.where(live, first, 0.0)
    gates_ref[1:2] = jnp.where(live, 1.0 - first, 0.0)


def slots_of(routes_ref, experts_count):
    sents, _, full_len = routes_ref.shape
    rows = sents * full_len
    ids = lax.broadcasted_iota(jnp.int32, (max(8, experts_count), full_len), 0)
    named = jnp.concatenate(
        [
            jnp.where((ids == routes_ref[s, 0:1]) | (ids == routes_ref[s, 1:2]), 1.0, 0.0)
            for s in range(sents)
        ],
        axis=1,
    )
    before = lax.broadcasted_iota(jnp.int32, (rows, rows), 0) < lax.broadcasted_iota(
        jnp.int32, (rows, rows), 1
    )
    earlier = jnp.dot(
        named.astype(jnp.bfloat16),
        jnp.where(before, 1.0, 0.0).astype(jnp.bfloat16),
        preferred_element_type=jnp.float32,
    )
    return named > 0.0, earlier


def select_kernel(core_ref, line_ref, routes_ref, own_ref, other_ref, *rest):
    pieces, (slots_ref, block_ref) = rest[:-2], rest[-2:]
    experts_count = len(pieces)
    full_len = own_ref.shape[0]
    capacity = pieces[0].shape[0]
    core = core_ref[0]
    block_ref[part_of(core, full_len)] = own_ref[...]
    block_ref[part_of(1 - core, full_len)] = other_ref[...]
    named, earlier = slots_of(routes_ref, experts_count)
    slots_ref[...] = earlier
    slot = jnp.where(named, earlier, -1.0)
    ids = lax.broadcasted_iota(jnp.int32, slot.shape, 0)
    numbers = lax.broadcasted_iota(jnp.int32, (capacity, slot.shape[1]), 0).astype(jnp.float32)
    for offset, piece_ref in enumerate(pieces):
        expert = line_ref[0] ^ offset
        wanted = jnp.sum(jnp.where(ids == expert, slot, 0.0), axis=0, keepdims=True)
        picks = jnp.where(numbers == wanted, 1.0, 0.0).astype(jnp.bfloat16)
        piece_ref[...] = jnp.dot(
            picks, block_ref[...], preferred_element_type=jnp.float32
        ).astype(jnp.bfloat16)


def pair_kernel(p_ref, q_ref, pair_ref):
    capacity = p_ref.shape[0]
    pair_ref[:capacity] = p_ref[...]
    pair_ref[capacity:] = q_ref[...]


def expert_kernel(core_ref, pair_ref, pair2_ref, in_ref, out_ref, keep_ref, send_ref, rows_ref):
    core = core_ref[0]
    half = pair_ref.shape[1]
    capacity = pair_ref.shape[0] // 2
    rows_ref[:, part_of(core, half)] = pair_ref[...]
    rows_ref[:, part_of(1 - core, half)] = pair2_ref[...]
    hidden = jnp.dot(rows_ref[...], in_ref[...], preferred_element_type=jnp.float32)
    hidden = jnp.maximum(hidden, 0.0).astype(jnp.bfloat16)
    send = jnp.dot(
        hidden, out_ref[:, part_of(1 - core, half)], preferred_element_type=jnp.float32
    ).astype(jnp.bfloat16)
    send_ref[0] = send[:capacity]
    send_ref[1] = send[capacity:]
    keep = jnp.dot(hidden, out_ref[:, part_of(core, half)], preferred_element_type=jnp.float32)
    keep_ref[0] = keep[:capacity]
    keep_ref[1] = keep[capacity:]


def load_kernel(in_in, out_in, in_ref, out_ref, sems):
    for copy in fetch(sems, (in_in, in_ref), (out_in, out_ref)):
        copy.wait()


def gated_sum(sent, line, routes, gates, slots_ref, rows):
    full_len = routes.shape[1]
    experts_count = slots_ref.shape[0]
    parts = [slots_ref[:, at : at + full_len] for at in range(0, slots_ref.shape[1], full_len)]
    slots = jnp.where(sent == 0, parts[0], parts[1])
    ids = lax.broadcasted_iota(jnp.int32, (experts_count, full_len), 0)
    numbers = lax.broadcasted_iota(jnp.int32, (full_len, rows.shape[0]), 1).astype(jnp.float32)
    capacity = rows.shape[0] // (lax.axis_size("expert") // 2)
    total = None
    for k in range(2):
        route = routes[k : k + 1]
        slot = jnp.sum(jnp.where(ids == route, slots, 0.0), axis=0, keepdims=True)
        place = (route ^ line).astype(jnp.float32) * capacity + slot
        place, gate = (
            jnp.broadcast_to(row, (full_len, full_len)).T[:, :1]
            for row in (place, gates[k : k + 1])
        )
        picks = jnp.where(numbers == place, 1.0, 0.0).astype(jnp.bfloat16)
        term = gate * jnp.dot(picks, rows, preferred_element_type=jnp.float32)
        total = term if total is None else total + term
    return total


def combine_other_kernel(core_ref, line_ref, routes_ref, gates_ref, slots_ref, *rest):
    pieces, (other_ref, rows_ref) = rest[:-2], rest[-2:]
    capacity = pieces[0].shape[0]
    for offset, piece_ref in enumerate(pieces):
        rows_ref[offset * capacity : (offset + 1) * capacity] = piece_ref[...]
    sent = 1 - core_ref[0]
    other_ref[...] = gated_sum(
        sent, line_ref[0], routes_ref[sent], gates_ref[...], slots_ref, rows_ref[...]
    ).astype(jnp.bfloat16)


def combine_own_kernel(
    core_ref, line_ref, routes_ref, gates_ref, slots_ref, rows_ref, state_ref, own_ref
):
    core = core_ref[0]
    summed = gated_sum(
        core, line_ref[0], routes_ref[core], gates_ref[...], slots_ref, rows_ref[...]
    )
    own_ref[...] = add_rounded(state_ref[:, part_of(core, own_ref.shape[1])], summed)


def finish_kernel(core_ref, state_ref, own_ref, other_ref, mixed_ref):
    core = core_ref[0]
    half = own_ref.shape[-1]
    mixed_ref[:, part_of(core, half)] = own_ref[...]
    span = part_of(1 - core, half)
    mixed_ref[:, span] = add_rounded(state_ref[:, span], other_ref[...].astype(jnp.float32))


def swap(values):
    return lax.ppermute(values, "section", [(0, 1), (1, 0)])


def swap_owner(values):
    owners = lax.axis_size("expert")
    return lax.ppermute(values, "expert", [(i, i ^ 1) for i in range(owners)])


def exchange(values, offset):
    owners = lax.axis_size("expert")
    return lax.ppermute(values, "expert", [(i, i ^ (2 * offset)) for i in range(owners)])


def after_kernel(*refs):
    pass


def after(value, *firsts):
    return pl.pallas_call(
        after_kernel,
        out_shape=jax.ShapeDtypeStruct(value.shape, value.dtype),
        in_specs=[pl.BlockSpec(memory_space=pl.ANY)] * (1 + len(firsts)),
        out_specs=pl.BlockSpec(memory_space=pl.ANY),
        input_output_aliases={0: 0},
        compiler_params=pltpu.CompilerParams(vmem_limit_bytes=2**20),
        name="after",
    )(value, *firsts)


def attend(
    core, decoder_states, memory_keys, memory_values, source_lengths, target_lengths, routes,
    attn_gain, ffn_gain, router,
):
    full_len, width = decoder_states.shape[1:]
    half = (full_len, width // 2)
    memory = memory_keys.shape[1:]
    other_keys, other_values = swap(memory_keys), swap(memory_values)
    own, query, rest = call(
        attend_own_kernel,
        "attend_own",
        [(half, jnp.bfloat16)] * 3,
        [core, source_lengths],
        [],
        [decoder_states, attn_gain[None], memory_keys, memory_values],
        scratch=[
            pltpu.VMEM((full_len, width), jnp.bfloat16),
            pltpu.VMEM((1, width), jnp.float32),
            pltpu.VMEM(memory, jnp.bfloat16),
            pltpu.VMEM(memory, jnp.bfloat16),
            pltpu.VMEM((full_len, width), jnp.bfloat16),
            pltpu.SemaphoreType.DMA((4,)),
        ],
    )
    return call(
        attend_other_kernel,
        "attend_other",
        [
            ((full_len, width), jnp.bfloat16),
            (half, jnp.bfloat16),
            (half, jnp.bfloat16),
            ((2, full_len), jnp.float32),
            (routes.shape, jnp.int32),
        ],
        [core, source_lengths],
        [own, query, rest, other_keys, other_values],
        [ffn_gain[None], router.T, routes, target_lengths],
        scratch=[
            pltpu.VMEM((1, width), jnp.float32),
            pltpu.VMEM(router.shape[::-1], jnp.bfloat16),
            pltpu.SMEM(target_lengths.shape, jnp.int32),
            pltpu.VMEM((full_len, width), jnp.bfloat16),
            pltpu.SemaphoreType.DMA((4,)),
        ],
    )


def line_experts(core, state, keep, send, gates, routes, fc_in, fc_out, capacity):
    full_len, width = state.shape
    half = width // 2
    count = lax.axis_size("expert") // 2
    line = (lax.axis_index("expert") // 2).astype(jnp.int32).reshape(1)
    other = swap(send)
    other_gates = swap(gates)
    piece = ((capacity, half), jnp.bfloat16)
    *selected, slots = call(
        select_kernel,
        "select",
        [piece] * count + [((max(8, count), 2 * full_len), jnp.float32)],
        [core, line],
        [routes, keep, other],
        scratch=[pltpu.VMEM((2 * full_len, half), jnp.bfloat16)],
    )
    near_in, near_out = call(
        load_kernel,
        "load",
        [(fc_in.shape, jnp.bfloat16), (fc_out.shape, jnp.bfloat16)],
        [],
        [],
        [fc_in, fc_out],
        scratch=[pltpu.SemaphoreType.DMA((2,))],
    )
    both_blocks = [((2 * capacity, half), jnp.bfloat16)]

    def run(own, other):
        keep, sent = call(
            expert_kernel,
            "expert",
            [((2, capacity, half), jnp.float32), ((2, capacity, half), jnp.bfloat16)],
            [core],
            [own, other, near_in, near_out],
            scratch=[pltpu.VMEM((2 * capacity, width), jnp.bfloat16)],
            vmem_mib=16,
        )
        return keep, swap(sent)

    def sums(keep, moving):
        both = keep + moving.astype(jnp.float32)
        return both, both[1].astype(jnp.bfloat16)

    def whole(both, across):
        return (both[0] + across.astype(jnp.float32)).astype(jnp.bfloat16)

    travelling = [exchange(selected[r], r) for r in range(1, count)]
    home = [None] * count
    ps, qs, kept, halves, wholes, boths = {}, {}, {}, {}, {}, {}
    p = selected[0]
    q = swap_owner(p)
    ps[0], qs[0] = p, q
    p = travelling[0]
    p = after(p, near_in)
    q = swap_owner(p)
    ps[1], qs[1] = p, q
    p = travelling[1]
    q = swap_owner(p)
    ps[2], qs[2] = p, q
    p = travelling[2]
    q = swap_owner(p)
    ps[3], qs[3] = p, q
    p, q = ps[0], qs[0]
    (own,) = call(pair_kernel, "pair", both_blocks, [], [p, q])
    q2 = swap(own)
    kept[0], moving = run(own, q2)
    boths[0], halves[0] = sums(kept[0], moving)
    p, q = ps[2], qs[2]
    q = after(q, travelling[2], qs[1])
    (own,) = call(pair_kernel, "pair", both_blocks, [], [p, q])
    q2 = swap(own)
    q2 = after(q2, kept[0])
    kept[2], moving = run(own, q2)
    boths[2], halves[2] = sums(kept[2], moving)
    p, q = ps[1], qs[1]
    q = after(q, kept[2])
    (own,) = call(pair_kernel, "pair", both_blocks, [], [p, q])
    q2 = swap(own)
    kept[1], moving = run(own, q2)
    boths[1], halves[1] = sums(kept[1], moving)
    p, q = ps[3], qs[3]
    q = after(q, kept[2])
    (own,) = call(pair_kernel, "pair", both_blocks, [], [p, q])
    q2 = swap(own)
    q2 = after(q2, kept[1], halves[2])
    kept[3], moving = run(own, q2)
    boths[3], halves[3] = sums(kept[3], moving)
    leaving = halves[2]
    across = swap_owner(leaving)
    wholes[2] = whole(boths[2], across)
    home[2] = exchange(wholes[2], 2)
    leaving = halves[3]
    across = swap_owner(leaving)
    wholes[3] = whole(boths[3], across)
    home[3] = exchange(wholes[3], 3)
    leaving = halves[1]
    leaving = after(leaving, halves[3])
    across = swap_owner(leaving)
    wholes[1] = whole(boths[1], across)
    home[1] = exchange(wholes[1], 1)
    leaving = halves[0]
    leaving = after(leaving, wholes[3])
    across = swap_owner(leaving)
    wholes[0] = whole(boths[0], across)
    home[0] = wholes[0]
    leaving, rows = call(
        combine_other_kernel,
        "combine_other",
        [((full_len, half), jnp.bfloat16), ((count * capacity, half), jnp.bfloat16)],
        [core, line],
        [routes, other_gates, slots, *home],
    )
    arriving = swap(leaving)
    (own,) = call(
        combine_own_kernel,
        "combine_own",
        [((full_len, half), jnp.bfloat16)],
        [core, line],
        [routes, gates, slots, rows, state],
    )
    (mixed,) = call(
        finish_kernel,
        "finish",
        [((full_len, width), jnp.bfloat16)],
        [core],
        [state, own, arriving],
    )
    return mixed


def expert_apply(slot_rows, fc_in, fc_out):
    width = slot_rows.shape[-1]
    flat_rows = slot_rows.reshape(-1, width)
    hidden = jax.nn.relu(jnp.dot(flat_rows, fc_in, preferred_element_type=jnp.float32)).astype(
        jnp.bfloat16
    )
    produced = jnp.dot(hidden, fc_out, preferred_element_type=jnp.float32)
    return produced.reshape(slot_rows.shape[0], slot_rows.shape[1], width)


def sparse_experts(normed, target_lengths, routes, router, fc_in, fc_out, capacity):
    full_len, width = normed.shape
    all_normed = lax.all_gather(normed[None], "section", axis=0, tiled=True)
    block_sents = all_normed.shape[0]
    block_rows = block_sents * full_len
    tok_rows = all_normed.reshape(block_rows, width)
    owners = lax.axis_size("expert")
    experts_count = owners // 2
    chosen_ids = routes.reshape(block_rows, 2)
    logits = jnp.dot(tok_rows, router, preferred_element_type=jnp.float32)
    onehot = chosen_ids[:, :, None] == jnp.arange(experts_count, dtype=jnp.int32)
    chosen = jnp.sum(jnp.where(onehot, logits[:, None, :], 0.0), axis=-1)
    first = jax.nn.sigmoid(chosen[:, 0] - chosen[:, 1])
    gates = jnp.stack([first, 1.0 - first], axis=-1)
    live = (jnp.arange(full_len, dtype=jnp.int32)[None, :] < target_lengths[:, None]).reshape(
        block_rows
    )
    flags = onehot.reshape(block_rows * 2, experts_count).astype(jnp.int32)
    earlier = jnp.cumsum(flags, axis=0) - flags
    slot = jnp.sum(flags * earlier, axis=-1).reshape(block_rows, 2)
    position = chosen_ids * capacity + slot
    dump_index = experts_count * capacity
    target = jnp.where(live[:, None], position, dump_index)
    row_ids = jnp.broadcast_to(jnp.arange(block_rows, dtype=jnp.int32)[:, None], (block_rows, 2))
    table = (
        jnp.full((dump_index + 1,), block_rows, jnp.int32)
        .at[target.reshape(-1)]
        .set(row_ids.reshape(-1))[:dump_index]
    )
    padded = jnp.concatenate([tok_rows, jnp.zeros((1, width), jnp.bfloat16)], axis=0)
    slot_buffer = padded[table].reshape(experts_count, capacity, width)
    outgoing = jnp.repeat(slot_buffer, 2, axis=0)
    returned = lax.all_to_all(
        expert_apply(
            lax.all_to_all(outgoing, "expert", split_axis=0, concat_axis=0, tiled=True),
            fc_in,
            fc_out,
        ).astype(jnp.bfloat16),
        "expert",
        split_axis=0,
        concat_axis=0,
        tiled=True,
    ).astype(jnp.float32)
    partial_value = jnp.sum(returned.reshape(experts_count, 2, capacity, width), axis=1)
    fetched = partial_value.reshape(dump_index, width)[jnp.where(live[:, None], position, 0)]
    weight = gates * live[:, None].astype(jnp.float32)
    contrib = jnp.sum(weight[:, :, None] * fetched, axis=1).reshape(block_sents, full_len, width)
    summed = lax.psum_scatter(contrib, "section", scatter_dimension=0, tiled=True)
    return summed[0]


def local(
    decoder_states,
    memory_keys,
    memory_values,
    source_lengths,
    target_lengths,
    routes,
    attn_gain,
    ffn_gain,
    router,
    fc_in,
    fc_out,
):
    core = lax.axis_index("section").astype(jnp.int32).reshape(1)
    by_choice = jnp.transpose(routes, (0, 2, 1))
    state, keep, send, gates, by_choice = attend(
        core, decoder_states, memory_keys, memory_values, source_lengths, target_lengths, by_choice,
        attn_gain, ffn_gain, router,
    )
    block_rows = routes.shape[0] * routes.shape[1]
    experts_count = router.shape[1]
    capacity = 2 * max(1, 3 * block_rows // (2 * experts_count))
    if capacity % 16 == 0 and experts_count & (experts_count - 1) == 0:
        mixed = line_experts(core, state, keep, send, gates, by_choice, fc_in, fc_out, capacity)
    else:
        halves = jnp.stack([keep, send])
        normed = jnp.concatenate([halves[core[0]], halves[1 - core[0]]], axis=-1)
        summed = sparse_experts(normed, target_lengths, routes, router, fc_in, fc_out, capacity)
        mixed = (state.astype(jnp.float32) + summed).astype(jnp.bfloat16)
    return mixed[None]


def solution(mesh):
    placed = (
        P(("groups", "expert", "section"), None, None),
        P(("groups", "expert"), None, "section"),
        P(("groups", "expert"), None, "section"),
        P(("groups", "expert", "section")),
        P(("groups", "expert")),
        P(("groups", "expert"), None, None),
        P(),
        P(),
        P(),
        P(None, ("expert", "section")),
        P(("expert", "section"), None),
    )
    return jax.shard_map(
        local,
        mesh=mesh,
        in_specs=placed,
        out_specs=P(("groups", "expert", "section"), None, None),
        check_vma=False,
    )
```

```python
import functools

import jax
import jax.numpy as jnp
from jax import lax
from jax.experimental import pallas as pl
from jax.experimental.pallas import tpu as pltpu
from jax.sharding import PartitionSpec as P

HEAD_DIM = 128


def layer_norm(values, gain):
    centered = values - jnp.mean(values, axis=-1, keepdims=True)
    spread = jnp.mean(centered * centered, axis=-1, keepdims=True)
    return (centered * lax.rsqrt(spread + 1e-05) * gain).astype(jnp.bfloat16)


VMEM = pl.BlockSpec(memory_space=pltpu.VMEM)
SMEM = pl.BlockSpec(memory_space=pltpu.SMEM)
HBM = pl.BlockSpec(memory_space=pltpu.HBM)


def call(kernel, name, outs, scalars, arrays, far=(), scratch=(), vmem_mib=12):
    return pl.pallas_call(
        kernel,
        out_shape=tuple(jax.ShapeDtypeStruct(*out) for out in outs),
        in_specs=[SMEM] * len(scalars) + [VMEM] * len(arrays) + [HBM] * len(far),
        out_specs=(VMEM,) * len(outs),
        scratch_shapes=list(scratch),
        compiler_params=pltpu.CompilerParams(vmem_limit_bytes=vmem_mib * 2**20),
        name=name,
    )(*scalars, *arrays, *(pltpu.with_memory_space_constraint(a, pltpu.HBM) for a in far))


def fetch(sems, *pairs):
    copies = [
        pltpu.make_async_copy(source, target, sems.at[i]) for i, (source, target) in enumerate(pairs)
    ]
    for copy in copies:
        copy.start()
    return copies


def part_of(part, half):
    return pl.ds(pl.multiple_of(part * half, half), half)


def attend_half(queries, keys, values, length):
    rows = queries.shape[0]
    heads = [slice(at, at + HEAD_DIM) for at in range(0, queries.shape[1], HEAD_DIM)]
    scores = jnp.concatenate(
        [
            lax.dot_general(
                queries[:, head],
                keys[:, head],
                (((1,), (1,)), ((), ())),
                preferred_element_type=jnp.float32,
            )
            for head in heads
        ],
        axis=0,
    ) * HEAD_DIM ** (-0.5)
    valid = lax.broadcasted_iota(jnp.int32, (1, keys.shape[0]), 1) < length
    scores = jnp.where(valid, scores, -jnp.inf)
    expon = jnp.exp(scores - jnp.max(scores, axis=-1, keepdims=True))
    weights = (expon / jnp.sum(expon, axis=-1, keepdims=True)).astype(jnp.bfloat16)
    return jnp.concatenate(
        [
            jnp.dot(
                weights[i * rows : (i + 1) * rows],
                values[:, head],
                preferred_element_type=jnp.float32,
            )
            for i, head in enumerate(heads)
        ],
        axis=1,
    )


def add_rounded(x, attended):
    return (x.astype(jnp.float32) + attended).astype(jnp.bfloat16)


def attend_own_kernel(
    core_ref,
    source_ref,
    x_in,
    gain_in,
    keys_in,
    values_in,
    state_ref,
    query_ref,
    rest_ref,
    x_ref,
    gain_ref,
    keys_ref,
    values_ref,
    scratch_ref,
    sems,
):
    core = core_ref[0]
    copies = fetch(
        sems,
        (x_in.at[0], x_ref),
        (gain_in, gain_ref),
        (keys_in.at[core], keys_ref),
        (values_in.at[core], values_ref),
    )
    half = keys_ref.shape[1]
    copies[0].wait()
    copies[1].wait()
    scratch_ref[...] = layer_norm(x_ref[...].astype(jnp.float32), gain_ref[...])
    own, other = part_of(core, half), part_of(1 - core, half)
    query_ref[...] = scratch_ref[:, other]
    rest_ref[...] = x_ref[:, other]
    copies[2].wait()
    copies[3].wait()
    attended = attend_half(scratch_ref[:, own], keys_ref[...], values_ref[...], source_ref[0])
    state_ref[...] = add_rounded(x_ref[:, own], attended)


def attend_other_kernel(
    core_ref,
    source_ref,
    own_ref,
    query_ref,
    rest_ref,
    keys_ref,
    values_ref,
    gain_in,
    router_in,
    routes_in,
    target_in,
    state_ref,
    keep_ref,
    send_ref,
    gates_ref,
    routes_ref,
    gain_ref,
    router_ref,
    target_ref,
    scratch_ref,
    sems,
):
    core = core_ref[0]
    copies = fetch(
        sems,
        (gain_in, gain_ref),
        (router_in, router_ref),
        (routes_in, routes_ref),
        (target_in, target_ref),
    )
    full_len, half = own_ref.shape
    own, other = part_of(core, half), part_of(1 - core, half)
    attended = attend_half(query_ref[...], keys_ref[core], values_ref[core], source_ref[0])
    state_ref[:, own] = own_ref[...]
    state_ref[:, other] = add_rounded(rest_ref[...], attended)
    copies[0].wait()
    scratch_ref[...] = layer_norm(state_ref[...].astype(jnp.float32), gain_ref[...])
    keep_ref[...] = scratch_ref[:, own]
    send_ref[...] = scratch_ref[:, other]
    for copy in copies[1:]:
        copy.wait()
    logits = lax.dot_general(
        router_ref[...],
        scratch_ref[...],
        (((1,), (1,)), ((), ())),
        preferred_element_type=jnp.float32,
    )
    names = lax.broadcasted_iota(jnp.int32, logits.shape, 0)
    routes = routes_ref[core]
    chosen = [
        jnp.sum(jnp.where(names == routes[k : k + 1], logits, 0.0), axis=0, keepdims=True)
        for k in range(2)
    ]
    first = jax.nn.sigmoid(chosen[0] - chosen[1])
    live = lax.broadcasted_iota(jnp.int32, (1, full_len), 1) < target_ref[core]
    gates_ref[0:1] = jnp.where(live, first, 0.0)
    gates_ref[1:2] = jnp.where(live, 1.0 - first, 0.0)


def slots_of(routes_ref, experts_count):
    sents, _, full_len = routes_ref.shape
    rows = sents * full_len
    ids = lax.broadcasted_iota(jnp.int32, (max(8, experts_count), full_len), 0)
    named = jnp.concatenate(
        [
            jnp.where((ids == routes_ref[s, 0:1]) | (ids == routes_ref[s, 1:2]), 1.0, 0.0)
            for s in range(sents)
        ],
        axis=1,
    )
    before = lax.broadcasted_iota(jnp.int32, (rows, rows), 0) < lax.broadcasted_iota(
        jnp.int32, (rows, rows), 1
    )
    earlier = jnp.dot(
        named.astype(jnp.bfloat16),
        jnp.where(before, 1.0, 0.0).astype(jnp.bfloat16),
        preferred_element_type=jnp.float32,
    )
    return named > 0.0, earlier


def select_kernel(core_ref, line_ref, routes_ref, own_ref, other_ref, *rest):
    pieces, (slots_ref, block_ref) = rest[:-2], rest[-2:]
    experts_count = len(pieces)
    full_len = own_ref.shape[0]
    capacity = pieces[0].shape[0]
    core = core_ref[0]
    block_ref[part_of(core, full_len)] = own_ref[...]
    block_ref[part_of(1 - core, full_len)] = other_ref[...]
    named, earlier = slots_of(routes_ref, experts_count)
    slots_ref[...] = earlier
    slot = jnp.where(named, earlier, -1.0)
    ids = lax.broadcasted_iota(jnp.int32, slot.shape, 0)
    numbers = lax.broadcasted_iota(jnp.int32, (capacity, slot.shape[1]), 0).astype(jnp.float32)
    for offset, piece_ref in enumerate(pieces):
        expert = line_ref[0] ^ offset
        wanted = jnp.sum(jnp.where(ids == expert, slot, 0.0), axis=0, keepdims=True)
        picks = jnp.where(numbers == wanted, 1.0, 0.0).astype(jnp.bfloat16)
        piece_ref[...] = jnp.dot(
            picks, block_ref[...], preferred_element_type=jnp.float32
        ).astype(jnp.bfloat16)


def expert_kernel(
    core_ref, p_ref, q_ref, p2_ref, q2_ref, in_ref, out_ref, keep_ref, send_ref, rows_ref
):
    core = core_ref[0]
    capacity, half = p_ref.shape
    rows_ref[:capacity, part_of(core, half)] = p_ref[...]
    rows_ref[capacity:, part_of(core, half)] = q_ref[...]
    rows_ref[:capacity, part_of(1 - core, half)] = p2_ref[...]
    rows_ref[capacity:, part_of(1 - core, half)] = q2_ref[...]
    hidden = jnp.dot(rows_ref[...], in_ref[...], preferred_element_type=jnp.float32)
    hidden = jnp.maximum(hidden, 0.0).astype(jnp.bfloat16)
    send = jnp.dot(
        hidden, out_ref[:, part_of(1 - core, half)], preferred_element_type=jnp.float32
    ).astype(jnp.bfloat16)
    send_ref[0] = send[:capacity]
    send_ref[1] = send[capacity:]
    keep = jnp.dot(hidden, out_ref[:, part_of(core, half)], preferred_element_type=jnp.float32)
    keep_ref[0] = keep[:capacity]
    keep_ref[1] = keep[capacity:]


def load_kernel(in_in, out_in, in_ref, out_ref, sems):
    for copy in fetch(sems, (in_in, in_ref), (out_in, out_ref)):
        copy.wait()


def gated_sum(sent, line, routes, gates, slots_ref, rows):
    full_len = routes.shape[1]
    experts_count = slots_ref.shape[0]
    parts = [slots_ref[:, at : at + full_len] for at in range(0, slots_ref.shape[1], full_len)]
    slots = jnp.where(sent == 0, parts[0], parts[1])
    ids = lax.broadcasted_iota(jnp.int32, (experts_count, full_len), 0)
    numbers = lax.broadcasted_iota(jnp.int32, (full_len, rows.shape[0]), 1).astype(jnp.float32)
    capacity = rows.shape[0] // (lax.axis_size("expert") // 2)
    total = None
    for k in range(2):
        route = routes[k : k + 1]
        slot = jnp.sum(jnp.where(ids == route, slots, 0.0), axis=0, keepdims=True)
        place = (route ^ line).astype(jnp.float32) * capacity + slot
        place, gate = (
            jnp.broadcast_to(row, (full_len, full_len)).T[:, :1]
            for row in (place, gates[k : k + 1])
        )
        picks = jnp.where(numbers == place, 1.0, 0.0).astype(jnp.bfloat16)
        term = gate * jnp.dot(picks, rows, preferred_element_type=jnp.float32)
        total = term if total is None else total + term
    return total


def combine_other_kernel(core_ref, line_ref, routes_ref, gates_ref, slots_ref, *rest):
    pieces, (other_ref, rows_ref) = rest[:-2], rest[-2:]
    capacity = pieces[0].shape[0]
    for offset, piece_ref in enumerate(pieces):
        rows_ref[offset * capacity : (offset + 1) * capacity] = piece_ref[...]
    sent = 1 - core_ref[0]
    other_ref[...] = gated_sum(
        sent, line_ref[0], routes_ref[sent], gates_ref[...], slots_ref, rows_ref[...]
    ).astype(jnp.bfloat16)


def combine_own_kernel(
    core_ref, line_ref, routes_ref, gates_ref, slots_ref, rows_ref, state_ref, own_ref
):
    core = core_ref[0]
    summed = gated_sum(
        core, line_ref[0], routes_ref[core], gates_ref[...], slots_ref, rows_ref[...]
    )
    own_ref[...] = add_rounded(state_ref[:, part_of(core, own_ref.shape[1])], summed)


def finish_kernel(core_ref, state_ref, own_ref, other_ref, mixed_ref):
    core = core_ref[0]
    half = own_ref.shape[-1]
    mixed_ref[:, part_of(core, half)] = own_ref[...]
    span = part_of(1 - core, half)
    mixed_ref[:, span] = add_rounded(state_ref[:, span], other_ref[...].astype(jnp.float32))


def swap(values):
    return lax.ppermute(values, "section", [(0, 1), (1, 0)])


def swap_owner(values):
    owners = lax.axis_size("expert")
    return lax.ppermute(values, "expert", [(i, i ^ 1) for i in range(owners)])


def exchange(values, offset):
    owners = lax.axis_size("expert")
    return lax.ppermute(values, "expert", [(i, i ^ (2 * offset)) for i in range(owners)])


def after_kernel(*refs):
    pass


def after(value, *firsts):
    return pl.pallas_call(
        after_kernel,
        out_shape=jax.ShapeDtypeStruct(value.shape, value.dtype),
        in_specs=[pl.BlockSpec(memory_space=pl.ANY)] * (1 + len(firsts)),
        out_specs=pl.BlockSpec(memory_space=pl.ANY),
        input_output_aliases={0: 0},
        compiler_params=pltpu.CompilerParams(vmem_limit_bytes=2**20),
        name="after",
    )(value, *firsts)


def attend(
    core, decoder_states, memory_keys, memory_values, source_lengths, target_lengths, routes,
    attn_gain, ffn_gain, router,
):
    full_len, width = decoder_states.shape[1:]
    half = (full_len, width // 2)
    memory = memory_keys.shape[1:]
    other_keys, other_values = swap(memory_keys), swap(memory_values)
    own, query, rest = call(
        attend_own_kernel,
        "attend_own",
        [(half, jnp.bfloat16)] * 3,
        [core, source_lengths],
        [],
        [decoder_states, attn_gain[None], memory_keys, memory_values],
        scratch=[
            pltpu.VMEM((full_len, width), jnp.bfloat16),
            pltpu.VMEM((1, width), jnp.float32),
            pltpu.VMEM(memory, jnp.bfloat16),
            pltpu.VMEM(memory, jnp.bfloat16),
            pltpu.VMEM((full_len, width), jnp.bfloat16),
            pltpu.SemaphoreType.DMA((4,)),
        ],
    )
    return call(
        attend_other_kernel,
        "attend_other",
        [
            ((full_len, width), jnp.bfloat16),
            (half, jnp.bfloat16),
            (half, jnp.bfloat16),
            ((2, full_len), jnp.float32),
            (routes.shape, jnp.int32),
        ],
        [core, source_lengths],
        [own, query, rest, other_keys, other_values],
        [ffn_gain[None], router.T, routes, target_lengths],
        scratch=[
            pltpu.VMEM((1, width), jnp.float32),
            pltpu.VMEM(router.shape[::-1], jnp.bfloat16),
            pltpu.SMEM(target_lengths.shape, jnp.int32),
            pltpu.VMEM((full_len, width), jnp.bfloat16),
            pltpu.SemaphoreType.DMA((4,)),
        ],
    )


def line_experts(core, state, keep, send, gates, routes, fc_in, fc_out, capacity):
    full_len, width = state.shape
    half = width // 2
    count = lax.axis_size("expert") // 2
    line = (lax.axis_index("expert") // 2).astype(jnp.int32).reshape(1)
    other = swap(send)
    other_gates = swap(gates)
    piece = ((capacity, half), jnp.bfloat16)
    *selected, slots = call(
        select_kernel,
        "select",
        [piece] * count + [((max(8, count), 2 * full_len), jnp.float32)],
        [core, line],
        [routes, keep, other],
        scratch=[pltpu.VMEM((2 * full_len, half), jnp.bfloat16)],
    )
    near_in, near_out = call(
        load_kernel,
        "load",
        [(fc_in.shape, jnp.bfloat16), (fc_out.shape, jnp.bfloat16)],
        [],
        [],
        [fc_in, fc_out],
        scratch=[pltpu.SemaphoreType.DMA((2,))],
    )
    def run(p, q, p2, q2):
        keep, sent = call(
            expert_kernel,
            "expert",
            [((2, capacity, half), jnp.float32), ((2, capacity, half), jnp.bfloat16)],
            [core],
            [p, q, p2, q2, near_in, near_out],
            scratch=[pltpu.VMEM((2 * capacity, width), jnp.bfloat16)],
            vmem_mib=16,
        )
        return keep, swap(sent)

    def sums(keep, moving):
        both = keep + moving.astype(jnp.float32)
        return both, both[1].astype(jnp.bfloat16)

    def whole(both, across):
        return (both[0] + across.astype(jnp.float32)).astype(jnp.bfloat16)

    travelling = [exchange(selected[r], r) for r in range(1, count)]
    home = [None] * count
    ps, qs, kept, halves, wholes, boths = {}, {}, {}, {}, {}, {}
    p = selected[0]
    q = swap_owner(p)
    ps[0], qs[0] = p, q
    p = travelling[0]
    p = after(p, near_in)
    q = swap_owner(p)
    ps[1], qs[1] = p, q
    p = travelling[1]
    q = swap_owner(p)
    ps[2], qs[2] = p, q
    p = travelling[2]
    q = swap_owner(p)
    ps[3], qs[3] = p, q
    p, q = ps[0], qs[0]
    p2, q2 = swap(p), swap(q)
    kept[0], moving = run(p, q, p2, q2)
    boths[0], halves[0] = sums(kept[0], moving)
    p, q = ps[1], qs[1]
    p2, q2 = swap(p), swap(q)
    kept[1], moving = run(p, q, p2, q2)
    boths[1], halves[1] = sums(kept[1], moving)
    p, q = ps[2], qs[2]
    p2, q2 = swap(p), swap(q)
    q2 = after(q2, kept[0], kept[1])
    kept[2], moving = run(p, q, p2, q2)
    boths[2], halves[2] = sums(kept[2], moving)
    p, q = ps[3], qs[3]
    q = after(q, kept[2])
    p2, q2 = swap(p), swap(q)
    q2 = after(q2, halves[2])
    kept[3], moving = run(p, q, p2, q2)
    boths[3], halves[3] = sums(kept[3], moving)
    leaving = halves[2]
    across = swap_owner(leaving)
    wholes[2] = whole(boths[2], across)
    home[2] = exchange(wholes[2], 2)
    leaving = halves[3]
    across = swap_owner(leaving)
    wholes[3] = whole(boths[3], across)
    home[3] = exchange(wholes[3], 3)
    leaving = halves[1]
    leaving = after(leaving, halves[3])
    across = swap_owner(leaving)
    wholes[1] = whole(boths[1], across)
    home[1] = exchange(wholes[1], 1)
    leaving = halves[0]
    leaving = after(leaving, wholes[3])
    across = swap_owner(leaving)
    wholes[0] = whole(boths[0], across)
    home[0] = wholes[0]
    leaving, rows = call(
        combine_other_kernel,
        "combine_other",
        [((full_len, half), jnp.bfloat16), ((count * capacity, half), jnp.bfloat16)],
        [core, line],
        [routes, other_gates, slots, *home],
    )
    arriving = swap(leaving)
    (own,) = call(
        combine_own_kernel,
        "combine_own",
        [((full_len, half), jnp.bfloat16)],
        [core, line],
        [routes, gates, slots, rows, state],
    )
    (mixed,) = call(
        finish_kernel,
        "finish",
        [((full_len, width), jnp.bfloat16)],
        [core],
        [state, own, arriving],
    )
    return mixed


def expert_apply(slot_rows, fc_in, fc_out):
    width = slot_rows.shape[-1]
    flat_rows = slot_rows.reshape(-1, width)
    hidden = jax.nn.relu(jnp.dot(flat_rows, fc_in, preferred_element_type=jnp.float32)).astype(
        jnp.bfloat16
    )
    produced = jnp.dot(hidden, fc_out, preferred_element_type=jnp.float32)
    return produced.reshape(slot_rows.shape[0], slot_rows.shape[1], width)


def sparse_experts(normed, target_lengths, routes, router, fc_in, fc_out, capacity):
    full_len, width = normed.shape
    all_normed = lax.all_gather(normed[None], "section", axis=0, tiled=True)
    block_sents = all_normed.shape[0]
    block_rows = block_sents * full_len
    tok_rows = all_normed.reshape(block_rows, width)
    owners = lax.axis_size("expert")
    experts_count = owners // 2
    chosen_ids = routes.reshape(block_rows, 2)
    logits = jnp.dot(tok_rows, router, preferred_element_type=jnp.float32)
    onehot = chosen_ids[:, :, None] == jnp.arange(experts_count, dtype=jnp.int32)
    chosen = jnp.sum(jnp.where(onehot, logits[:, None, :], 0.0), axis=-1)
    first = jax.nn.sigmoid(chosen[:, 0] - chosen[:, 1])
    gates = jnp.stack([first, 1.0 - first], axis=-1)
    live = (jnp.arange(full_len, dtype=jnp.int32)[None, :] < target_lengths[:, None]).reshape(
        block_rows
    )
    flags = onehot.reshape(block_rows * 2, experts_count).astype(jnp.int32)
    earlier = jnp.cumsum(flags, axis=0) - flags
    slot = jnp.sum(flags * earlier, axis=-1).reshape(block_rows, 2)
    position = chosen_ids * capacity + slot
    dump_index = experts_count * capacity
    target = jnp.where(live[:, None], position, dump_index)
    row_ids = jnp.broadcast_to(jnp.arange(block_rows, dtype=jnp.int32)[:, None], (block_rows, 2))
    table = (
        jnp.full((dump_index + 1,), block_rows, jnp.int32)
        .at[target.reshape(-1)]
        .set(row_ids.reshape(-1))[:dump_index]
    )
    padded = jnp.concatenate([tok_rows, jnp.zeros((1, width), jnp.bfloat16)], axis=0)
    slot_buffer = padded[table].reshape(experts_count, capacity, width)
    outgoing = jnp.repeat(slot_buffer, 2, axis=0)
    returned = lax.all_to_all(
        expert_apply(
            lax.all_to_all(outgoing, "expert", split_axis=0, concat_axis=0, tiled=True),
            fc_in,
            fc_out,
        ).astype(jnp.bfloat16),
        "expert",
        split_axis=0,
        concat_axis=0,
        tiled=True,
    ).astype(jnp.float32)
    partial_value = jnp.sum(returned.reshape(experts_count, 2, capacity, width), axis=1)
    fetched = partial_value.reshape(dump_index, width)[jnp.where(live[:, None], position, 0)]
    weight = gates * live[:, None].astype(jnp.float32)
    contrib = jnp.sum(weight[:, :, None] * fetched, axis=1).reshape(block_sents, full_len, width)
    summed = lax.psum_scatter(contrib, "section", scatter_dimension=0, tiled=True)
    return summed[0]


def local(
    decoder_states,
    memory_keys,
    memory_values,
    source_lengths,
    target_lengths,
    routes,
    attn_gain,
    ffn_gain,
    router,
    fc_in,
    fc_out,
):
    core = lax.axis_index("section").astype(jnp.int32).reshape(1)
    by_choice = jnp.transpose(routes, (0, 2, 1))
    state, keep, send, gates, by_choice = attend(
        core, decoder_states, memory_keys, memory_values, source_lengths, target_lengths, by_choice,
        attn_gain, ffn_gain, router,
    )
    block_rows = routes.shape[0] * routes.shape[1]
    experts_count = router.shape[1]
    capacity = 2 * max(1, 3 * block_rows // (2 * experts_count))
    if capacity % 16 == 0 and experts_count & (experts_count - 1) == 0:
        mixed = line_experts(core, state, keep, send, gates, by_choice, fc_in, fc_out, capacity)
    else:
        halves = jnp.stack([keep, send])
        normed = jnp.concatenate([halves[core[0]], halves[1 - core[0]]], axis=-1)
        summed = sparse_experts(normed, target_lengths, routes, router, fc_in, fc_out, capacity)
        mixed = (state.astype(jnp.float32) + summed).astype(jnp.bfloat16)
    return mixed[None]


def solution(mesh):
    placed = (
        P(("groups", "expert", "section"), None, None),
        P(("groups", "expert"), None, "section"),
        P(("groups", "expert"), None, "section"),
        P(("groups", "expert", "section")),
        P(("groups", "expert")),
        P(("groups", "expert"), None, None),
        P(),
        P(),
        P(),
        P(None, ("expert", "section")),
        P(("expert", "section"), None),
    )
    return jax.shard_map(
        local,
        mesh=mesh,
        in_specs=placed,
        out_specs=P(("groups", "expert", "section"), None, None),
        check_vma=False,
    )
```

```python
import functools

import jax
import jax.numpy as jnp
from jax import lax
from jax.experimental import pallas as pl
from jax.experimental.pallas import tpu as pltpu
from jax.sharding import PartitionSpec as P

HEAD_DIM = 128


def layer_norm(values, gain):
    centered = values - jnp.mean(values, axis=-1, keepdims=True)
    spread = jnp.mean(centered * centered, axis=-1, keepdims=True)
    return (centered * lax.rsqrt(spread + 1e-05) * gain).astype(jnp.bfloat16)


VMEM = pl.BlockSpec(memory_space=pltpu.VMEM)
SMEM = pl.BlockSpec(memory_space=pltpu.SMEM)
HBM = pl.BlockSpec(memory_space=pltpu.HBM)


def call(kernel, name, outs, scalars, arrays, far=(), scratch=(), vmem_mib=12):
    return pl.pallas_call(
        kernel,
        out_shape=tuple(jax.ShapeDtypeStruct(*out) for out in outs),
        in_specs=[SMEM] * len(scalars) + [VMEM] * len(arrays) + [HBM] * len(far),
        out_specs=(VMEM,) * len(outs),
        scratch_shapes=list(scratch),
        compiler_params=pltpu.CompilerParams(vmem_limit_bytes=vmem_mib * 2**20),
        name=name,
    )(*scalars, *arrays, *(pltpu.with_memory_space_constraint(a, pltpu.HBM) for a in far))


def fetch(sems, *pairs):
    copies = [
        pltpu.make_async_copy(source, target, sems.at[i]) for i, (source, target) in enumerate(pairs)
    ]
    for copy in copies:
        copy.start()
    return copies


def part_of(part, half):
    return pl.ds(pl.multiple_of(part * half, half), half)


def attend_half(queries, keys, values, length):
    rows = queries.shape[0]
    heads = [slice(at, at + HEAD_DIM) for at in range(0, queries.shape[1], HEAD_DIM)]
    scores = jnp.concatenate(
        [
            lax.dot_general(
                queries[:, head],
                keys[:, head],
                (((1,), (1,)), ((), ())),
                preferred_element_type=jnp.float32,
            )
            for head in heads
        ],
        axis=0,
    ) * HEAD_DIM ** (-0.5)
    valid = lax.broadcasted_iota(jnp.int32, (1, keys.shape[0]), 1) < length
    scores = jnp.where(valid, scores, -jnp.inf)
    expon = jnp.exp(scores - jnp.max(scores, axis=-1, keepdims=True))
    weights = (expon / jnp.sum(expon, axis=-1, keepdims=True)).astype(jnp.bfloat16)
    return jnp.concatenate(
        [
            jnp.dot(
                weights[i * rows : (i + 1) * rows],
                values[:, head],
                preferred_element_type=jnp.float32,
            )
            for i, head in enumerate(heads)
        ],
        axis=1,
    )


def add_rounded(x, attended):
    return (x.astype(jnp.float32) + attended).astype(jnp.bfloat16)


def attend_own_kernel(
    core_ref,
    source_ref,
    x_in,
    gain_in,
    keys_in,
    values_in,
    state_ref,
    query_ref,
    rest_ref,
    x_ref,
    gain_ref,
    keys_ref,
    values_ref,
    scratch_ref,
    sems,
):
    core = core_ref[0]
    copies = fetch(
        sems,
        (x_in.at[0], x_ref),
        (gain_in, gain_ref),
        (keys_in.at[core], keys_ref),
        (values_in.at[core], values_ref),
    )
    half = keys_ref.shape[1]
    copies[0].wait()
    copies[1].wait()
    scratch_ref[...] = layer_norm(x_ref[...].astype(jnp.float32), gain_ref[...])
    own, other = part_of(core, half), part_of(1 - core, half)
    query_ref[...] = scratch_ref[:, other]
    rest_ref[...] = x_ref[:, other]
    copies[2].wait()
    copies[3].wait()
    attended = attend_half(scratch_ref[:, own], keys_ref[...], values_ref[...], source_ref[0])
    state_ref[...] = add_rounded(x_ref[:, own], attended)


def attend_other_kernel(
    core_ref,
    source_ref,
    own_ref,
    query_ref,
    rest_ref,
    keys_ref,
    values_ref,
    gain_in,
    router_in,
    routes_in,
    target_in,
    state_ref,
    keep_ref,
    send_ref,
    gates_ref,
    routes_ref,
    gain_ref,
    router_ref,
    target_ref,
    scratch_ref,
    sems,
):
    core = core_ref[0]
    copies = fetch(
        sems,
        (gain_in, gain_ref),
        (router_in, router_ref),
        (routes_in, routes_ref),
        (target_in, target_ref),
    )
    full_len, half = own_ref.shape
    own, other = part_of(core, half), part_of(1 - core, half)
    attended = attend_half(query_ref[...], keys_ref[core], values_ref[core], source_ref[0])
    state_ref[:, own] = own_ref[...]
    state_ref[:, other] = add_rounded(rest_ref[...], attended)
    copies[0].wait()
    scratch_ref[...] = layer_norm(state_ref[...].astype(jnp.float32), gain_ref[...])
    keep_ref[...] = scratch_ref[:, own]
    send_ref[...] = scratch_ref[:, other]
    for copy in copies[1:]:
        copy.wait()
    logits = lax.dot_general(
        router_ref[...],
        scratch_ref[...],
        (((1,), (1,)), ((), ())),
        preferred_element_type=jnp.float32,
    )
    names = lax.broadcasted_iota(jnp.int32, logits.shape, 0)
    routes = routes_ref[core]
    chosen = [
        jnp.sum(jnp.where(names == routes[k : k + 1], logits, 0.0), axis=0, keepdims=True)
        for k in range(2)
    ]
    first = jax.nn.sigmoid(chosen[0] - chosen[1])
    live = lax.broadcasted_iota(jnp.int32, (1, full_len), 1) < target_ref[core]
    gates_ref[0:1] = jnp.where(live, first, 0.0)
    gates_ref[1:2] = jnp.where(live, 1.0 - first, 0.0)


def slots_of(routes_ref, experts_count):
    sents, _, full_len = routes_ref.shape
    rows = sents * full_len
    ids = lax.broadcasted_iota(jnp.int32, (max(8, experts_count), full_len), 0)
    named = jnp.concatenate(
        [
            jnp.where((ids == routes_ref[s, 0:1]) | (ids == routes_ref[s, 1:2]), 1.0, 0.0)
            for s in range(sents)
        ],
        axis=1,
    )
    before = lax.broadcasted_iota(jnp.int32, (rows, rows), 0) < lax.broadcasted_iota(
        jnp.int32, (rows, rows), 1
    )
    earlier = jnp.dot(
        named.astype(jnp.bfloat16),
        jnp.where(before, 1.0, 0.0).astype(jnp.bfloat16),
        preferred_element_type=jnp.float32,
    )
    return named > 0.0, earlier


def select_kernel(core_ref, line_ref, routes_ref, own_ref, other_ref, *rest):
    pieces, (slots_ref, block_ref) = rest[:-2], rest[-2:]
    experts_count = len(pieces)
    full_len = own_ref.shape[0]
    capacity = pieces[0].shape[0]
    core = core_ref[0]
    block_ref[part_of(core, full_len)] = own_ref[...]
    block_ref[part_of(1 - core, full_len)] = other_ref[...]
    named, earlier = slots_of(routes_ref, experts_count)
    slots_ref[...] = earlier
    slot = jnp.where(named, earlier, -1.0)
    ids = lax.broadcasted_iota(jnp.int32, slot.shape, 0)
    numbers = lax.broadcasted_iota(jnp.int32, (capacity, slot.shape[1]), 0).astype(jnp.float32)
    for offset, piece_ref in enumerate(pieces):
        expert = line_ref[0] ^ offset
        wanted = jnp.sum(jnp.where(ids == expert, slot, 0.0), axis=0, keepdims=True)
        picks = jnp.where(numbers == wanted, 1.0, 0.0).astype(jnp.bfloat16)
        piece_ref[...] = jnp.dot(
            picks, block_ref[...], preferred_element_type=jnp.float32
        ).astype(jnp.bfloat16)


def expert_kernel(
    core_ref, p_ref, q_ref, p2_ref, q2_ref, in_ref, out_ref, keep_ref, send_ref, rows_ref
):
    core = core_ref[0]
    capacity, half = p_ref.shape
    rows_ref[:capacity, part_of(core, half)] = p_ref[...]
    rows_ref[capacity:, part_of(core, half)] = q_ref[...]
    rows_ref[:capacity, part_of(1 - core, half)] = p2_ref[...]
    rows_ref[capacity:, part_of(1 - core, half)] = q2_ref[...]
    hidden = jnp.dot(rows_ref[...], in_ref[...], preferred_element_type=jnp.float32)
    hidden = jnp.maximum(hidden, 0.0).astype(jnp.bfloat16)
    send = jnp.dot(
        hidden, out_ref[:, part_of(1 - core, half)], preferred_element_type=jnp.float32
    ).astype(jnp.bfloat16)
    send_ref[0] = send[:capacity]
    send_ref[1] = send[capacity:]
    keep = jnp.dot(hidden, out_ref[:, part_of(core, half)], preferred_element_type=jnp.float32)
    keep_ref[0] = keep[:capacity]
    keep_ref[1] = keep[capacity:]


def load_kernel(in_in, out_in, in_ref, out_ref, sems):
    for copy in fetch(sems, (in_in, in_ref), (out_in, out_ref)):
        copy.wait()


def gated_sum(sent, line, routes, gates, slots_ref, rows):
    full_len = routes.shape[1]
    experts_count = slots_ref.shape[0]
    parts = [slots_ref[:, at : at + full_len] for at in range(0, slots_ref.shape[1], full_len)]
    slots = jnp.where(sent == 0, parts[0], parts[1])
    ids = lax.broadcasted_iota(jnp.int32, (experts_count, full_len), 0)
    numbers = lax.broadcasted_iota(jnp.int32, (full_len, rows.shape[0]), 1).astype(jnp.float32)
    capacity = rows.shape[0] // (lax.axis_size("expert") // 2)
    total = None
    for k in range(2):
        route = routes[k : k + 1]
        slot = jnp.sum(jnp.where(ids == route, slots, 0.0), axis=0, keepdims=True)
        place = (route ^ line).astype(jnp.float32) * capacity + slot
        place, gate = (
            jnp.broadcast_to(row, (full_len, full_len)).T[:, :1]
            for row in (place, gates[k : k + 1])
        )
        picks = jnp.where(numbers == place, 1.0, 0.0).astype(jnp.bfloat16)
        term = gate * jnp.dot(picks, rows, preferred_element_type=jnp.float32)
        total = term if total is None else total + term
    return total


def combine_other_kernel(core_ref, line_ref, routes_ref, gates_ref, slots_ref, *rest):
    pieces, (other_ref, rows_ref) = rest[:-2], rest[-2:]
    capacity = pieces[0].shape[0]
    for offset, piece_ref in enumerate(pieces):
        rows_ref[offset * capacity : (offset + 1) * capacity] = piece_ref[...]
    sent = 1 - core_ref[0]
    other_ref[...] = gated_sum(
        sent, line_ref[0], routes_ref[sent], gates_ref[...], slots_ref, rows_ref[...]
    ).astype(jnp.bfloat16)


def combine_own_kernel(
    core_ref, line_ref, routes_ref, gates_ref, slots_ref, rows_ref, state_ref, own_ref
):
    core = core_ref[0]
    summed = gated_sum(
        core, line_ref[0], routes_ref[core], gates_ref[...], slots_ref, rows_ref[...]
    )
    own_ref[...] = add_rounded(state_ref[:, part_of(core, own_ref.shape[1])], summed)


def finish_kernel(core_ref, state_ref, own_ref, other_ref, mixed_ref):
    core = core_ref[0]
    half = own_ref.shape[-1]
    mixed_ref[:, part_of(core, half)] = own_ref[...]
    span = part_of(1 - core, half)
    mixed_ref[:, span] = add_rounded(state_ref[:, span], other_ref[...].astype(jnp.float32))


def swap(values):
    return lax.ppermute(values, "section", [(0, 1), (1, 0)])


def swap_owner(values):
    owners = lax.axis_size("expert")
    return lax.ppermute(values, "expert", [(i, i ^ 1) for i in range(owners)])


def exchange(values, offset):
    owners = lax.axis_size("expert")
    return lax.ppermute(values, "expert", [(i, i ^ (2 * offset)) for i in range(owners)])


def after_kernel(*refs):
    pass


def after(value, *firsts):
    return pl.pallas_call(
        after_kernel,
        out_shape=jax.ShapeDtypeStruct(value.shape, value.dtype),
        in_specs=[pl.BlockSpec(memory_space=pl.ANY)] * (1 + len(firsts)),
        out_specs=pl.BlockSpec(memory_space=pl.ANY),
        input_output_aliases={0: 0},
        compiler_params=pltpu.CompilerParams(vmem_limit_bytes=2**20),
        name="after",
    )(value, *firsts)


def attend(
    core, decoder_states, memory_keys, memory_values, source_lengths, target_lengths, routes,
    attn_gain, ffn_gain, router,
):
    full_len, width = decoder_states.shape[1:]
    half = (full_len, width // 2)
    memory = memory_keys.shape[1:]
    other_keys, other_values = swap(memory_keys), swap(memory_values)
    own, query, rest = call(
        attend_own_kernel,
        "attend_own",
        [(half, jnp.bfloat16)] * 3,
        [core, source_lengths],
        [],
        [decoder_states, attn_gain[None], memory_keys, memory_values],
        scratch=[
            pltpu.VMEM((full_len, width), jnp.bfloat16),
            pltpu.VMEM((1, width), jnp.float32),
            pltpu.VMEM(memory, jnp.bfloat16),
            pltpu.VMEM(memory, jnp.bfloat16),
            pltpu.VMEM((full_len, width), jnp.bfloat16),
            pltpu.SemaphoreType.DMA((4,)),
        ],
    )
    return call(
        attend_other_kernel,
        "attend_other",
        [
            ((full_len, width), jnp.bfloat16),
            (half, jnp.bfloat16),
            (half, jnp.bfloat16),
            ((2, full_len), jnp.float32),
            (routes.shape, jnp.int32),
        ],
        [core, source_lengths],
        [own, query, rest, other_keys, other_values],
        [ffn_gain[None], router.T, routes, target_lengths],
        scratch=[
            pltpu.VMEM((1, width), jnp.float32),
            pltpu.VMEM(router.shape[::-1], jnp.bfloat16),
            pltpu.SMEM(target_lengths.shape, jnp.int32),
            pltpu.VMEM((full_len, width), jnp.bfloat16),
            pltpu.SemaphoreType.DMA((4,)),
        ],
    )


def line_experts(core, state, keep, send, gates, routes, fc_in, fc_out, capacity):
    full_len, width = state.shape
    half = width // 2
    count = lax.axis_size("expert") // 2
    line = (lax.axis_index("expert") // 2).astype(jnp.int32).reshape(1)
    other = swap(send)
    other_gates = swap(gates)
    piece = ((capacity, half), jnp.bfloat16)
    *selected, slots = call(
        select_kernel,
        "select",
        [piece] * count + [((max(8, count), 2 * full_len), jnp.float32)],
        [core, line],
        [routes, keep, other],
        scratch=[pltpu.VMEM((2 * full_len, half), jnp.bfloat16)],
    )
    near_in, near_out = call(
        load_kernel,
        "load",
        [(fc_in.shape, jnp.bfloat16), (fc_out.shape, jnp.bfloat16)],
        [],
        [],
        [fc_in, fc_out],
        scratch=[pltpu.SemaphoreType.DMA((2,))],
    )
    def run(p, q, p2, q2):
        keep, sent = call(
            expert_kernel,
            "expert",
            [((2, capacity, half), jnp.float32), ((2, capacity, half), jnp.bfloat16)],
            [core],
            [p, q, p2, q2, near_in, near_out],
            scratch=[pltpu.VMEM((2 * capacity, width), jnp.bfloat16)],
            vmem_mib=16,
        )
        return keep, swap(sent)

    def sums(keep, moving):
        both = keep + moving.astype(jnp.float32)
        return both, both[1].astype(jnp.bfloat16)

    def whole(both, across):
        return (both[0] + across.astype(jnp.float32)).astype(jnp.bfloat16)

    travelling = [exchange(selected[r], r) for r in range(1, count)]
    home = [None] * count
    ps, qs, kept, halves, wholes, boths = {}, {}, {}, {}, {}, {}
    p = selected[0]
    q = swap_owner(p)
    ps[0], qs[0] = p, q
    p = travelling[0]
    p = after(p, near_in)
    q = swap_owner(p)
    ps[1], qs[1] = p, q
    p = travelling[1]
    q = swap_owner(p)
    ps[2], qs[2] = p, q
    p = travelling[2]
    q = swap_owner(p)
    ps[3], qs[3] = p, q
    p, q = ps[0], qs[0]
    p2, q2 = swap(p), swap(q)
    kept[0], moving = run(p, q, p2, q2)
    boths[0], halves[0] = sums(kept[0], moving)
    p, q = ps[2], qs[2]
    q = after(q, qs[1])
    p2, q2 = swap(p), swap(q)
    q2 = after(q2, kept[0])
    kept[2], moving = run(p, q, p2, q2)
    boths[2], halves[2] = sums(kept[2], moving)
    p, q = ps[3], qs[3]
    q = after(q, kept[2])
    p2, q2 = swap(p), swap(q)
    q2 = after(q2, halves[2])
    kept[3], moving = run(p, q, p2, q2)
    boths[3], halves[3] = sums(kept[3], moving)
    p, q = ps[1], qs[1]
    p2, q2 = swap(p), swap(q)
    q2 = after(q2, kept[3])
    kept[1], moving = run(p, q, p2, q2)
    boths[1], halves[1] = sums(kept[1], moving)
    leaving = halves[2]
    across = swap_owner(leaving)
    wholes[2] = whole(boths[2], across)
    home[2] = exchange(wholes[2], 2)
    leaving = halves[3]
    across = swap_owner(leaving)
    wholes[3] = whole(boths[3], across)
    home[3] = exchange(wholes[3], 3)
    leaving = halves[1]
    leaving = after(leaving, halves[3])
    across = swap_owner(leaving)
    wholes[1] = whole(boths[1], across)
    home[1] = exchange(wholes[1], 1)
    leaving = halves[0]
    leaving = after(leaving, wholes[3])
    across = swap_owner(leaving)
    wholes[0] = whole(boths[0], across)
    home[0] = wholes[0]
    leaving, rows = call(
        combine_other_kernel,
        "combine_other",
        [((full_len, half), jnp.bfloat16), ((count * capacity, half), jnp.bfloat16)],
        [core, line],
        [routes, other_gates, slots, *home],
    )
    arriving = swap(leaving)
    (own,) = call(
        combine_own_kernel,
        "combine_own",
        [((full_len, half), jnp.bfloat16)],
        [core, line],
        [routes, gates, slots, rows, state],
    )
    (mixed,) = call(
        finish_kernel,
        "finish",
        [((full_len, width), jnp.bfloat16)],
        [core],
        [state, own, arriving],
    )
    return mixed


def expert_apply(slot_rows, fc_in, fc_out):
    width = slot_rows.shape[-1]
    flat_rows = slot_rows.reshape(-1, width)
    hidden = jax.nn.relu(jnp.dot(flat_rows, fc_in, preferred_element_type=jnp.float32)).astype(
        jnp.bfloat16
    )
    produced = jnp.dot(hidden, fc_out, preferred_element_type=jnp.float32)
    return produced.reshape(slot_rows.shape[0], slot_rows.shape[1], width)


def sparse_experts(normed, target_lengths, routes, router, fc_in, fc_out, capacity):
    full_len, width = normed.shape
    all_normed = lax.all_gather(normed[None], "section", axis=0, tiled=True)
    block_sents = all_normed.shape[0]
    block_rows = block_sents * full_len
    tok_rows = all_normed.reshape(block_rows, width)
    owners = lax.axis_size("expert")
    experts_count = owners // 2
    chosen_ids = routes.reshape(block_rows, 2)
    logits = jnp.dot(tok_rows, router, preferred_element_type=jnp.float32)
    onehot = chosen_ids[:, :, None] == jnp.arange(experts_count, dtype=jnp.int32)
    chosen = jnp.sum(jnp.where(onehot, logits[:, None, :], 0.0), axis=-1)
    first = jax.nn.sigmoid(chosen[:, 0] - chosen[:, 1])
    gates = jnp.stack([first, 1.0 - first], axis=-1)
    live = (jnp.arange(full_len, dtype=jnp.int32)[None, :] < target_lengths[:, None]).reshape(
        block_rows
    )
    flags = onehot.reshape(block_rows * 2, experts_count).astype(jnp.int32)
    earlier = jnp.cumsum(flags, axis=0) - flags
    slot = jnp.sum(flags * earlier, axis=-1).reshape(block_rows, 2)
    position = chosen_ids * capacity + slot
    dump_index = experts_count * capacity
    target = jnp.where(live[:, None], position, dump_index)
    row_ids = jnp.broadcast_to(jnp.arange(block_rows, dtype=jnp.int32)[:, None], (block_rows, 2))
    table = (
        jnp.full((dump_index + 1,), block_rows, jnp.int32)
        .at[target.reshape(-1)]
        .set(row_ids.reshape(-1))[:dump_index]
    )
    padded = jnp.concatenate([tok_rows, jnp.zeros((1, width), jnp.bfloat16)], axis=0)
    slot_buffer = padded[table].reshape(experts_count, capacity, width)
    outgoing = jnp.repeat(slot_buffer, 2, axis=0)
    returned = lax.all_to_all(
        expert_apply(
            lax.all_to_all(outgoing, "expert", split_axis=0, concat_axis=0, tiled=True),
            fc_in,
            fc_out,
        ).astype(jnp.bfloat16),
        "expert",
        split_axis=0,
        concat_axis=0,
        tiled=True,
    ).astype(jnp.float32)
    partial_value = jnp.sum(returned.reshape(experts_count, 2, capacity, width), axis=1)
    fetched = partial_value.reshape(dump_index, width)[jnp.where(live[:, None], position, 0)]
    weight = gates * live[:, None].astype(jnp.float32)
    contrib = jnp.sum(weight[:, :, None] * fetched, axis=1).reshape(block_sents, full_len, width)
    summed = lax.psum_scatter(contrib, "section", scatter_dimension=0, tiled=True)
    return summed[0]


def local(
    decoder_states,
    memory_keys,
    memory_values,
    source_lengths,
    target_lengths,
    routes,
    attn_gain,
    ffn_gain,
    router,
    fc_in,
    fc_out,
):
    core = lax.axis_index("section").astype(jnp.int32).reshape(1)
    by_choice = jnp.transpose(routes, (0, 2, 1))
    state, keep, send, gates, by_choice = attend(
        core, decoder_states, memory_keys, memory_values, source_lengths, target_lengths, by_choice,
        attn_gain, ffn_gain, router,
    )
    block_rows = routes.shape[0] * routes.shape[1]
    experts_count = router.shape[1]
    capacity = 2 * max(1, 3 * block_rows // (2 * experts_count))
    if capacity % 16 == 0 and experts_count & (experts_count - 1) == 0:
        mixed = line_experts(core, state, keep, send, gates, by_choice, fc_in, fc_out, capacity)
    else:
        halves = jnp.stack([keep, send])
        normed = jnp.concatenate([halves[core[0]], halves[1 - core[0]]], axis=-1)
        summed = sparse_experts(normed, target_lengths, routes, router, fc_in, fc_out, capacity)
        mixed = (state.astype(jnp.float32) + summed).astype(jnp.bfloat16)
    return mixed[None]


def solution(mesh):
    placed = (
        P(("groups", "expert", "section"), None, None),
        P(("groups", "expert"), None, "section"),
        P(("groups", "expert"), None, "section"),
        P(("groups", "expert", "section")),
        P(("groups", "expert")),
        P(("groups", "expert"), None, None),
        P(),
        P(),
        P(),
        P(None, ("expert", "section")),
        P(("expert", "section"), None),
    )
    return jax.shard_map(
        local,
        mesh=mesh,
        in_specs=placed,
        out_specs=P(("groups", "expert", "section"), None, None),
        check_vma=False,
    )
```

```python
import functools

import jax
import jax.numpy as jnp
from jax import lax
from jax.experimental import pallas as pl
from jax.experimental.pallas import tpu as pltpu
from jax.sharding import PartitionSpec as P

HEAD_DIM = 128


def layer_norm(values, gain):
    centered = values - jnp.mean(values, axis=-1, keepdims=True)
    spread = jnp.mean(centered * centered, axis=-1, keepdims=True)
    return (centered * lax.rsqrt(spread + 1e-05) * gain).astype(jnp.bfloat16)


VMEM = pl.BlockSpec(memory_space=pltpu.VMEM)
SMEM = pl.BlockSpec(memory_space=pltpu.SMEM)
HBM = pl.BlockSpec(memory_space=pltpu.HBM)


def call(kernel, name, outs, scalars, arrays, far=(), scratch=(), vmem_mib=12):
    return pl.pallas_call(
        kernel,
        out_shape=tuple(jax.ShapeDtypeStruct(*out) for out in outs),
        in_specs=[SMEM] * len(scalars) + [VMEM] * len(arrays) + [HBM] * len(far),
        out_specs=(VMEM,) * len(outs),
        scratch_shapes=list(scratch),
        compiler_params=pltpu.CompilerParams(vmem_limit_bytes=vmem_mib * 2**20),
        name=name,
    )(*scalars, *arrays, *(pltpu.with_memory_space_constraint(a, pltpu.HBM) for a in far))


def fetch(sems, *pairs):
    copies = [
        pltpu.make_async_copy(source, target, sems.at[i]) for i, (source, target) in enumerate(pairs)
    ]
    for copy in copies:
        copy.start()
    return copies


def part_of(part, half):
    return pl.ds(pl.multiple_of(part * half, half), half)


def attend_half(queries, keys, values, length):
    rows = queries.shape[0]
    heads = [slice(at, at + HEAD_DIM) for at in range(0, queries.shape[1], HEAD_DIM)]
    scores = jnp.concatenate(
        [
            lax.dot_general(
                queries[:, head],
                keys[:, head],
                (((1,), (1,)), ((), ())),
                preferred_element_type=jnp.float32,
            )
            for head in heads
        ],
        axis=0,
    ) * HEAD_DIM ** (-0.5)
    valid = lax.broadcasted_iota(jnp.int32, (1, keys.shape[0]), 1) < length
    scores = jnp.where(valid, scores, -jnp.inf)
    expon = jnp.exp(scores - jnp.max(scores, axis=-1, keepdims=True))
    weights = (expon / jnp.sum(expon, axis=-1, keepdims=True)).astype(jnp.bfloat16)
    return jnp.concatenate(
        [
            jnp.dot(
                weights[i * rows : (i + 1) * rows],
                values[:, head],
                preferred_element_type=jnp.float32,
            )
            for i, head in enumerate(heads)
        ],
        axis=1,
    )


def add_rounded(x, attended):
    return (x.astype(jnp.float32) + attended).astype(jnp.bfloat16)


def attend_own_kernel(
    core_ref,
    source_ref,
    x_in,
    gain_in,
    keys_in,
    values_in,
    state_ref,
    query_ref,
    rest_ref,
    x_ref,
    gain_ref,
    keys_ref,
    values_ref,
    scratch_ref,
    sems,
):
    core = core_ref[0]
    copies = fetch(
        sems,
        (x_in.at[0], x_ref),
        (gain_in, gain_ref),
        (keys_in.at[core], keys_ref),
        (values_in.at[core], values_ref),
    )
    half = keys_ref.shape[1]
    copies[0].wait()
    copies[1].wait()
    scratch_ref[...] = layer_norm(x_ref[...].astype(jnp.float32), gain_ref[...])
    own, other = part_of(core, half), part_of(1 - core, half)
    query_ref[...] = scratch_ref[:, other]
    rest_ref[...] = x_ref[:, other]
    copies[2].wait()
    copies[3].wait()
    attended = attend_half(scratch_ref[:, own], keys_ref[...], values_ref[...], source_ref[0])
    state_ref[...] = add_rounded(x_ref[:, own], attended)


def attend_other_kernel(
    core_ref,
    source_ref,
    own_ref,
    query_ref,
    rest_ref,
    keys_ref,
    values_ref,
    gain_in,
    router_in,
    routes_in,
    target_in,
    state_ref,
    keep_ref,
    send_ref,
    gates_ref,
    routes_ref,
    gain_ref,
    router_ref,
    target_ref,
    scratch_ref,
    sems,
):
    core = core_ref[0]
    copies = fetch(
        sems,
        (gain_in, gain_ref),
        (router_in, router_ref),
        (routes_in, routes_ref),
        (target_in, target_ref),
    )
    full_len, half = own_ref.shape
    own, other = part_of(core, half), part_of(1 - core, half)
    attended = attend_half(query_ref[...], keys_ref[core], values_ref[core], source_ref[0])
    state_ref[:, own] = own_ref[...]
    state_ref[:, other] = add_rounded(rest_ref[...], attended)
    copies[0].wait()
    scratch_ref[...] = layer_norm(state_ref[...].astype(jnp.float32), gain_ref[...])
    keep_ref[...] = scratch_ref[:, own]
    send_ref[...] = scratch_ref[:, other]
    for copy in copies[1:]:
        copy.wait()
    logits = lax.dot_general(
        router_ref[...],
        scratch_ref[...],
        (((1,), (1,)), ((), ())),
        preferred_element_type=jnp.float32,
    )
    names = lax.broadcasted_iota(jnp.int32, logits.shape, 0)
    routes = routes_ref[core]
    chosen = [
        jnp.sum(jnp.where(names == routes[k : k + 1], logits, 0.0), axis=0, keepdims=True)
        for k in range(2)
    ]
    first = jax.nn.sigmoid(chosen[0] - chosen[1])
    live = lax.broadcasted_iota(jnp.int32, (1, full_len), 1) < target_ref[core]
    gates_ref[0:1] = jnp.where(live, first, 0.0)
    gates_ref[1:2] = jnp.where(live, 1.0 - first, 0.0)


def slots_of(routes_ref, experts_count):
    sents, _, full_len = routes_ref.shape
    rows = sents * full_len
    ids = lax.broadcasted_iota(jnp.int32, (max(8, experts_count), full_len), 0)
    named = jnp.concatenate(
        [
            jnp.where((ids == routes_ref[s, 0:1]) | (ids == routes_ref[s, 1:2]), 1.0, 0.0)
            for s in range(sents)
        ],
        axis=1,
    )
    before = lax.broadcasted_iota(jnp.int32, (rows, rows), 0) < lax.broadcasted_iota(
        jnp.int32, (rows, rows), 1
    )
    earlier = jnp.dot(
        named.astype(jnp.bfloat16),
        jnp.where(before, 1.0, 0.0).astype(jnp.bfloat16),
        preferred_element_type=jnp.float32,
    )
    return named > 0.0, earlier


def select_kernel(core_ref, line_ref, routes_ref, own_ref, other_ref, *rest):
    pieces, (slots_ref, block_ref) = rest[:-2], rest[-2:]
    experts_count = len(pieces)
    full_len = own_ref.shape[0]
    capacity = pieces[0].shape[0]
    core = core_ref[0]
    block_ref[part_of(core, full_len)] = own_ref[...]
    block_ref[part_of(1 - core, full_len)] = other_ref[...]
    named, earlier = slots_of(routes_ref, experts_count)
    slots_ref[...] = earlier
    slot = jnp.where(named, earlier, -1.0)
    ids = lax.broadcasted_iota(jnp.int32, slot.shape, 0)
    numbers = lax.broadcasted_iota(jnp.int32, (capacity, slot.shape[1]), 0).astype(jnp.float32)
    for offset, piece_ref in enumerate(pieces):
        expert = line_ref[0] ^ offset
        wanted = jnp.sum(jnp.where(ids == expert, slot, 0.0), axis=0, keepdims=True)
        picks = jnp.where(numbers == wanted, 1.0, 0.0).astype(jnp.bfloat16)
        piece_ref[...] = jnp.dot(
            picks, block_ref[...], preferred_element_type=jnp.float32
        ).astype(jnp.bfloat16)


def expert_kernel(
    core_ref, p_ref, q_ref, p2_ref, q2_ref, in_ref, out_ref, keep_ref, send_ref, rows_ref
):
    core = core_ref[0]
    capacity, half = p_ref.shape
    rows_ref[:capacity, part_of(core, half)] = p_ref[...]
    rows_ref[capacity:, part_of(core, half)] = q_ref[...]
    rows_ref[:capacity, part_of(1 - core, half)] = p2_ref[...]
    rows_ref[capacity:, part_of(1 - core, half)] = q2_ref[...]
    hidden = jnp.dot(rows_ref[...], in_ref[...], preferred_element_type=jnp.float32)
    hidden = jnp.maximum(hidden, 0.0).astype(jnp.bfloat16)
    send = jnp.dot(
        hidden, out_ref[:, part_of(1 - core, half)], preferred_element_type=jnp.float32
    ).astype(jnp.bfloat16)
    send_ref[0] = send[:capacity]
    send_ref[1] = send[capacity:]
    keep = jnp.dot(hidden, out_ref[:, part_of(core, half)], preferred_element_type=jnp.float32)
    keep_ref[0] = keep[:capacity]
    keep_ref[1] = keep[capacity:]


def load_kernel(in_in, out_in, in_ref, out_ref, sems):
    for copy in fetch(sems, (in_in, in_ref), (out_in, out_ref)):
        copy.wait()


def gated_sum(sent, line, routes, gates, slots_ref, rows):
    full_len = routes.shape[1]
    experts_count = slots_ref.shape[0]
    parts = [slots_ref[:, at : at + full_len] for at in range(0, slots_ref.shape[1], full_len)]
    slots = jnp.where(sent == 0, parts[0], parts[1])
    ids = lax.broadcasted_iota(jnp.int32, (experts_count, full_len), 0)
    numbers = lax.broadcasted_iota(jnp.int32, (full_len, rows.shape[0]), 1).astype(jnp.float32)
    capacity = rows.shape[0] // (lax.axis_size("expert") // 2)
    total = None
    for k in range(2):
        route = routes[k : k + 1]
        slot = jnp.sum(jnp.where(ids == route, slots, 0.0), axis=0, keepdims=True)
        place = (route ^ line).astype(jnp.float32) * capacity + slot
        place, gate = (
            jnp.broadcast_to(row, (full_len, full_len)).T[:, :1]
            for row in (place, gates[k : k + 1])
        )
        picks = jnp.where(numbers == place, 1.0, 0.0).astype(jnp.bfloat16)
        term = gate * jnp.dot(picks, rows, preferred_element_type=jnp.float32)
        total = term if total is None else total + term
    return total


def combine_other_kernel(core_ref, line_ref, routes_ref, gates_ref, slots_ref, *rest):
    pieces, (other_ref, rows_ref) = rest[:-2], rest[-2:]
    capacity = pieces[0].shape[0]
    for offset, piece_ref in enumerate(pieces):
        rows_ref[offset * capacity : (offset + 1) * capacity] = piece_ref[...]
    sent = 1 - core_ref[0]
    other_ref[...] = gated_sum(
        sent, line_ref[0], routes_ref[sent], gates_ref[...], slots_ref, rows_ref[...]
    ).astype(jnp.bfloat16)


def combine_own_kernel(
    core_ref, line_ref, routes_ref, gates_ref, slots_ref, rows_ref, state_ref, own_ref
):
    core = core_ref[0]
    summed = gated_sum(
        core, line_ref[0], routes_ref[core], gates_ref[...], slots_ref, rows_ref[...]
    )
    own_ref[...] = add_rounded(state_ref[:, part_of(core, own_ref.shape[1])], summed)


def finish_kernel(core_ref, state_ref, own_ref, other_ref, mixed_ref):
    core = core_ref[0]
    half = own_ref.shape[-1]
    mixed_ref[:, part_of(core, half)] = own_ref[...]
    span = part_of(1 - core, half)
    mixed_ref[:, span] = add_rounded(state_ref[:, span], other_ref[...].astype(jnp.float32))


def swap(values):
    return lax.ppermute(values, "section", [(0, 1), (1, 0)])


def swap_owner(values):
    owners = lax.axis_size("expert")
    return lax.ppermute(values, "expert", [(i, i ^ 1) for i in range(owners)])


def exchange(values, offset):
    owners = lax.axis_size("expert")
    return lax.ppermute(values, "expert", [(i, i ^ (2 * offset)) for i in range(owners)])


def after_kernel(*refs):
    pass


def after(value, *firsts):
    return pl.pallas_call(
        after_kernel,
        out_shape=jax.ShapeDtypeStruct(value.shape, value.dtype),
        in_specs=[pl.BlockSpec(memory_space=pl.ANY)] * (1 + len(firsts)),
        out_specs=pl.BlockSpec(memory_space=pl.ANY),
        input_output_aliases={0: 0},
        compiler_params=pltpu.CompilerParams(vmem_limit_bytes=2**20),
        name="after",
    )(value, *firsts)


def attend(
    core, decoder_states, memory_keys, memory_values, source_lengths, target_lengths, routes,
    attn_gain, ffn_gain, router,
):
    full_len, width = decoder_states.shape[1:]
    half = (full_len, width // 2)
    memory = memory_keys.shape[1:]
    other_keys, other_values = swap(memory_keys), swap(memory_values)
    own, query, rest = call(
        attend_own_kernel,
        "attend_own",
        [(half, jnp.bfloat16)] * 3,
        [core, source_lengths],
        [],
        [decoder_states, attn_gain[None], memory_keys, memory_values],
        scratch=[
            pltpu.VMEM((full_len, width), jnp.bfloat16),
            pltpu.VMEM((1, width), jnp.float32),
            pltpu.VMEM(memory, jnp.bfloat16),
            pltpu.VMEM(memory, jnp.bfloat16),
            pltpu.VMEM((full_len, width), jnp.bfloat16),
            pltpu.SemaphoreType.DMA((4,)),
        ],
    )
    return call(
        attend_other_kernel,
        "attend_other",
        [
            ((full_len, width), jnp.bfloat16),
            (half, jnp.bfloat16),
            (half, jnp.bfloat16),
            ((2, full_len), jnp.float32),
            (routes.shape, jnp.int32),
        ],
        [core, source_lengths],
        [own, query, rest, other_keys, other_values],
        [ffn_gain[None], router.T, routes, target_lengths],
        scratch=[
            pltpu.VMEM((1, width), jnp.float32),
            pltpu.VMEM(router.shape[::-1], jnp.bfloat16),
            pltpu.SMEM(target_lengths.shape, jnp.int32),
            pltpu.VMEM((full_len, width), jnp.bfloat16),
            pltpu.SemaphoreType.DMA((4,)),
        ],
    )


def line_experts(core, state, keep, send, gates, routes, fc_in, fc_out, capacity):
    full_len, width = state.shape
    half = width // 2
    count = lax.axis_size("expert") // 2
    line = (lax.axis_index("expert") // 2).astype(jnp.int32).reshape(1)
    other = swap(send)
    other_gates = swap(gates)
    piece = ((capacity, half), jnp.bfloat16)
    *selected, slots = call(
        select_kernel,
        "select",
        [piece] * count + [((max(8, count), 2 * full_len), jnp.float32)],
        [core, line],
        [routes, keep, other],
        scratch=[pltpu.VMEM((2 * full_len, half), jnp.bfloat16)],
    )
    near_in, near_out = call(
        load_kernel,
        "load",
        [(fc_in.shape, jnp.bfloat16), (fc_out.shape, jnp.bfloat16)],
        [],
        [],
        [fc_in, fc_out],
        scratch=[pltpu.SemaphoreType.DMA((2,))],
    )
    def run(p, q, p2, q2):
        keep, sent = call(
            expert_kernel,
            "expert",
            [((2, capacity, half), jnp.float32), ((2, capacity, half), jnp.bfloat16)],
            [core],
            [p, q, p2, q2, near_in, near_out],
            scratch=[pltpu.VMEM((2 * capacity, width), jnp.bfloat16)],
            vmem_mib=16,
        )
        return keep, swap(sent)

    def sums(keep, moving):
        both = keep + moving.astype(jnp.float32)
        return both, both[1].astype(jnp.bfloat16)

    def whole(both, across):
        return (both[0] + across.astype(jnp.float32)).astype(jnp.bfloat16)

    travelling = [exchange(selected[r], r) for r in range(1, count)]
    home = [None] * count
    ps, qs, kept, halves, wholes, boths = {}, {}, {}, {}, {}, {}
    p = selected[0]
    q = swap_owner(p)
    ps[0], qs[0] = p, q
    p = travelling[0]
    q = swap_owner(p)
    ps[1], qs[1] = p, q
    p = travelling[1]
    p = after(p, near_in)
    q = swap_owner(p)
    ps[2], qs[2] = p, q
    p = travelling[2]
    q = swap_owner(p)
    ps[3], qs[3] = p, q
    p, q = ps[0], qs[0]
    p2, q2 = swap(p), swap(q)
    kept[0], moving = run(p, q, p2, q2)
    boths[0], halves[0] = sums(kept[0], moving)
    p, q = ps[2], qs[2]
    p2, q2 = swap(p), swap(q)
    q2 = after(q2, kept[0])
    kept[2], moving = run(p, q, p2, q2)
    boths[2], halves[2] = sums(kept[2], moving)
    p, q = ps[1], qs[1]
    p2, q2 = swap(p), swap(q)
    kept[1], moving = run(p, q, p2, q2)
    boths[1], halves[1] = sums(kept[1], moving)
    p, q = ps[3], qs[3]
    q = after(q, kept[2])
    p2, q2 = swap(p), swap(q)
    q2 = after(q2, kept[1], halves[2])
    kept[3], moving = run(p, q, p2, q2)
    boths[3], halves[3] = sums(kept[3], moving)
    leaving = halves[2]
    across = swap_owner(leaving)
    wholes[2] = whole(boths[2], across)
    home[2] = exchange(wholes[2], 2)
    leaving = halves[3]
    across = swap_owner(leaving)
    wholes[3] = whole(boths[3], across)
    home[3] = exchange(wholes[3], 3)
    leaving = halves[1]
    leaving = after(leaving, halves[3])
    across = swap_owner(leaving)
    wholes[1] = whole(boths[1], across)
    home[1] = exchange(wholes[1], 1)
    leaving = halves[0]
    leaving = after(leaving, wholes[3])
    across = swap_owner(leaving)
    wholes[0] = whole(boths[0], across)
    home[0] = wholes[0]
    leaving, rows = call(
        combine_other_kernel,
        "combine_other",
        [((full_len, half), jnp.bfloat16), ((count * capacity, half), jnp.bfloat16)],
        [core, line],
        [routes, other_gates, slots, *home],
    )
    arriving = swap(leaving)
    (own,) = call(
        combine_own_kernel,
        "combine_own",
        [((full_len, half), jnp.bfloat16)],
        [core, line],
        [routes, gates, slots, rows, state],
    )
    (mixed,) = call(
        finish_kernel,
        "finish",
        [((full_len, width), jnp.bfloat16)],
        [core],
        [state, own, arriving],
    )
    return mixed


def expert_apply(slot_rows, fc_in, fc_out):
    width = slot_rows.shape[-1]
    flat_rows = slot_rows.reshape(-1, width)
    hidden = jax.nn.relu(jnp.dot(flat_rows, fc_in, preferred_element_type=jnp.float32)).astype(
        jnp.bfloat16
    )
    produced = jnp.dot(hidden, fc_out, preferred_element_type=jnp.float32)
    return produced.reshape(slot_rows.shape[0], slot_rows.shape[1], width)


def sparse_experts(normed, target_lengths, routes, router, fc_in, fc_out, capacity):
    full_len, width = normed.shape
    all_normed = lax.all_gather(normed[None], "section", axis=0, tiled=True)
    block_sents = all_normed.shape[0]
    block_rows = block_sents * full_len
    tok_rows = all_normed.reshape(block_rows, width)
    owners = lax.axis_size("expert")
    experts_count = owners // 2
    chosen_ids = routes.reshape(block_rows, 2)
    logits = jnp.dot(tok_rows, router, preferred_element_type=jnp.float32)
    onehot = chosen_ids[:, :, None] == jnp.arange(experts_count, dtype=jnp.int32)
    chosen = jnp.sum(jnp.where(onehot, logits[:, None, :], 0.0), axis=-1)
    first = jax.nn.sigmoid(chosen[:, 0] - chosen[:, 1])
    gates = jnp.stack([first, 1.0 - first], axis=-1)
    live = (jnp.arange(full_len, dtype=jnp.int32)[None, :] < target_lengths[:, None]).reshape(
        block_rows
    )
    flags = onehot.reshape(block_rows * 2, experts_count).astype(jnp.int32)
    earlier = jnp.cumsum(flags, axis=0) - flags
    slot = jnp.sum(flags * earlier, axis=-1).reshape(block_rows, 2)
    position = chosen_ids * capacity + slot
    dump_index = experts_count * capacity
    target = jnp.where(live[:, None], position, dump_index)
    row_ids = jnp.broadcast_to(jnp.arange(block_rows, dtype=jnp.int32)[:, None], (block_rows, 2))
    table = (
        jnp.full((dump_index + 1,), block_rows, jnp.int32)
        .at[target.reshape(-1)]
        .set(row_ids.reshape(-1))[:dump_index]
    )
    padded = jnp.concatenate([tok_rows, jnp.zeros((1, width), jnp.bfloat16)], axis=0)
    slot_buffer = padded[table].reshape(experts_count, capacity, width)
    outgoing = jnp.repeat(slot_buffer, 2, axis=0)
    returned = lax.all_to_all(
        expert_apply(
            lax.all_to_all(outgoing, "expert", split_axis=0, concat_axis=0, tiled=True),
            fc_in,
            fc_out,
        ).astype(jnp.bfloat16),
        "expert",
        split_axis=0,
        concat_axis=0,
        tiled=True,
    ).astype(jnp.float32)
    partial_value = jnp.sum(returned.reshape(experts_count, 2, capacity, width), axis=1)
    fetched = partial_value.reshape(dump_index, width)[jnp.where(live[:, None], position, 0)]
    weight = gates * live[:, None].astype(jnp.float32)
    contrib = jnp.sum(weight[:, :, None] * fetched, axis=1).reshape(block_sents, full_len, width)
    summed = lax.psum_scatter(contrib, "section", scatter_dimension=0, tiled=True)
    return summed[0]


def local(
    decoder_states,
    memory_keys,
    memory_values,
    source_lengths,
    target_lengths,
    routes,
    attn_gain,
    ffn_gain,
    router,
    fc_in,
    fc_out,
):
    core = lax.axis_index("section").astype(jnp.int32).reshape(1)
    by_choice = jnp.transpose(routes, (0, 2, 1))
    state, keep, send, gates, by_choice = attend(
        core, decoder_states, memory_keys, memory_values, source_lengths, target_lengths, by_choice,
        attn_gain, ffn_gain, router,
    )
    block_rows = routes.shape[0] * routes.shape[1]
    experts_count = router.shape[1]
    capacity = 2 * max(1, 3 * block_rows // (2 * experts_count))
    if capacity % 16 == 0 and experts_count & (experts_count - 1) == 0:
        mixed = line_experts(core, state, keep, send, gates, by_choice, fc_in, fc_out, capacity)
    else:
        halves = jnp.stack([keep, send])
        normed = jnp.concatenate([halves[core[0]], halves[1 - core[0]]], axis=-1)
        summed = sparse_experts(normed, target_lengths, routes, router, fc_in, fc_out, capacity)
        mixed = (state.astype(jnp.float32) + summed).astype(jnp.bfloat16)
    return mixed[None]


def solution(mesh):
    placed = (
        P(("groups", "expert", "section"), None, None),
        P(("groups", "expert"), None, "section"),
        P(("groups", "expert"), None, "section"),
        P(("groups", "expert", "section")),
        P(("groups", "expert")),
        P(("groups", "expert"), None, None),
        P(),
        P(),
        P(),
        P(None, ("expert", "section")),
        P(("expert", "section"), None),
    )
    return jax.shard_map(
        local,
        mesh=mesh,
        in_specs=placed,
        out_specs=P(("groups", "expert", "section"), None, None),
        check_vma=False,
    )
```

```python
import functools

import jax
import jax.numpy as jnp
from jax import lax
from jax.experimental import pallas as pl
from jax.experimental.pallas import tpu as pltpu
from jax.sharding import PartitionSpec as P

HEAD_DIM = 128


def layer_norm(values, gain):
    centered = values - jnp.mean(values, axis=-1, keepdims=True)
    spread = jnp.mean(centered * centered, axis=-1, keepdims=True)
    return (centered * lax.rsqrt(spread + 1e-05) * gain).astype(jnp.bfloat16)


VMEM = pl.BlockSpec(memory_space=pltpu.VMEM)
SMEM = pl.BlockSpec(memory_space=pltpu.SMEM)
HBM = pl.BlockSpec(memory_space=pltpu.HBM)


def call(kernel, name, outs, scalars, arrays, far=(), scratch=(), vmem_mib=12):
    return pl.pallas_call(
        kernel,
        out_shape=tuple(jax.ShapeDtypeStruct(*out) for out in outs),
        in_specs=[SMEM] * len(scalars) + [VMEM] * len(arrays) + [HBM] * len(far),
        out_specs=(VMEM,) * len(outs),
        scratch_shapes=list(scratch),
        compiler_params=pltpu.CompilerParams(vmem_limit_bytes=vmem_mib * 2**20),
        name=name,
    )(*scalars, *arrays, *(pltpu.with_memory_space_constraint(a, pltpu.HBM) for a in far))


def fetch(sems, *pairs):
    copies = [
        pltpu.make_async_copy(source, target, sems.at[i]) for i, (source, target) in enumerate(pairs)
    ]
    for copy in copies:
        copy.start()
    return copies


def part_of(part, half):
    return pl.ds(pl.multiple_of(part * half, half), half)


def attend_half(queries, keys, values, length):
    rows = queries.shape[0]
    heads = [slice(at, at + HEAD_DIM) for at in range(0, queries.shape[1], HEAD_DIM)]
    scores = jnp.concatenate(
        [
            lax.dot_general(
                queries[:, head],
                keys[:, head],
                (((1,), (1,)), ((), ())),
                preferred_element_type=jnp.float32,
            )
            for head in heads
        ],
        axis=0,
    ) * HEAD_DIM ** (-0.5)
    valid = lax.broadcasted_iota(jnp.int32, (1, keys.shape[0]), 1) < length
    scores = jnp.where(valid, scores, -jnp.inf)
    expon = jnp.exp(scores - jnp.max(scores, axis=-1, keepdims=True))
    weights = (expon / jnp.sum(expon, axis=-1, keepdims=True)).astype(jnp.bfloat16)
    return jnp.concatenate(
        [
            jnp.dot(
                weights[i * rows : (i + 1) * rows],
                values[:, head],
                preferred_element_type=jnp.float32,
            )
            for i, head in enumerate(heads)
        ],
        axis=1,
    )


def add_rounded(x, attended):
    return (x.astype(jnp.float32) + attended).astype(jnp.bfloat16)


def attend_own_kernel(
    core_ref,
    source_ref,
    x_in,
    gain_in,
    keys_in,
    values_in,
    state_ref,
    query_ref,
    rest_ref,
    x_ref,
    gain_ref,
    keys_ref,
    values_ref,
    scratch_ref,
    sems,
):
    core = core_ref[0]
    copies = fetch(
        sems,
        (x_in.at[0], x_ref),
        (gain_in, gain_ref),
        (keys_in.at[core], keys_ref),
        (values_in.at[core], values_ref),
    )
    half = keys_ref.shape[1]
    copies[0].wait()
    copies[1].wait()
    scratch_ref[...] = layer_norm(x_ref[...].astype(jnp.float32), gain_ref[...])
    own, other = part_of(core, half), part_of(1 - core, half)
    query_ref[...] = scratch_ref[:, other]
    rest_ref[...] = x_ref[:, other]
    copies[2].wait()
    copies[3].wait()
    attended = attend_half(scratch_ref[:, own], keys_ref[...], values_ref[...], source_ref[0])
    state_ref[...] = add_rounded(x_ref[:, own], attended)


def attend_other_kernel(
    core_ref,
    source_ref,
    own_ref,
    query_ref,
    rest_ref,
    keys_ref,
    values_ref,
    gain_in,
    router_in,
    routes_in,
    target_in,
    state_ref,
    keep_ref,
    send_ref,
    gates_ref,
    routes_ref,
    gain_ref,
    router_ref,
    target_ref,
    scratch_ref,
    sems,
):
    core = core_ref[0]
    copies = fetch(
        sems,
        (gain_in, gain_ref),
        (router_in, router_ref),
        (routes_in, routes_ref),
        (target_in, target_ref),
    )
    full_len, half = own_ref.shape
    own, other = part_of(core, half), part_of(1 - core, half)
    attended = attend_half(query_ref[...], keys_ref[core], values_ref[core], source_ref[0])
    state_ref[:, own] = own_ref[...]
    state_ref[:, other] = add_rounded(rest_ref[...], attended)
    copies[0].wait()
    scratch_ref[...] = layer_norm(state_ref[...].astype(jnp.float32), gain_ref[...])
    keep_ref[...] = scratch_ref[:, own]
    send_ref[...] = scratch_ref[:, other]
    for copy in copies[1:]:
        copy.wait()
    logits = lax.dot_general(
        router_ref[...],
        scratch_ref[...],
        (((1,), (1,)), ((), ())),
        preferred_element_type=jnp.float32,
    )
    names = lax.broadcasted_iota(jnp.int32, logits.shape, 0)
    routes = routes_ref[core]
    chosen = [
        jnp.sum(jnp.where(names == routes[k : k + 1], logits, 0.0), axis=0, keepdims=True)
        for k in range(2)
    ]
    first = jax.nn.sigmoid(chosen[0] - chosen[1])
    live = lax.broadcasted_iota(jnp.int32, (1, full_len), 1) < target_ref[core]
    gates_ref[0:1] = jnp.where(live, first, 0.0)
    gates_ref[1:2] = jnp.where(live, 1.0 - first, 0.0)


def slots_of(routes_ref, experts_count):
    sents, _, full_len = routes_ref.shape
    rows = sents * full_len
    ids = lax.broadcasted_iota(jnp.int32, (max(8, experts_count), full_len), 0)
    named = jnp.concatenate(
        [
            jnp.where((ids == routes_ref[s, 0:1]) | (ids == routes_ref[s, 1:2]), 1.0, 0.0)
            for s in range(sents)
        ],
        axis=1,
    )
    before = lax.broadcasted_iota(jnp.int32, (rows, rows), 0) < lax.broadcasted_iota(
        jnp.int32, (rows, rows), 1
    )
    earlier = jnp.dot(
        named.astype(jnp.bfloat16),
        jnp.where(before, 1.0, 0.0).astype(jnp.bfloat16),
        preferred_element_type=jnp.float32,
    )
    return named > 0.0, earlier


def select_kernel(core_ref, line_ref, routes_ref, own_ref, other_ref, *rest):
    pieces, (slots_ref, block_ref) = rest[:-2], rest[-2:]
    experts_count = len(pieces)
    full_len = own_ref.shape[0]
    capacity = pieces[0].shape[0]
    core = core_ref[0]
    block_ref[part_of(core, full_len)] = own_ref[...]
    block_ref[part_of(1 - core, full_len)] = other_ref[...]
    named, earlier = slots_of(routes_ref, experts_count)
    slots_ref[...] = earlier
    slot = jnp.where(named, earlier, -1.0)
    ids = lax.broadcasted_iota(jnp.int32, slot.shape, 0)
    numbers = lax.broadcasted_iota(jnp.int32, (capacity, slot.shape[1]), 0).astype(jnp.float32)
    for offset, piece_ref in enumerate(pieces):
        expert = line_ref[0] ^ offset
        wanted = jnp.sum(jnp.where(ids == expert, slot, 0.0), axis=0, keepdims=True)
        picks = jnp.where(numbers == wanted, 1.0, 0.0).astype(jnp.bfloat16)
        piece_ref[...] = jnp.dot(
            picks, block_ref[...], preferred_element_type=jnp.float32
        ).astype(jnp.bfloat16)


def expert_kernel(
    core_ref, p_ref, q_ref, p2_ref, q2_ref, in_ref, out_ref, keep_ref, send_ref, rows_ref
):
    core = core_ref[0]
    capacity, half = p_ref.shape
    rows_ref[:capacity, part_of(core, half)] = p_ref[...]
    rows_ref[capacity:, part_of(core, half)] = q_ref[...]
    rows_ref[:capacity, part_of(1 - core, half)] = p2_ref[...]
    rows_ref[capacity:, part_of(1 - core, half)] = q2_ref[...]
    hidden = jnp.dot(rows_ref[...], in_ref[...], preferred_element_type=jnp.float32)
    hidden = jnp.maximum(hidden, 0.0).astype(jnp.bfloat16)
    send = jnp.dot(
        hidden, out_ref[:, part_of(1 - core, half)], preferred_element_type=jnp.float32
    ).astype(jnp.bfloat16)
    send_ref[0] = send[:capacity]
    send_ref[1] = send[capacity:]
    keep = jnp.dot(hidden, out_ref[:, part_of(core, half)], preferred_element_type=jnp.float32)
    keep_ref[0] = keep[:capacity]
    keep_ref[1] = keep[capacity:]


def load_kernel(in_in, out_in, in_ref, out_ref, sems):
    for copy in fetch(sems, (in_in, in_ref), (out_in, out_ref)):
        copy.wait()


def gated_sum(sent, line, routes, gates, slots_ref, pieces):
    full_len = routes.shape[1]
    experts_count = slots_ref.shape[0]
    parts = [slots_ref[:, at : at + full_len] for at in range(0, slots_ref.shape[1], full_len)]
    slots = jnp.where(sent == 0, parts[0], parts[1])
    ids = lax.broadcasted_iota(jnp.int32, (experts_count, full_len), 0)
    capacity = pieces[0].shape[0]
    numbers = lax.broadcasted_iota(jnp.int32, (full_len, capacity), 1).astype(jnp.float32)
    total = None
    for k in range(2):
        route = routes[k : k + 1]
        slot = jnp.sum(jnp.where(ids == route, slots, 0.0), axis=0, keepdims=True)
        place = (route ^ line).astype(jnp.float32) * capacity + slot
        place, gate = (
            jnp.broadcast_to(row, (full_len, full_len)).T[:, :1]
            for row in (place, gates[k : k + 1])
        )
        found = None
        for offset, piece in enumerate(pieces):
            picks = jnp.where(numbers == place - offset * capacity, 1.0, 0.0).astype(jnp.bfloat16)
            part = jnp.dot(picks, piece[...], preferred_element_type=jnp.float32)
            found = part if found is None else found + part
        total = gate * found if total is None else total + gate * found
    return total


def combine_other_kernel(core_ref, line_ref, routes_ref, gates_ref, slots_ref, *rest):
    pieces, other_ref = rest[:-1], rest[-1]
    sent = 1 - core_ref[0]
    other_ref[...] = gated_sum(
        sent, line_ref[0], routes_ref[sent], gates_ref[...], slots_ref, pieces
    ).astype(jnp.bfloat16)


def combine_own_kernel(core_ref, line_ref, routes_ref, gates_ref, slots_ref, state_ref, *rest):
    pieces, own_ref = rest[:-1], rest[-1]
    core = core_ref[0]
    summed = gated_sum(core, line_ref[0], routes_ref[core], gates_ref[...], slots_ref, pieces)
    own_ref[...] = add_rounded(state_ref[:, part_of(core, own_ref.shape[1])], summed)


def finish_kernel(core_ref, state_ref, own_ref, other_ref, mixed_ref):
    core = core_ref[0]
    half = own_ref.shape[-1]
    mixed_ref[:, part_of(core, half)] = own_ref[...]
    span = part_of(1 - core, half)
    mixed_ref[:, span] = add_rounded(state_ref[:, span], other_ref[...].astype(jnp.float32))


def swap(values):
    return lax.ppermute(values, "section", [(0, 1), (1, 0)])


def swap_owner(values):
    owners = lax.axis_size("expert")
    return lax.ppermute(values, "expert", [(i, i ^ 1) for i in range(owners)])


def exchange(values, offset):
    owners = lax.axis_size("expert")
    return lax.ppermute(values, "expert", [(i, i ^ (2 * offset)) for i in range(owners)])


def after_kernel(*refs):
    pass


def after(value, *firsts):
    return pl.pallas_call(
        after_kernel,
        out_shape=jax.ShapeDtypeStruct(value.shape, value.dtype),
        in_specs=[pl.BlockSpec(memory_space=pl.ANY)] * (1 + len(firsts)),
        out_specs=pl.BlockSpec(memory_space=pl.ANY),
        input_output_aliases={0: 0},
        compiler_params=pltpu.CompilerParams(vmem_limit_bytes=2**20),
        name="after",
    )(value, *firsts)


def attend(
    core, decoder_states, memory_keys, memory_values, source_lengths, target_lengths, routes,
    attn_gain, ffn_gain, router,
):
    full_len, width = decoder_states.shape[1:]
    half = (full_len, width // 2)
    memory = memory_keys.shape[1:]
    other_keys, other_values = swap(memory_keys), swap(memory_values)
    own, query, rest = call(
        attend_own_kernel,
        "attend_own",
        [(half, jnp.bfloat16)] * 3,
        [core, source_lengths],
        [],
        [decoder_states, attn_gain[None], memory_keys, memory_values],
        scratch=[
            pltpu.VMEM((full_len, width), jnp.bfloat16),
            pltpu.VMEM((1, width), jnp.float32),
            pltpu.VMEM(memory, jnp.bfloat16),
            pltpu.VMEM(memory, jnp.bfloat16),
            pltpu.VMEM((full_len, width), jnp.bfloat16),
            pltpu.SemaphoreType.DMA((4,)),
        ],
    )
    return call(
        attend_other_kernel,
        "attend_other",
        [
            ((full_len, width), jnp.bfloat16),
            (half, jnp.bfloat16),
            (half, jnp.bfloat16),
            ((2, full_len), jnp.float32),
            (routes.shape, jnp.int32),
        ],
        [core, source_lengths],
        [own, query, rest, other_keys, other_values],
        [ffn_gain[None], router.T, routes, target_lengths],
        scratch=[
            pltpu.VMEM((1, width), jnp.float32),
            pltpu.VMEM(router.shape[::-1], jnp.bfloat16),
            pltpu.SMEM(target_lengths.shape, jnp.int32),
            pltpu.VMEM((full_len, width), jnp.bfloat16),
            pltpu.SemaphoreType.DMA((4,)),
        ],
    )


def line_experts(core, state, keep, send, gates, routes, fc_in, fc_out, capacity):
    full_len, width = state.shape
    half = width // 2
    count = lax.axis_size("expert") // 2
    line = (lax.axis_index("expert") // 2).astype(jnp.int32).reshape(1)
    other = swap(send)
    other_gates = swap(gates)
    piece = ((capacity, half), jnp.bfloat16)
    *selected, slots = call(
        select_kernel,
        "select",
        [piece] * count + [((max(8, count), 2 * full_len), jnp.float32)],
        [core, line],
        [routes, keep, other],
        scratch=[pltpu.VMEM((2 * full_len, half), jnp.bfloat16)],
    )
    near_in, near_out = call(
        load_kernel,
        "load",
        [(fc_in.shape, jnp.bfloat16), (fc_out.shape, jnp.bfloat16)],
        [],
        [],
        [fc_in, fc_out],
        scratch=[pltpu.SemaphoreType.DMA((2,))],
    )
    def run(p, q, p2, q2):
        keep, sent = call(
            expert_kernel,
            "expert",
            [((2, capacity, half), jnp.float32), ((2, capacity, half), jnp.bfloat16)],
            [core],
            [p, q, p2, q2, near_in, near_out],
            scratch=[pltpu.VMEM((2 * capacity, width), jnp.bfloat16)],
            vmem_mib=16,
        )
        return keep, swap(sent)

    def sums(keep, moving):
        both = keep + moving.astype(jnp.float32)
        return both, both[1].astype(jnp.bfloat16)

    def whole(both, across):
        return (both[0] + across.astype(jnp.float32)).astype(jnp.bfloat16)

    travelling = [exchange(selected[r], r) for r in range(1, count)]
    home = [None] * count
    ps, qs, kept, halves, wholes, boths = {}, {}, {}, {}, {}, {}
    p = selected[0]
    q = swap_owner(p)
    ps[0], qs[0] = p, q
    p = travelling[0]
    p = after(p, near_in)
    q = swap_owner(p)
    ps[1], qs[1] = p, q
    p = travelling[1]
    q = swap_owner(p)
    ps[2], qs[2] = p, q
    p = travelling[2]
    q = swap_owner(p)
    ps[3], qs[3] = p, q
    p, q = ps[0], qs[0]
    p2, q2 = swap(p), swap(q)
    kept[0], moving = run(p, q, p2, q2)
    boths[0], halves[0] = sums(kept[0], moving)
    p, q = ps[1], qs[1]
    p2, q2 = swap(p), swap(q)
    kept[1], moving = run(p, q, p2, q2)
    boths[1], halves[1] = sums(kept[1], moving)
    p, q = ps[2], qs[2]
    p2, q2 = swap(p), swap(q)
    q2 = after(q2, kept[0], kept[1])
    kept[2], moving = run(p, q, p2, q2)
    boths[2], halves[2] = sums(kept[2], moving)
    p, q = ps[3], qs[3]
    q = after(q, kept[2])
    p2, q2 = swap(p), swap(q)
    q2 = after(q2, halves[2])
    kept[3], moving = run(p, q, p2, q2)
    boths[3], halves[3] = sums(kept[3], moving)
    leaving = halves[2]
    across = swap_owner(leaving)
    wholes[2] = whole(boths[2], across)
    home[2] = exchange(wholes[2], 2)
    leaving = halves[3]
    across = swap_owner(leaving)
    wholes[3] = whole(boths[3], across)
    home[3] = exchange(wholes[3], 3)
    leaving = halves[1]
    leaving = after(leaving, halves[3])
    across = swap_owner(leaving)
    wholes[1] = whole(boths[1], across)
    home[1] = exchange(wholes[1], 1)
    leaving = halves[0]
    leaving = after(leaving, wholes[3])
    across = swap_owner(leaving)
    wholes[0] = whole(boths[0], across)
    home[0] = wholes[0]
    (leaving,) = call(
        combine_other_kernel,
        "combine_other",
        [((full_len, half), jnp.bfloat16)],
        [core, line],
        [routes, other_gates, slots, *home],
    )
    arriving = swap(leaving)
    (own,) = call(
        combine_own_kernel,
        "combine_own",
        [((full_len, half), jnp.bfloat16)],
        [core, line],
        [routes, gates, slots, state, *home],
    )
    (mixed,) = call(
        finish_kernel,
        "finish",
        [((full_len, width), jnp.bfloat16)],
        [core],
        [state, own, arriving],
    )
    return mixed


def expert_apply(slot_rows, fc_in, fc_out):
    width = slot_rows.shape[-1]
    flat_rows = slot_rows.reshape(-1, width)
    hidden = jax.nn.relu(jnp.dot(flat_rows, fc_in, preferred_element_type=jnp.float32)).astype(
        jnp.bfloat16
    )
    produced = jnp.dot(hidden, fc_out, preferred_element_type=jnp.float32)
    return produced.reshape(slot_rows.shape[0], slot_rows.shape[1], width)


def sparse_experts(normed, target_lengths, routes, router, fc_in, fc_out, capacity):
    full_len, width = normed.shape
    all_normed = lax.all_gather(normed[None], "section", axis=0, tiled=True)
    block_sents = all_normed.shape[0]
    block_rows = block_sents * full_len
    tok_rows = all_normed.reshape(block_rows, width)
    owners = lax.axis_size("expert")
    experts_count = owners // 2
    chosen_ids = routes.reshape(block_rows, 2)
    logits = jnp.dot(tok_rows, router, preferred_element_type=jnp.float32)
    onehot = chosen_ids[:, :, None] == jnp.arange(experts_count, dtype=jnp.int32)
    chosen = jnp.sum(jnp.where(onehot, logits[:, None, :], 0.0), axis=-1)
    first = jax.nn.sigmoid(chosen[:, 0] - chosen[:, 1])
    gates = jnp.stack([first, 1.0 - first], axis=-1)
    live = (jnp.arange(full_len, dtype=jnp.int32)[None, :] < target_lengths[:, None]).reshape(
        block_rows
    )
    flags = onehot.reshape(block_rows * 2, experts_count).astype(jnp.int32)
    earlier = jnp.cumsum(flags, axis=0) - flags
    slot = jnp.sum(flags * earlier, axis=-1).reshape(block_rows, 2)
    position = chosen_ids * capacity + slot
    dump_index = experts_count * capacity
    target = jnp.where(live[:, None], position, dump_index)
    row_ids = jnp.broadcast_to(jnp.arange(block_rows, dtype=jnp.int32)[:, None], (block_rows, 2))
    table = (
        jnp.full((dump_index + 1,), block_rows, jnp.int32)
        .at[target.reshape(-1)]
        .set(row_ids.reshape(-1))[:dump_index]
    )
    padded = jnp.concatenate([tok_rows, jnp.zeros((1, width), jnp.bfloat16)], axis=0)
    slot_buffer = padded[table].reshape(experts_count, capacity, width)
    outgoing = jnp.repeat(slot_buffer, 2, axis=0)
    returned = lax.all_to_all(
        expert_apply(
            lax.all_to_all(outgoing, "expert", split_axis=0, concat_axis=0, tiled=True),
            fc_in,
            fc_out,
        ).astype(jnp.bfloat16),
        "expert",
        split_axis=0,
        concat_axis=0,
        tiled=True,
    ).astype(jnp.float32)
    partial_value = jnp.sum(returned.reshape(experts_count, 2, capacity, width), axis=1)
    fetched = partial_value.reshape(dump_index, width)[jnp.where(live[:, None], position, 0)]
    weight = gates * live[:, None].astype(jnp.float32)
    contrib = jnp.sum(weight[:, :, None] * fetched, axis=1).reshape(block_sents, full_len, width)
    summed = lax.psum_scatter(contrib, "section", scatter_dimension=0, tiled=True)
    return summed[0]


def local(
    decoder_states,
    memory_keys,
    memory_values,
    source_lengths,
    target_lengths,
    routes,
    attn_gain,
    ffn_gain,
    router,
    fc_in,
    fc_out,
):
    core = lax.axis_index("section").astype(jnp.int32).reshape(1)
    by_choice = jnp.transpose(routes, (0, 2, 1))
    state, keep, send, gates, by_choice = attend(
        core, decoder_states, memory_keys, memory_values, source_lengths, target_lengths, by_choice,
        attn_gain, ffn_gain, router,
    )
    block_rows = routes.shape[0] * routes.shape[1]
    experts_count = router.shape[1]
    capacity = 2 * max(1, 3 * block_rows // (2 * experts_count))
    if capacity % 16 == 0 and experts_count & (experts_count - 1) == 0:
        mixed = line_experts(core, state, keep, send, gates, by_choice, fc_in, fc_out, capacity)
    else:
        halves = jnp.stack([keep, send])
        normed = jnp.concatenate([halves[core[0]], halves[1 - core[0]]], axis=-1)
        summed = sparse_experts(normed, target_lengths, routes, router, fc_in, fc_out, capacity)
        mixed = (state.astype(jnp.float32) + summed).astype(jnp.bfloat16)
    return mixed[None]


def solution(mesh):
    placed = (
        P(("groups", "expert", "section"), None, None),
        P(("groups", "expert"), None, "section"),
        P(("groups", "expert"), None, "section"),
        P(("groups", "expert", "section")),
        P(("groups", "expert")),
        P(("groups", "expert"), None, None),
        P(),
        P(),
        P(),
        P(None, ("expert", "section")),
        P(("expert", "section"), None),
    )
    return jax.shard_map(
        local,
        mesh=mesh,
        in_specs=placed,
        out_specs=P(("groups", "expert", "section"), None, None),
        check_vma=False,
    )
```

```python
import functools

import jax
import jax.numpy as jnp
from jax import lax
from jax.experimental import pallas as pl
from jax.experimental.pallas import tpu as pltpu
from jax.sharding import PartitionSpec as P

HEAD_DIM = 128


def layer_norm(values, gain):
    centered = values - jnp.mean(values, axis=-1, keepdims=True)
    spread = jnp.mean(centered * centered, axis=-1, keepdims=True)
    return (centered * lax.rsqrt(spread + 1e-05) * gain).astype(jnp.bfloat16)


VMEM = pl.BlockSpec(memory_space=pltpu.VMEM)
SMEM = pl.BlockSpec(memory_space=pltpu.SMEM)
HBM = pl.BlockSpec(memory_space=pltpu.HBM)


def call(kernel, name, outs, scalars, arrays, far=(), scratch=(), vmem_mib=12):
    return pl.pallas_call(
        kernel,
        out_shape=tuple(jax.ShapeDtypeStruct(*out) for out in outs),
        in_specs=[SMEM] * len(scalars) + [VMEM] * len(arrays) + [HBM] * len(far),
        out_specs=(VMEM,) * len(outs),
        scratch_shapes=list(scratch),
        compiler_params=pltpu.CompilerParams(vmem_limit_bytes=vmem_mib * 2**20),
        name=name,
    )(*scalars, *arrays, *(pltpu.with_memory_space_constraint(a, pltpu.HBM) for a in far))


def fetch(sems, *pairs):
    copies = [
        pltpu.make_async_copy(source, target, sems.at[i]) for i, (source, target) in enumerate(pairs)
    ]
    for copy in copies:
        copy.start()
    return copies


def part_of(part, half):
    return pl.ds(pl.multiple_of(part * half, half), half)


def attend_half(queries, keys, values, length):
    rows = queries.shape[0]
    heads = [slice(at, at + HEAD_DIM) for at in range(0, queries.shape[1], HEAD_DIM)]
    scores = jnp.concatenate(
        [
            lax.dot_general(
                queries[:, head],
                keys[:, head],
                (((1,), (1,)), ((), ())),
                preferred_element_type=jnp.float32,
            )
            for head in heads
        ],
        axis=0,
    ) * HEAD_DIM ** (-0.5)
    valid = lax.broadcasted_iota(jnp.int32, (1, keys.shape[0]), 1) < length
    scores = jnp.where(valid, scores, -jnp.inf)
    expon = jnp.exp(scores - jnp.max(scores, axis=-1, keepdims=True))
    weights = (expon * (1.0 / jnp.sum(expon, axis=-1, keepdims=True))).astype(jnp.bfloat16)
    return jnp.concatenate(
        [
            jnp.dot(
                weights[i * rows : (i + 1) * rows],
                values[:, head],
                preferred_element_type=jnp.float32,
            )
            for i, head in enumerate(heads)
        ],
        axis=1,
    )


def add_rounded(x, attended):
    return (x.astype(jnp.float32) + attended).astype(jnp.bfloat16)


def attend_own_kernel(
    core_ref,
    source_ref,
    x_in,
    gain_in,
    keys_in,
    values_in,
    state_ref,
    query_ref,
    rest_ref,
    x_ref,
    gain_ref,
    keys_ref,
    values_ref,
    scratch_ref,
    sems,
):
    core = core_ref[0]
    copies = fetch(
        sems,
        (x_in.at[0], x_ref),
        (gain_in, gain_ref),
        (keys_in.at[core], keys_ref),
        (values_in.at[core], values_ref),
    )
    half = keys_ref.shape[1]
    copies[0].wait()
    copies[1].wait()
    scratch_ref[...] = layer_norm(x_ref[...].astype(jnp.float32), gain_ref[...])
    own, other = part_of(core, half), part_of(1 - core, half)
    query_ref[...] = scratch_ref[:, other]
    rest_ref[...] = x_ref[:, other]
    copies[2].wait()
    copies[3].wait()
    attended = attend_half(scratch_ref[:, own], keys_ref[...], values_ref[...], source_ref[0])
    state_ref[...] = add_rounded(x_ref[:, own], attended)


def attend_other_kernel(
    core_ref,
    source_ref,
    own_ref,
    query_ref,
    rest_ref,
    keys_ref,
    values_ref,
    gain_in,
    router_in,
    routes_in,
    target_in,
    state_ref,
    keep_ref,
    send_ref,
    gates_ref,
    routes_ref,
    gain_ref,
    router_ref,
    target_ref,
    scratch_ref,
    sems,
):
    core = core_ref[0]
    copies = fetch(
        sems,
        (gain_in, gain_ref),
        (router_in, router_ref),
        (routes_in, routes_ref),
        (target_in, target_ref),
    )
    full_len, half = own_ref.shape
    own, other = part_of(core, half), part_of(1 - core, half)
    attended = attend_half(query_ref[...], keys_ref[core], values_ref[core], source_ref[0])
    state_ref[:, own] = own_ref[...]
    state_ref[:, other] = add_rounded(rest_ref[...], attended)
    copies[0].wait()
    scratch_ref[...] = layer_norm(state_ref[...].astype(jnp.float32), gain_ref[...])
    keep_ref[...] = scratch_ref[:, own]
    send_ref[...] = scratch_ref[:, other]
    for copy in copies[1:]:
        copy.wait()
    logits = lax.dot_general(
        router_ref[...],
        scratch_ref[...],
        (((1,), (1,)), ((), ())),
        preferred_element_type=jnp.float32,
    )
    names = lax.broadcasted_iota(jnp.int32, logits.shape, 0)
    routes = routes_ref[core]
    chosen = [
        jnp.sum(jnp.where(names == routes[k : k + 1], logits, 0.0), axis=0, keepdims=True)
        for k in range(2)
    ]
    first = jax.nn.sigmoid(chosen[0] - chosen[1])
    live = lax.broadcasted_iota(jnp.int32, (1, full_len), 1) < target_ref[core]
    gates_ref[0:1] = jnp.where(live, first, 0.0)
    gates_ref[1:2] = jnp.where(live, 1.0 - first, 0.0)


def slots_of(routes_ref, experts_count):
    sents, _, full_len = routes_ref.shape
    rows = sents * full_len
    ids = lax.broadcasted_iota(jnp.int32, (max(8, experts_count), full_len), 0)
    named = jnp.concatenate(
        [
            jnp.where((ids == routes_ref[s, 0:1]) | (ids == routes_ref[s, 1:2]), 1.0, 0.0)
            for s in range(sents)
        ],
        axis=1,
    )
    before = lax.broadcasted_iota(jnp.int32, (rows, rows), 0) < lax.broadcasted_iota(
        jnp.int32, (rows, rows), 1
    )
    earlier = jnp.dot(
        named.astype(jnp.bfloat16),
        jnp.where(before, 1.0, 0.0).astype(jnp.bfloat16),
        preferred_element_type=jnp.float32,
    )
    return named > 0.0, earlier


def select_kernel(core_ref, line_ref, routes_ref, own_ref, other_ref, *rest):
    pieces, (slots_ref, block_ref) = rest[:-2], rest[-2:]
    experts_count = len(pieces)
    full_len = own_ref.shape[0]
    capacity = pieces[0].shape[0]
    core = core_ref[0]
    block_ref[part_of(core, full_len)] = own_ref[...]
    block_ref[part_of(1 - core, full_len)] = other_ref[...]
    named, earlier = slots_of(routes_ref, experts_count)
    slots_ref[...] = earlier
    slot = jnp.where(named, earlier, -1.0)
    ids = lax.broadcasted_iota(jnp.int32, slot.shape, 0)
    numbers = lax.broadcasted_iota(jnp.int32, (capacity, slot.shape[1]), 0).astype(jnp.float32)
    for offset, piece_ref in enumerate(pieces):
        expert = line_ref[0] ^ offset
        wanted = jnp.sum(jnp.where(ids == expert, slot, 0.0), axis=0, keepdims=True)
        picks = jnp.where(numbers == wanted, 1.0, 0.0).astype(jnp.bfloat16)
        piece_ref[...] = jnp.dot(
            picks, block_ref[...], preferred_element_type=jnp.float32
        ).astype(jnp.bfloat16)


def expert_kernel(
    core_ref, p_ref, q_ref, p2_ref, q2_ref, in_ref, out_ref, keep_ref, send_ref, rows_ref
):
    core = core_ref[0]
    capacity, half = p_ref.shape
    rows_ref[:capacity, part_of(core, half)] = p_ref[...]
    rows_ref[capacity:, part_of(core, half)] = q_ref[...]
    rows_ref[:capacity, part_of(1 - core, half)] = p2_ref[...]
    rows_ref[capacity:, part_of(1 - core, half)] = q2_ref[...]
    hidden = jnp.dot(rows_ref[...], in_ref[...], preferred_element_type=jnp.float32)
    hidden = jnp.maximum(hidden, 0.0).astype(jnp.bfloat16)
    send = jnp.dot(
        hidden, out_ref[:, part_of(1 - core, half)], preferred_element_type=jnp.float32
    ).astype(jnp.bfloat16)
    send_ref[0] = send[:capacity]
    send_ref[1] = send[capacity:]
    keep = jnp.dot(hidden, out_ref[:, part_of(core, half)], preferred_element_type=jnp.float32)
    keep_ref[0] = keep[:capacity]
    keep_ref[1] = keep[capacity:]


def load_kernel(in_in, out_in, in_ref, out_ref, sems):
    for copy in fetch(sems, (in_in, in_ref), (out_in, out_ref)):
        copy.wait()


def gated_sum(sent, line, routes, gates, slots_ref, pieces):
    full_len = routes.shape[1]
    experts_count = slots_ref.shape[0]
    parts = [slots_ref[:, at : at + full_len] for at in range(0, slots_ref.shape[1], full_len)]
    slots = jnp.where(sent == 0, parts[0], parts[1])
    ids = lax.broadcasted_iota(jnp.int32, (experts_count, full_len), 0)
    capacity = pieces[0].shape[0]
    numbers = lax.broadcasted_iota(jnp.int32, (full_len, capacity), 1).astype(jnp.float32)
    total = None
    for k in range(2):
        route = routes[k : k + 1]
        slot = jnp.sum(jnp.where(ids == route, slots, 0.0), axis=0, keepdims=True)
        place = (route ^ line).astype(jnp.float32) * capacity + slot
        place, gate = (
            jnp.broadcast_to(row, (full_len, full_len)).T[:, :1]
            for row in (place, gates[k : k + 1])
        )
        found = None
        for offset, piece in enumerate(pieces):
            picks = jnp.where(numbers == place - offset * capacity, 1.0, 0.0).astype(jnp.bfloat16)
            part = jnp.dot(picks, piece[...], preferred_element_type=jnp.float32)
            found = part if found is None else found + part
        total = gate * found if total is None else total + gate * found
    return total


def combine_other_kernel(core_ref, line_ref, routes_ref, gates_ref, slots_ref, *rest):
    pieces, other_ref = rest[:-1], rest[-1]
    sent = 1 - core_ref[0]
    other_ref[...] = gated_sum(
        sent, line_ref[0], routes_ref[sent], gates_ref[...], slots_ref, pieces
    ).astype(jnp.bfloat16)


def combine_own_kernel(core_ref, line_ref, routes_ref, gates_ref, slots_ref, state_ref, *rest):
    pieces, own_ref = rest[:-1], rest[-1]
    core = core_ref[0]
    summed = gated_sum(core, line_ref[0], routes_ref[core], gates_ref[...], slots_ref, pieces)
    own_ref[...] = add_rounded(state_ref[:, part_of(core, own_ref.shape[1])], summed)


def finish_kernel(core_ref, state_ref, own_ref, other_ref, mixed_ref):
    core = core_ref[0]
    half = own_ref.shape[-1]
    mixed_ref[:, part_of(core, half)] = own_ref[...]
    span = part_of(1 - core, half)
    mixed_ref[:, span] = add_rounded(state_ref[:, span], other_ref[...].astype(jnp.float32))


def swap(values):
    return lax.ppermute(values, "section", [(0, 1), (1, 0)])


def swap_owner(values):
    owners = lax.axis_size("expert")
    return lax.ppermute(values, "expert", [(i, i ^ 1) for i in range(owners)])


def exchange(values, offset):
    owners = lax.axis_size("expert")
    return lax.ppermute(values, "expert", [(i, i ^ (2 * offset)) for i in range(owners)])


def after_kernel(*refs):
    pass


def after(value, *firsts):
    return pl.pallas_call(
        after_kernel,
        out_shape=jax.ShapeDtypeStruct(value.shape, value.dtype),
        in_specs=[pl.BlockSpec(memory_space=pl.ANY)] * (1 + len(firsts)),
        out_specs=pl.BlockSpec(memory_space=pl.ANY),
        input_output_aliases={0: 0},
        compiler_params=pltpu.CompilerParams(vmem_limit_bytes=2**20),
        name="after",
    )(value, *firsts)


def attend(
    core, decoder_states, memory_keys, memory_values, source_lengths, target_lengths, routes,
    attn_gain, ffn_gain, router,
):
    full_len, width = decoder_states.shape[1:]
    half = (full_len, width // 2)
    memory = memory_keys.shape[1:]
    other_keys, other_values = swap(memory_keys), swap(memory_values)
    own, query, rest = call(
        attend_own_kernel,
        "attend_own",
        [(half, jnp.bfloat16)] * 3,
        [core, source_lengths],
        [],
        [decoder_states, attn_gain[None], memory_keys, memory_values],
        scratch=[
            pltpu.VMEM((full_len, width), jnp.bfloat16),
            pltpu.VMEM((1, width), jnp.float32),
            pltpu.VMEM(memory, jnp.bfloat16),
            pltpu.VMEM(memory, jnp.bfloat16),
            pltpu.VMEM((full_len, width), jnp.bfloat16),
            pltpu.SemaphoreType.DMA((4,)),
        ],
    )
    return call(
        attend_other_kernel,
        "attend_other",
        [
            ((full_len, width), jnp.bfloat16),
            (half, jnp.bfloat16),
            (half, jnp.bfloat16),
            ((2, full_len), jnp.float32),
            (routes.shape, jnp.int32),
        ],
        [core, source_lengths],
        [own, query, rest, other_keys, other_values],
        [ffn_gain[None], router.T, routes, target_lengths],
        scratch=[
            pltpu.VMEM((1, width), jnp.float32),
            pltpu.VMEM(router.shape[::-1], jnp.bfloat16),
            pltpu.SMEM(target_lengths.shape, jnp.int32),
            pltpu.VMEM((full_len, width), jnp.bfloat16),
            pltpu.SemaphoreType.DMA((4,)),
        ],
    )


def line_experts(core, state, keep, send, gates, routes, fc_in, fc_out, capacity):
    full_len, width = state.shape
    half = width // 2
    count = lax.axis_size("expert") // 2
    line = (lax.axis_index("expert") // 2).astype(jnp.int32).reshape(1)
    other = swap(send)
    other_gates = swap(gates)
    piece = ((capacity, half), jnp.bfloat16)
    *selected, slots = call(
        select_kernel,
        "select",
        [piece] * count + [((max(8, count), 2 * full_len), jnp.float32)],
        [core, line],
        [routes, keep, other],
        scratch=[pltpu.VMEM((2 * full_len, half), jnp.bfloat16)],
    )
    near_in, near_out = call(
        load_kernel,
        "load",
        [(fc_in.shape, jnp.bfloat16), (fc_out.shape, jnp.bfloat16)],
        [],
        [],
        [fc_in, fc_out],
        scratch=[pltpu.SemaphoreType.DMA((2,))],
    )
    def run(p, q, p2, q2):
        keep, sent = call(
            expert_kernel,
            "expert",
            [((2, capacity, half), jnp.float32), ((2, capacity, half), jnp.bfloat16)],
            [core],
            [p, q, p2, q2, near_in, near_out],
            scratch=[pltpu.VMEM((2 * capacity, width), jnp.bfloat16)],
            vmem_mib=16,
        )
        return keep, swap(sent)

    def sums(keep, moving):
        both = keep + moving.astype(jnp.float32)
        return both, both[1].astype(jnp.bfloat16)

    def whole(both, across):
        return (both[0] + across.astype(jnp.float32)).astype(jnp.bfloat16)

    travelling = [exchange(selected[r], r) for r in range(1, count)]
    home = [None] * count
    ps, qs, kept, halves, wholes, boths = {}, {}, {}, {}, {}, {}
    p = selected[0]
    q = swap_owner(p)
    ps[0], qs[0] = p, q
    p = travelling[0]
    p = after(p, near_in)
    q = swap_owner(p)
    ps[1], qs[1] = p, q
    p = travelling[1]
    q = swap_owner(p)
    ps[2], qs[2] = p, q
    p = travelling[2]
    q = swap_owner(p)
    ps[3], qs[3] = p, q
    p, q = ps[0], qs[0]
    p2, q2 = swap(p), swap(q)
    kept[0], moving = run(p, q, p2, q2)
    boths[0], halves[0] = sums(kept[0], moving)
    p, q = ps[1], qs[1]
    p2, q2 = swap(p), swap(q)
    kept[1], moving = run(p, q, p2, q2)
    boths[1], halves[1] = sums(kept[1], moving)
    p, q = ps[2], qs[2]
    p2, q2 = swap(p), swap(q)
    q2 = after(q2, kept[0], kept[1])
    kept[2], moving = run(p, q, p2, q2)
    boths[2], halves[2] = sums(kept[2], moving)
    p, q = ps[3], qs[3]
    q = after(q, kept[2])
    p2, q2 = swap(p), swap(q)
    q2 = after(q2, halves[2])
    kept[3], moving = run(p, q, p2, q2)
    boths[3], halves[3] = sums(kept[3], moving)
    leaving = halves[2]
    across = swap_owner(leaving)
    wholes[2] = whole(boths[2], across)
    home[2] = exchange(wholes[2], 2)
    leaving = halves[3]
    across = swap_owner(leaving)
    wholes[3] = whole(boths[3], across)
    home[3] = exchange(wholes[3], 3)
    leaving = halves[1]
    leaving = after(leaving, halves[3])
    across = swap_owner(leaving)
    wholes[1] = whole(boths[1], across)
    home[1] = exchange(wholes[1], 1)
    leaving = halves[0]
    leaving = after(leaving, wholes[3])
    across = swap_owner(leaving)
    wholes[0] = whole(boths[0], across)
    home[0] = wholes[0]
    (leaving,) = call(
        combine_other_kernel,
        "combine_other",
        [((full_len, half), jnp.bfloat16)],
        [core, line],
        [routes, other_gates, slots, *home],
    )
    arriving = swap(leaving)
    (own,) = call(
        combine_own_kernel,
        "combine_own",
        [((full_len, half), jnp.bfloat16)],
        [core, line],
        [routes, gates, slots, state, *home],
    )
    (mixed,) = call(
        finish_kernel,
        "finish",
        [((full_len, width), jnp.bfloat16)],
        [core],
        [state, own, arriving],
    )
    return mixed


def expert_apply(slot_rows, fc_in, fc_out):
    width = slot_rows.shape[-1]
    flat_rows = slot_rows.reshape(-1, width)
    hidden = jax.nn.relu(jnp.dot(flat_rows, fc_in, preferred_element_type=jnp.float32)).astype(
        jnp.bfloat16
    )
    produced = jnp.dot(hidden, fc_out, preferred_element_type=jnp.float32)
    return produced.reshape(slot_rows.shape[0], slot_rows.shape[1], width)


def sparse_experts(normed, target_lengths, routes, router, fc_in, fc_out, capacity):
    full_len, width = normed.shape
    all_normed = lax.all_gather(normed[None], "section", axis=0, tiled=True)
    block_sents = all_normed.shape[0]
    block_rows = block_sents * full_len
    tok_rows = all_normed.reshape(block_rows, width)
    owners = lax.axis_size("expert")
    experts_count = owners // 2
    chosen_ids = routes.reshape(block_rows, 2)
    logits = jnp.dot(tok_rows, router, preferred_element_type=jnp.float32)
    onehot = chosen_ids[:, :, None] == jnp.arange(experts_count, dtype=jnp.int32)
    chosen = jnp.sum(jnp.where(onehot, logits[:, None, :], 0.0), axis=-1)
    first = jax.nn.sigmoid(chosen[:, 0] - chosen[:, 1])
    gates = jnp.stack([first, 1.0 - first], axis=-1)
    live = (jnp.arange(full_len, dtype=jnp.int32)[None, :] < target_lengths[:, None]).reshape(
        block_rows
    )
    flags = onehot.reshape(block_rows * 2, experts_count).astype(jnp.int32)
    earlier = jnp.cumsum(flags, axis=0) - flags
    slot = jnp.sum(flags * earlier, axis=-1).reshape(block_rows, 2)
    position = chosen_ids * capacity + slot
    dump_index = experts_count * capacity
    target = jnp.where(live[:, None], position, dump_index)
    row_ids = jnp.broadcast_to(jnp.arange(block_rows, dtype=jnp.int32)[:, None], (block_rows, 2))
    table = (
        jnp.full((dump_index + 1,), block_rows, jnp.int32)
        .at[target.reshape(-1)]
        .set(row_ids.reshape(-1))[:dump_index]
    )
    padded = jnp.concatenate([tok_rows, jnp.zeros((1, width), jnp.bfloat16)], axis=0)
    slot_buffer = padded[table].reshape(experts_count, capacity, width)
    outgoing = jnp.repeat(slot_buffer, 2, axis=0)
    returned = lax.all_to_all(
        expert_apply(
            lax.all_to_all(outgoing, "expert", split_axis=0, concat_axis=0, tiled=True),
            fc_in,
            fc_out,
        ).astype(jnp.bfloat16),
        "expert",
        split_axis=0,
        concat_axis=0,
        tiled=True,
    ).astype(jnp.float32)
    partial_value = jnp.sum(returned.reshape(experts_count, 2, capacity, width), axis=1)
    fetched = partial_value.reshape(dump_index, width)[jnp.where(live[:, None], position, 0)]
    weight = gates * live[:, None].astype(jnp.float32)
    contrib = jnp.sum(weight[:, :, None] * fetched, axis=1).reshape(block_sents, full_len, width)
    summed = lax.psum_scatter(contrib, "section", scatter_dimension=0, tiled=True)
    return summed[0]


def local(
    decoder_states,
    memory_keys,
    memory_values,
    source_lengths,
    target_lengths,
    routes,
    attn_gain,
    ffn_gain,
    router,
    fc_in,
    fc_out,
):
    core = lax.axis_index("section").astype(jnp.int32).reshape(1)
    by_choice = jnp.transpose(routes, (0, 2, 1))
    state, keep, send, gates, by_choice = attend(
        core, decoder_states, memory_keys, memory_values, source_lengths, target_lengths, by_choice,
        attn_gain, ffn_gain, router,
    )
    block_rows = routes.shape[0] * routes.shape[1]
    experts_count = router.shape[1]
    capacity = 2 * max(1, 3 * block_rows // (2 * experts_count))
    if capacity % 16 == 0 and experts_count & (experts_count - 1) == 0:
        mixed = line_experts(core, state, keep, send, gates, by_choice, fc_in, fc_out, capacity)
    else:
        halves = jnp.stack([keep, send])
        normed = jnp.concatenate([halves[core[0]], halves[1 - core[0]]], axis=-1)
        summed = sparse_experts(normed, target_lengths, routes, router, fc_in, fc_out, capacity)
        mixed = (state.astype(jnp.float32) + summed).astype(jnp.bfloat16)
    return mixed[None]


def solution(mesh):
    placed = (
        P(("groups", "expert", "section"), None, None),
        P(("groups", "expert"), None, "section"),
        P(("groups", "expert"), None, "section"),
        P(("groups", "expert", "section")),
        P(("groups", "expert")),
        P(("groups", "expert"), None, None),
        P(),
        P(),
        P(),
        P(None, ("expert", "section")),
        P(("expert", "section"), None),
    )
    return jax.shard_map(
        local,
        mesh=mesh,
        in_specs=placed,
        out_specs=P(("groups", "expert", "section"), None, None),
        check_vma=False,
    )
```
